32 devices in a mesh: seq: 8 (over z, y), head: 4 (over x, core).
Axes of the slice: x: 2, y: 2, z: 4, core: 2. Of those that a mesh axis runs over, the one named last changes fastest.
Arguments:
- hidden_in: bfloat16 [2, 16384, 768], P(None, 'seq'), may hold values from -6 to 6
- output_cotangent: bfloat16 [2, 16384, 768], P(None, 'seq', 'head'), may hold values from -6 to 6
- input_norm_scale_gain: float32 [768], replicated, may hold values from 0.5 to 1.5
- z_proj: bfloat16 [768, 1536], P(None, 'head'), may hold values from -0.21875 to 0.21875
- x_proj: bfloat16 [768, 1536], P(None, 'head'), may hold values from -0.21875 to 0.21875
- bc_proj: bfloat16 [768, 256], replicated, may hold values from -0.21875 to 0.21875
- dt_proj: bfloat16 [768, 24], P(None, 'head'), may hold values from -0.21875 to 0.21875
- conv_x_weight: float32 [1536, 4], P('head'), may hold values from -3 to 3
- conv_x_bias: float32 [1536], P('head'), may hold values from -1.2 to 1.2
- conv_bc_weight: float32 [256, 4], replicated, may hold values from -3 to 3
- conv_bc_bias: float32 [256], replicated, may hold values from -1.2 to 1.2
- dt_bias: float32 [24], P('head'), may hold values from -2 to 0.5
- a_log: float32 [24], P('head')
- d_skip: float32 [24], P('head'), may hold values from 0.5 to 1.5
- out_norm_gain: float32 [1536], P('head'), may hold values from 0.5 to 1.5
- out_proj: bfloat16 [1536, 768], P('head'), may hold values from -0.15625 to 0.15625
- doc_starts: int32 [2, 84], replicated, may hold values from 0 to 16384, as said below
Outputs:
- layer_out: bfloat16 [2, 16384, 768], P(None, 'seq', 'head')
- input_grad: bfloat16 [2, 16384, 768], P(None, 'seq', 'head')
- grad_in_norm_gain: float32 [768], P('head')
- grad_z_proj: float32 [768, 1536], P(None, 'head')
- grad_x_proj: float32 [768, 1536], P(None, 'head')
- grad_bc_proj: float32 [768, 256], replicated
- grad_dt_proj: float32 [768, 24], P(None, 'head')
- grad_conv_x_weight: float32 [1536, 4], P('head')
- grad_conv_x_bias: float32 [1536], P('head')
- grad_conv_bc_weight: float32 [256, 4], replicated
- grad_conv_bc_bias: float32 [256], replicated
- grad_dt_bias: float32 [24], P('head')
- grad_a_log: float32 [24], P('head')
- grad_d_skip: float32 [24], P('head')
- grad_out_norm_gain: float32 [1536], P('head')
- grad_out_proj: float32 [1536, 768], P('head')
The draws below stay inside these ranges and needn't reach their ends.
Inputs may be any that keep to these rules, and one draw needn't show every extreme that they name: doc_starts[b] holds the first positions of sequence b's documents in rising order, beginning with 0; every slot after the last document holds 16384.
All inputs are finite; a program needn't handle non-finite values.
Results may differ from the reference program's by a relative error of at most 0.0075.
The reference program's roundings to bfloat16 on the way count: a program that leaves them out, or rounds other values in their place, can miss the bound.
Values may be sent and summed in bfloat16 or wider, within the bound.
A program may use at most 256 MiB of HBM per device.

```python
import math
import jax
import jax.numpy as jnp
from jax import lax

D = 768
DI = 1536
HEADS = 24
STATE = 128
CONV = 4
GROUP = 256
TOK_DEV = 2048
BATCH = 2
DOC_LO = 200
DOC_HI = 2000
SEQ_LEN = 16384
DOCS = 84


def draw_a_log(key, part):
    key = jax.random.fold_in(key, 7)
    share = 0.5
    chosen = jax.random.uniform(jax.random.fold_in(key, 1), (HEADS,)) < share
    slow_rate = jnp.exp(jax.random.uniform(jax.random.fold_in(key, 2), (HEADS,), minval=math.log(0.3), maxval=math.log(1.5))) / SEQ_LEN
    fast_rate = jnp.exp(jax.random.uniform(jax.random.fold_in(key, 3), (HEADS,), minval=math.log(0.05), maxval=math.log(0.1)))
    return jnp.log(jnp.where(chosen, slow_rate, fast_rate)).astype(jnp.float32)


def draw_doc_starts(key, part):
    key = jax.random.fold_in(key, 11)
    pick = jax.random.randint(jax.random.fold_in(key, 1), (), 0, BATCH)
    lengths = jax.random.randint(jax.random.fold_in(key, 2), (BATCH, DOCS), DOC_LO, DOC_HI + 1)
    starts = jnp.minimum(jnp.cumsum(lengths, axis=1) - lengths, SEQ_LEN)
    head_len = jax.random.randint(jax.random.fold_in(key, 3), (), 1, TOK_DEV)
    tail_len = jax.random.randint(jax.random.fold_in(key, 4), (), 1, TOK_DEV)
    slots = jnp.arange(DOCS, dtype=jnp.int32)
    spanning = jnp.where(slots == 0, 0, jnp.where(slots == 1, head_len, jnp.where(slots == 2, SEQ_LEN - tail_len, SEQ_LEN)))
    rows = jnp.arange(BATCH, dtype=jnp.int32)[:, None]
    return jnp.where(rows == pick, spanning[None, :], starts).astype(jnp.int32)


def levels(stream_key, extent, cuts, least, largest):
    level = 1.0
    for position, blocks in cuts:
        draws = jax.random.uniform(jax.random.fold_in(jax.random.fold_in(stream_key, 6), position), (blocks,), jnp.float32, least / len(cuts), largest / len(cuts))
        level = level * jnp.repeat(jnp.exp(draws), extent[position] // blocks).reshape((-1,) + (1,) * (len(extent) - 1 - position))
    return level


def noise(own_key, extent, scale, most, shards=(), kind=jnp.bfloat16):
    drawn = jax.random.normal(own_key, extent, jnp.float32) * scale
    if len(shards) > 0:
        drawn = levels(own_key, extent, shards, -0.22, 0.18) * drawn
    return jnp.clip(drawn, min=-most, max=most).astype(kind)


def setup_inputs(seed: int = 0) -> dict:
    splits = jax.random.split(jax.random.key(seed), 18)
    return {
        "hidden_in": noise(splits[0], (BATCH, SEQ_LEN, D), 1.0, 6.0, ((1, 8),)),
        "output_cotangent": noise(splits[1], (BATCH, SEQ_LEN, D), 1.0, 6.0, ((1, 8), (2, 4))),
        "input_norm_scale_gain": jnp.clip(1.0 + 0.1 * jax.random.normal(splits[2], (D,), jnp.float32), 0.5, 1.5),
        "z_proj": noise(splits[3], (D, DI), D ** -0.5, 0.21875, ((1, 4),)),
        "x_proj": noise(splits[4], (D, DI), D ** -0.5, 0.21875, ((1, 4),)),
        "bc_proj": noise(splits[5], (D, 2 * STATE), D ** -0.5, 0.21875),
        "dt_proj": noise(splits[6], (D, HEADS), D ** -0.5, 0.21875, ((1, 4),)),
        "conv_x_weight": noise(splits[7], (DI, CONV), CONV ** -0.5, 3.0, ((0, 4),), jnp.float32),
        "conv_x_bias": noise(splits[8], (DI,), 0.3, 1.2, ((0, 4),), jnp.float32),
        "conv_bc_weight": noise(splits[9], (2 * STATE, CONV), CONV ** -0.5, 3.0, (), jnp.float32),
        "conv_bc_bias": noise(splits[10], (2 * STATE,), 0.3, 1.2, (), jnp.float32),
        "dt_bias": jnp.clip(-2.0 + 2.5 * jax.random.uniform(splits[11], (HEADS,), jnp.float32) ** levels(splits[11], (HEADS,), ((0, 4),), -0.2, 0.2), -2.0, 0.5),
        "a_log": draw_a_log(jax.random.fold_in(splits[17], 71), 0),
        "d_skip": jnp.clip(0.5 + 1.0 * jax.random.uniform(splits[13], (HEADS,), jnp.float32) ** levels(splits[13], (HEADS,), ((0, 4),), -0.2, 0.2), 0.5, 1.5),
        "out_norm_gain": jnp.clip(1.0 + 0.1 * jax.random.normal(splits[14], (DI,), jnp.float32), 0.5, 1.5),
        "out_proj": noise(splits[15], (DI, D), DI ** -0.5, 0.15625, ((0, 4),)),
        "doc_starts": draw_doc_starts(jax.random.fold_in(splits[17], 71), 0),
    }


highest = lax.Precision.HIGHEST
epsilon = 1e-05

@jax.custom_vjp
def low(v):
    return lax.optimization_barrier(v.astype(jnp.bfloat16)).astype(jnp.float32)

@jax.custom_vjp
def low_back(v):
    return v

def low_keep(v):
    return (low(v), None)

def low_pass(kept, grad):
    return (grad,)

def back_keep(v):
    return (v, None)

def back_low(kept, grad):
    return (low(grad),)
low.defvjp(low_keep, low_pass)
low_back.defvjp(back_keep, back_low)

def segment_ids(doc_starts, length):
    places = jnp.arange(length, dtype=jnp.int32)
    counted = lax.optimization_barrier(jnp.sum((doc_starts[:, None, :] <= places[None, :, None]).astype(jnp.int32), axis=-1))
    return counted.astype(jnp.int32) - 1

def group_step(carry, block):
    states, seg_prev = carry
    values, bmat, cmat, delta, logdec, seg = block
    span = seg.shape[1]
    cumul = jnp.cumsum(logdec, axis=1)
    causal = jnp.arange(span)[:, None] >= jnp.arange(span)[None, :]
    inside = (seg[:, :, None] == seg[:, None, :]) & causal
    spread = cumul[:, :, None, :] - cumul[:, None, :, :]
    decay = jnp.exp(jnp.where(inside[..., None], spread, -jnp.inf))
    scores = jnp.einsum('btn,bsn->bts', cmat, bmat, precision=highest)
    weights = low(scores[..., None] * decay * delta[:, None, :, :])
    intra = jnp.einsum('btsh,bshp->bthp', weights, values, precision=highest)
    ending = cumul[:, -1]
    kappa = jnp.where((seg == seg_prev[:, None])[..., None], jnp.exp(cumul), 0.0)
    inter = kappa[..., None] * jnp.einsum('btn,bhpn->bthp', cmat, states, precision=highest)
    tail_keep = jnp.where((seg == seg[:, -1:])[..., None], jnp.exp(ending[:, None, :] - cumul), 0.0)
    omega = tail_keep * delta
    own_state = jnp.einsum('bshp,bsn->bhpn', values * omega[..., None], bmat, precision=highest)
    carry_keep = jnp.where((seg[:, -1] == seg_prev)[:, None], jnp.exp(ending), 0.0)
    return ((carry_keep[..., None, None] * states + own_state, seg[:, -1].astype(jnp.int32)), intra + inter)

def forward(hidden, norm_gain, z_proj, x_proj, bc_proj, dt_proj, conv_x_weight, conv_x_bias, conv_bc_weight, conv_bc_bias, dt_bias, a_log, d_skip, out_norm_gain, out_proj, seg):
    batch, length, feature_width = hidden.shape
    inner = z_proj.shape[1]
    heads = dt_proj.shape[1]
    head_dim = inner // heads
    state_dim = bc_proj.shape[1] // 2
    taps = conv_x_weight.shape[1]
    reciprocal_root = lax.rsqrt(lax.optimization_barrier(jnp.mean(hidden * hidden, axis=-1, keepdims=True)) + epsilon)
    normalized_rows = low(hidden * reciprocal_root * norm_gain)
    gate = low_back(jnp.einsum('bld,de->ble', normalized_rows, z_proj, precision=highest))
    mixed = jnp.concatenate([jnp.einsum('bld,de->ble', normalized_rows, x_proj, precision=highest), jnp.einsum('bld,de->ble', normalized_rows, bc_proj, precision=highest)], axis=-1)
    conv_in = low(low_back(mixed))
    raw_dt = low_back(jnp.einsum('bld,de->ble', normalized_rows, dt_proj, precision=highest))
    conv_weight = jnp.concatenate([conv_x_weight, conv_bc_weight], axis=0)
    conv_bias = jnp.concatenate([conv_x_bias, conv_bc_bias], axis=0)
    padded = jnp.pad(conv_in, ((0, 0), (taps - 1, 0), (0, 0)))
    seg_pad = jnp.pad(seg, ((0, 0), (taps - 1, 0)), constant_values=-1)
    conv_out = jnp.broadcast_to(conv_bias, conv_in.shape)
    for tap_index in range(taps):
        same_doc = (seg_pad[:, tap_index:tap_index + length] == seg)[..., None]
        conv_out = conv_out + jnp.where(same_doc, padded[:, tap_index:tap_index + length] * conv_weight[:, tap_index], 0.0)
    activ = low(jax.nn.silu(conv_out))
    values = activ[..., :inner].reshape(batch, length, heads, head_dim)
    bmat = activ[..., inner:inner + state_dim]
    cmat = activ[..., inner + state_dim:]
    delta = jax.nn.softplus(raw_dt + dt_bias)
    logdec = -delta * jnp.exp(a_log)
    count = length // GROUP

    def blocks(array):
        return jnp.moveaxis(array.reshape((batch, count, GROUP) + array.shape[2:]), 1, 0)
    start = (jnp.zeros((batch, heads, head_dim, state_dim), hidden.dtype), jnp.full((batch,), -1, jnp.int32))
    _, pieces = lax.scan(jax.checkpoint(group_step), start, (blocks(values), blocks(bmat), blocks(cmat), blocks(delta), blocks(logdec), blocks(seg)))
    ssd = jnp.moveaxis(pieces, 0, 1).reshape(batch, length, heads, head_dim)
    ssd = low_back((ssd + d_skip[:, None] * values).reshape(batch, length, inner))
    gated = ssd * jax.nn.silu(gate)
    norm_scale = lax.rsqrt(lax.optimization_barrier(jnp.mean(gated * gated, axis=-1, keepdims=True)) + epsilon)
    normed_out = low(gated * norm_scale * out_norm_gain)
    return hidden + jnp.einsum('ble,ed->bld', normed_out, out_proj, precision=highest)

def reference(hidden_in, output_cotangent, input_norm_scale_gain, z_proj, x_proj, bc_proj, dt_proj, conv_x_weight, conv_x_bias, conv_bc_weight, conv_bc_bias, dt_bias, a_log, d_skip, out_norm_gain, out_proj, doc_starts):
    seg = segment_ids(doc_starts, hidden_in.shape[1])
    floats = [item.astype(jnp.float32) for item in (hidden_in, input_norm_scale_gain, z_proj, x_proj, bc_proj, dt_proj, conv_x_weight, conv_x_bias, conv_bc_weight, conv_bc_bias, dt_bias, a_log, d_skip, out_norm_gain, out_proj)]

    def apply(*params):
        return forward(*params, seg)
    output, pullback = jax.vjp(apply, *floats)
    grads = pullback(output_cotangent.astype(jnp.float32))
    return (output.astype(jnp.bfloat16), grads[0].astype(jnp.bfloat16), grads[1], grads[2], grads[3], grads[4], grads[5], grads[6], grads[7], grads[8], grads[9], grads[10], grads[11], grads[12], grads[13], grads[14])
```

```python
import functools

import jax
import jax.numpy as jnp
import numpy as np
from jax import lax
from jax.experimental import pallas as pl
from jax.experimental.pallas import tpu as pltpu
from jax.sharding import PartitionSpec as P

GROUP = 256
HALF = 128
LANES = 128
HEAD_DIM = 64
EPS = 1e-05
LOG2E = 1.4426950408889634
f32 = jnp.float32
bf16 = jnp.bfloat16
HIGHEST = lax.Precision.HIGHEST
ROWS = 32


def dot(a, b, ca=1, cb=0, precision=None):
    return lax.dot_general(
        a, b, (((ca,), (cb,)), ((), ())), precision=precision, preferred_element_type=f32
    )


def split2(x):
    hi = x.astype(bf16)
    return hi, (x - hi.astype(f32)).astype(bf16)


def expand(x, ex):
    hi = x.astype(bf16).astype(f32)
    rest = x - hi
    mid = rest.astype(bf16).astype(f32)
    low = rest - mid
    packed = hi + pltpu.roll(mid, 32, 1) + pltpu.roll(low, 64, 1)
    return dot(packed.astype(bf16), ex)


def lanes_below(x, count):
    return jnp.where(lax.broadcasted_iota(jnp.int32, x.shape, 1) < count, x, 0.0)


def sigmoid(x):
    return 1.0 / (1.0 + jnp.exp(-x))


def softplus(x):
    return jnp.maximum(x, 0.0) + jnp.log1p(jnp.exp(-jnp.abs(x)))


def fold8(x):
    total = x[0:8]
    for r in range(8, x.shape[0], 8):
        total = total + x[r : r + 8]
    return total


def expansion(width):
    heads = width // HEAD_DIM
    ex = np.zeros((LANES, width), np.float32)
    for part in range(3):
        for h in range(heads):
            ex[32 * part + h, h * HEAD_DIM : (h + 1) * HEAD_DIM] = 1.0
    red = np.zeros((width, LANES), np.float32)
    for h in range(heads):
        red[h * HEAD_DIM : (h + 1) * HEAD_DIM, h] = 1.0
    return jnp.asarray(ex, bf16), jnp.asarray(red, bf16)


def run(kernel, grid, ins, outs, scratch=(), flops=0, moved=0, prefetch=()):
    def spec(shape, block, imap):
        if block is None:
            rank = len(shape)
            return pl.BlockSpec(shape, lambda *_: (0,) * rank)
        return pl.BlockSpec(block, imap)

    return pl.pallas_call(
        kernel,
        grid_spec=pltpu.PrefetchScalarGridSpec(
            num_scalar_prefetch=len(prefetch),
            grid=grid,
            in_specs=[spec(a.shape, b, m) for a, b, m in ins],
            out_specs=[spec(s, b, m) for s, _, b, m in outs],
            scratch_shapes=list(scratch),
        ),
        out_shape=[jax.ShapeDtypeStruct(s, d) for s, d, _, _ in outs],
        compiler_params=pltpu.CompilerParams(vmem_limit_bytes=56 << 20),
        cost_estimate=pl.CostEstimate(flops=flops, bytes_accessed=moved, transcendentals=0),
    )(*prefetch, *[a for a, _, _ in ins])


def conv_rows(ext, age, taps, bias, r, cols):
    acc = jnp.broadcast_to(bias[:, cols], (ROWS, LANES))
    for k in range(4):
        back = 3 - k
        term = ext[8 + r - back : 8 + r - back + ROWS, cols] * taps[k : k + 1, cols]
        if back:
            term = jnp.where(age >= back, term, 0.0)
        acc = acc + term
    return acc


def norm_kernel(
    meta, hid, edge, gain, bc, taps, bias, age, normed, nedge, ci, co, bmat, cmat, ext
):
    def rms(x):
        x = x.astype(f32)
        r = lax.rsqrt(jnp.sum(x * x, axis=1, keepdims=True) / x.shape[1] + EPS)
        return (x * r * gain[...]).astype(bf16)

    @pl.when(pl.program_id(0) == 0)
    def _():
        rows = rms(edge[...])
        nedge[...] = rows
        ext[0:8] = dot(rows, bc[...]).astype(bf16).astype(f32)[8:16]

    @pl.when(pl.program_id(0) > 0)
    def _():
        ext[0:8] = ext[GROUP : GROUP + 8]

    for r in range(0, GROUP, ROWS):
        normed[r : r + ROWS] = rms(hid[0, r : r + ROWS])
    low = dot(normed[...], bc[...]).astype(bf16)
    ci[...] = low
    ext[8 : 8 + GROUP] = low.astype(f32)
    for r in range(0, GROUP, ROWS):
        a = age[r : r + ROWS]
        for j, out in enumerate((bmat, cmat)):
            cols = slice(j * LANES, (j + 1) * LANES)
            v = conv_rows(ext, a, taps, bias, r, cols)
            co[r : r + ROWS, cols] = v
            out[r : r + ROWS] = (v * sigmoid(v)).astype(bf16)


def front_kernel(
    normed, nedge, wa, wb, taps, bias, dtp, dtb, rate, bmat, age, tril, ex,
    ci, co, val, pre, cum, lin, kb, ck, tot, ktot,
    ext, running, kept, omx, ohi, olo,
):
    i = pl.program_id(0)
    width = val.shape[1]
    part = width // 2

    @pl.when(i == 0)
    def _():
        running[...] = jnp.zeros_like(running)
        kept[...] = jnp.ones_like(kept)
        for w, at in ((wa, 0), (wb, part)):
            ext[0:8, at : at + part] = dot(nedge[...], w[...]).astype(bf16).astype(f32)[8:16]

    @pl.when(i > 0)
    def _():
        ext[0:8] = ext[GROUP : GROUP + 8]

    for w, at in ((wa, 0), (wb, part)):
        low = dot(normed[...], w[...]).astype(bf16)
        ci[:, at : at + part] = low
        ext[8 : 8 + GROUP, at : at + part] = low.astype(f32)
    raw = dot(normed[...], dtp[...], 1, 1) + dtb[...]
    pre[...] = raw
    delta = softplus(raw)
    c = dot(tril[...], delta * rate[...], precision=HIGHEST)
    cum[...] = c
    end = c[GROUP - 1 : GROUP]
    age_end = age[GROUP - 1 : GROUP]
    left = GROUP - 1 - lax.broadcasted_iota(jnp.int32, c.shape, 0)
    omega = jnp.where(left <= age_end, jnp.exp(end - c), 0.0) * delta
    omx[...] = expand(lanes_below(omega, width // HEAD_DIM), ex[...])
    keep = jnp.where(age_end >= GROUP, jnp.exp(end), 0.0)
    keep = lanes_below(jnp.broadcast_to(keep, (8, LANES)), width // HEAD_DIM)
    keepx = expand(keep, ex[...])
    for r in range(0, GROUP, ROWS):
        a = age[r : r + ROWS]
        rows = slice(r, r + ROWS)
        for j in range(width // LANES):
            cols = slice(j * LANES, (j + 1) * LANES)
            v = conv_rows(ext, a, taps, bias, r, cols)
            co[rows, cols] = v
            act = (v * sigmoid(v)).astype(bf16)
            val[rows, cols] = act
            ohi[rows, cols], olo[rows, cols] = split2(omx[rows, cols] * act.astype(f32))
    own = dot(bmat[...], ohi[...], 0, 0) + dot(bmat[...], olo[...], 0, 0)
    lin[0] = running[...]
    kb[0] = kept[...]
    ck[0] = keepx
    running[...] = keepx[0:1] * running[...] + own
    kept[...] = keepx * kept[...]
    tot[...] = running[...]
    ktot[...] = kept[...]


def pair_masks(x, lane_axis_shape):
    lane = lax.broadcasted_iota(jnp.int32, lane_axis_shape, 1)
    zero = jnp.zeros_like(x)
    return jnp.where(lane < HEAD_DIM, x, zero), jnp.where(lane >= HEAD_DIM, x, zero)


def intra_kernel(val, bmat, cmat, age, pre, cum, dskip, part):
    t = lax.broadcasted_iota(jnp.int32, (HALF, HALF), 0)
    s = lax.broadcasted_iota(jnp.int32, (HALF, HALF), 1)
    scores = dot(cmat[...], bmat[...], 1, 1)
    a0, a1 = age[0:HALF], age[HALF:]
    gap = t - s
    s00 = jnp.where((gap >= 0) & (gap <= a0), scores[:HALF, :HALF], 0.0)
    s11 = jnp.where((gap >= 0) & (gap <= a1), scores[HALF:, HALF:], 0.0)
    s10 = jnp.where(gap + HALF <= a1, scores[HALF:, :HALF], 0.0)
    c2 = cum[...] * LOG2E
    rows = (c2 - jnp.log2(softplus(pre[...]))).T
    for j in range(val.shape[1] // LANES):
        cols = slice(j * LANES, (j + 1) * LANES)
        v = val[:, cols]
        vm = pair_masks(v, v.shape)
        tops, bottoms = [], []
        for which in range(2):
            h = 2 * j + which
            col0 = jnp.broadcast_to(c2[:HALF, h : h + 1], (HALF, HALF))
            col1 = jnp.broadcast_to(c2[HALF:, h : h + 1], (HALF, HALF))
            r0 = rows[h : h + 1, :HALF]
            r1 = rows[h : h + 1, HALF:]
            tops.append((s00 * jnp.exp2(jnp.minimum(col0 - r0, 60.0))).astype(bf16))
            bottoms.append((s10 * jnp.exp2(col1 - r0)).astype(bf16))
            bottoms.append((s11 * jnp.exp2(jnp.minimum(col1 - r1, 60.0))).astype(bf16))
        top = dot(jnp.concatenate(tops, axis=1), jnp.concatenate([vm[0][:HALF], vm[1][:HALF]], axis=0))
        bottom = dot(jnp.concatenate(bottoms, axis=1), jnp.concatenate([vm[0], vm[1]], axis=0))
        skip = dskip[:, cols]
        part[:HALF, cols] = top + skip * v[:HALF].astype(f32)
        part[HALF:, cols] = bottom + skip * v[HALF:].astype(f32)


def mid_kernel(
    meta, hid, normed, z0, z1, z2, z3, o0, o1, o2, o3, cot, cmat, age, ex, red, gain,
    part_a, part_b, val_a, val_b, cum_a, cum_b, lin_a, lin_b, kb_a, kb_b, ck_a, ck_b, arr_a, arr_b,
    pieces, nout, cotx, dssd, dgate, dcin, dkk_a, dkk_b,
    lout_a, lout_b, ka_a, ka_b, tot_a, tot_b, ktot_a, ktot_b, ggain, gskip,
    gate, dno, read, kx, ssd_s, sig_s, khi, klo, rhi, rlo, run_a, run_b, kept_a, kept_b,
):
    i = pl.program_id(0)
    inner = nout.shape[1]
    width = inner // 2
    tiles = inner // LANES
    heads = width // HEAD_DIM
    quarter = inner // 4

    @pl.when(i == 0)
    def _():
        for ref in (run_a, run_b, ggain, gskip):
            ref[...] = jnp.zeros_like(ref)
        for ref in (kept_a, kept_b):
            ref[...] = jnp.ones_like(ref)

    cotan = jnp.concatenate([cot[0], cot[1], cot[2], cot[3]], axis=1)
    cotx[...] = cotan
    states = []
    for half, (lin, kb, arr, cum) in enumerate(
        ((lin_a, kb_a, arr_a, cum_a), (lin_b, kb_b, arr_b, cum_b))
    ):
        cols = slice(half * width, (half + 1) * width)
        hi, lo = split2(lin[0] + kb[0, 0:1] * arr[...])
        states.append((hi, lo))
        read[:, cols] = dot(cmat[...], hi) + dot(cmat[...], lo)
        since = lax.broadcasted_iota(jnp.int32, age.shape, 0)
        kappa = jnp.where(age[...] > since, jnp.exp(cum[...]), 0.0)
        kx[:, cols] = expand(lanes_below(kappa, heads), ex[...])
    for k, (z, o) in enumerate(((z0, o0), (z1, o1), (z2, o2), (z3, o3))):
        cols = slice(k * quarter, (k + 1) * quarter)
        gate[:, cols] = dot(normed[...], z[...])
        dno[:, cols] = dot(cotan, o[...], 1, 1)

    def rows_body(step, _):
        rows = pl.ds(pl.multiple_of(step * ROWS, ROWS), ROWS)
        squares = jnp.zeros((ROWS, LANES), f32)
        inners = jnp.zeros((ROWS, LANES), f32)
        for j in range(tiles):
            cols = slice(j * LANES, (j + 1) * LANES)
            part = part_a if j < tiles // 2 else part_b
            pcols = slice(cols.start % width, cols.start % width + LANES)
            ssd = part[rows, pcols] + kx[rows, cols] * read[rows, cols]
            g = gate[rows, cols]
            sig = sigmoid(g)
            gated = ssd * (g * sig)
            squares += gated * gated
            inners += gated * (dno[rows, cols] * gain[:, cols])
            ssd_s[rows, cols] = ssd
            sig_s[rows, cols] = sig
        rg = lax.rsqrt(jnp.sum(squares, axis=1, keepdims=True) / inner + EPS)
        stat = rg * rg * (jnp.sum(inners, axis=1, keepdims=True) / inner)
        rg = jnp.broadcast_to(rg, (ROWS, LANES))
        stat = jnp.broadcast_to(stat, (ROWS, LANES))
        for j in range(tiles):
            cols = slice(j * LANES, (j + 1) * LANES)
            val = val_a if j < tiles // 2 else val_b
            pcols = slice(cols.start % width, cols.start % width + LANES)
            ssd, sig, g, d = ssd_s[rows, cols], sig_s[rows, cols], gate[rows, cols], dno[rows, cols]
            act = g * sig
            gated = ssd * act
            yhat = gated * rg
            nout[rows, cols] = (yhat * gain[:, cols]).astype(bf16)
            ggain[:, cols] += fold8(d * yhat)
            dgated = rg * (d * gain[:, cols] - gated * stat)
            low = (dgated * act).astype(bf16)
            dssd[rows, cols] = low
            dgate[rows, cols] = (dgated * ssd * (sig * (1.0 + g * (1.0 - sig)))).astype(bf16)
            dy = low.astype(f32)
            gskip[:, cols] += fold8(dy * val[rows, pcols].astype(f32))
            kd = kx[rows, cols] * dy
            khi[rows, cols], klo[rows, cols] = split2(kd)
            rhi[rows, cols], rlo[rows, cols] = split2(kd * read[rows, cols])
        return 0

    lax.fori_loop(0, GROUP // ROWS, rows_body, 0)
    out = hid[0].astype(f32)
    for k, o in enumerate((o0, o1, o2, o3)):
        out = out + dot(nout[:, k * quarter : (k + 1) * quarter], o[...])
    out = out.astype(bf16)
    piece = out.shape[1] // 4
    for k in range(4):
        pieces[k] = out[:, k * piece : (k + 1) * piece]
    dc = None
    for half, (dkk, ck, lout, ka, tot, ktot, running, kept) in enumerate(
        (
            (dkk_a, ck_a, lout_a, ka_a, tot_a, ktot_a, run_a, kept_a),
            (dkk_b, ck_b, lout_b, ka_b, tot_b, ktot_b, run_b, kept_b),
        )
    ):
        cols = slice(half * width, (half + 1) * width)
        hi, lo = states[half]
        dkk[...] = dot(rhi[:, cols], red[...]) + dot(rlo[:, cols], red[...])
        term = dot(khi[:, cols], hi, 1, 1) + dot(khi[:, cols], lo, 1, 1) + dot(klo[:, cols], hi, 1, 1)
        dc = term if dc is None else dc + term
        own = dot(cmat[...], khi[:, cols], 0, 0) + dot(cmat[...], klo[:, cols], 0, 0)
        lout[0] = running[...]
        ka[0] = kept[...]
        running[...] = ck[0, 0:1] * running[...] + own
        kept[...] = ck[0] * kept[...]
        tot[...] = running[...]
        ktot[...] = kept[...]
    dcin[...] = dc


def pairs_kernel(val, dssd, bmat, cmat, ager, pre, cum, dvi, dbi, dci, rflow, cflow, rft):
    s = lax.broadcasted_iota(jnp.int32, (HALF, HALF), 0)
    t = lax.broadcasted_iota(jnp.int32, (HALF, HALF), 1)
    scores = dot(bmat[...], cmat[...], 1, 1)
    a0, a1 = ager[0:1, :HALF], ager[0:1, HALF:]
    gap = t - s
    m00 = (gap >= 0) & (gap <= a0)
    m11 = (gap >= 0) & (gap <= a1)
    m01 = gap + HALF <= a1
    s00 = jnp.where(m00, scores[:HALF, :HALF], 0.0)
    s11 = jnp.where(m11, scores[HALF:, HALF:], 0.0)
    s01 = jnp.where(m01, scores[:HALF, HALF:], 0.0)
    c2 = cum[...] * LOG2E
    cr = c2 - jnp.log2(softplus(pre[...]))
    c2t = c2.T
    lane = lax.broadcasted_iota(jnp.int32, (HALF, LANES), 1)
    zero = jnp.zeros((HALF, HALF), f32)
    d00, d01, d11 = zero, zero, zero
    cf0, cf1 = zero, zero
    rft[...] = jnp.zeros_like(rft)
    for j in range(val.shape[1] // LANES):
        cols = slice(j * LANES, (j + 1) * LANES)
        v = val[:, cols]
        dy = dssd[:, cols]
        vm = pair_masks(v, v.shape)
        dm = pair_masks(dy, dy.shape)
        tops, bottoms = [], []
        for which in range(2):
            h = 2 * j + which
            col0 = jnp.broadcast_to(cr[:HALF, h : h + 1], (HALF, HALF))
            col1 = jnp.broadcast_to(cr[HALF:, h : h + 1], (HALF, HALF))
            r0 = c2t[h : h + 1, :HALF]
            r1 = c2t[h : h + 1, HALF:]
            e00 = jnp.exp2(jnp.minimum(r0 - col0, 60.0))
            e01 = jnp.exp2(r1 - col0)
            e11 = jnp.exp2(jnp.minimum(r1 - col1, 60.0))
            tops.append((s00 * e00).astype(bf16))
            tops.append((s01 * e01).astype(bf16))
            bottoms.append((s11 * e11).astype(bf16))
            w0 = dot(vm[which][:HALF], dy, 1, 1)
            w1 = dot(vm[which][HALF:], dy[HALF:], 1, 1)
            de00 = w0[:, :HALF] * e00
            de01 = w0[:, HALF:] * e01
            de11 = w1 * e11
            d00 += de00
            d01 += de01
            d11 += de11
            f00 = de00 * s00
            f01 = de01 * s01
            f11 = de11 * s11
            rft[h : h + 1, :HALF] = jnp.sum(f00, axis=0, keepdims=True)
            rft[h : h + 1, HALF:] = jnp.sum(f01 + f11, axis=0, keepdims=True)
            cf0 = jnp.where(lane == h, jnp.sum(f00 + f01, axis=1, keepdims=True), cf0)
            cf1 = jnp.where(lane == h, jnp.sum(f11, axis=1, keepdims=True), cf1)
        dvi[:HALF, cols] = dot(jnp.concatenate(tops, axis=1), jnp.concatenate([dm[0], dm[1]], axis=0))
        dvi[HALF:, cols] = dot(
            jnp.concatenate(bottoms, axis=1), jnp.concatenate([dm[0][HALF:], dm[1][HALF:]], axis=0)
        )
    cflow[:HALF] = cf0
    cflow[HALF:] = cf1
    rflow[...] = rft[...].T
    d00 = split2(jnp.where(m00, d00, 0.0))
    d01 = split2(jnp.where(m01, d01, 0.0))
    d11 = split2(jnp.where(m11, d11, 0.0))
    b0, b1, c0, c1 = bmat[:HALF], bmat[HALF:], cmat[:HALF], cmat[HALF:]
    dbi[:HALF] = dot(d00[0], c0) + dot(d00[1], c0) + dot(d01[0], c1) + dot(d01[1], c1)
    dbi[HALF:] = dot(d11[0], c1) + dot(d11[1], c1)
    dci[:HALF] = dot(d00[0], b0, 0, 0) + dot(d00[1], b0, 0, 0)
    dci[HALF:] = (
        dot(d01[0], b0, 0, 0) + dot(d01[1], b0, 0, 0) + dot(d11[0], b1, 0, 0) + dot(d11[1], b1, 0, 0)
    )


def slope(x):
    sig = sigmoid(x)
    return sig * (1.0 + x * (1.0 - sig))


def conv_back(i, dco, agex, age, ci, taps, dci, tail, head, gw):
    width = ci.shape[1]
    for r in range(0, GROUP, ROWS):
        ages = [agex[r + m : r + m + ROWS] for m in range(4)]
        for j in range(width // LANES):
            cols = slice(j * LANES, (j + 1) * LANES)
            c = ci[r : r + ROWS, cols].astype(f32)
            acc = None
            for m in range(4):
                x = dco[r + m : r + m + ROWS, cols]
                if m:
                    x = jnp.where(ages[m] >= m, x, 0.0)
                term = x * taps[3 - m : 4 - m, cols]
                acc = term if acc is None else acc + term
                gw[8 * (3 - m) : 8 * (3 - m) + 8, cols] += fold8(x * c)
            dci[r : r + ROWS, cols] = acc.astype(bf16)
            if r == GROUP - ROWS:

                @pl.when(i == 0)
                def _():
                    tail[:, cols] = acc[ROWS - 8 :]

    head[...] = dco[0:8]


def start_next(i, dco, agex, gw, gb):
    @pl.when(i == 0)
    def _():
        dco[GROUP : GROUP + 8] = jnp.zeros((8, dco.shape[1]), f32)
        agex[GROUP : GROUP + 8] = jnp.zeros((8, LANES), jnp.int32)
        gw[...] = jnp.zeros_like(gw)
        gb[...] = jnp.zeros_like(gb)

    @pl.when(i > 0)
    def _():
        dco[GROUP : GROUP + 8] = dco[0:8]
        agex[GROUP : GROUP + 8] = agex[0:8]


def back_kernel(
    val, dssd, dvi, bmat, co, ci, age, pre, cum, lout, ka, leav, lin, kb, arr, ck, rflow, cflow, dkk,
    dskip, taps, rate, tril, ex, red,
    dci, tail, head, dbin, draw, gw, gb, galog, gdtb,
    dco, agex, back, omx, ohi, olo, vhi, vlo,
):
    i = pl.program_id(0)
    width = val.shape[1]
    heads = width // HEAD_DIM
    start_next(i, dco, agex, gw, gb)

    @pl.when(i == 0)
    def _():
        galog[...] = jnp.zeros_like(galog)
        gdtb[...] = jnp.zeros_like(gdtb)

    agex[0:GROUP] = age[...]
    ds = lout[0] + ka[0, 0:1] * leav[...]
    dhi, dlo = split2(ds)
    back[...] = dot(bmat[...], dhi) + dot(bmat[...], dlo)
    p = pre[...]
    delta = softplus(p)
    c = cum[...]
    end = c[GROUP - 1 : GROUP]
    age_end = age[GROUP - 1 : GROUP]
    row = lax.broadcasted_iota(jnp.int32, c.shape, 0)
    tail_keep = jnp.where(GROUP - 1 - row <= age_end, jnp.exp(end - c), 0.0)
    omega = tail_keep * delta
    omx[...] = expand(lanes_below(omega, heads), ex[...])
    for r in range(0, GROUP, ROWS):
        rows = slice(r, r + ROWS)
        for j in range(width // LANES):
            cols = slice(j * LANES, (j + 1) * LANES)
            v = val[rows, cols].astype(f32)
            b = back[rows, cols]
            o = omx[rows, cols]
            dval = dskip[:, cols] * dssd[rows, cols].astype(f32) + dvi[rows, cols] + o * b
            ohi[rows, cols], olo[rows, cols] = split2(o * v)
            vhi[rows, cols], vlo[rows, cols] = split2(v * b)
            d = dval * slope(co[rows, cols])
            dco[rows, cols] = d
            gb[:, cols] += fold8(d)
    dbin[...] = dot(ohi[...], dhi, 1, 1) + dot(ohi[...], dlo, 1, 1) + dot(olo[...], dhi, 1, 1)
    domega = dot(vhi[...], red[...]) + dot(vlo[...], red[...])
    flow = domega * omega
    sin = lin[0] + kb[0, 0:1] * arr[...]
    carry = jnp.broadcast_to(jnp.sum(ds * sin, axis=0, keepdims=True), (8, width))
    carry = dot(carry, red[...].astype(f32), precision=HIGHEST)[0:1]
    keep = jnp.where(age_end >= GROUP, jnp.exp(end), 0.0)
    dcum = rflow[...] - cflow[...] + dkk[...] - flow
    ending = jnp.sum(flow, axis=0, keepdims=True) + carry * keep
    dcum = dcum + jnp.where(row == GROUP - 1, ending, 0.0)
    dlog = dot(tril[...], dcum, 0, 0, precision=HIGHEST)
    sig = sigmoid(p)
    ratio = jnp.where(delta > 1e-30, sig / delta, 1.0)
    drf = cflow[...] * ratio + (domega * tail_keep + dlog * rate[...]) * sig
    drf = lanes_below(drf, heads)
    draw[...] = drf.astype(bf16)
    gdtb[...] += fold8(drf)
    galog[...] += fold8(dlog * delta)
    conv_back(i, dco, agex, age, ci, taps, dci, tail, head, gw)


def maps_kernel(
    dbi_a, dbi_b, dbin_a, dbin_b, dci_a, dci_b, dcin, co, ci, age, taps, dci, tail, head, gw, gb, dco, agex
):
    i = pl.program_id(0)
    start_next(i, dco, agex, gw, gb)
    agex[0:GROUP] = age[...]
    for r in range(0, GROUP, ROWS):
        rows = slice(r, r + ROWS)
        db = dbi_a[rows] + dbi_b[rows] + dbin_a[rows] + dbin_b[rows]
        dc = dci_a[rows] + dci_b[rows] + dcin[rows]
        for j, d in enumerate((db, dc)):
            cols = slice(j * LANES, (j + 1) * LANES)
            d = d * slope(co[rows, cols])
            dco[rows, cols] = d
            gb[:, cols] += fold8(d)
    conv_back(i, dco, agex, age, ci, taps, dci, tail, head, gw)


def final_kernel(
    meta, hid, cotx, gain, dgate, z0, z1, z2, z3, dx_a, dx_b, x0, x1, x2, x3, dbc, bc, dr_a, dr_b, dt_a, dt_b,
    pieces, ggain, acc_s,
):
    @pl.when(pl.program_id(0) == 0)
    def _():
        ggain[...] = jnp.zeros_like(ggain)

    quarter = z0.shape[1]
    acc = dot(dbc[...], bc[...], 1, 1) + dot(dr_a[...], dt_a[...]) + dot(dr_b[...], dt_b[...])
    for k, (z, x) in enumerate(((z0, x0), (z1, x1), (z2, x2), (z3, x3))):
        acc = acc + dot(dgate[:, k * quarter : (k + 1) * quarter], z[...], 1, 1)
        dx = dx_a if k < 2 else dx_b
        at = (k % 2) * quarter
        acc = acc + dot(dx[:, at : at + quarter], x[...], 1, 1)
    acc_s[...] = acc
    piece = acc.shape[1] // 4
    for r in range(0, GROUP, ROWS):
        rows = slice(r, r + ROWS)
        x = hid[0, rows].astype(f32)
        rinv = lax.rsqrt(jnp.sum(x * x, axis=1, keepdims=True) / x.shape[1] + EPS)
        xhat = x * rinv
        d = acc_s[rows]
        ggain[...] += fold8(d * xhat)
        dx = d * gain[...]
        mean = jnp.sum(dx * xhat, axis=1, keepdims=True) / x.shape[1]
        out = (cotx[rows].astype(f32) + rinv * (dx - xhat * mean)).astype(bf16)
        for k in range(4):
            pieces[k, rows] = out[:, k * piece : (k + 1) * piece]


def scan_kernel(reverse, n, x, keep, out):
    state = jnp.zeros(x.shape[1:], f32)
    for step in range(n):
        at = n - 1 - step if reverse else step
        out[at] = state
        if step < n - 1:
            state = keep[at] * state + x[at]


def shards(
    hidden_in,
    output_cotangent,
    input_norm_scale_gain,
    z_proj,
    x_proj,
    bc_proj,
    dt_proj,
    conv_x_weight,
    conv_x_bias,
    conv_bc_weight,
    conv_bc_bias,
    dt_bias,
    a_log,
    d_skip,
    out_norm_gain,
    out_proj,
    doc_starts,
):
    batch, tokens, features = hidden_in.shape
    quarter = z_proj.shape[1]
    width = 2 * quarter
    inner = 4 * quarter
    heads = dt_proj.shape[1]
    seqs = lax.axis_size("seq")
    head_devices = lax.axis_size("head")
    parts = head_devices // batch
    chunk = tokens // parts
    count = chunk // GROUP
    si, hi_ = lax.axis_index("seq"), lax.axis_index("head")
    seq_of, half = hi_ // parts, hi_ % parts
    meta = jnp.stack([seq_of, half * count]).astype(jnp.int32)
    core = [(h, h ^ 1) for h in range(head_devices)]
    across = [(h, h ^ 2) for h in range(head_devices)]

    def swap(x):
        return lax.ppermute(x, "head", core)

    def cross(x):
        return lax.ppermute(x, "head", across)

    def spread(x):
        x2 = cross(x)
        return [x, swap(x), x2, swap(x2)]

    small = jnp.concatenate(
        [
            conv_x_weight.T,
            conv_x_bias[None],
            out_norm_gain[None],
            jnp.pad(jnp.concatenate([dt_bias, a_log, d_skip])[None], ((0, 1), (0, quarter - 3 * heads))),
            jnp.pad(dt_proj.T.astype(f32), ((0, 8 - heads), (0, 0))).reshape(8 * features // quarter, quarter),
        ],
        axis=0,
    )
    edge = jnp.where(
        half == 0,
        lax.ppermute(
            lax.dynamic_slice(hidden_in, (seq_of, tokens - 16, 0), (1, 16, features))[0],
            "seq",
            [(s, s + 1) for s in range(seqs - 1)],
        ),
        lax.dynamic_slice(hidden_in, (seq_of, chunk - 16, 0), (1, 16, features))[0],
    )
    smalls = spread(small)
    xs = spread(x_proj)
    zs = spread(z_proj)
    os_ = spread(out_proj)
    cots = lax.all_to_all(
        output_cotangent.reshape(head_devices, chunk, features // head_devices), "head", 0, 0
    )

    first_pos = si * tokens + half * chunk
    places = first_pos + jnp.arange(chunk, dtype=jnp.int32)
    starts = lax.dynamic_slice(doc_starts, (seq_of, 0), (1, doc_starts.shape[1]))[0]
    first = jnp.max(jnp.where(starts[None, :] <= places[:, None], starts[None, :], 0), axis=1)
    age1 = places - first
    age = jnp.broadcast_to(age1[:, None], (chunk, LANES))
    ager = jnp.broadcast_to(age1[None, :], (8, chunk))

    ex, red = expansion(width)
    tril = jnp.asarray(np.tril(np.ones((GROUP, GROUP), np.float32)))
    hid_map = lambda i, m: (m[0], m[1] + i, 0)
    here = lambda i, *_: (i, 0)
    gain_in = input_norm_scale_gain[None]

    taps_bc = conv_bc_weight.T
    normed, nedge, ci_bc, co_bc, bmat, cmat = run(
        norm_kernel,
        (count,),
        [
            (hidden_in, (1, GROUP, features), hid_map),
            (edge, None, None),
            (gain_in, None, None),
            (bc_proj, None, None),
            (taps_bc, None, None),
            (conv_bc_bias[None], None, None),
            (age, (GROUP, LANES), here),
        ],
        [
            ((chunk, features), bf16, (GROUP, features), here),
            ((16, features), bf16, None, None),
            ((chunk, 2 * LANES), bf16, (GROUP, 2 * LANES), here),
            ((chunk, 2 * LANES), f32, (GROUP, 2 * LANES), here),
            ((chunk, LANES), bf16, (GROUP, LANES), here),
            ((chunk, LANES), bf16, (GROUP, LANES), here),
        ],
        [pltpu.VMEM((GROUP + 8, 2 * LANES), f32)],
        flops=2 * chunk * features * 256,
        moved=6_000_000,
        prefetch=(meta,),
    )

    def join(k, rows):
        return jnp.concatenate([smalls[k][rows], smalls[k + 1][rows]], axis=1)

    def lane_pack(k, at):
        row = jnp.concatenate(
            [smalls[k][6, at * heads : (at + 1) * heads], smalls[k + 1][6, at * heads : (at + 1) * heads]]
        )
        return jnp.pad(row, (0, LANES - 2 * heads))[None]

    halves = []
    for k in (0, 2):
        taps = join(k, slice(0, 4))
        bias = join(k, slice(4, 5))
        dtp = jnp.concatenate(
            [smalls[k + n][8:].reshape(8, features)[:heads] for n in range(2)], axis=0
        ).astype(bf16)
        dtp = jnp.pad(dtp, ((0, LANES - 2 * heads), (0, 0)))
        rate = -jnp.exp(lane_pack(k, 1))
        dskip = jnp.repeat(lane_pack(k, 2)[0, : 2 * heads], HEAD_DIM)[None]
        outs = run(
            front_kernel,
            (count,),
            [
                (normed, (GROUP, features), here),
                (nedge, None, None),
                (xs[k], None, None),
                (xs[k + 1], None, None),
                (taps, None, None),
                (bias, None, None),
                (dtp, None, None),
                (lane_pack(k, 0), None, None),
                (rate, None, None),
                (bmat, (GROUP, LANES), here),
                (age, (GROUP, LANES), here),
                (tril, None, None),
                (ex, None, None),
            ],
            [
                ((chunk, width), bf16, (GROUP, width), here),
                ((chunk, width), f32, (GROUP, width), here),
                ((chunk, width), bf16, (GROUP, width), here),
                ((chunk, LANES), f32, (GROUP, LANES), here),
                ((chunk, LANES), f32, (GROUP, LANES), here),
                ((count, LANES, width), f32, (1, LANES, width), lambda i: (i, 0, 0)),
                ((count, 8, width), f32, (1, 8, width), lambda i: (i, 0, 0)),
                ((count, 8, width), f32, (1, 8, width), lambda i: (i, 0, 0)),
                ((LANES, width), f32, None, None),
                ((8, width), f32, None, None),
            ],
            [
                pltpu.VMEM((GROUP + 8, width), f32),
                pltpu.VMEM((LANES, width), f32),
                pltpu.VMEM((8, width), f32),
                pltpu.VMEM((GROUP, width), f32),
                pltpu.VMEM((GROUP, width), bf16),
                pltpu.VMEM((GROUP, width), bf16),
            ],
            flops=2 * chunk * features * 1024 * 4,
            moved=16_000_000,
        )
        names = ("ci", "co", "val", "pre", "cum", "lin", "kb", "ck", "tot", "ktot")
        d = dict(zip(names, outs))
        d.update(taps=taps, bias=bias, dtp=dtp, rate=rate, dskip=dskip)
        halves.append(d)

    for d in halves:
        d["part"] = run(
            intra_kernel,
            (count,),
            [
                (d["val"], (GROUP, width), here),
                (bmat, (GROUP, LANES), here),
                (cmat, (GROUP, LANES), here),
                (age, (GROUP, LANES), here),
                (d["pre"], (GROUP, LANES), here),
                (d["cum"], (GROUP, LANES), here),
                (d["dskip"], None, None),
            ],
            [((chunk, width), f32, (GROUP, width), here)],
            flops=10_000_000_000,
            moved=8_000_000,
        )[0]

    def exchange(tots, ktots, reverse):
        a, b = tots
        ka, kb = ktots
        mine = jnp.concatenate(
            [
                jnp.concatenate([a[:, :quarter], b[:, :quarter]], axis=1),
                jnp.concatenate([ka[:, :quarter], kb[:, :quarter]], axis=1),
            ],
            axis=0,
        )
        other = jnp.concatenate(
            [
                jnp.concatenate([a[:, quarter:], b[:, quarter:]], axis=1),
                jnp.concatenate([ka[:, quarter:], kb[:, quarter:]], axis=1),
            ],
            axis=0,
        )
        got = swap(other)
        leads = (half == 0) if not reverse else (half == 1)
        lead = jnp.where(leads, mine, got)
        follow = jnp.where(leads, got, mine)
        lead_s, lead_k = lead[:LANES], lead[LANES : LANES + 1]
        follow_s, follow_k = follow[:LANES], follow[LANES : LANES + 1]
        chip_s = follow_k * lead_s + follow_s
        chip_k = lead_k * follow_k
        per = LANES // seqs
        keeps = lax.all_gather(chip_k, "seq", axis=0)
        spread_s = lax.all_to_all(chip_s.reshape(seqs, per, width), "seq", 0, 0)
        scanned = pl.pallas_call(
            functools.partial(scan_kernel, reverse, seqs),
            out_shape=jax.ShapeDtypeStruct((seqs, per, width), f32),
        )(spread_s, keeps)
        arriving = lax.all_to_all(scanned, "seq", 0, 0).reshape(LANES, width)
        second = lead_k * arriving + lead_s
        own = jnp.where(leads, arriving, second)
        theirs = swap(jnp.where(leads, second, arriving))
        return (
            jnp.concatenate([own[:, :quarter], theirs[:, :quarter]], axis=1),
            jnp.concatenate([own[:, quarter:], theirs[:, quarter:]], axis=1),
        )

    ha, hb = halves
    arr = exchange((ha["tot"], hb["tot"]), (ha["ktot"], hb["ktot"]), False)

    gain_out = jnp.concatenate([s[5:6] for s in smalls], axis=1)
    rev = lambda i, *_: (count - 1 - i, 0)
    rev3 = lambda i, *_: (count - 1 - i, 0, 0)
    rev_hid = lambda i, m: (m[0], m[1] + count - 1 - i, 0)
    piece = features // 4
    wide = (GROUP, inner)
    half_in = (GROUP, width)
    state_block = (1, LANES, width)
    keep_block = (1, 8, width)
    outs = run(
        mid_kernel,
        (count,),
        [
            (hidden_in, (1, GROUP, features), rev_hid),
            (normed, (GROUP, features), rev),
            *[(z, None, None) for z in zs],
            *[(o, None, None) for o in os_],
            (cots, (4, GROUP, piece), lambda i, *_: (0, count - 1 - i, 0)),
            (cmat, (GROUP, LANES), rev),
            (age, (GROUP, LANES), rev),
            (ex, None, None),
            (red, None, None),
            (gain_out, None, None),
            *[(d["part"], half_in, rev) for d in halves],
            *[(d["val"], half_in, rev) for d in halves],
            *[(d["cum"], (GROUP, LANES), rev) for d in halves],
            *[(d["lin"], state_block, rev3) for d in halves],
            *[(d["kb"], keep_block, rev3) for d in halves],
            *[(d["ck"], keep_block, rev3) for d in halves],
            *[(a, None, None) for a in arr],
        ],
        [
            ((4, chunk, piece), bf16, (4, GROUP, piece), lambda i, *_: (0, count - 1 - i, 0)),
            ((chunk, inner), bf16, wide, rev),
            ((chunk, features), bf16, (GROUP, features), rev),
            ((chunk, inner), bf16, wide, rev),
            ((chunk, inner), bf16, wide, rev),
            ((chunk, LANES), f32, (GROUP, LANES), rev),
            ((chunk, LANES), f32, (GROUP, LANES), rev),
            ((chunk, LANES), f32, (GROUP, LANES), rev),
            ((count, LANES, width), f32, state_block, rev3),
            ((count, LANES, width), f32, state_block, rev3),
            ((count, 8, width), f32, keep_block, rev3),
            ((count, 8, width), f32, keep_block, rev3),
            ((LANES, width), f32, None, None),
            ((LANES, width), f32, None, None),
            ((8, width), f32, None, None),
            ((8, width), f32, None, None),
            ((8, inner), f32, None, None),
            ((8, inner), f32, None, None),
        ],
        [pltpu.VMEM(wide, f32)] * 6
        + [pltpu.VMEM(wide, bf16)] * 4
        + [pltpu.VMEM((LANES, width), f32)] * 2
        + [pltpu.VMEM((8, width), f32)] * 2,
        flops=30_000_000_000,
        moved=50_000_000,
        prefetch=(meta,),
    )
    pieces, nout, cotx, dssd, dgate, dcin, ha["dkk"], hb["dkk"], ha["lout"], hb["lout"] = outs[:10]
    ha["ka"], hb["ka"], dtot_a, dtot_b, dk_a, dk_b, ggain_out, gskip = outs[10:]
    layer_out = lax.all_to_all(pieces, "head", 0, 0).reshape(batch, tokens, piece)

    for n, d in enumerate(halves):
        d["dvi"], d["dbi"], d["dci_c"], d["rflow"], d["cflow"] = run(
            pairs_kernel,
            (count,),
            [
                (d["val"], half_in, here),
                (dssd, half_in, lambda i, n=n: (i, n)),
                (bmat, (GROUP, LANES), here),
                (cmat, (GROUP, LANES), here),
                (ager, (8, GROUP), lambda i: (0, i)),
                (d["pre"], (GROUP, LANES), here),
                (d["cum"], (GROUP, LANES), here),
            ],
            [
                ((chunk, width), f32, half_in, here),
                ((chunk, LANES), f32, (GROUP, LANES), here),
                ((chunk, LANES), f32, (GROUP, LANES), here),
                ((chunk, LANES), f32, (GROUP, LANES), here),
                ((chunk, LANES), f32, (GROUP, LANES), here),
            ],
            [pltpu.VMEM((LANES, GROUP), f32)],
            flops=15_000_000_000,
            moved=10_000_000,
        )

    leav = exchange((dtot_a, dtot_b), (dk_a, dk_b), True)

    for n, d in enumerate(halves):
        outs = run(
            back_kernel,
            (count,),
            [
                (d["val"], half_in, rev),
                (dssd, half_in, lambda i, n=n: (count - 1 - i, n)),
                (d["dvi"], half_in, rev),
                (bmat, (GROUP, LANES), rev),
                (d["co"], half_in, rev),
                (d["ci"], half_in, rev),
                (age, (GROUP, LANES), rev),
                (d["pre"], (GROUP, LANES), rev),
                (d["cum"], (GROUP, LANES), rev),
                (d["lout"], state_block, rev3),
                (d["ka"], keep_block, rev3),
                (leav[n], None, None),
                (d["lin"], state_block, rev3),
                (d["kb"], keep_block, rev3),
                (arr[n], None, None),
                (d["ck"], keep_block, rev3),
                (d["rflow"], (GROUP, LANES), rev),
                (d["cflow"], (GROUP, LANES), rev),
                (d["dkk"], (GROUP, LANES), rev),
                (d["dskip"], None, None),
                (d["taps"], None, None),
                (d["rate"], None, None),
                (tril, None, None),
                (ex, None, None),
                (red, None, None),
            ],
            [
                ((chunk, width), bf16, half_in, rev),
                ((8, width), f32, None, None),
                ((8, width), f32, None, None),
                ((chunk, LANES), f32, (GROUP, LANES), rev),
                ((chunk, LANES), bf16, (GROUP, LANES), rev),
                ((32, width), f32, None, None),
                ((8, width), f32, None, None),
                ((8, LANES), f32, None, None),
                ((8, LANES), f32, None, None),
            ],
            [
                pltpu.VMEM((GROUP + 8, width), f32),
                pltpu.VMEM((GROUP + 8, LANES), jnp.int32),
                pltpu.VMEM(half_in, f32),
                pltpu.VMEM(half_in, f32),
            ]
            + [pltpu.VMEM(half_in, bf16)] * 4,
            flops=15_000_000_000,
            moved=20_000_000,
        )
        names = ("dx", "tail", "head", "dbin", "draw", "gw", "gb", "galog", "gdtb")
        d.update(zip(names, outs))

    dbc, tail_bc, head_bc, gw_bc, gb_bc = run(
        maps_kernel,
        (count,),
        [
            *[(d["dbi"], (GROUP, LANES), rev) for d in halves],
            *[(d["dbin"], (GROUP, LANES), rev) for d in halves],
            *[(d["dci_c"], (GROUP, LANES), rev) for d in halves],
            (dcin, (GROUP, LANES), rev),
            (co_bc, (GROUP, 2 * LANES), rev),
            (ci_bc, (GROUP, 2 * LANES), rev),
            (age, (GROUP, LANES), rev),
            (taps_bc, None, None),
        ],
        [
            ((chunk, 2 * LANES), bf16, (GROUP, 2 * LANES), rev),
            ((8, 2 * LANES), f32, None, None),
            ((8, 2 * LANES), f32, None, None),
            ((32, 2 * LANES), f32, None, None),
            ((8, 2 * LANES), f32, None, None),
        ],
        [pltpu.VMEM((GROUP + 8, 2 * LANES), f32), pltpu.VMEM((GROUP + 8, LANES), jnp.int32)],
        flops=2_000_000_000,
        moved=8_000_000,
    )

    heads_out = jnp.concatenate([ha["head"], hb["head"], head_bc], axis=1)
    heads_out = jnp.concatenate(
        [heads_out[:, 0:quarter], heads_out[:, quarter:width], heads_out[:, width:]], axis=1
    )
    pairs = []
    for s in range(seqs):
        for b in range(batch):
            for p in range(parts):
                if p > 0:
                    pairs.append((s * head_devices + b * parts + p, s * head_devices + b * parts + p - 1))
                elif s > 0:
                    pairs.append((s * head_devices + b * parts, (s - 1) * head_devices + b * parts + parts - 1))
    flipped = jnp.concatenate(
        [
            heads_out[:, quarter : 2 * quarter],
            heads_out[:, 0:quarter],
            heads_out[:, 3 * quarter : 4 * quarter],
            heads_out[:, 2 * quarter : 3 * quarter],
            heads_out[:, 4 * quarter :],
        ],
        axis=1,
    )
    got = lax.ppermute(flipped, ("seq", "head"), pairs)
    next_places = first_pos + chunk + jnp.arange(8, dtype=jnp.int32)
    next_first = jnp.max(jnp.where(starts[None, :] <= next_places[:, None], starts[None, :], 0), axis=1)
    next_age = next_places - next_first
    taps_all = jnp.concatenate([ha["taps"], hb["taps"], taps_bc], axis=1)
    tail_all = jnp.concatenate([ha["tail"], hb["tail"], tail_bc], axis=1)
    ci_all = jnp.concatenate([ha["ci"][-8:], hb["ci"][-8:], ci_bc[-8:]], axis=1).astype(f32)
    gw_fix = [jnp.zeros((tail_all.shape[1],), f32)] * 4
    for m in range(1, 4):
        masked = jnp.where((next_age >= m)[:m, None], got[:m], 0.0)
        rows = jnp.concatenate([jnp.zeros((8 - m, got.shape[1]), f32), masked], axis=0)
        tail_all = tail_all + rows * taps_all[3 - m]
        gw_fix[3 - m] = jnp.sum(rows * ci_all, axis=0)
    tail_low = tail_all.astype(bf16)
    gw_fix = jnp.stack(gw_fix)
    dxs = [
        lax.dynamic_update_slice(x, tail_low[:, at : at + x.shape[1]], (chunk - 8, 0))
        for x, at in ((ha["dx"], 0), (hb["dx"], width), (dbc, inner))
    ]

    dt_rows = [d["dtp"] for d in halves]
    in_pieces, ggain_in = run(
        final_kernel,
        (count,),
        [
            (hidden_in, (1, GROUP, features), hid_map),
            (cotx, (GROUP, features), here),
            (gain_in, None, None),
            (dgate, wide, here),
            *[(z, None, None) for z in zs],
            (dxs[0], half_in, here),
            (dxs[1], half_in, here),
            *[(x, None, None) for x in xs],
            (dxs[2], (GROUP, 2 * LANES), here),
            (bc_proj, None, None),
            (ha["draw"], (GROUP, LANES), here),
            (hb["draw"], (GROUP, LANES), here),
            (dt_rows[0], None, None),
            (dt_rows[1], None, None),
        ],
        [
            ((4, chunk, piece), bf16, (4, GROUP, piece), lambda i, *_: (0, i, 0)),
            ((8, features), f32, None, None),
        ],
        [pltpu.VMEM((GROUP, features), f32)],
        flops=12_000_000_000,
        moved=20_000_000,
        prefetch=(meta,),
    )
    input_grad = lax.all_to_all(in_pieces, "head", 0, 0).reshape(batch, tokens, piece)

    def token_dot(a, b):
        return lax.dot_general(a, b, (((0,), (0,)), ((), ())), preferred_element_type=f32)

    def reduce_slots(slots):
        one = slots[0] + swap(slots[1].astype(bf16)).astype(f32)
        two = slots[2] + swap(slots[3].astype(bf16)).astype(f32)
        return one + cross(two.astype(bf16)).astype(f32)

    def reduce_exact(slots):
        one = slots[0] + swap(slots[1])
        two = slots[2] + swap(slots[3])
        return one + cross(two)

    g_out = [token_dot(nout[:, k * quarter : (k + 1) * quarter], cotx) for k in range(4)]
    g_z = [token_dot(normed, dgate[:, k * quarter : (k + 1) * quarter]) for k in range(4)]
    g_x = [
        token_dot(normed, dxs[k // 2][:, (k % 2) * quarter : (k % 2 + 1) * quarter]) for k in range(4)
    ]
    g_bc = token_dot(normed, dxs[2])
    g_dt = [token_dot(d["draw"], normed) for d in halves]

    def slot_small(k):
        d = halves[k // 2]
        at = (k % 2) * quarter
        lane = (k % 2) * heads
        base = k // 2 * width
        gw = jnp.sum(d["gw"].reshape(4, 8, width), axis=1) + gw_fix[:, base : base + width]
        row = jnp.concatenate(
            [
                jnp.sum(d["gdtb"], axis=0)[lane : lane + heads],
                (jnp.sum(d["galog"], axis=0) * d["rate"][0])[lane : lane + heads],
                jnp.sum(
                    jnp.sum(gskip, axis=0)[k * quarter : (k + 1) * quarter].reshape(heads, HEAD_DIM), axis=1
                ),
            ]
        )
        return jnp.concatenate(
            [
                gw[:, at : at + quarter],
                jnp.sum(d["gb"], axis=0)[None, at : at + quarter],
                jnp.sum(ggain_out, axis=0)[None, k * quarter : (k + 1) * quarter],
                jnp.pad(row[None], ((0, 1), (0, quarter - 3 * heads))),
                jnp.pad(g_dt[k // 2][lane : lane + heads], ((0, 8 - heads), (0, 0))).reshape(
                    8 * features // quarter, quarter
                ),
            ],
            axis=0,
        )

    small_sum = reduce_exact([slot_small(k) for k in range(4)])
    big = [reduce_slots(g) for g in (g_z, g_x, g_out)]
    gw_bc = jnp.sum(gw_bc.reshape(4, 8, 2 * LANES), axis=1) + gw_fix[:, inner:]
    common = jnp.concatenate(
        [
            g_bc,
            gw_bc,
            jnp.sum(gb_bc, axis=0)[None],
            jnp.sum(ggain_in, axis=0).reshape(3, 2 * LANES),
        ],
        axis=0,
    )
    big, small_sum, common = lax.psum((big, small_sum, lax.psum(common, "head")), "seq")
    gi = common[features + 5 :].reshape(features)
    gi = lax.dynamic_slice(gi, (hi_ * piece,), (piece,))
    row = small_sum[6]
    g_dt_own = small_sum[8:].reshape(8, features)[:heads].T
    return (
        layer_out,
        input_grad,
        gi,
        big[0],
        big[1],
        common[:features],
        g_dt_own,
        small_sum[0:4].T,
        small_sum[4],
        common[features : features + 4].T,
        common[features + 4],
        row[:heads],
        row[heads : 2 * heads],
        row[2 * heads : 3 * heads],
        small_sum[5],
        big[2],
    )


def solution(mesh):
    return jax.shard_map(
        shards,
        mesh=mesh,
        in_specs=(
            P(None, "seq", None),
            P(None, "seq", "head"),
            P(),
            P(None, "head"),
            P(None, "head"),
            P(),
            P(None, "head"),
            P("head", None),
            P("head"),
            P(),
            P(),
            P("head"),
            P("head"),
            P("head"),
            P("head"),
            P("head", None),
            P(),
        ),
        out_specs=(
            P(None, "seq", "head"),
            P(None, "seq", "head"),
            P("head"),
            P(None, "head"),
            P(None, "head"),
            P(),
            P(None, "head"),
            P("head", None),
            P("head"),
            P(),
            P(),
            P("head"),
            P("head"),
            P("head"),
            P("head"),
            P("head", None),
        ),
        check_vma=False,
    )
```

```python
import functools

import jax
import jax.numpy as jnp
import numpy as np
from jax import lax
from jax.experimental import pallas as pl
from jax.experimental.pallas import tpu as pltpu
from jax.sharding import PartitionSpec as P

GROUP = 256
HALF = 128
LANES = 128
HEAD_DIM = 64
EPS = 1e-05
LOG2E = 1.4426950408889634
f32 = jnp.float32
bf16 = jnp.bfloat16
HIGHEST = lax.Precision.HIGHEST
ROWS = 32
MESH = pl.DeviceIdType.MESH


def dot(a, b, ca=1, cb=0, precision=None):
    return lax.dot_general(
        a, b, (((ca,), (cb,)), ((), ())), precision=precision, preferred_element_type=f32
    )


def split2(x):
    hi = x.astype(bf16)
    return hi, (x - hi.astype(f32)).astype(bf16)


def pack(x):
    hi = x.astype(bf16).astype(f32)
    rest = x - hi
    mid = rest.astype(bf16).astype(f32)
    return (hi + pltpu.roll(mid, 32, 1) + pltpu.roll(rest - mid, 64, 1)).astype(bf16)


def unpack(x):
    x = x.astype(f32)
    return lanes_below(x + pltpu.roll(x, LANES - 32, 1) + pltpu.roll(x, LANES - 64, 1), 12)


def expand(x, ex):
    return dot(pack(x), ex)


def lanes_below(x, count):
    return jnp.where(lax.broadcasted_iota(jnp.int32, x.shape, 1) < count, x, 0.0)


def sigmoid(x):
    return 1.0 / (1.0 + jnp.exp(-x))


def softplus(x):
    return jnp.maximum(x, 0.0) + jnp.log1p(jnp.exp(-jnp.abs(x)))


def fold8(x):
    total = x[0:8]
    for r in range(8, x.shape[0], 8):
        total = total + x[r : r + 8]
    return total


def expansion(width):
    heads = width // HEAD_DIM
    ex = np.zeros((LANES, width), np.float32)
    for part in range(3):
        for h in range(heads):
            ex[32 * part + h, h * HEAD_DIM : (h + 1) * HEAD_DIM] = 1.0
    red = np.zeros((width, LANES), np.float32)
    for h in range(heads):
        red[h * HEAD_DIM : (h + 1) * HEAD_DIM, h] = 1.0
    return jnp.asarray(ex, bf16), jnp.asarray(red, bf16)


def run(kernel, grid, ins, outs, scratch=(), flops=0, moved=0, prefetch=(), collective=None):
    def spec(shape, block, imap):
        if block is None:
            rank = len(shape)
            return pl.BlockSpec(shape, lambda *_: (0,) * rank)
        return pl.BlockSpec(block, imap)

    extra = {} if collective is None else {"collective_id": collective, "has_side_effects": True}
    return pl.pallas_call(
        kernel,
        grid_spec=pltpu.PrefetchScalarGridSpec(
            num_scalar_prefetch=len(prefetch),
            grid=grid,
            in_specs=[spec(a.shape, b, m) for a, b, m in ins],
            out_specs=[spec(s, b, m) for s, _, b, m in outs],
            scratch_shapes=list(scratch),
        ),
        out_shape=[jax.ShapeDtypeStruct(s, d) for s, d, _, _ in outs],
        compiler_params=pltpu.CompilerParams(vmem_limit_bytes=56 << 20, **extra),
        cost_estimate=pl.CostEstimate(flops=flops, bytes_accessed=moved, transcendentals=0),
    )(*prefetch, *[a for a, _, _ in ins])


def conv_rows(ext, age, taps, bias, r, cols):
    acc = jnp.broadcast_to(bias[:, cols], (ROWS, LANES))
    for k in range(4):
        back = 3 - k
        term = ext[8 + r - back : 8 + r - back + ROWS, cols] * taps[k : k + 1, cols]
        if back:
            term = jnp.where(age >= back, term, 0.0)
        acc = acc + term
    return acc


def rms(x, gain):
    x = x.astype(f32)
    r = lax.rsqrt(jnp.sum(x * x, axis=1, keepdims=True) / x.shape[1] + EPS)
    return (x * r * gain).astype(bf16)


def norm_kernel(me, hid, gain, bc, normed, ci):
    for r in range(0, GROUP, ROWS):
        normed[r : r + ROWS] = rms(hid[0, r : r + ROWS], gain[...])
    ci[...] = dot(normed[...], bc[...]).astype(bf16)


def front_kernel(with_maps, parts, me, *refs):
    ins, refs = refs[:11], refs[11:]
    normed, edge_far, edge_near, gain, wa, wb, sa, sb, age, tril, ex = ins
    if with_maps:
        (ci_bc, bc, taps_bc, bias_bc), refs = refs[:4], refs[4:]
    else:
        (bmat,), refs = refs[:1], refs[1:]
    (ci, co, val, pre, cum, lin, kb, ck, tot, kout, par, dtp), refs = refs[:12], refs[12:]
    if with_maps:
        (co_bc, bmat, cmat), refs = refs[:3], refs[3:]
    (ext, running, kept, omx, ohi, olo, dts), refs = refs[:7], refs[7:]
    if with_maps:
        (ext_bc,) = refs
    i = pl.program_id(0)
    width = val.shape[1]
    part = width // 2
    heads = part // HEAD_DIM

    @pl.when(i == 0)
    def _():
        running[...] = jnp.zeros_like(running)
        kept[...] = jnp.ones_like(kept)
        near = lax.rem(me[0], parts).astype(f32)
        edge = near * edge_near[0].astype(f32) + (1.0 - near) * edge_far[...].astype(f32)
        before = rms(edge, gain[...])
        for w, at in ((wa, 0), (wb, part)):
            ext[0:8, at : at + part] = dot(before, w[...]).astype(bf16).astype(f32)[8:16]
        if with_maps:
            ext_bc[0:8] = dot(before, bc[...]).astype(bf16).astype(f32)[8:16]
        par[...] = jnp.zeros_like(par)
        for s, at in ((sa, 0), (sb, part)):
            par[0:6, at : at + part] = s[0:6, :part]
        rows_a, rows_b = (jnp.broadcast_to(s[6:7, 0:LANES], (8, LANES)) for s in (sa, sb))

        def lanes(k):
            a = lanes_below(pltpu.roll(rows_a, (LANES - k * heads) % LANES, 1), heads)
            b = lanes_below(pltpu.roll(rows_b, (LANES - k * heads) % LANES, 1), heads)
            return a + pltpu.roll(b, heads, 1)

        par[7:8, LANES : 2 * LANES] = lanes(0)[0:1]
        par[7:8, 0:LANES] = -jnp.exp(lanes(1)[0:1])
        par[6:7] = expand(lanes(2), ex[...])[0:1]
        dts[...] = jnp.zeros_like(dts)
        dts[0:heads] = sa[8 : 8 + heads]
        dts[heads : 2 * heads] = sb[8 : 8 + heads]
        dtp[...] = dts[...].astype(bf16)

    @pl.when(i > 0)
    def _():
        ext[0:8] = ext[GROUP : GROUP + 8]
        if with_maps:
            ext_bc[0:8] = ext_bc[GROUP : GROUP + 8]

    taps, bias = par, par[4:5]
    rate, dtb = par[7:8, 0:LANES], par[7:8, LANES : 2 * LANES]
    for w, at in ((wa, 0), (wb, part)):
        low = dot(normed[...], w[...]).astype(bf16)
        ci[:, at : at + part] = low
        ext[8 : 8 + GROUP, at : at + part] = low.astype(f32)
    raw = dot(normed[...], dtp[...], 1, 1) + dtb
    pre[...] = raw
    delta = softplus(raw)
    c = dot(tril[...], delta * rate, precision=HIGHEST)
    cum[...] = c
    end = c[GROUP - 1 : GROUP]
    age_end = age[GROUP - 1 : GROUP]
    left = GROUP - 1 - lax.broadcasted_iota(jnp.int32, c.shape, 0)
    omega = jnp.where(left <= age_end, jnp.exp(end - c), 0.0) * delta
    omx[...] = expand(lanes_below(omega, 2 * heads), ex[...])
    keep = jnp.where(age_end >= GROUP, jnp.exp(end), 0.0)
    keep = lanes_below(jnp.broadcast_to(keep, (8, LANES)), 2 * heads)
    keepx = expand(keep, ex[...])
    if with_maps:
        ext_bc[8 : 8 + GROUP] = ci_bc[...].astype(f32)
        for r in range(0, GROUP, ROWS):
            a = age[r : r + ROWS]
            for j, out in enumerate((bmat, cmat)):
                cols = slice(j * LANES, (j + 1) * LANES)
                v = conv_rows(ext_bc, a, taps_bc, bias_bc, r, cols)
                co_bc[r : r + ROWS, cols] = v
                out[r : r + ROWS] = (v * sigmoid(v)).astype(bf16)
    for r in range(0, GROUP, ROWS):
        a = age[r : r + ROWS]
        rows = slice(r, r + ROWS)
        for j in range(width // LANES):
            cols = slice(j * LANES, (j + 1) * LANES)
            v = conv_rows(ext, a, taps, bias, r, cols)
            co[rows, cols] = v
            act = (v * sigmoid(v)).astype(bf16)
            val[rows, cols] = act
            ohi[rows, cols], olo[rows, cols] = split2(omx[rows, cols] * act.astype(f32))
    own = dot(bmat[...], ohi[...], 0, 0) + dot(bmat[...], olo[...], 0, 0)
    lin[0] = running[...]
    kb[0] = expand(lanes_below(kept[...], 2 * heads), ex[...])
    ck[0] = keepx
    running[...] = keepx[0:1] * running[...] + own
    kept[...] = keep * kept[...]
    tot[...] = running[...]
    kout[...] = kept[...]


class Exchange:
    def __init__(self, reverse, n, parts, tots, kouts, ex, own, other, scratch):
        self.reverse, self.n, self.tots, self.kouts, self.ex = reverse, n, tots, kouts, ex
        self.own, self.other = own, other
        (
            self.out, self.got, self.payload, self.spread, self.scanned, self.home, self.lead, self.lead_k, self.arr,
            self.theirs, self.last, self.swap_sems, self.to_sems, self.from_sems, self.back_to, self.back_from,
        ) = scratch
        self.me = lax.axis_index("seq")
        head = lax.axis_index("head")
        self.partner = head + 1 - 2 * lax.rem(head, 2)
        half = lax.rem(head, parts)
        self.leads = (half if reverse else 1 - half).astype(f32)
        self.per = LANES // n

    @staticmethod
    def scratch(n, width):
        rows = max(LANES // n, 8)
        return [
            pltpu.VMEM((LANES + 8, width), f32),
            pltpu.VMEM((LANES + 8, width), f32),
            pltpu.VMEM((n, rows, width + LANES), f32),
            pltpu.VMEM((n, rows, width + LANES), f32),
            pltpu.VMEM((n, rows, width), f32),
            pltpu.VMEM((n, rows, width), f32),
            pltpu.VMEM((LANES, width), f32),
            pltpu.VMEM((8, LANES), f32),
            pltpu.VMEM((LANES, width), f32),
            pltpu.VMEM((LANES, width), f32),
            pltpu.VMEM((LANES, width), f32),
            pltpu.SemaphoreType.DMA((4,)),
            pltpu.SemaphoreType.DMA((n,)),
            pltpu.SemaphoreType.DMA((n,)),
            pltpu.SemaphoreType.DMA((n,)),
            pltpu.SemaphoreType.DMA((n,)),
        ]

    def peers(self):
        for d in range(1, self.n):
            yield d, lax.rem(self.me + d, self.n), lax.rem(self.me + self.n - d, self.n)

    def swap(self, src, dst, sem):
        return pltpu.make_async_remote_copy(
            src_ref=src,
            dst_ref=dst,
            send_sem=self.swap_sems.at[sem],
            recv_sem=self.swap_sems.at[sem + 1],
            device_id={"head": self.partner},
            device_id_type=MESH,
        )

    def move(self, src, dst, d, to, send_sems, recv_sems):
        return pltpu.make_async_remote_copy(
            src_ref=src.at[to],
            dst_ref=dst.at[self.me],
            send_sem=send_sems.at[d],
            recv_sem=recv_sems.at[d],
            device_id={"seq": to},
            device_id_type=MESH,
        )

    def begin(self):
        barrier = pltpu.get_barrier_semaphore()
        pl.semaphore_signal(barrier, inc=1, device_id={"head": self.partner}, device_id_type=MESH)
        for _, to, _ in self.peers():
            pl.semaphore_signal(barrier, inc=1, device_id={"seq": to}, device_id_type=MESH)
        pl.semaphore_wait(barrier, self.n)
        part = self.out.shape[1] // 2
        heads = part // HEAD_DIM
        for k in range(2):
            self.out[0:LANES, k * part : (k + 1) * part] = self.tots[k][:, part:]
            rolled = pltpu.roll(self.kouts[k][...], LANES - heads, 1)
            self.out[LANES : LANES + 8, k * LANES : (k + 1) * LANES] = lanes_below(rolled, heads)
        self.out[LANES : LANES + 8, 2 * LANES :] = jnp.zeros((8, 2 * part - 2 * LANES), f32)
        self.swap(self.out, self.got, 0).start()

    def combine(self):
        self.swap(self.out, self.got, 0).wait()
        part = self.out.shape[1] // 2
        heads = part // HEAD_DIM
        leads, follows = self.leads, 1.0 - self.leads
        k_a, k_b = (lanes_below(k[...], heads) for k in self.kouts)
        mine_k = k_a + pltpu.roll(k_b, heads, 1)
        got_k = self.got[LANES : LANES + 8, 0:LANES] + pltpu.roll(
            self.got[LANES : LANES + 8, LANES : 2 * LANES], heads, 1
        )
        lk = leads * mine_k + follows * got_k
        fk = leads * got_k + follows * mine_k
        fkx = expand(fk, self.ex[...])[0:1]
        self.lead_k[...] = lk
        for k in range(2):
            cols = slice(k * part, (k + 1) * part)
            mine, got = self.tots[k][:, :part], self.got[0:LANES, cols]
            ls = leads * mine + follows * got
            self.lead[:, cols] = ls
            self.arr[:, cols] = fkx[:, cols] * ls + (leads * got + follows * mine)
        keep = (lk * fk)[0:1]
        rows = self.payload.shape[1]
        for s in range(self.n):
            self.payload[s, 0 : self.per, 0 : 2 * part] = self.arr[s * self.per : (s + 1) * self.per]
            self.payload[s, :, 2 * part :] = jnp.broadcast_to(keep, (rows, LANES))
        for d, to, _ in self.peers():
            self.move(self.payload, self.spread, d, to, self.to_sems, self.from_sems).start()
        self.spread[self.me] = self.payload[self.me]

    def scan(self):
        for d, to, _ in self.peers():
            self.move(self.payload, self.spread, d, to, self.to_sems, self.from_sems).wait()
        width = self.scanned.shape[2]
        rows = self.scanned.shape[1]
        state = jnp.zeros((rows, width), f32)
        for step in range(self.n):
            at = self.n - 1 - step if self.reverse else step
            self.scanned[at] = state
            if step < self.n - 1:
                keep = expand(self.spread[at, :, width:], self.ex[...])
                state = keep * state + self.spread[at, :, 0:width]
        for d, to, _ in self.peers():
            self.move(self.scanned, self.home, d, to, self.back_to, self.back_from).start()
        self.home[self.me] = self.scanned[self.me]

    def finish(self):
        for d, to, _ in self.peers():
            self.move(self.scanned, self.home, d, to, self.back_to, self.back_from).wait()
        for s in range(self.n):
            self.arr[s * self.per : (s + 1) * self.per] = self.home[s, 0 : self.per]
        leads, follows = self.leads, 1.0 - self.leads
        first = self.arr[...]
        second = expand(self.lead_k[...], self.ex[...])[0:1] * first + self.lead[...]
        self.theirs[...] = leads * second + follows * first
        copy = self.swap(self.theirs, self.last, 2)
        copy.start()
        self.own[...] = leads * first + follows * second
        copy.wait()
        self.other[...] = self.last[...]


def pair_masks(x, lane_axis_shape):
    lane = lax.broadcasted_iota(jnp.int32, lane_axis_shape, 1)
    zero = jnp.zeros_like(x)
    return jnp.where(lane < HEAD_DIM, x, zero), jnp.where(lane >= HEAD_DIM, x, zero)


def intra_unit(val, bmat, cmat, age, pre, cum, dskip, part):
    t = lax.broadcasted_iota(jnp.int32, (HALF, HALF), 0)
    s = lax.broadcasted_iota(jnp.int32, (HALF, HALF), 1)
    scores = dot(cmat[...], bmat[...], 1, 1)
    a0, a1 = age[0:HALF], age[HALF:]
    gap = t - s
    s00 = jnp.where((gap >= 0) & (gap <= a0), scores[:HALF, :HALF], 0.0)
    s11 = jnp.where((gap >= 0) & (gap <= a1), scores[HALF:, HALF:], 0.0)
    s10 = jnp.where(gap + HALF <= a1, scores[HALF:, :HALF], 0.0)
    c2 = cum[...] * LOG2E
    rows = (c2 - jnp.log2(softplus(pre[...]))).T
    for j in range(val.shape[1] // LANES):
        cols = slice(j * LANES, (j + 1) * LANES)
        v = val[:, cols]
        vm = pair_masks(v, v.shape)
        tops, bottoms = [], []
        for which in range(2):
            h = 2 * j + which
            col0 = jnp.broadcast_to(c2[:HALF, h : h + 1], (HALF, HALF))
            col1 = jnp.broadcast_to(c2[HALF:, h : h + 1], (HALF, HALF))
            r0 = rows[h : h + 1, :HALF]
            r1 = rows[h : h + 1, HALF:]
            tops.append((s00 * jnp.exp2(jnp.minimum(col0 - r0, 60.0))).astype(bf16))
            bottoms.append((s10 * jnp.exp2(col1 - r0)).astype(bf16))
            bottoms.append((s11 * jnp.exp2(jnp.minimum(col1 - r1, 60.0))).astype(bf16))
        top = dot(jnp.concatenate(tops, axis=1), jnp.concatenate([vm[0][:HALF], vm[1][:HALF]], axis=0))
        bottom = dot(jnp.concatenate(bottoms, axis=1), jnp.concatenate([vm[0], vm[1]], axis=0))
        skip = dskip[6:7, cols]
        part[:HALF, cols] = top + skip * v[:HALF].astype(f32)
        part[HALF:, cols] = bottom + skip * v[HALF:].astype(f32)


def intra_kernel(
    n, parts, count, val_a, val_b, bmat, cmat, age, pre_a, pre_b, cum_a, cum_b, par_a, par_b,
    tot_a, tot_b, k_a, k_b, ex, part_a, part_b, own, other, *scratch
):
    u = pl.program_id(0)
    states = Exchange(False, n, parts, (tot_a, tot_b), (k_a, k_b), ex, own, other, scratch)
    pl.when(u == 0)(states.begin)

    @pl.when(u < count)
    def _():
        intra_unit(val_a, bmat, cmat, age, pre_a, cum_a, par_a, part_a)

    @pl.when(u >= count)
    def _():
        intra_unit(val_b, bmat, cmat, age, pre_b, cum_b, par_b, part_b)

    pl.when(u == 0)(states.combine)
    pl.when(u == 2 * count - 3)(states.scan)
    pl.when(u == 2 * count - 1)(states.finish)


def arriving_half(own, other, half):
    part = own.shape[1] // 2
    cols = slice(half * part, (half + 1) * part)
    return jnp.concatenate([own[:, cols].astype(f32), other[:, cols].astype(f32)], axis=1)


def mid_kernel(
    meta, hid, normed, z0, z1, z2, z3, o0, o1, o2, o3, cot0, cot1, cot2, cot3, cmat, age, ex, red, par_a, par_b,
    part_a, part_b, val_a, val_b, cum_a, cum_b, lin_a, lin_b, kb_a, kb_b, ck_a, ck_b, arr, arr_other,
    piece0, piece1, piece2, piece3, nout, cotx, dssd, dgate, dcin, dkk_a, dkk_b,
    lout_a, lout_b, ka_a, ka_b, tot_a, tot_b, kout_a, kout_b, ggain, gskip,
    gate, dno, read, kx, ssd_s, sig_s, khi, klo, rhi, rlo, run_a, run_b, kept_a, kept_b, shuffle,
):
    i = pl.program_id(0)
    inner = nout.shape[1]
    width = inner // 2
    tiles = inner // LANES
    heads = width // HEAD_DIM
    quarter = inner // 4

    @pl.when(i == 0)
    def _():
        for ref in (run_a, run_b, ggain, gskip):
            ref[...] = jnp.zeros_like(ref)
        for ref in (kept_a, kept_b):
            ref[...] = jnp.ones_like(ref)

    me = meta[0]
    for k, cot in enumerate((cot0, cot1, cot2, cot3)):
        shuffle[me ^ k] = cot[...]
    cotan = jnp.concatenate([shuffle[0], shuffle[1], shuffle[2], shuffle[3]], axis=1)
    cotx[...] = cotan
    states = []
    for half, (lin, kb, cum) in enumerate(((lin_a, kb_a, cum_a), (lin_b, kb_b, cum_b))):
        cols = slice(half * width, (half + 1) * width)
        hi, lo = split2(lin[0] + kb[0, 0:1] * arriving_half(arr, arr_other, half))
        states.append((hi, lo))
        read[:, cols] = dot(cmat[...], hi) + dot(cmat[...], lo)
        since = lax.broadcasted_iota(jnp.int32, age.shape, 0)
        kappa = jnp.where(age[...] > since, jnp.exp(cum[...]), 0.0)
        kx[:, cols] = expand(lanes_below(kappa, heads), ex[...])
    for k, (z, o) in enumerate(((z0, o0), (z1, o1), (z2, o2), (z3, o3))):
        cols = slice(k * quarter, (k + 1) * quarter)
        gate[:, cols] = dot(normed[...], z[...])
        dno[:, cols] = dot(cotan, o[...], 1, 1)

    gains = [
        (par_a if j < tiles // 2 else par_b)[5:6, (j * LANES) % width : (j * LANES) % width + LANES]
        for j in range(tiles)
    ]

    def rows_body(step, _):
        rows = pl.ds(pl.multiple_of(step * ROWS, ROWS), ROWS)
        squares = jnp.zeros((ROWS, LANES), f32)
        inners = jnp.zeros((ROWS, LANES), f32)
        for j in range(tiles):
            cols = slice(j * LANES, (j + 1) * LANES)
            part = part_a if j < tiles // 2 else part_b
            pcols = slice(cols.start % width, cols.start % width + LANES)
            ssd = part[rows, pcols] + kx[rows, cols] * read[rows, cols]
            g = gate[rows, cols]
            sig = sigmoid(g)
            gated = ssd * (g * sig)
            squares += gated * gated
            inners += gated * (dno[rows, cols] * gains[j])
            ssd_s[rows, cols] = ssd
            sig_s[rows, cols] = sig
        rg = lax.rsqrt(jnp.sum(squares, axis=1, keepdims=True) / inner + EPS)
        stat = rg * rg * (jnp.sum(inners, axis=1, keepdims=True) / inner)
        rg = jnp.broadcast_to(rg, (ROWS, LANES))
        stat = jnp.broadcast_to(stat, (ROWS, LANES))
        for j in range(tiles):
            cols = slice(j * LANES, (j + 1) * LANES)
            val = val_a if j < tiles // 2 else val_b
            pcols = slice(cols.start % width, cols.start % width + LANES)
            ssd, sig, g, d = ssd_s[rows, cols], sig_s[rows, cols], gate[rows, cols], dno[rows, cols]
            act = g * sig
            gated = ssd * act
            yhat = gated * rg
            nout[rows, cols] = (yhat * gains[j]).astype(bf16)
            ggain[:, cols] += fold8(d * yhat)
            dgated = rg * (d * gains[j] - gated * stat)
            low = (dgated * act).astype(bf16)
            dssd[rows, cols] = low
            dgate[rows, cols] = (dgated * ssd * (sig * (1.0 + g * (1.0 - sig)))).astype(bf16)
            dy = low.astype(f32)
            gskip[:, cols] += fold8(dy * val[rows, pcols].astype(f32))
            kd = kx[rows, cols] * dy
            khi[rows, cols], klo[rows, cols] = split2(kd)
            rhi[rows, cols], rlo[rows, cols] = split2(kd * read[rows, cols])
        return 0

    lax.fori_loop(0, GROUP // ROWS, rows_body, 0)
    out = hid[0].astype(f32)
    for k, o in enumerate((o0, o1, o2, o3)):
        out = out + dot(nout[:, k * quarter : (k + 1) * quarter], o[...])
    out = out.astype(bf16)
    piece = out.shape[1] // 4
    for k in range(4):
        shuffle[k] = out[:, k * piece : (k + 1) * piece]
    for k, to in enumerate((piece0, piece1, piece2, piece3)):
        to[...] = shuffle[me ^ k]
    dc = None
    age_end = age[GROUP - 1 : GROUP]
    for half, (dkk, ck, cum, lout, ka, tot, kout, running, kept) in enumerate(
        (
            (dkk_a, ck_a, cum_a, lout_a, ka_a, tot_a, kout_a, run_a, kept_a),
            (dkk_b, ck_b, cum_b, lout_b, ka_b, tot_b, kout_b, run_b, kept_b),
        )
    ):
        cols = slice(half * width, (half + 1) * width)
        hi, lo = states[half]
        dkk[...] = dot(rhi[:, cols], red[...]) + dot(rlo[:, cols], red[...])
        term = dot(khi[:, cols], hi, 1, 1) + dot(khi[:, cols], lo, 1, 1) + dot(klo[:, cols], hi, 1, 1)
        dc = term if dc is None else dc + term
        own = dot(cmat[...], khi[:, cols], 0, 0) + dot(cmat[...], klo[:, cols], 0, 0)
        lout[0] = running[...]
        ka[0] = expand(lanes_below(kept[...], heads), ex[...])
        running[...] = ck[0, 0:1] * running[...] + own
        keep = jnp.where(age_end >= GROUP, jnp.exp(cum[GROUP - 1 : GROUP]), 0.0)
        kept[...] = lanes_below(jnp.broadcast_to(keep, (8, LANES)), heads) * kept[...]
        tot[...] = running[...]
        kout[...] = kept[...]
    dcin[...] = dc


def pairs_unit(val, dssd, bmat, cmat, ager, pre, cum, dvi, dbi, dci, rflow, cflow, rft):
    s = lax.broadcasted_iota(jnp.int32, (HALF, HALF), 0)
    t = lax.broadcasted_iota(jnp.int32, (HALF, HALF), 1)
    scores = dot(bmat[...], cmat[...], 1, 1)
    a0, a1 = ager[0:1, :HALF], ager[0:1, HALF:]
    gap = t - s
    m00 = (gap >= 0) & (gap <= a0)
    m11 = (gap >= 0) & (gap <= a1)
    m01 = gap + HALF <= a1
    s00 = jnp.where(m00, scores[:HALF, :HALF], 0.0)
    s11 = jnp.where(m11, scores[HALF:, HALF:], 0.0)
    s01 = jnp.where(m01, scores[:HALF, HALF:], 0.0)
    c2 = cum[...] * LOG2E
    cr = c2 - jnp.log2(softplus(pre[...]))
    c2t = c2.T
    lane = lax.broadcasted_iota(jnp.int32, (HALF, LANES), 1)
    zero = jnp.zeros((HALF, HALF), f32)
    d00, d01, d11 = zero, zero, zero
    cf0, cf1 = zero, zero
    rft[...] = jnp.zeros_like(rft)
    for j in range(val.shape[1] // LANES):
        cols = slice(j * LANES, (j + 1) * LANES)
        v = val[:, cols]
        dy = dssd[:, cols]
        vm = pair_masks(v, v.shape)
        dm = pair_masks(dy, dy.shape)
        tops, bottoms = [], []
        for which in range(2):
            h = 2 * j + which
            col0 = jnp.broadcast_to(cr[:HALF, h : h + 1], (HALF, HALF))
            col1 = jnp.broadcast_to(cr[HALF:, h : h + 1], (HALF, HALF))
            r0 = c2t[h : h + 1, :HALF]
            r1 = c2t[h : h + 1, HALF:]
            e00 = jnp.exp2(jnp.minimum(r0 - col0, 60.0))
            e01 = jnp.exp2(r1 - col0)
            e11 = jnp.exp2(jnp.minimum(r1 - col1, 60.0))
            tops.append((s00 * e00).astype(bf16))
            tops.append((s01 * e01).astype(bf16))
            bottoms.append((s11 * e11).astype(bf16))
            w0 = dot(vm[which][:HALF], dy, 1, 1)
            w1 = dot(vm[which][HALF:], dy[HALF:], 1, 1)
            de00 = w0[:, :HALF] * e00
            de01 = w0[:, HALF:] * e01
            de11 = w1 * e11
            d00 += de00
            d01 += de01
            d11 += de11
            f00 = de00 * s00
            f01 = de01 * s01
            f11 = de11 * s11
            rft[h : h + 1, :HALF] = jnp.sum(f00, axis=0, keepdims=True)
            rft[h : h + 1, HALF:] = jnp.sum(f01 + f11, axis=0, keepdims=True)
            cf0 = jnp.where(lane == h, jnp.sum(f00 + f01, axis=1, keepdims=True), cf0)
            cf1 = jnp.where(lane == h, jnp.sum(f11, axis=1, keepdims=True), cf1)
        dvi[:HALF, cols] = dot(jnp.concatenate(tops, axis=1), jnp.concatenate([dm[0], dm[1]], axis=0))
        dvi[HALF:, cols] = dot(
            jnp.concatenate(bottoms, axis=1), jnp.concatenate([dm[0][HALF:], dm[1][HALF:]], axis=0)
        )
    cflow[:HALF] = cf0
    cflow[HALF:] = cf1
    rflow[...] = rft[...].T
    d00 = split2(jnp.where(m00, d00, 0.0))
    d01 = split2(jnp.where(m01, d01, 0.0))
    d11 = split2(jnp.where(m11, d11, 0.0))
    b0, b1, c0, c1 = bmat[:HALF], bmat[HALF:], cmat[:HALF], cmat[HALF:]
    dbi[:HALF] = dot(d00[0], c0) + dot(d00[1], c0) + dot(d01[0], c1) + dot(d01[1], c1)
    dbi[HALF:] = dot(d11[0], c1) + dot(d11[1], c1)
    dci[:HALF] = dot(d00[0], b0, 0, 0) + dot(d00[1], b0, 0, 0)
    dci[HALF:] = (
        dot(d01[0], b0, 0, 0) + dot(d01[1], b0, 0, 0) + dot(d11[0], b1, 0, 0) + dot(d11[1], b1, 0, 0)
    )


def pairs_kernel(
    n, parts, count, val_a, val_b, dssd, bmat, cmat, ager, pre_a, pre_b, cum_a, cum_b, tot_a, tot_b, k_a, k_b, ex,
    dvi_a, dbi_a, dci_a, rflow_a, cflow_a, dvi_b, dbi_b, dci_b, rflow_b, cflow_b, own, other, rft, *scratch
):
    u = pl.program_id(0)
    states = Exchange(True, n, parts, (tot_a, tot_b), (k_a, k_b), ex, own, other, scratch)
    pl.when(u == 0)(states.begin)

    @pl.when(u < count)
    def _():
        pairs_unit(val_a, dssd, bmat, cmat, ager, pre_a, cum_a, dvi_a, dbi_a, dci_a, rflow_a, cflow_a, rft)

    @pl.when(u >= count)
    def _():
        pairs_unit(val_b, dssd, bmat, cmat, ager, pre_b, cum_b, dvi_b, dbi_b, dci_b, rflow_b, cflow_b, rft)

    pl.when(u == 0)(states.combine)
    pl.when(u == 2 * count - 4)(states.scan)
    pl.when(u == 2 * count - 1)(states.finish)


def slope(x):
    sig = sigmoid(x)
    return sig * (1.0 + x * (1.0 - sig))


def conv_back(i, dco, agex, age, ci, taps, dci, tail, head, gw):
    width = ci.shape[1]
    for r in range(0, GROUP, ROWS):
        ages = [agex[r + m : r + m + ROWS] for m in range(4)]
        for j in range(width // LANES):
            cols = slice(j * LANES, (j + 1) * LANES)
            c = ci[r : r + ROWS, cols].astype(f32)
            acc = None
            for m in range(4):
                x = dco[r + m : r + m + ROWS, cols]
                if m:
                    x = jnp.where(ages[m] >= m, x, 0.0)
                term = x * taps[3 - m : 4 - m, cols]
                acc = term if acc is None else acc + term
                gw[8 * (3 - m) : 8 * (3 - m) + 8, cols] += fold8(x * c)
            dci[r : r + ROWS, cols] = acc.astype(bf16)
            if r == GROUP - ROWS:

                @pl.when(i == 0)
                def _():
                    tail[:, cols] = acc[ROWS - 8 :]

    head[...] = dco[0:8]


def start_next(i, dco, agex, gw, gb):
    @pl.when(i == 0)
    def _():
        dco[GROUP : GROUP + 8] = jnp.zeros((8, dco.shape[1]), f32)
        agex[GROUP : GROUP + 8] = jnp.zeros((8, LANES), jnp.int32)
        gw[...] = jnp.zeros_like(gw)
        gb[...] = jnp.zeros_like(gb)

    @pl.when(i > 0)
    def _():
        dco[GROUP : GROUP + 8] = dco[0:8]
        agex[GROUP : GROUP + 8] = agex[0:8]


def back_kernel(
    half, val, dssd, dvi, bmat, co, ci, age, pre, cum, lout, ka, leav, leav_other, lin, kb, arr, arr_other,
    rflow, cflow, dkk, par, tril, ex, red,
    dci, tail, head, draw, gw, gb, galog, gdtb,
    dco, agex, back, omx, vhi, vlo,
):
    i = pl.program_id(0)
    width = val.shape[1]
    heads = width // HEAD_DIM
    start_next(i, dco, agex, gw, gb)

    @pl.when(i == 0)
    def _():
        galog[...] = jnp.zeros_like(galog)
        gdtb[...] = jnp.zeros_like(gdtb)

    agex[0:GROUP] = age[...]
    ds = lout[0] + ka[0, 0:1] * arriving_half(leav, leav_other, half)
    dhi, dlo = split2(ds)
    back[...] = dot(bmat[...], dhi) + dot(bmat[...], dlo)
    p = pre[...]
    delta = softplus(p)
    c = cum[...]
    end = c[GROUP - 1 : GROUP]
    age_end = age[GROUP - 1 : GROUP]
    row = lax.broadcasted_iota(jnp.int32, c.shape, 0)
    tail_keep = jnp.where(GROUP - 1 - row <= age_end, jnp.exp(end - c), 0.0)
    omega = tail_keep * delta
    omx[...] = expand(lanes_below(omega, heads), ex[...])
    for r in range(0, GROUP, ROWS):
        rows = slice(r, r + ROWS)
        for j in range(width // LANES):
            cols = slice(j * LANES, (j + 1) * LANES)
            v = val[rows, cols].astype(f32)
            b = back[rows, cols]
            o = omx[rows, cols]
            dval = par[6:7, cols] * dssd[rows, cols].astype(f32) + dvi[rows, cols] + o * b
            vhi[rows, cols], vlo[rows, cols] = split2(v * b)
            d = dval * slope(co[rows, cols])
            dco[rows, cols] = d
            gb[:, cols] += fold8(d)
    domega = dot(vhi[...], red[...]) + dot(vlo[...], red[...])
    flow = domega * omega
    sin = lin[0] + kb[0, 0:1] * arriving_half(arr, arr_other, half)
    carry = jnp.broadcast_to(jnp.sum(ds * sin, axis=0, keepdims=True), (8, width))
    carry = dot(carry, red[...].astype(f32), precision=HIGHEST)[0:1]
    keep = jnp.where(age_end >= GROUP, jnp.exp(end), 0.0)
    dcum = rflow[...] - cflow[...] + dkk[...] - flow
    ending = jnp.sum(flow, axis=0, keepdims=True) + carry * keep
    dcum = dcum + jnp.where(row == GROUP - 1, ending, 0.0)
    dlog = dot(tril[...], dcum, 0, 0, precision=HIGHEST)
    sig = sigmoid(p)
    ratio = jnp.where(delta > 1e-30, sig / delta, 1.0)
    rate = par[7:8, 0:LANES]
    drf = cflow[...] * ratio + (domega * tail_keep + dlog * rate) * sig
    drf = lanes_below(drf, heads)
    draw[...] = drf.astype(bf16)
    gdtb[...] += fold8(drf)
    galog[...] += fold8(dlog * delta * rate)
    conv_back(i, dco, agex, age, ci, par, dci, tail, head, gw)


def maps_kernel(
    dbi_a, dbi_b, dci_a, dci_b, dcin, co, ci, age, taps,
    val_a, val_b, pre_a, pre_b, cum_a, cum_b, lout_a, lout_b, ka_a, ka_b, leav, leav_other, ex,
    dci, tail, head, gw, gb, dco, agex, dbin,
):
    i = pl.program_id(0)
    start_next(i, dco, agex, gw, gb)
    agex[0:GROUP] = age[...]
    age_end = age[GROUP - 1 : GROUP]
    width = val_a.shape[1]
    row = lax.broadcasted_iota(jnp.int32, (GROUP, LANES), 0)
    total = dbi_a[...] + dbi_b[...]
    for half, (val, pre, cum, lout, ka) in enumerate(
        ((val_a, pre_a, cum_a, lout_a, ka_a), (val_b, pre_b, cum_b, lout_b, ka_b))
    ):
        dhi, dlo = split2(lout[0] + ka[0, 0:1] * arriving_half(leav, leav_other, half))
        c = cum[...]
        tail_keep = jnp.where(GROUP - 1 - row <= age_end, jnp.exp(c[GROUP - 1 : GROUP] - c), 0.0)
        omx = expand(lanes_below(tail_keep * softplus(pre[...]), width // HEAD_DIM), ex[...])
        ohi, olo = split2(omx * val[...].astype(f32))
        total = total + dot(ohi, dhi, 1, 1) + dot(ohi, dlo, 1, 1) + dot(olo, dhi, 1, 1)
    dbin[...] = total
    for r in range(0, GROUP, ROWS):
        rows = slice(r, r + ROWS)
        dc = dci_a[rows] + dci_b[rows] + dcin[rows]
        for j, d in enumerate((dbin[rows], dc)):
            cols = slice(j * LANES, (j + 1) * LANES)
            d = d * slope(co[rows, cols])
            dco[rows, cols] = d
            gb[:, cols] += fold8(d)
    conv_back(i, dco, agex, age, ci, taps, dci, tail, head, gw)


def mended(x, last, scr):
    scr[...] = x[...]

    @pl.when(pl.program_id(0) == pl.num_programs(0) - 1)
    def _():
        scr[GROUP - 16 :] = last[...]

    return scr


def early_kernel(dgate, z0, z1, z2, z3, dbc, last_bc, bc, dx, last, x2, x3, dr, dt, out, scr_bc, scr):
    quarter = z0.shape[1]
    dbc = mended(dbc, last_bc, scr_bc)
    dx = mended(dx, last, scr)
    acc = dot(dbc[...], bc[...], 1, 1) + dot(dr[...], dt[...])
    for k, z in enumerate((z0, z1, z2, z3)):
        acc = acc + dot(dgate[:, k * quarter : (k + 1) * quarter], z[...], 1, 1)
    for k, x in enumerate((x2, x3)):
        acc = acc + dot(dx[:, k * quarter : (k + 1) * quarter], x[...], 1, 1)
    out[...] = acc


def final_kernel(
    meta, hid, cotx, gain, early, dx, last, x0, x1, dr, dt,
    piece0, piece1, piece2, piece3, ggain, acc_s, shuffle, scr,
):
    @pl.when(pl.program_id(0) == 0)
    def _():
        ggain[...] = jnp.zeros_like(ggain)

    quarter = x0.shape[1]
    dx = mended(dx, last, scr)
    acc = early[...] + dot(dr[...], dt[...])
    for k, x in enumerate((x0, x1)):
        acc = acc + dot(dx[:, k * quarter : (k + 1) * quarter], x[...], 1, 1)
    acc_s[...] = acc
    piece = acc.shape[1] // 4
    for r in range(0, GROUP, ROWS):
        rows = slice(r, r + ROWS)
        x = hid[0, rows].astype(f32)
        rinv = lax.rsqrt(jnp.sum(x * x, axis=1, keepdims=True) / x.shape[1] + EPS)
        xhat = x * rinv
        d = acc_s[rows]
        ggain[...] += fold8(d * xhat)
        dxh = d * gain[...]
        mean = jnp.sum(dxh * xhat, axis=1, keepdims=True) / x.shape[1]
        out = (cotx[rows].astype(f32) + rinv * (dxh - xhat * mean)).astype(bf16)
        for k in range(4):
            shuffle[k, rows] = out[:, k * piece : (k + 1) * piece]
    for k, to in enumerate((piece0, piece1, piece2, piece3)):
        to[...] = shuffle[meta[0] ^ k]


def grads_kernel(pairs, *refs):
    lhs, rhs, (keep, send) = refs[: pairs[0]], refs[pairs[0] : -2], refs[-2:]
    part = keep.shape[2]
    for p, (a, b, at) in enumerate(pairs[1]):
        res = dot(lhs[a][...], rhs[b][:, at : at + 2 * part], 0, 0)
        keep[p] = res[:, :part]
        send[p] = res[:, part:].astype(bf16)


def mend(got, tail, ci, next_age, taps, dx, scr, last, flip):
    g = got[...]
    if flip:
        part = g.shape[1] // 2
        g = jnp.concatenate([g[:, part:], g[:, :part]], axis=1)
    rows = scr.shape[0]
    scr[...] = dx[...]
    ending = ci[rows - 16 :].astype(f32)[8:16]
    row = lax.broadcasted_iota(jnp.int32, (8, LANES), 0)
    fixed, sums = [], []
    for j in range(g.shape[1] // LANES):
        cols = slice(j * LANES, (j + 1) * LANES)
        acc = tail[:, cols]
        parts = [jnp.zeros((1, LANES), f32)] * 4
        for m in range(1, 4):
            use = (row >= 8 - m) & (pltpu.roll(next_age[...], 8 - m, 0) >= m)
            x = jnp.where(use, pltpu.roll(g[:, cols], 8 - m, 0), 0.0)
            acc = acc + x * taps[3 - m : 4 - m, cols]
            parts[3 - m] = jnp.sum(x * ending[:, cols], axis=0, keepdims=True)
        fixed.append(acc)
        sums.append(jnp.concatenate(parts, axis=0))
    fixed = jnp.concatenate(fixed, axis=1)
    before = dx[rows - 16 :].astype(f32)[0:8]
    scr[rows - 16 :] = jnp.concatenate([before, fixed], axis=0).astype(bf16)
    last[...] = scr[rows - 16 :]
    return jnp.concatenate(sums, axis=1)


def half_grads_kernel(
    at, normed, dx, got, tail, ci, next_age, par, draw, gw, gb, galog, gdtb, gskip, ggain, red,
    keep, send, small_keep, small_send, last, scr,
):
    i = pl.program_id(0)
    part = keep.shape[1]
    heads = part // HEAD_DIM
    width = 2 * part

    @pl.when(i == 0)
    def _():
        fix = mend(got, tail, ci, next_age, par, dx, scr, last, True)
        for to in (small_keep, small_send):
            to[...] = jnp.zeros_like(to)
        taps = [jnp.sum(gw[8 * k : 8 * k + 8], axis=0, keepdims=True) for k in range(4)]
        taps = jnp.concatenate(taps, axis=0) + fix
        bias = jnp.sum(gb[...], axis=0, keepdims=True)
        cols = slice(at * width, (at + 1) * width)
        gain = jnp.sum(ggain[:, cols], axis=0, keepdims=True)
        skip = jnp.broadcast_to(jnp.sum(gskip[:, cols], axis=0, keepdims=True), (8, width))
        skip = dot(skip, red[...].astype(f32), precision=HIGHEST)
        step = jnp.broadcast_to(jnp.sum(gdtb[...], axis=0, keepdims=True), (8, LANES))
        log = jnp.broadcast_to(jnp.sum(galog[...], axis=0, keepdims=True), (8, LANES))
        for k, to in enumerate((small_keep, small_send)):
            mine = slice(k * part, (k + 1) * part)
            to[0:4, 0:part] = taps[:, mine]
            to[4:5, 0:part] = bias[:, mine]
            to[5:6, 0:part] = gain[:, mine]
            row = jnp.zeros((8, LANES), f32)
            for place, x in enumerate((step, log, skip)):
                x = lanes_below(pltpu.roll(x, (LANES - k * heads) % LANES, 1), heads)
                row = row + pltpu.roll(x, place * heads, 1)
            to[6:7, 0:LANES] = row[0:1]

    res = dot(normed[...], scr[...], 0, 0)
    keep[...] = res[:, :part]
    send[...] = res[:, part:].astype(bf16)
    dt = dot(draw[...], normed[...], 0, 0)
    cols = pl.ds(pl.multiple_of(i * GROUP, GROUP), GROUP)
    small_keep[8:16, cols] = dt[0:8]
    small_send[8:16, cols] = pltpu.roll(dt, LANES - heads, 0)[0:8]


def maps_grads_kernel(normed, dx, got, tail, ci, next_age, taps, gw, gb, keep, small, last, scr):
    @pl.when(pl.program_id(0) == 0)
    def _():
        fix = mend(got, tail, ci, next_age, taps, dx, scr, last, False)
        small[...] = jnp.zeros_like(small)
        sums = [jnp.sum(gw[8 * k : 8 * k + 8], axis=0, keepdims=True) for k in range(4)]
        small[0:4] = jnp.concatenate(sums, axis=0) + fix
        small[4:5] = jnp.sum(gb[...], axis=0, keepdims=True)

    keep[...] = dot(normed[...], scr[...], 0, 0)


def shards(
    hidden_in,
    output_cotangent,
    input_norm_scale_gain,
    z_proj,
    x_proj,
    bc_proj,
    dt_proj,
    conv_x_weight,
    conv_x_bias,
    conv_bc_weight,
    conv_bc_bias,
    dt_bias,
    a_log,
    d_skip,
    out_norm_gain,
    out_proj,
    doc_starts,
):
    batch, tokens, features = hidden_in.shape
    quarter = z_proj.shape[1]
    width = 2 * quarter
    inner = 4 * quarter
    heads = dt_proj.shape[1]
    seqs = lax.axis_size("seq")
    head_devices = lax.axis_size("head")
    parts = head_devices // batch
    chunk = tokens // parts
    count = chunk // GROUP
    si, hi_ = lax.axis_index("seq"), lax.axis_index("head")
    seq_of, half = hi_ // parts, hi_ % parts
    core = [(h, h ^ 1) for h in range(head_devices)]
    across = [(h, h ^ 2) for h in range(head_devices)]
    corner = [(h, h ^ 3) for h in range(head_devices)]
    meta = jnp.reshape(hi_, (1,)).astype(jnp.int32)

    def swap(x):
        return lax.ppermute(x, "head", core)

    def cross(x):
        return lax.ppermute(x, "head", across)

    def after(x, *others):
        return lax.optimization_barrier((x,) + others)[0]

    hid_map = lambda i, m: (m[0] // parts, lax.rem(m[0], parts) * count + i, 0)
    rev_hid = lambda i, m: (m[0] // parts, lax.rem(m[0], parts) * count + count - 1 - i, 0)
    here = lambda i, *_: (i, 0)
    here3 = lambda i, *_: (i, 0, 0)
    rev = lambda i, *_: (count - 1 - i, 0)
    rev3 = lambda i, *_: (count - 1 - i, 0, 0)
    gain_in = input_norm_scale_gain[None]
    taps_bc = conv_bc_weight.T
    lane_block = (GROUP, LANES)
    map_block = (GROUP, 2 * LANES)
    wide = (GROUP, inner)
    half_in = (GROUP, width)
    state_block = (1, LANES, width)
    keep_block = (1, 8, width)
    piece = features // head_devices

    x_far = cross(x_proj)
    small = jnp.concatenate(
        [
            jnp.pad(conv_x_weight.T, ((0, 0), (0, features - quarter))),
            jnp.pad(conv_x_bias, (0, features - quarter))[None],
            jnp.pad(out_norm_gain, (0, features - quarter))[None],
            jnp.pad(jnp.concatenate([dt_bias, a_log, d_skip]), (0, features - 3 * heads))[None],
            jnp.zeros((1, features), f32),
            jnp.pad(dt_proj.T.astype(f32), ((0, 8 - heads), (0, 0))),
        ],
        axis=0,
    )
    small_far = cross(small)
    z_far = cross(after(z_proj, x_far))
    o_far = cross(after(out_proj, z_far))
    xs = [x_proj, swap(x_proj), x_far, swap(x_far)]
    smalls = [small, swap(small), small_far, swap(small_far)]
    zs = [z_proj, swap(z_proj), z_far, swap(z_far)]
    os_ = [out_proj, swap(out_proj), o_far, swap(o_far)]
    edge_far = lax.ppermute(
        lax.dynamic_slice(hidden_in, (seq_of, tokens - 16, 0), (1, 16, features))[0],
        "seq",
        [(s, s + 1) for s in range(seqs - 1)],
    )
    cots = []
    for k in range(4):
        to = hi_ ^ k
        mine = lax.dynamic_slice(
            output_cotangent, (to // parts, (to % parts) * chunk, 0), (1, chunk, piece)
        )[0]
        if k == 1:
            mine = swap(mine)
        elif k:
            mine = lax.ppermute(after(mine, o_far), "head", across if k == 2 else corner)
        cots.append(mine)

    first_pos = si * tokens + half * chunk
    starts = lax.dynamic_slice(doc_starts, (seq_of, 0), (1, doc_starts.shape[1]))[0]

    def age_of(places):
        found = jnp.where(starts[None, :] <= places[:, None], starts[None, :], 0)
        return places - jnp.max(found, axis=1)

    age1 = age_of(first_pos + jnp.arange(chunk, dtype=jnp.int32))
    next_age = age_of(first_pos + chunk + jnp.arange(8, dtype=jnp.int32))
    next_age = jnp.broadcast_to(next_age[:, None], (8, LANES))
    age = jnp.broadcast_to(age1[:, None], (chunk, LANES))
    ager = jnp.broadcast_to(age1[None, :], (8, chunk))

    ex, red = expansion(width)
    tril = jnp.asarray(np.tril(np.ones((GROUP, GROUP), np.float32)))

    normed, ci_bc = run(
        norm_kernel,
        (count,),
        [
            (hidden_in, (1, GROUP, features), hid_map),
            (gain_in, None, None),
            (bc_proj, None, None),
        ],
        [
            ((chunk, features), bf16, (GROUP, features), here),
            ((chunk, 2 * LANES), bf16, map_block, here),
        ],
        flops=2 * chunk * features * 256,
        moved=6_000_000,
        prefetch=(meta,),
    )

    halves = []
    for n, k in enumerate((0, 2)):
        maps_in = [
            (ci_bc, map_block, here),
            (bc_proj, None, None),
            (taps_bc, None, None),
            (conv_bc_bias[None], None, None),
        ]
        maps_out = [
            ((chunk, 2 * LANES), f32, map_block, here),
            ((chunk, LANES), bf16, lane_block, here),
            ((chunk, LANES), bf16, lane_block, here),
        ]
        outs = run(
            functools.partial(front_kernel, n == 0, parts),
            (count,),
            [
                (normed, (GROUP, features), here),
                (edge_far, None, None),
                (hidden_in, (1, 16, features), lambda i, m: (m[0] // parts, chunk // 16 - 1, 0)),
                (gain_in, None, None),
                (xs[k], None, None),
                (xs[k + 1], None, None),
                (smalls[k], None, None),
                (smalls[k + 1], None, None),
                (age, lane_block, here),
                (tril, None, None),
                (ex, None, None),
            ]
            + (maps_in if n == 0 else [(bmat, lane_block, here)]),
            [
                ((chunk, width), bf16, half_in, here),
                ((chunk, width), f32, half_in, here),
                ((chunk, width), bf16, half_in, here),
                ((chunk, LANES), f32, lane_block, here),
                ((chunk, LANES), f32, lane_block, here),
                ((count, LANES, width), f32, state_block, here3),
                ((count, 8, width), f32, keep_block, here3),
                ((count, 8, width), f32, keep_block, here3),
                ((LANES, width), f32, None, None),
                ((8, LANES), f32, None, None),
                ((8, width), f32, None, None),
                ((LANES, features), bf16, None, None),
            ]
            + (maps_out if n == 0 else []),
            [
                pltpu.VMEM((GROUP + 8, width), f32),
                pltpu.VMEM((LANES, width), f32),
                pltpu.VMEM((8, LANES), f32),
                pltpu.VMEM(half_in, f32),
                pltpu.VMEM(half_in, bf16),
                pltpu.VMEM(half_in, bf16),
                pltpu.VMEM((LANES, features), f32),
            ]
            + ([pltpu.VMEM((GROUP + 8, 2 * LANES), f32)] if n == 0 else []),
            flops=2 * chunk * features * 1024 * 4,
            moved=16_000_000,
            prefetch=(meta,),
        )
        names = ("ci", "co", "val", "pre", "cum", "lin", "kb", "ck", "tot", "kout", "par", "dtp")
        d = dict(zip(names, outs))
        if n == 0:
            co_bc, bmat, cmat = outs[12:]
        halves.append(d)
    ha, hb = halves

    lo_block = lambda u: (jnp.minimum(u, count - 1), 0)
    hi_block = lambda u: (jnp.maximum(u - count, 0), 0)
    any_block = lambda u: (lax.rem(u, count), 0)

    def both(name, block):
        return [(ha[name], block, lo_block), (hb[name], block, hi_block)]

    def whole(*arrays):
        return [(a, None, None) for a in arrays]

    ha["part"], hb["part"], *arr = run(
        functools.partial(intra_kernel, seqs, parts, count),
        (2 * count,),
        both("val", half_in)
        + [(bmat, lane_block, any_block), (cmat, lane_block, any_block), (age, lane_block, any_block)]
        + both("pre", lane_block)
        + both("cum", lane_block)
        + whole(ha["par"], hb["par"], ha["tot"], hb["tot"], ha["kout"], hb["kout"], ex),
        [
            ((chunk, width), f32, half_in, lo_block),
            ((chunk, width), f32, half_in, hi_block),
            ((LANES, width), f32, None, None),
            ((LANES, width), f32, None, None),
        ],
        Exchange.scratch(seqs, width),
        flops=25_000_000_000,
        moved=16_000_000,
        collective=1,
    )

    outs = run(
        mid_kernel,
        (count,),
        [
            (hidden_in, (1, GROUP, features), rev_hid),
            (normed, (GROUP, features), rev),
            *whole(*zs, *os_),
            *[(c, (GROUP, piece), rev) for c in cots],
            (cmat, lane_block, rev),
            (age, lane_block, rev),
            *whole(ex, red, ha["par"], hb["par"]),
            *[(d["part"], half_in, rev) for d in halves],
            *[(d["val"], half_in, rev) for d in halves],
            *[(d["cum"], lane_block, rev) for d in halves],
            *[(d["lin"], state_block, rev3) for d in halves],
            *[(d["kb"], keep_block, rev3) for d in halves],
            *[(d["ck"], keep_block, rev3) for d in halves],
            *whole(*arr),
        ],
        [((chunk, piece), bf16, (GROUP, piece), rev)] * 4
        + [
            ((chunk, inner), bf16, wide, rev),
            ((chunk, features), bf16, (GROUP, features), rev),
            ((chunk, inner), bf16, wide, rev),
            ((chunk, inner), bf16, wide, rev),
            ((chunk, LANES), f32, lane_block, rev),
            ((chunk, LANES), f32, lane_block, rev),
            ((chunk, LANES), f32, lane_block, rev),
            ((count, LANES, width), f32, state_block, rev3),
            ((count, LANES, width), f32, state_block, rev3),
            ((count, 8, width), f32, keep_block, rev3),
            ((count, 8, width), f32, keep_block, rev3),
            ((LANES, width), f32, None, None),
            ((LANES, width), f32, None, None),
            ((8, LANES), f32, None, None),
            ((8, LANES), f32, None, None),
            ((8, inner), f32, None, None),
            ((8, inner), f32, None, None),
        ],
        [pltpu.VMEM(wide, f32)] * 6
        + [pltpu.VMEM(wide, bf16)] * 4
        + [pltpu.VMEM((LANES, width), f32)] * 2
        + [pltpu.VMEM((8, LANES), f32)] * 2
        + [pltpu.VMEM((4, GROUP, piece), bf16)],
        flops=30_000_000_000,
        moved=50_000_000,
        prefetch=(meta,),
    )
    out_pieces, outs = outs[:4], outs[4:]
    nout, cotx, dssd, dgate, dcin, ha["dkk"], hb["dkk"], ha["lout"], hb["lout"], ha["ka"], hb["ka"] = outs[:11]
    dtot_a, dtot_b, dk_a, dk_b, ggain_out, gskip = outs[11:]

    def trade_pieces(pieces):
        return [pieces[0], swap(pieces[1]), cross(pieces[2]), lax.ppermute(pieces[3], "head", corner)]

    def place_pieces(got):
        odd, far = hi_ % 2 == 1, hi_ // 2 == 1
        a = [jnp.where(odd, got[k ^ 1], got[k]) for k in range(4)]
        a = [jnp.where(far, a[k ^ 2], a[k]) for k in range(4)]
        return jnp.stack(a).reshape(batch, tokens, piece)

    pairs = ((0, 0, 0), (1, 1, 0), (0, 0, width), (1, 1, width))
    shape = (4, features, quarter)
    block = (4, GROUP, quarter)
    keep1, send1 = run(
        functools.partial(grads_kernel, (2, pairs)),
        (features // GROUP,),
        [(a, (chunk, GROUP), lambda i: (0, i)) for a in (normed, cotx)] + whole(dgate, nout),
        [(shape, f32, block, lambda i: (0, i, 0)), (shape, bf16, block, lambda i: (0, i, 0))],
        flops=8 * features * width * chunk,
        moved=20_000_000,
    )
    got1 = swap(send1).astype(f32)
    far1 = cross((keep1[2:] + got1[2:]).astype(bf16)).astype(f32)

    outs = run(
        functools.partial(pairs_kernel, seqs, parts, count),
        (2 * count,),
        both("val", half_in)
        + [
            (dssd, half_in, lambda u: (lax.rem(u, count), u // count)),
            (bmat, lane_block, any_block),
            (cmat, lane_block, any_block),
            (ager, (8, GROUP), lambda u: (0, lax.rem(u, count))),
        ]
        + both("pre", lane_block)
        + both("cum", lane_block)
        + whole(dtot_a, dtot_b, dk_a, dk_b, after(ex, send1)),
        [
            (shape, f32, (GROUP, shape[1]), imap)
            for imap in (lo_block, hi_block)
            for shape in [(chunk, width)] + [(chunk, LANES)] * 4
        ]
        + [((LANES, width), f32, None, None)] * 2,
        [pltpu.VMEM((LANES, GROUP), f32)] + Exchange.scratch(seqs, width),
        flops=25_000_000_000,
        moved=20_000_000,
        collective=2,
    )
    names = ("dvi", "dbi", "dci_c", "rflow", "cflow")
    ha.update(zip(names, outs[:5]))
    hb.update(zip(names, outs[5:10]))
    leav = outs[10:]

    sum1 = (keep1[:2] + got1[:2] + far1).astype(bf16)
    out_pieces = after(tuple(out_pieces), leav[0])

    def seq_sum(x):
        rows, cols = x.shape
        x = lax.all_to_all(x.reshape(seqs, rows // seqs, cols), "seq", 0, 0)
        x = jnp.sum(x.astype(f32), axis=0).astype(bf16)
        x = lax.all_to_all(jnp.broadcast_to(x[None], (seqs,) + x.shape), "seq", 0, 0)
        return x.reshape(rows, cols).astype(f32)

    def share_sum(x):
        return jnp.sum(lax.all_to_all(jnp.broadcast_to(x[None], (seqs,) + x.shape), "seq", 0, 0), axis=0)

    chain = []
    for s in range(seqs):
        for b in range(batch):
            at = s * head_devices + b * parts
            chain += [(at + p, at + p - 1) for p in range(1, parts)]
            if s > 0:
                chain.append((at, at - head_devices + parts - 1))

    def from_next(head):
        return lax.ppermute(head, ("seq", "head"), chain)

    dbc, tail_bc, head_bc, gw_bc, gb_bc = run(
        maps_kernel,
        (count,),
        [
            *[(d["dbi"], lane_block, rev) for d in halves],
            *[(d["dci_c"], lane_block, rev) for d in halves],
            (after(dcin, sum1), lane_block, rev),
            (co_bc, map_block, rev),
            (ci_bc, map_block, rev),
            (age, lane_block, rev),
            (taps_bc, None, None),
            *[(d["val"], half_in, rev) for d in halves],
            *[(d["pre"], lane_block, rev) for d in halves],
            *[(d["cum"], lane_block, rev) for d in halves],
            *[(d["lout"], state_block, rev3) for d in halves],
            *[(d["ka"], keep_block, rev3) for d in halves],
            *whole(*leav, ex),
        ],
        [
            ((chunk, 2 * LANES), bf16, map_block, rev),
            ((8, 2 * LANES), f32, None, None),
            ((8, 2 * LANES), f32, None, None),
            ((32, 2 * LANES), f32, None, None),
            ((8, 2 * LANES), f32, None, None),
        ],
        [
            pltpu.VMEM((GROUP + 8, 2 * LANES), f32),
            pltpu.VMEM((GROUP + 8, LANES), jnp.int32),
            pltpu.VMEM(lane_block, f32),
        ],
        flops=5_000_000_000,
        moved=8_000_000,
    )
    share1 = lax.all_to_all(
        sum1.reshape(2, seqs, features // seqs, quarter).transpose(1, 0, 2, 3), "seq", 0, 0
    )
    got_bc = from_next(head_bc)
    traded = trade_pieces(out_pieces)
    order = (dbc,)

    for n in (1, 0):
        d = halves[n]
        outs = run(
            functools.partial(back_kernel, n),
            (count,),
            [
                (d["val"], half_in, rev),
                (dssd, half_in, lambda i, n=n: (count - 1 - i, n)),
                (d["dvi"], half_in, rev),
                (bmat, lane_block, rev),
                (d["co"], half_in, rev),
                (d["ci"], half_in, rev),
                (age, lane_block, rev),
                (d["pre"], lane_block, rev),
                (d["cum"], lane_block, rev),
                (d["lout"], state_block, rev3),
                (d["ka"], keep_block, rev3),
                *whole(*leav),
                (d["lin"], state_block, rev3),
                (d["kb"], keep_block, rev3),
                *whole(*arr),
                (d["rflow"], lane_block, rev),
                (d["cflow"], lane_block, rev),
                (d["dkk"], lane_block, rev),
                *whole(after(d["par"], *order), tril, ex, red),
            ],
            [
                ((chunk, width), bf16, half_in, rev),
                ((8, width), f32, None, None),
                ((8, width), f32, None, None),
                ((chunk, LANES), bf16, lane_block, rev),
                ((32, width), f32, None, None),
                ((8, width), f32, None, None),
                ((8, LANES), f32, None, None),
                ((8, LANES), f32, None, None),
            ],
            [
                pltpu.VMEM((GROUP + 8, width), f32),
                pltpu.VMEM((GROUP + 8, LANES), jnp.int32),
                pltpu.VMEM(half_in, f32),
                pltpu.VMEM(half_in, f32),
            ]
            + [pltpu.VMEM(half_in, bf16)] * 2,
            flops=10_000_000_000,
            moved=20_000_000,
        )
        d.update(zip(("dx", "tail", "head", "draw", "gw", "gb", "galog", "gdtb"), outs))
        got = from_next(d["head"])
        if n == 1:
            g_bc, small_bc, last_bc = run(
                maps_grads_kernel,
                (features // GROUP,),
                [(normed, (chunk, GROUP), lambda i: (0, i))]
                + whole(dbc, got_bc, tail_bc, ci_bc, next_age, taps_bc, gw_bc, gb_bc),
                [
                    ((features, 2 * LANES), f32, map_block, here),
                    ((8, 2 * LANES), f32, None, None),
                    ((16, 2 * LANES), bf16, None, None),
                ],
                [pltpu.VMEM((chunk, 2 * LANES), bf16)],
                flops=1_000_000_000,
                moved=4_000_000,
            )
            g_bc = g_bc + swap(g_bc.astype(bf16)).astype(f32)
        d["keep"], send, d["small"], small_send, d["last"] = run(
            functools.partial(half_grads_kernel, n),
            (features // GROUP,),
            [(normed, (chunk, GROUP), lambda i: (0, i))]
            + whole(
                d["dx"], got, d["tail"], d["ci"], next_age, d["par"], d["draw"],
                d["gw"], d["gb"], d["galog"], d["gdtb"], gskip, ggain_out, red,
            ),
            [
                ((features, quarter), f32, (GROUP, quarter), here),
                ((features, quarter), bf16, (GROUP, quarter), here),
                ((16, features), f32, None, None),
                ((16, features), f32, None, None),
                ((16, width), bf16, None, None),
            ],
            [pltpu.VMEM((chunk, width), bf16)],
            flops=2_500_000_000,
            moved=5_000_000,
        )
        d["sum"] = d["keep"] + swap(send).astype(f32)
        d["small"] = d["small"] + swap(small_send)
        if n == 1:
            far2 = cross(d["sum"].astype(bf16))
            small_far2 = cross(d["small"])
            far_bc = cross(g_bc.astype(bf16))
            early = run(
                early_kernel,
                (count,),
                [
                    (dgate, wide, here),
                    *whole(*zs),
                    (dbc, map_block, here),
                    *whole(last_bc, bc_proj),
                    (d["dx"], half_in, here),
                    *whole(d["last"], xs[2], xs[3]),
                    (d["draw"], lane_block, here),
                    (d["dtp"], None, None),
                ],
                [((chunk, features), f32, (GROUP, features), here)],
                [pltpu.VMEM(map_block, bf16), pltpu.VMEM(half_in, bf16)],
                flops=6_000_000_000,
                moved=12_000_000,
            )[0]
            share1 = jnp.sum(after(share1, d["draw"]).astype(f32), axis=0).astype(bf16)
            sum1 = lax.all_to_all(jnp.broadcast_to(share1[None], (seqs,) + share1.shape), "seq", 0, 0)
            order = (early, share1, *traded)

    sum1 = after(sum1, ha["keep"]).transpose(1, 0, 2, 3).reshape(2, features, quarter).astype(f32)
    grad_out = sum1[1].T
    final = run(
        final_kernel,
        (count,),
        [
            (hidden_in, (1, GROUP, features), hid_map),
            (cotx, (GROUP, features), here),
            (gain_in, None, None),
            (early, (GROUP, features), here),
            (ha["dx"], half_in, here),
            *whole(ha["last"], xs[0], xs[1]),
            (ha["draw"], lane_block, here),
            (after(ha["dtp"], sum1), None, None),
        ],
        [((chunk, piece), bf16, (GROUP, piece), here)] * 4 + [((8, features), f32, None, None)],
        [pltpu.VMEM((GROUP, features), f32), pltpu.VMEM((4, GROUP, piece), bf16), pltpu.VMEM(half_in, bf16)],
        flops=5_000_000_000,
        moved=10_000_000,
        prefetch=(meta,),
    )
    sum2 = seq_sum((ha["sum"] + far2.astype(f32)).astype(bf16))
    g_bc = seq_sum((g_bc + far_bc.astype(f32)).astype(bf16))
    layer_out = place_pieces(traded)
    input_grad = place_pieces(trade_pieces(final[:4]))
    gi = jnp.sum(final[4], axis=0).reshape(features // LANES, LANES)
    gi = gi + swap(gi)
    gi = gi + cross(gi)
    gi = share_sum(gi).reshape(features)
    gi = lax.dynamic_slice(gi, (hi_ * piece,), (piece,))
    small_bc = small_bc + swap(small_bc)
    small_bc = small_bc + cross(small_bc)
    small_sum = ha["small"] + small_far2
    small_sum = share_sum(
        jnp.concatenate([small_sum, jnp.pad(small_bc, ((0, 0), (0, features - 2 * LANES)))], axis=0)
    )
    row = small_sum[6]
    return (
        layer_out,
        input_grad,
        gi,
        sum1[0],
        sum2,
        g_bc,
        small_sum[8 : 8 + heads].T,
        small_sum[0:4, :quarter].T,
        small_sum[4, :quarter],
        small_sum[16:20, : 2 * LANES].T,
        small_sum[20, : 2 * LANES],
        row[:heads],
        row[heads : 2 * heads],
        row[2 * heads : 3 * heads],
        small_sum[5, :quarter],
        grad_out,
    )


def solution(mesh):
    return jax.shard_map(
        shards,
        mesh=mesh,
        in_specs=(
            P(None, "seq", None),
            P(None, "seq", "head"),
            P(),
            P(None, "head"),
            P(None, "head"),
            P(),
            P(None, "head"),
            P("head", None),
            P("head"),
            P(),
            P(),
            P("head"),
            P("head"),
            P("head"),
            P("head"),
            P("head", None),
            P(),
        ),
        out_specs=(
            P(None, "seq", "head"),
            P(None, "seq", "head"),
            P("head"),
            P(None, "head"),
            P(None, "head"),
            P(),
            P(None, "head"),
            P("head", None),
            P("head"),
            P(),
            P(),
            P("head"),
            P("head"),
            P("head"),
            P("head"),
            P("head", None),
        ),
        check_vma=False,
    )
```

```python
import functools

import jax
import jax.numpy as jnp
import numpy as np
from jax import lax
from jax.experimental import pallas as pl
from jax.experimental.pallas import tpu as pltpu
from jax.sharding import PartitionSpec as P

GROUP = 256
HALF = 128
LANES = 128
HEAD_DIM = 64
EPS = 1e-05
LOG2E = 1.4426950408889634
f32 = jnp.float32
bf16 = jnp.bfloat16
HIGHEST = lax.Precision.HIGHEST
ROWS = 32
MESH = pl.DeviceIdType.MESH


def dot(a, b, ca=1, cb=0, precision=None):
    return lax.dot_general(
        a, b, (((ca,), (cb,)), ((), ())), precision=precision, preferred_element_type=f32
    )


def split2(x):
    hi = x.astype(bf16)
    return hi, (x - hi.astype(f32)).astype(bf16)


def pack(x):
    hi = x.astype(bf16).astype(f32)
    rest = x - hi
    mid = rest.astype(bf16).astype(f32)
    return (hi + pltpu.roll(mid, 32, 1) + pltpu.roll(rest - mid, 64, 1)).astype(bf16)


def unpack(x):
    x = x.astype(f32)
    return lanes_below(x + pltpu.roll(x, LANES - 32, 1) + pltpu.roll(x, LANES - 64, 1), 12)


def expand(x, ex):
    return dot(pack(x), ex)


def lanes_below(x, count):
    return jnp.where(lax.broadcasted_iota(jnp.int32, x.shape, 1) < count, x, 0.0)


def sigmoid(x):
    return 1.0 / (1.0 + jnp.exp(-x))


def softplus(x):
    return jnp.maximum(x, 0.0) + jnp.log1p(jnp.exp(-jnp.abs(x)))


def fold8(x):
    total = x[0:8]
    for r in range(8, x.shape[0], 8):
        total = total + x[r : r + 8]
    return total


def expansion(width):
    heads = width // HEAD_DIM
    ex = np.zeros((LANES, width), np.float32)
    for part in range(3):
        for h in range(heads):
            ex[32 * part + h, h * HEAD_DIM : (h + 1) * HEAD_DIM] = 1.0
    red = np.zeros((width, LANES), np.float32)
    for h in range(heads):
        red[h * HEAD_DIM : (h + 1) * HEAD_DIM, h] = 1.0
    return jnp.asarray(ex, bf16), jnp.asarray(red, bf16)


def run(kernel, grid, ins, outs, scratch=(), flops=0, moved=0, prefetch=(), collective=None):
    def spec(shape, block, imap):
        if block is pl.ANY:
            return pl.BlockSpec(memory_space=pl.ANY)
        if block is None:
            rank = len(shape)
            return pl.BlockSpec(shape, lambda *_: (0,) * rank)
        return pl.BlockSpec(block, imap)

    extra = {} if collective is None else {"collective_id": collective, "has_side_effects": True}
    return pl.pallas_call(
        kernel,
        grid_spec=pltpu.PrefetchScalarGridSpec(
            num_scalar_prefetch=len(prefetch),
            grid=grid,
            in_specs=[spec(a.shape, b, m) for a, b, m in ins],
            out_specs=[spec(s, b, m) for s, _, b, m in outs],
            scratch_shapes=list(scratch),
        ),
        out_shape=[jax.ShapeDtypeStruct(s, d) for s, d, _, _ in outs],
        compiler_params=pltpu.CompilerParams(vmem_limit_bytes=56 << 20, **extra),
        cost_estimate=pl.CostEstimate(flops=flops, bytes_accessed=moved, transcendentals=0),
    )(*prefetch, *[a for a, _, _ in ins])


def conv_rows(ext, age, taps, bias, r, cols):
    acc = jnp.broadcast_to(bias[:, cols], (ROWS, LANES))
    for k in range(4):
        back = 3 - k
        term = ext[8 + r - back : 8 + r - back + ROWS, cols] * taps[k : k + 1, cols]
        if back:
            term = jnp.where(age >= back, term, 0.0)
        acc = acc + term
    return acc


def rms(x, gain):
    x = x.astype(f32)
    r = lax.rsqrt(jnp.sum(x * x, axis=1, keepdims=True) / x.shape[1] + EPS)
    return (x * r * gain).astype(bf16)


def norm_kernel(me, hid, gain, bc, normed, ci):
    for r in range(0, GROUP, ROWS):
        normed[r : r + ROWS] = rms(hid[0, r : r + ROWS], gain[...])
    ci[...] = dot(normed[...], bc[...]).astype(bf16)


def front_kernel(with_maps, parts, me, *refs):
    ins, refs = refs[:11], refs[11:]
    normed, edge_far, edge_near, gain, wa, wb, sa, sb, age, tril, ex = ins
    if with_maps:
        (ci_bc, bc, taps_bc, bias_bc), refs = refs[:4], refs[4:]
    else:
        (bmat,), refs = refs[:1], refs[1:]
    (ci, co, val, pre, cum, lin, kb, ck, tot, kout, par, dtp), refs = refs[:12], refs[12:]
    if with_maps:
        (co_bc, bmat, cmat), refs = refs[:3], refs[3:]
    (ext, running, kept, omx, ohi, olo, dts), refs = refs[:7], refs[7:]
    if with_maps:
        (ext_bc,) = refs
    i = pl.program_id(0)
    width = val.shape[1]
    part = width // 2
    heads = part // HEAD_DIM

    @pl.when(i == 0)
    def _():
        running[...] = jnp.zeros_like(running)
        kept[...] = jnp.ones_like(kept)
        near = lax.rem(me[0], parts).astype(f32)
        edge = near * edge_near[0].astype(f32) + (1.0 - near) * edge_far[...].astype(f32)
        before = rms(edge, gain[...])
        for w, at in ((wa, 0), (wb, part)):
            ext[0:8, at : at + part] = dot(before, w[...]).astype(bf16).astype(f32)[8:16]
        if with_maps:
            ext_bc[0:8] = dot(before, bc[...]).astype(bf16).astype(f32)[8:16]
        par[...] = jnp.zeros_like(par)
        for s, at in ((sa, 0), (sb, part)):
            par[0:6, at : at + part] = s[0:6, :part]
        rows_a, rows_b = (jnp.broadcast_to(s[6:7, 0:LANES], (8, LANES)) for s in (sa, sb))

        def lanes(k):
            a = lanes_below(pltpu.roll(rows_a, (LANES - k * heads) % LANES, 1), heads)
            b = lanes_below(pltpu.roll(rows_b, (LANES - k * heads) % LANES, 1), heads)
            return a + pltpu.roll(b, heads, 1)

        par[7:8, LANES : 2 * LANES] = lanes(0)[0:1]
        par[7:8, 0:LANES] = -jnp.exp(lanes(1)[0:1])
        par[6:7] = expand(lanes(2), ex[...])[0:1]
        dts[...] = jnp.zeros_like(dts)
        dts[0:heads] = sa[8 : 8 + heads]
        dts[heads : 2 * heads] = sb[8 : 8 + heads]
        dtp[...] = dts[...].astype(bf16)

    @pl.when(i > 0)
    def _():
        ext[0:8] = ext[GROUP : GROUP + 8]
        if with_maps:
            ext_bc[0:8] = ext_bc[GROUP : GROUP + 8]

    taps, bias = par, par[4:5]
    rate, dtb = par[7:8, 0:LANES], par[7:8, LANES : 2 * LANES]
    for w, at in ((wa, 0), (wb, part)):
        low = dot(normed[...], w[...]).astype(bf16)
        ci[:, at : at + part] = low
        ext[8 : 8 + GROUP, at : at + part] = low.astype(f32)
    raw = dot(normed[...], dtp[...], 1, 1) + dtb
    pre[...] = raw
    delta = softplus(raw)
    c = dot(tril[...], delta * rate, precision=HIGHEST)
    cum[...] = c
    end = c[GROUP - 1 : GROUP]
    age_end = age[GROUP - 1 : GROUP]
    left = GROUP - 1 - lax.broadcasted_iota(jnp.int32, c.shape, 0)
    omega = jnp.where(left <= age_end, jnp.exp(end - c), 0.0) * delta
    omx[...] = expand(lanes_below(omega, 2 * heads), ex[...])
    keep = jnp.where(age_end >= GROUP, jnp.exp(end), 0.0)
    keep = lanes_below(jnp.broadcast_to(keep, (8, LANES)), 2 * heads)
    keepx = expand(keep, ex[...])
    if with_maps:
        ext_bc[8 : 8 + GROUP] = ci_bc[...].astype(f32)
        for r in range(0, GROUP, ROWS):
            a = age[r : r + ROWS]
            for j, out in enumerate((bmat, cmat)):
                cols = slice(j * LANES, (j + 1) * LANES)
                v = conv_rows(ext_bc, a, taps_bc, bias_bc, r, cols)
                co_bc[r : r + ROWS, cols] = v
                out[r : r + ROWS] = (v * sigmoid(v)).astype(bf16)
    for r in range(0, GROUP, ROWS):
        a = age[r : r + ROWS]
        rows = slice(r, r + ROWS)
        for j in range(width // LANES):
            cols = slice(j * LANES, (j + 1) * LANES)
            v = conv_rows(ext, a, taps, bias, r, cols)
            co[rows, cols] = v
            act = (v * sigmoid(v)).astype(bf16)
            val[rows, cols] = act
            ohi[rows, cols], olo[rows, cols] = split2(omx[rows, cols] * act.astype(f32))
    own = dot(bmat[...], ohi[...], 0, 0) + dot(bmat[...], olo[...], 0, 0)
    lin[0] = running[...]
    kb[0] = expand(lanes_below(kept[...], 2 * heads), ex[...])
    ck[0] = keepx
    running[...] = keepx[0:1] * running[...] + own
    kept[...] = keep * kept[...]
    tot[...] = running[...]
    kout[...] = kept[...]


class Exchange:
    def __init__(self, reverse, n, parts, tots, kouts, ex, own, other, scratch):
        self.reverse, self.n, self.tots, self.kouts, self.ex = reverse, n, tots, kouts, ex
        self.own, self.other = own, other
        (
            self.out, self.got, self.payload, self.spread, self.scanned, self.home, self.lead, self.lead_k, self.arr,
            self.theirs, self.last, self.swap_sems, self.to_sems, self.from_sems, self.back_to, self.back_from,
        ) = scratch
        self.me = lax.axis_index("seq")
        head = lax.axis_index("head")
        self.partner = head + 1 - 2 * lax.rem(head, 2)
        half = lax.rem(head, parts)
        self.leads = (half if reverse else 1 - half).astype(f32)
        self.per = LANES // n

    @staticmethod
    def scratch(n, width):
        rows = max(LANES // n, 8)
        return [
            pltpu.VMEM((LANES + 8, width), f32),
            pltpu.VMEM((LANES + 8, width), f32),
            pltpu.VMEM((n, rows, width + LANES), f32),
            pltpu.VMEM((n, rows, width + LANES), f32),
            pltpu.VMEM((n, rows, width), f32),
            pltpu.VMEM((n, rows, width), f32),
            pltpu.VMEM((LANES, width), f32),
            pltpu.VMEM((8, LANES), f32),
            pltpu.VMEM((LANES, width), f32),
            pltpu.VMEM((LANES, width), f32),
            pltpu.VMEM((LANES, width), f32),
            pltpu.SemaphoreType.DMA((4,)),
            pltpu.SemaphoreType.DMA((n,)),
            pltpu.SemaphoreType.DMA((n,)),
            pltpu.SemaphoreType.DMA((n,)),
            pltpu.SemaphoreType.DMA((n,)),
        ]

    def peers(self):
        for d in range(1, self.n):
            yield d, lax.rem(self.me + d, self.n), lax.rem(self.me + self.n - d, self.n)

    def swap(self, src, dst, sem):
        return pltpu.make_async_remote_copy(
            src_ref=src,
            dst_ref=dst,
            send_sem=self.swap_sems.at[sem],
            recv_sem=self.swap_sems.at[sem + 1],
            device_id={"head": self.partner},
            device_id_type=MESH,
        )

    def move(self, src, dst, d, to, send_sems, recv_sems):
        return pltpu.make_async_remote_copy(
            src_ref=src.at[to],
            dst_ref=dst.at[self.me],
            send_sem=send_sems.at[d],
            recv_sem=recv_sems.at[d],
            device_id={"seq": to},
            device_id_type=MESH,
        )

    def begin(self, others=()):
        barrier = pltpu.get_barrier_semaphore()
        for head in others:
            pl.semaphore_signal(barrier, inc=1, device_id={"head": head}, device_id_type=MESH)
        pl.semaphore_signal(barrier, inc=1, device_id={"head": self.partner}, device_id_type=MESH)
        for _, to, _ in self.peers():
            pl.semaphore_signal(barrier, inc=1, device_id={"seq": to}, device_id_type=MESH)
        pl.semaphore_wait(barrier, self.n + len(others))
        part = self.out.shape[1] // 2
        heads = part // HEAD_DIM
        for k in range(2):
            self.out[0:LANES, k * part : (k + 1) * part] = self.tots[k][:, part:]
            rolled = pltpu.roll(self.kouts[k][...], LANES - heads, 1)
            self.out[LANES : LANES + 8, k * LANES : (k + 1) * LANES] = lanes_below(rolled, heads)
        self.out[LANES : LANES + 8, 2 * LANES :] = jnp.zeros((8, 2 * part - 2 * LANES), f32)
        self.swap(self.out, self.got, 0).start()

    def combine(self):
        self.swap(self.out, self.got, 0).wait()
        part = self.out.shape[1] // 2
        heads = part // HEAD_DIM
        leads, follows = self.leads, 1.0 - self.leads
        k_a, k_b = (lanes_below(k[...], heads) for k in self.kouts)
        mine_k = k_a + pltpu.roll(k_b, heads, 1)
        got_k = self.got[LANES : LANES + 8, 0:LANES] + pltpu.roll(
            self.got[LANES : LANES + 8, LANES : 2 * LANES], heads, 1
        )
        lk = leads * mine_k + follows * got_k
        fk = leads * got_k + follows * mine_k
        fkx = expand(fk, self.ex[...])[0:1]
        self.lead_k[...] = lk
        for k in range(2):
            cols = slice(k * part, (k + 1) * part)
            mine, got = self.tots[k][:, :part], self.got[0:LANES, cols]
            ls = leads * mine + follows * got
            self.lead[:, cols] = ls
            self.arr[:, cols] = fkx[:, cols] * ls + (leads * got + follows * mine)
        keep = (lk * fk)[0:1]
        rows = self.payload.shape[1]
        for s in range(self.n):
            self.payload[s, 0 : self.per, 0 : 2 * part] = self.arr[s * self.per : (s + 1) * self.per]
            self.payload[s, :, 2 * part :] = jnp.broadcast_to(keep, (rows, LANES))
        for d, to, _ in self.peers():
            self.move(self.payload, self.spread, d, to, self.to_sems, self.from_sems).start()
        self.spread[self.me] = self.payload[self.me]

    def scan(self):
        for d, to, _ in self.peers():
            self.move(self.payload, self.spread, d, to, self.to_sems, self.from_sems).wait()
        width = self.scanned.shape[2]
        rows = self.scanned.shape[1]
        state = jnp.zeros((rows, width), f32)
        for step in range(self.n):
            at = self.n - 1 - step if self.reverse else step
            self.scanned[at] = state
            if step < self.n - 1:
                keep = expand(self.spread[at, :, width:], self.ex[...])
                state = keep * state + self.spread[at, :, 0:width]
        for d, to, _ in self.peers():
            self.move(self.scanned, self.home, d, to, self.back_to, self.back_from).start()
        self.home[self.me] = self.scanned[self.me]

    def finish(self):
        for d, to, _ in self.peers():
            self.move(self.scanned, self.home, d, to, self.back_to, self.back_from).wait()
        for s in range(self.n):
            self.arr[s * self.per : (s + 1) * self.per] = self.home[s, 0 : self.per]
        leads, follows = self.leads, 1.0 - self.leads
        first = self.arr[...]
        second = expand(self.lead_k[...], self.ex[...])[0:1] * first + self.lead[...]
        self.theirs[...] = leads * second + follows * first
        copy = self.swap(self.theirs, self.last, 2)
        copy.start()
        self.own[...] = leads * first + follows * second
        copy.wait()
        self.other[...] = self.last[...]


def pair_masks(x, lane_axis_shape):
    lane = lax.broadcasted_iota(jnp.int32, lane_axis_shape, 1)
    zero = jnp.zeros_like(x)
    return jnp.where(lane < HEAD_DIM, x, zero), jnp.where(lane >= HEAD_DIM, x, zero)


def intra_unit(val, bmat, cmat, age, pre, cum, dskip, part):
    t = lax.broadcasted_iota(jnp.int32, (HALF, HALF), 0)
    s = lax.broadcasted_iota(jnp.int32, (HALF, HALF), 1)
    scores = dot(cmat[...], bmat[...], 1, 1)
    a0, a1 = age[0:HALF], age[HALF:]
    gap = t - s
    s00 = jnp.where((gap >= 0) & (gap <= a0), scores[:HALF, :HALF], 0.0)
    s11 = jnp.where((gap >= 0) & (gap <= a1), scores[HALF:, HALF:], 0.0)
    s10 = jnp.where(gap + HALF <= a1, scores[HALF:, :HALF], 0.0)
    c2 = cum[...] * LOG2E
    rows = (c2 - jnp.log2(softplus(pre[...]))).T
    for j in range(val.shape[1] // LANES):
        cols = slice(j * LANES, (j + 1) * LANES)
        v = val[:, cols]
        vm = pair_masks(v, v.shape)
        tops, bottoms = [], []
        for which in range(2):
            h = 2 * j + which
            col0 = jnp.broadcast_to(c2[:HALF, h : h + 1], (HALF, HALF))
            col1 = jnp.broadcast_to(c2[HALF:, h : h + 1], (HALF, HALF))
            r0 = rows[h : h + 1, :HALF]
            r1 = rows[h : h + 1, HALF:]
            tops.append((s00 * jnp.exp2(jnp.minimum(col0 - r0, 60.0))).astype(bf16))
            bottoms.append((s10 * jnp.exp2(col1 - r0)).astype(bf16))
            bottoms.append((s11 * jnp.exp2(jnp.minimum(col1 - r1, 60.0))).astype(bf16))
        top = dot(jnp.concatenate(tops, axis=1), jnp.concatenate([vm[0][:HALF], vm[1][:HALF]], axis=0))
        bottom = dot(jnp.concatenate(bottoms, axis=1), jnp.concatenate([vm[0], vm[1]], axis=0))
        skip = dskip[6:7, cols]
        part[:HALF, cols] = top + skip * v[:HALF].astype(f32)
        part[HALF:, cols] = bottom + skip * v[HALF:].astype(f32)


def intra_kernel(
    n, parts, count, val_a, val_b, bmat, cmat, age, pre_a, pre_b, cum_a, cum_b, par_a, par_b,
    tot_a, tot_b, k_a, k_b, ex, part_a, part_b, own, other, *scratch
):
    u = pl.program_id(0)
    states = Exchange(False, n, parts, (tot_a, tot_b), (k_a, k_b), ex, own, other, scratch)
    pl.when(u == 0)(states.begin)

    @pl.when(u < count)
    def _():
        intra_unit(val_a, bmat, cmat, age, pre_a, cum_a, par_a, part_a)

    @pl.when(u >= count)
    def _():
        intra_unit(val_b, bmat, cmat, age, pre_b, cum_b, par_b, part_b)

    pl.when(u == 0)(states.combine)
    pl.when(u == 2 * count - 3)(states.scan)
    pl.when(u == 2 * count - 1)(states.finish)


def arriving_half(own, other, half):
    part = own.shape[1] // 2
    cols = slice(half * part, (half + 1) * part)
    return jnp.concatenate([own[:, cols].astype(f32), other[:, cols].astype(f32)], axis=1)


def mid_kernel(
    meta, hid, normed, z0, z1, z2, z3, o0, o1, o2, o3, cot0, cot1, cot2, cot3, cmat, age, ex, red, par_a, par_b,
    part_a, part_b, val_a, val_b, cum_a, cum_b, lin_a, lin_b, kb_a, kb_b, ck_a, ck_b, arr, arr_other,
    pieces, hidc, nout, cotx, dssd, dgate, dcin, dkk_a, dkk_b,
    lout_a, lout_b, ka_a, ka_b, tot_a, tot_b, kout_a, kout_b, ggain, gskip,
    gate, dno, read, kx, ssd_s, sig_s, khi, klo, rhi, rlo, run_a, run_b, kept_a, kept_b, shuffle,
):
    i = pl.program_id(0)
    inner = nout.shape[1]
    width = inner // 2
    tiles = inner // LANES
    heads = width // HEAD_DIM
    quarter = inner // 4

    @pl.when(i == 0)
    def _():
        for ref in (run_a, run_b, ggain, gskip):
            ref[...] = jnp.zeros_like(ref)
        for ref in (kept_a, kept_b):
            ref[...] = jnp.ones_like(ref)

    me = meta[0]
    hidc[...] = hid[0]
    for k, cot in enumerate((cot0, cot1, cot2, cot3)):
        shuffle[me ^ k] = cot[...]
    cotan = jnp.concatenate([shuffle[0], shuffle[1], shuffle[2], shuffle[3]], axis=0).T
    cotx[...] = cotan
    states = []
    for half, (lin, kb, cum) in enumerate(((lin_a, kb_a, cum_a), (lin_b, kb_b, cum_b))):
        cols = slice(half * width, (half + 1) * width)
        hi, lo = split2(lin[0] + kb[0, 0:1] * arriving_half(arr, arr_other, half))
        states.append((hi, lo))
        read[:, cols] = dot(cmat[...], hi) + dot(cmat[...], lo)
        since = lax.broadcasted_iota(jnp.int32, age.shape, 0)
        kappa = jnp.where(age[...] > since, jnp.exp(cum[...]), 0.0)
        kx[:, cols] = expand(lanes_below(kappa, heads), ex[...])
    for k, (z, o) in enumerate(((z0, o0), (z1, o1), (z2, o2), (z3, o3))):
        cols = slice(k * quarter, (k + 1) * quarter)
        gate[:, cols] = dot(normed[...], z[...])
        dno[:, cols] = dot(cotan, o[...], 1, 1)

    gains = [
        (par_a if j < tiles // 2 else par_b)[5:6, (j * LANES) % width : (j * LANES) % width + LANES]
        for j in range(tiles)
    ]

    def rows_body(step, _):
        rows = pl.ds(pl.multiple_of(step * ROWS, ROWS), ROWS)
        squares = jnp.zeros((ROWS, LANES), f32)
        inners = jnp.zeros((ROWS, LANES), f32)
        for j in range(tiles):
            cols = slice(j * LANES, (j + 1) * LANES)
            part = part_a if j < tiles // 2 else part_b
            pcols = slice(cols.start % width, cols.start % width + LANES)
            ssd = part[rows, pcols] + kx[rows, cols] * read[rows, cols]
            g = gate[rows, cols]
            sig = sigmoid(g)
            gated = ssd * (g * sig)
            squares += gated * gated
            inners += gated * (dno[rows, cols] * gains[j])
            ssd_s[rows, cols] = ssd
            sig_s[rows, cols] = sig
        rg = lax.rsqrt(jnp.sum(squares, axis=1, keepdims=True) / inner + EPS)
        stat = rg * rg * (jnp.sum(inners, axis=1, keepdims=True) / inner)
        rg = jnp.broadcast_to(rg, (ROWS, LANES))
        stat = jnp.broadcast_to(stat, (ROWS, LANES))
        for j in range(tiles):
            cols = slice(j * LANES, (j + 1) * LANES)
            val = val_a if j < tiles // 2 else val_b
            pcols = slice(cols.start % width, cols.start % width + LANES)
            ssd, sig, g, d = ssd_s[rows, cols], sig_s[rows, cols], gate[rows, cols], dno[rows, cols]
            act = g * sig
            gated = ssd * act
            yhat = gated * rg
            nout[rows, cols] = (yhat * gains[j]).astype(bf16)
            ggain[:, cols] += fold8(d * yhat)
            dgated = rg * (d * gains[j] - gated * stat)
            low = (dgated * act).astype(bf16)
            dssd[rows, cols] = low
            dgate[rows, cols] = (dgated * ssd * (sig * (1.0 + g * (1.0 - sig)))).astype(bf16)
            dy = low.astype(f32)
            gskip[:, cols] += fold8(dy * val[rows, pcols].astype(f32))
            kd = kx[rows, cols] * dy
            khi[rows, cols], klo[rows, cols] = split2(kd)
            rhi[rows, cols], rlo[rows, cols] = split2(kd * read[rows, cols])
        return 0

    lax.fori_loop(0, GROUP // ROWS, rows_body, 0)
    out = hid[0].astype(f32)
    for k, o in enumerate((o0, o1, o2, o3)):
        out = out + dot(nout[:, k * quarter : (k + 1) * quarter], o[...])
    out = out.astype(bf16).T
    piece = out.shape[0] // 4
    for k in range(4):
        pieces[k] = out[k * piece : (k + 1) * piece]
    dc = None
    age_end = age[GROUP - 1 : GROUP]
    for half, (dkk, ck, cum, lout, ka, tot, kout, running, kept) in enumerate(
        (
            (dkk_a, ck_a, cum_a, lout_a, ka_a, tot_a, kout_a, run_a, kept_a),
            (dkk_b, ck_b, cum_b, lout_b, ka_b, tot_b, kout_b, run_b, kept_b),
        )
    ):
        cols = slice(half * width, (half + 1) * width)
        hi, lo = states[half]
        dkk[...] = dot(rhi[:, cols], red[...]) + dot(rlo[:, cols], red[...])
        term = dot(khi[:, cols], hi, 1, 1) + dot(khi[:, cols], lo, 1, 1) + dot(klo[:, cols], hi, 1, 1)
        dc = term if dc is None else dc + term
        own = dot(cmat[...], khi[:, cols], 0, 0) + dot(cmat[...], klo[:, cols], 0, 0)
        lout[0] = running[...]
        ka[0] = expand(lanes_below(kept[...], heads), ex[...])
        running[...] = ck[0, 0:1] * running[...] + own
        keep = jnp.where(age_end >= GROUP, jnp.exp(cum[GROUP - 1 : GROUP]), 0.0)
        kept[...] = lanes_below(jnp.broadcast_to(keep, (8, LANES)), heads) * kept[...]
        tot[...] = running[...]
        kout[...] = kept[...]
    dcin[...] = dc


def pairs_unit(val, dssd, bmat, cmat, ager, pre, cum, dvi, dbi, dci, rflow, cflow, rft):
    s = lax.broadcasted_iota(jnp.int32, (HALF, HALF), 0)
    t = lax.broadcasted_iota(jnp.int32, (HALF, HALF), 1)
    scores = dot(bmat[...], cmat[...], 1, 1)
    a0, a1 = ager[0:1, :HALF], ager[0:1, HALF:]
    gap = t - s
    m00 = (gap >= 0) & (gap <= a0)
    m11 = (gap >= 0) & (gap <= a1)
    m01 = gap + HALF <= a1
    s00 = jnp.where(m00, scores[:HALF, :HALF], 0.0)
    s11 = jnp.where(m11, scores[HALF:, HALF:], 0.0)
    s01 = jnp.where(m01, scores[:HALF, HALF:], 0.0)
    c2 = cum[...] * LOG2E
    cr = c2 - jnp.log2(softplus(pre[...]))
    c2t = c2.T
    lane = lax.broadcasted_iota(jnp.int32, (HALF, LANES), 1)
    zero = jnp.zeros((HALF, HALF), f32)
    d00, d01, d11 = zero, zero, zero
    cf0, cf1 = zero, zero
    rft[...] = jnp.zeros_like(rft)
    for j in range(val.shape[1] // LANES):
        cols = slice(j * LANES, (j + 1) * LANES)
        v = val[:, cols]
        dy = dssd[:, cols]
        vm = pair_masks(v, v.shape)
        dm = pair_masks(dy, dy.shape)
        tops, bottoms = [], []
        for which in range(2):
            h = 2 * j + which
            col0 = jnp.broadcast_to(cr[:HALF, h : h + 1], (HALF, HALF))
            col1 = jnp.broadcast_to(cr[HALF:, h : h + 1], (HALF, HALF))
            r0 = c2t[h : h + 1, :HALF]
            r1 = c2t[h : h + 1, HALF:]
            e00 = jnp.exp2(jnp.minimum(r0 - col0, 60.0))
            e01 = jnp.exp2(r1 - col0)
            e11 = jnp.exp2(jnp.minimum(r1 - col1, 60.0))
            tops.append((s00 * e00).astype(bf16))
            tops.append((s01 * e01).astype(bf16))
            bottoms.append((s11 * e11).astype(bf16))
            w0 = dot(vm[which][:HALF], dy, 1, 1)
            w1 = dot(vm[which][HALF:], dy[HALF:], 1, 1)
            de00 = w0[:, :HALF] * e00
            de01 = w0[:, HALF:] * e01
            de11 = w1 * e11
            d00 += de00
            d01 += de01
            d11 += de11
            f00 = de00 * s00
            f01 = de01 * s01
            f11 = de11 * s11
            rft[h : h + 1, :HALF] = jnp.sum(f00, axis=0, keepdims=True)
            rft[h : h + 1, HALF:] = jnp.sum(f01 + f11, axis=0, keepdims=True)
            cf0 = jnp.where(lane == h, jnp.sum(f00 + f01, axis=1, keepdims=True), cf0)
            cf1 = jnp.where(lane == h, jnp.sum(f11, axis=1, keepdims=True), cf1)
        dvi[:HALF, cols] = dot(jnp.concatenate(tops, axis=1), jnp.concatenate([dm[0], dm[1]], axis=0))
        dvi[HALF:, cols] = dot(
            jnp.concatenate(bottoms, axis=1), jnp.concatenate([dm[0][HALF:], dm[1][HALF:]], axis=0)
        )
    cflow[:HALF] = cf0
    cflow[HALF:] = cf1
    rflow[...] = rft[...].T
    d00 = split2(jnp.where(m00, d00, 0.0))
    d01 = split2(jnp.where(m01, d01, 0.0))
    d11 = split2(jnp.where(m11, d11, 0.0))
    b0, b1, c0, c1 = bmat[:HALF], bmat[HALF:], cmat[:HALF], cmat[HALF:]
    dbi[:HALF] = dot(d00[0], c0) + dot(d00[1], c0) + dot(d01[0], c1) + dot(d01[1], c1)
    dbi[HALF:] = dot(d11[0], c1) + dot(d11[1], c1)
    dci[:HALF] = dot(d00[0], b0, 0, 0) + dot(d00[1], b0, 0, 0)
    dci[HALF:] = (
        dot(d01[0], b0, 0, 0) + dot(d01[1], b0, 0, 0) + dot(d11[0], b1, 0, 0) + dot(d11[1], b1, 0, 0)
    )


def outer_kernel(
    n, parts, count, tiles, normed, cotx, dgate, nout,
    val_a, val_b, dssd, bmat, cmat, ager, pre_a, pre_b, cum_a, cum_b, tot_a, tot_b, k_a, k_b, ex,
    dvi_a, dbi_a, dci_a, rflow_a, cflow_a, dvi_b, dbi_b, dci_b, rflow_b, cflow_b, own, other, share, zo,
    rft, keep, send, got, far_out, far_in, sems, *scratch
):
    u = pl.program_id(0)
    v = u - 4 * tiles
    states = Exchange(True, n, parts, (tot_a, tot_b), (k_a, k_b), ex, own, other, scratch[3:])
    sums = Scatter(n, scratch[:3])
    share_rows = zo.shape[0] // n
    across = lax.rem(lax.axis_index("head") + 2, 4)

    def trade(src, dst, sem, head):
        return pltpu.make_async_remote_copy(
            src_ref=src,
            dst_ref=dst,
            send_sem=sems.at[0, sem],
            recv_sem=sems.at[1, sem],
            device_id={"head": head},
            device_id_type=MESH,
        )

    def swap(half, m):
        return trade(send.at[half, m], got.at[half, m], 2 * half + m, states.partner)

    def cross(m):
        return trade(far_out.at[m], far_in.at[m], 4 + m, across)

    def cross_after(m):
        swap(0, m).wait()
        far_out[m] = (keep[0, m] + got[0, m].astype(f32)).astype(bf16)
        cross(m).start()

    pl.when(u == 0)(functools.partial(states.begin, (across,)))

    @pl.when(u == tiles)
    def _():
        swap(0, 0).start()

    @pl.when(u == 2 * tiles)
    def _():
        swap(0, 1).start()
        cross_after(0)

    @pl.when(u == 3 * tiles)
    def _():
        swap(1, 0).start()
        cross_after(1)

    @pl.when(v == 0)
    def _():
        swap(1, 1).start()
        states.scan()

    part = keep.shape[3]
    rows = pl.ds(pl.multiple_of(lax.rem(u, tiles) * GROUP, GROUP), GROUP)
    for m, (a, b) in enumerate(((normed, dgate), (cotx, nout))):

        @pl.when((v < 0) & (lax.rem(u // tiles, 2) == m))
        def _():
            res = dot(a[...], b[...], 0, 0)
            half = u // (2 * tiles)
            keep[half, m, rows] = res[:, :part]
            send[half, m, rows] = res[:, part:].astype(bf16)

    @pl.when((v >= 0) & (v < count))
    def _():
        pairs_unit(val_a, dssd, bmat, cmat, ager, pre_a, cum_a, dvi_a, dbi_a, dci_a, rflow_a, cflow_a, rft)

    @pl.when(v >= count)
    def _():
        pairs_unit(val_b, dssd, bmat, cmat, ager, pre_b, cum_b, dvi_b, dbi_b, dci_b, rflow_b, cflow_b, rft)

    pl.when(u == 1)(states.combine)

    @pl.when(v == count - 1)
    def _():
        swap(1, 0).wait()
        cross(0).wait()

        def total(s):
            at = slice(s * share_rows, (s + 1) * share_rows)
            return keep[1, 0, at] + got[1, 0, at].astype(f32) + far_in[0, at].astype(f32)

        sums.start(total)

    @pl.when(v == 2 * count - 1)
    def _():
        states.finish()
        swap(1, 1).wait()
        cross(1).wait()
        zo[...] = (keep[1, 1] + got[1, 1].astype(f32) + far_in[1].astype(f32)).astype(bf16)
        share[...] = sums.finish()


def slope(x):
    sig = sigmoid(x)
    return sig * (1.0 + x * (1.0 - sig))


def conv_back(i, dco, agex, age, ci, taps, dci, tail, head, gw):
    width = ci.shape[1]
    for r in range(0, GROUP, ROWS):
        ages = [agex[r + m : r + m + ROWS] for m in range(4)]
        for j in range(width // LANES):
            cols = slice(j * LANES, (j + 1) * LANES)
            c = ci[r : r + ROWS, cols].astype(f32)
            acc = None
            for m in range(4):
                x = dco[r + m : r + m + ROWS, cols]
                if m:
                    x = jnp.where(ages[m] >= m, x, 0.0)
                term = x * taps[3 - m : 4 - m, cols]
                acc = term if acc is None else acc + term
                gw[8 * (3 - m) : 8 * (3 - m) + 8, cols] += fold8(x * c)
            dci[r : r + ROWS, cols] = acc.astype(bf16)
            if r == GROUP - ROWS:

                @pl.when(i == 0)
                def _():
                    tail[:, cols] = acc[ROWS - 8 :]

    head[...] = dco[0:8]


def start_next(i, dco, agex, gw, gb):
    @pl.when(i == 0)
    def _():
        dco[GROUP : GROUP + 8] = jnp.zeros((8, dco.shape[1]), f32)
        agex[GROUP : GROUP + 8] = jnp.zeros((8, LANES), jnp.int32)
        gw[...] = jnp.zeros_like(gw)
        gb[...] = jnp.zeros_like(gb)

    @pl.when(i > 0)
    def _():
        dco[GROUP : GROUP + 8] = dco[0:8]
        agex[GROUP : GROUP + 8] = agex[0:8]


def back_step(
    half, i, val, dssd, dvi, bmat, co, ci, age, pre, cum, lout, ka, leav, leav_other, lin, kb, arr, arr_other,
    rflow, cflow, dkk, par, tril, ex, red,
    dci, tail, head, draw, gw, gb, galog, gdtb,
    dco, agex, back, omx, vhi, vlo,
):
    width = val.shape[1]
    heads = width // HEAD_DIM
    start_next(i, dco, agex, gw, gb)

    @pl.when(i == 0)
    def _():
        galog[...] = jnp.zeros_like(galog)
        gdtb[...] = jnp.zeros_like(gdtb)

    agex[0:GROUP] = age[...]
    ds = lout[0] + ka[0, 0:1] * arriving_half(leav, leav_other, half)
    dhi, dlo = split2(ds)
    back[...] = dot(bmat[...], dhi) + dot(bmat[...], dlo)
    p = pre[...]
    delta = softplus(p)
    c = cum[...]
    end = c[GROUP - 1 : GROUP]
    age_end = age[GROUP - 1 : GROUP]
    row = lax.broadcasted_iota(jnp.int32, c.shape, 0)
    tail_keep = jnp.where(GROUP - 1 - row <= age_end, jnp.exp(end - c), 0.0)
    omega = tail_keep * delta
    omx[...] = expand(lanes_below(omega, heads), ex[...])
    for r in range(0, GROUP, ROWS):
        rows = slice(r, r + ROWS)
        for j in range(width // LANES):
            cols = slice(j * LANES, (j + 1) * LANES)
            v = val[rows, cols].astype(f32)
            b = back[rows, cols]
            o = omx[rows, cols]
            dval = par[6:7, cols] * dssd[rows, cols].astype(f32) + dvi[rows, cols] + o * b
            vhi[rows, cols], vlo[rows, cols] = split2(v * b)
            d = dval * slope(co[rows, cols])
            dco[rows, cols] = d
            gb[:, cols] += fold8(d)
    domega = dot(vhi[...], red[...]) + dot(vlo[...], red[...])
    flow = domega * omega
    sin = lin[0] + kb[0, 0:1] * arriving_half(arr, arr_other, half)
    carry = jnp.broadcast_to(jnp.sum(ds * sin, axis=0, keepdims=True), (8, width))
    carry = dot(carry, red[...].astype(f32), precision=HIGHEST)[0:1]
    keep = jnp.where(age_end >= GROUP, jnp.exp(end), 0.0)
    dcum = rflow[...] - cflow[...] + dkk[...] - flow
    ending = jnp.sum(flow, axis=0, keepdims=True) + carry * keep
    dcum = dcum + jnp.where(row == GROUP - 1, ending, 0.0)
    dlog = dot(tril[...], dcum, 0, 0, precision=HIGHEST)
    sig = sigmoid(p)
    ratio = jnp.where(delta > 1e-30, sig / delta, 1.0)
    rate = par[7:8, 0:LANES]
    drf = cflow[...] * ratio + (domega * tail_keep + dlog * rate) * sig
    drf = lanes_below(drf, heads)
    draw[...] = drf.astype(bf16)
    gdtb[...] += fold8(drf)
    galog[...] += fold8(dlog * delta * rate)
    conv_back(i, dco, agex, age, ci, par, dci, tail, head, gw)


def maps_step(
    i, dbi_a, dbi_b, dci_a, dci_b, dcin, co, ci, age, taps,
    val_a, val_b, pre_a, pre_b, cum_a, cum_b, lout_a, lout_b, ka_a, ka_b, leav, leav_other, ex,
    dci, tail, head, gw, gb, dco, agex, dbin,
):
    start_next(i, dco, agex, gw, gb)
    agex[0:GROUP] = age[...]
    age_end = age[GROUP - 1 : GROUP]
    width = val_a.shape[1]
    row = lax.broadcasted_iota(jnp.int32, (GROUP, LANES), 0)
    total = dbi_a[...] + dbi_b[...]
    for half, (val, pre, cum, lout, ka) in enumerate(
        ((val_a, pre_a, cum_a, lout_a, ka_a), (val_b, pre_b, cum_b, lout_b, ka_b))
    ):
        dhi, dlo = split2(lout[0] + ka[0, 0:1] * arriving_half(leav, leav_other, half))
        c = cum[...]
        tail_keep = jnp.where(GROUP - 1 - row <= age_end, jnp.exp(c[GROUP - 1 : GROUP] - c), 0.0)
        omx = expand(lanes_below(tail_keep * softplus(pre[...]), width // HEAD_DIM), ex[...])
        ohi, olo = split2(omx * val[...].astype(f32))
        total = total + dot(ohi, dhi, 1, 1) + dot(ohi, dlo, 1, 1) + dot(olo, dhi, 1, 1)
    dbin[...] = total
    for r in range(0, GROUP, ROWS):
        rows = slice(r, r + ROWS)
        dc = dci_a[rows] + dci_b[rows] + dcin[rows]
        for j, d in enumerate((dbin[rows], dc)):
            cols = slice(j * LANES, (j + 1) * LANES)
            d = d * slope(co[rows, cols])
            dco[rows, cols] = d
            gb[:, cols] += fold8(d)
    conv_back(i, dco, agex, age, ci, taps, dci, tail, head, gw)


def mended(x, last, scr):
    scr[...] = x[...]

    @pl.when(pl.program_id(0) == pl.num_programs(0) - 1)
    def _():
        scr[GROUP - 16 :] = last[...]

    return scr


def padded_rows(x, rows):
    if x.shape[0] == rows:
        return x
    return jnp.concatenate([x, jnp.zeros((rows - x.shape[0], x.shape[1]), x.dtype)], axis=0)


def up16(rows):
    return (rows + 15) // 16 * 16


class Scatter:
    def __init__(self, n, scratch):
        self.n, self.me = n, lax.axis_index("seq")
        self.out, self.got, self.sems = scratch

    @staticmethod
    def scratch(n, rows, cols):
        pad = up16(rows)
        return [
            pltpu.VMEM((n, pad, cols), bf16),
            pltpu.VMEM((n, pad, cols), bf16),
            pltpu.SemaphoreType.DMA((2, n)),
        ]

    def move(self, d):
        to = lax.rem(self.me + d, self.n)
        return pltpu.make_async_remote_copy(
            src_ref=self.out.at[to],
            dst_ref=self.got.at[self.me],
            send_sem=self.sems.at[0, d],
            recv_sem=self.sems.at[1, d],
            device_id={"seq": to},
            device_id_type=MESH,
        )

    def start(self, share):
        for s in range(self.n):
            self.out[s] = padded_rows(share(s), self.out.shape[1]).astype(bf16)
        for d in range(1, self.n):
            self.move(d).start()
        self.got[self.me] = self.out[self.me]

    def finish(self):
        for d in range(1, self.n):
            self.move(d).wait()
        total = self.got[0].astype(f32)
        for s in range(1, self.n):
            total = total + self.got[s].astype(f32)
        return total.astype(bf16)


class Gather:
    def __init__(self, n, scratch):
        self.n, self.me = n, lax.axis_index("seq")
        self.mine, self.all, self.sems = scratch

    @staticmethod
    def scratch(n, rows, cols):
        pad = up16(rows)
        return [
            pltpu.VMEM((pad, cols), bf16),
            pltpu.VMEM((n, pad, cols), bf16),
            pltpu.SemaphoreType.DMA((2, n)),
        ]

    def move(self, d):
        return pltpu.make_async_remote_copy(
            src_ref=self.mine,
            dst_ref=self.all.at[self.me],
            send_sem=self.sems.at[0, d],
            recv_sem=self.sems.at[1, d],
            device_id={"seq": lax.rem(self.me + d, self.n)},
            device_id_type=MESH,
        )

    def start(self, share):
        self.mine[...] = share
        for d in range(1, self.n):
            self.move(d).start()
        self.all[self.me] = share

    def finish(self):
        for d in range(1, self.n):
            self.move(d).wait()

    def rows(self, s, count):
        return self.all[s].astype(f32)[:count]


def tail_kernel(
    n, parts, count,
    hid, cotx, gain, dgate, z0, z1, z2, z3, dbc, last_bc, bcw, dxb, last_b, x2, x3, drb, dtb,
    dx, x0, x1, dr, dt, keep, send, far, small_keep, small_send, small_far, common, bc,
    grad_in, gx, gbc, small,
    acc_s, low, shuffle, scr_b, scr_bc, ggain, got, got_small, slots, com_got, gi_out, gi_got, gi_sum, gi_all, small_got, small_mine, small_all,
    bc_out, bc_got, bc_own, bc_heads, piece_send, piece_recv, swap_sems, small_sems, *shares,
):
    i = pl.program_id(0)
    s_me = lax.axis_index("seq")
    h_me = lax.axis_index("head")
    near = h_me + 1 - 2 * lax.rem(h_me, 2)
    heads = [h_me, near, lax.rem(h_me + 2, 4), lax.rem(near + 2, 4)]
    chunk = count * GROUP
    quarter = x0.shape[1]
    features = gain.shape[1]
    tiles = features // LANES
    gx_sum, gx_all = Scatter(n, shares[:3]), Gather(n, shares[3:6])
    bc_rows = features // 4 // n
    bc_sum, bc_all = Scatter(n, shares[6:9]), Gather(n, shares[9:12])

    def trade(src, dst, k, sem):
        return pltpu.make_async_remote_copy(
            src_ref=src,
            dst_ref=dst,
            send_sem=swap_sems.at[2 * sem],
            recv_sem=swap_sems.at[2 * sem + 1],
            device_id={"head": heads[k]},
            device_id_type=MESH,
        )

    def bc_trade(k):
        return trade(bc_out.at[heads[k]], bc_got.at[k], k, 6 + k)

    def common_trade(k):
        return trade(common, com_got.at[k], k, 9 + k)

    def gi_trade(k):
        return trade(gi_out, gi_got.at[k], k, 12 + k)

    def gi_spread(d):
        return pltpu.make_async_remote_copy(
            src_ref=gi_sum,
            dst_ref=gi_all.at[s_me],
            send_sem=small_sems.at[4, d],
            recv_sem=small_sems.at[5, d],
            device_id={"seq": lax.rem(s_me + d, n)},
            device_id_type=MESH,
        )

    def place(head, step):
        cols = pl.ds(pl.multiple_of(lax.rem(head, parts) * chunk + step * GROUP, GROUP), GROUP)
        return grad_in.at[head // parts, :, cols]

    def piece_copy(step, k):
        src = shuffle.at[step, heads[k]]
        if k == 0:
            return pltpu.make_async_copy(src, place(h_me, step), piece_send.at[step, 0])
        return pltpu.make_async_remote_copy(
            src_ref=src,
            dst_ref=place(h_me, step),
            send_sem=piece_send.at[step, k],
            recv_sem=piece_recv.at[step, k],
            device_id={"head": heads[k]},
            device_id_type=MESH,
        )

    def spread_small(d, gather):
        to = lax.rem(s_me + d, n)
        if gather:
            src, dst, kind = small_mine, small_all.at[s_me], 2
        else:
            src, dst, kind = slots.at[to], small_got.at[s_me], 0
        return pltpu.make_async_remote_copy(
            src_ref=src,
            dst_ref=dst,
            send_sem=small_sems.at[kind, d],
            recv_sem=small_sems.at[kind + 1, d],
            device_id={"seq": to},
            device_id_type=MESH,
        )

    @pl.when(i == 0)
    def _():
        ggain[...] = jnp.zeros_like(ggain)
        barrier = pltpu.get_barrier_semaphore()
        for k in range(1, 4):
            pl.semaphore_signal(barrier, inc=1, device_id={"head": heads[k]}, device_id_type=MESH)
        for d in range(1, n):
            pl.semaphore_signal(barrier, inc=1, device_id={"seq": lax.rem(s_me + d, n)}, device_id_type=MESH)
        pl.semaphore_wait(barrier, n + 2)
        trade(send, got, 1, 0).start()
        for q in range(4):
            bc_out[q] = bc[q * (features // 4) : (q + 1) * (features // 4)].astype(bf16)
        for k in (2, 3, 1):
            bc_trade(k).start()
        trade(small_send, got_small, 1, 1).start()
        for k in range(1, 4):
            common_trade(k).start()

    dbc = mended(dbc, last_bc, scr_bc)
    dxb = mended(dxb, last_b, scr_b)
    acc = dot(dbc[...], bcw[...], 1, 1) + dot(dr[...], dt[...]) + dot(drb[...], dtb[...])
    for k, (z, x) in enumerate(((z0, x0), (z1, x1), (z2, x2), (z3, x3))):
        d, at = (dx if k < 2 else dxb), (k % 2) * quarter
        acc = acc + dot(dgate[:, k * quarter : (k + 1) * quarter], z[...], 1, 1)
        acc = acc + dot(d[:, at : at + quarter], x[...], 1, 1)
    acc_s[...] = acc
    piece = features // 4
    for r in range(0, GROUP, ROWS):
        rows = slice(r, r + ROWS)
        x = hid[rows].astype(f32)
        rinv = lax.rsqrt(jnp.sum(x * x, axis=1, keepdims=True) / x.shape[1] + EPS)
        xhat = x * rinv
        d = acc_s[rows]
        ggain[...] += fold8(d * xhat)
        dxh = d * gain[...]
        mean = jnp.sum(dxh * xhat, axis=1, keepdims=True) / x.shape[1]
        out = (cotx[rows].astype(f32) + rinv * (dxh - xhat * mean)).astype(bf16)
        low[rows] = out
    turned = low[...].T
    for k in range(4):
        shuffle[i, k] = turned[k * piece : (k + 1) * piece]
    for k in (2, 3, 1, 0):
        piece_copy(i, k).start()

    @pl.when(i == 0)
    def _():
        trade(send, got, 1, 0).wait()
        share = features // n

        def gx_share(s):
            rows = slice(s * share, (s + 1) * share)
            return keep[rows] + got[rows].astype(f32) + far[rows].astype(f32)

        gx_sum.start(gx_share)

    @pl.when(i == 1)
    def _():
        total = bc[pl.ds(pl.multiple_of(h_me * (features // 4), 8), features // 4)]
        for k in range(1, 4):
            bc_trade(k).wait()
            total = total + bc_got[k].astype(f32)
        bc_own[...] = total
        bc_sum.start(lambda s: bc_own[s * bc_rows : (s + 1) * bc_rows])
        trade(small_send, got_small, 1, 1).wait()
        both = common[...]
        for k in range(1, 4):
            common_trade(k).wait()
            both = both + com_got[k]
        both = jnp.concatenate([both, jnp.zeros((8, features - 2 * LANES), f32)], axis=1)
        both = jnp.concatenate([small_keep[...] + got_small[...] + small_far[...], both], axis=0)
        for t in range(tiles):
            slots[t] = both[:, t * LANES : (t + 1) * LANES]
        for d in range(1, n):
            pl.when(lax.rem(s_me + d, n) < tiles)(spread_small(d, False).start)

    @pl.when(i == 2)
    def _():
        for d in range(1, n):
            pl.when(lax.rem(s_me + d, n) < tiles)(spread_small(d, False).wait_send)

        @pl.when(s_me < tiles)
        def _():
            small_got[s_me] = slots[s_me]
            for d in range(1, n):
                spread_small(d, False).wait_recv()
            total = small_got[0]
            for s in range(1, n):
                total = total + small_got[s]
            small_mine[...] = total
            for d in range(1, n):
                spread_small(d, True).start()
            small_all[s_me] = total

        bc_all.start(bc_sum.finish())

    @pl.when(i == count - 1)
    def _():
        row = jnp.sum(ggain[...], axis=0, keepdims=True)
        gi_out[...] = jnp.broadcast_to(row, gi_out.shape)
        for k in range(1, 4):
            gi_trade(k).start()
        gx_all.start(gx_sum.finish())
        bc_all.finish()
        for k in range(1, 4):
            trade(bc_all.all, bc_heads.at[h_me], k, 3 + k).start()
        bc_heads[h_me] = bc_all.all[...]
        total = gi_out[...]
        for k in range(1, 4):
            gi_trade(k).wait()
            total = total + gi_got[k]
        gi_sum[...] = total
        for d in range(1, n):
            gi_spread(d).start()
        for k in range(1, 4):
            trade(bc_all.all, bc_heads.at[h_me], k, 3 + k).wait()
        for q in range(4):
            for s in range(n):
                at = (q * n + s) * bc_rows
                gbc[at : at + bc_rows] = bc_heads[q, s].astype(f32)[:bc_rows]

        @pl.when(s_me < tiles)
        def _():
            for d in range(1, n):
                spread_small(d, True).wait_send()

        for d in range(1, n):
            pl.when(lax.rem(s_me + n - d, n) < tiles)(spread_small(d, True).wait_recv)
        for t in range(tiles):
            small[0:24, t * LANES : (t + 1) * LANES] = small_all[t]
        gi_all[s_me] = total
        for d in range(1, n):
            gi_spread(d).wait()
        for s in range(n):
            if s:
                total = total + gi_all[lax.rem(s_me + s, n)]
        small[24:32] = total
        for step in range(count):
            for k in range(4):
                if k == 0:
                    piece_copy(step, 0).wait()
                else:
                    piece_copy(step, k).wait_send()
                    piece_copy(step, k).wait_recv()
        gx_all.finish()
        for s in range(n):
            rows = slice(s * (features // n), (s + 1) * (features // n))
            gx[rows] = gx_all.rows(s, features // n)


def mend(got, tail, ci, next_age, taps, dx, scr, last, flip):
    g = got[...]
    if flip:
        part = g.shape[1] // 2
        g = jnp.concatenate([g[:, part:], g[:, :part]], axis=1)
    rows = scr.shape[0]
    if dx is not None:
        scr[...] = dx[...]
    ending = ci[...].astype(f32)[8:16]
    row = lax.broadcasted_iota(jnp.int32, (8, LANES), 0)
    fixed, sums = [], []
    for j in range(g.shape[1] // LANES):
        cols = slice(j * LANES, (j + 1) * LANES)
        acc = tail[:, cols]
        parts = [jnp.zeros((1, LANES), f32)] * 4
        for m in range(1, 4):
            use = (row >= 8 - m) & (pltpu.roll(next_age[...], 8 - m, 0) >= m)
            x = jnp.where(use, pltpu.roll(g[:, cols], 8 - m, 0), 0.0)
            acc = acc + x * taps[3 - m : 4 - m, cols]
            parts[3 - m] = jnp.sum(x * ending[:, cols], axis=0, keepdims=True)
        fixed.append(acc)
        sums.append(jnp.concatenate(parts, axis=0))
    fixed = jnp.concatenate(fixed, axis=1)
    before = scr[rows - 16 :].astype(f32)[0:8]
    scr[rows - 16 :] = jnp.concatenate([before, fixed], axis=0).astype(bf16)
    if last is not None:
        last[...] = scr[rows - 16 :]
    return jnp.concatenate(sums, axis=1)


def small_sums(at, fix, gw, gb, galog, gdtb, gskip, ggain, red, small_keep, small_send):
    part = red.shape[0] // 2
    heads = part // HEAD_DIM
    width = 2 * part
    for to in (small_keep, small_send):
        to[...] = jnp.zeros_like(to)
    taps = [jnp.sum(gw[8 * k : 8 * k + 8], axis=0, keepdims=True) for k in range(4)]
    taps = jnp.concatenate(taps, axis=0) + fix
    bias = jnp.sum(gb[...], axis=0, keepdims=True)
    cols = slice(at * width, (at + 1) * width)
    gain = jnp.sum(ggain[:, cols], axis=0, keepdims=True)
    skip = jnp.broadcast_to(jnp.sum(gskip[:, cols], axis=0, keepdims=True), (8, width))
    skip = dot(skip, red[...].astype(f32), precision=HIGHEST)
    step = jnp.broadcast_to(jnp.sum(gdtb[...], axis=0, keepdims=True), (8, LANES))
    log = jnp.broadcast_to(jnp.sum(galog[...], axis=0, keepdims=True), (8, LANES))
    for k, to in enumerate((small_keep, small_send)):
        mine = slice(k * part, (k + 1) * part)
        to[0:4, 0:part] = taps[:, mine]
        to[4:5, 0:part] = bias[:, mine]
        to[5:6, 0:part] = gain[:, mine]
        row = jnp.zeros((8, LANES), f32)
        for place, x in enumerate((step, log, skip)):
            x = lanes_below(pltpu.roll(x, (LANES - k * heads) % LANES, 1), heads)
            row = row + pltpu.roll(x, place * heads, 1)
        to[6:7, 0:LANES] = row[0:1]


def half_tile(tile, normed, dx, draw, keep, send, small_keep, small_send):
    part = keep.shape[1]
    heads = part // HEAD_DIM
    res = dot(normed[...], dx[...], 0, 0)
    keep[...] = res[:, :part]
    send[...] = res[:, part:].astype(bf16)
    dt = dot(draw[...], normed[...], 0, 0)
    cols = pl.ds(pl.multiple_of(tile * GROUP, GROUP), GROUP)
    small_keep[8:16, cols] = dt[0:8]
    small_send[8:16, cols] = pltpu.roll(dt, LANES - heads, 0)[0:8]


def turn_kernel(n, parts, count, *refs):
    maps_in, refs = refs[:22], refs[22:]
    back_in, refs = refs[:24], refs[24:]
    (own, share, pieces), refs = refs[:3], refs[3:]
    maps_out, refs = refs[:5], refs[5:]
    back_out, refs = refs[:8], refs[8:]
    (share_out, gathered, placed), refs = refs[:3], refs[3:]
    maps_scr, refs = refs[:3], refs[3:]
    back_scr, refs = refs[:6], refs[6:]
    (piece_sems,), refs = refs[:1], refs[1:]
    u = pl.program_id(0)
    sums, shares = Scatter(n, refs[:3]), Gather(n, refs[3:])
    rows = own.shape[0] // n
    me = lax.axis_index("seq")
    head = lax.axis_index("head")
    near = head + 1 - 2 * lax.rem(head, 2)
    heads = [head, near, lax.rem(head + 2, 4), lax.rem(near + 2, 4)]
    chunk = pieces.shape[2]

    def piece_copy(k):
        cols = pl.ds(pl.multiple_of(lax.rem(head, parts) * chunk, chunk), chunk)
        src, dst = pieces.at[heads[k]], placed.at[head // parts, :, cols]
        if k == 0:
            return pltpu.make_async_copy(src, dst, piece_sems.at[0, 0])
        return pltpu.make_async_remote_copy(
            src_ref=src,
            dst_ref=dst,
            send_sem=piece_sems.at[0, k],
            recv_sem=piece_sems.at[1, k],
            device_id={"head": heads[k]},
            device_id_type=MESH,
        )

    @pl.when(u == 0)
    def _():
        barrier = pltpu.get_barrier_semaphore()
        for k in range(1, 4):
            pl.semaphore_signal(barrier, inc=1, device_id={"head": heads[k]}, device_id_type=MESH)
        for d in range(1, n):
            pl.semaphore_signal(barrier, inc=1, device_id={"seq": lax.rem(me + d, n)}, device_id_type=MESH)
        pl.semaphore_wait(barrier, n + 2)
        shares.start(share[...])
        sums.start(lambda s: own[s * rows : (s + 1) * rows].astype(f32))
        for k in (2, 3, 1, 0):
            piece_copy(k).start()

    @pl.when(u < count)
    def _():
        maps_step(u, *maps_in, *maps_out, *maps_scr)

    @pl.when(u >= count)
    def _():
        back_step(1, u - count, *back_in, *back_out, *back_scr)

    @pl.when(u == 2 * count - 1)
    def _():
        share_out[...] = sums.finish()
        shares.finish()
        for s in range(n):
            gathered[s * rows : (s + 1) * rows] = shares.rows(s, rows)
        for k in range(4):
            piece_copy(k).wait()


def late_kernel(n, parts, count, tiles, *refs):
    back_in, refs = refs[:24], refs[24:]
    (
        normed, dx_b, tail_b, head_b, ci_b, par_b, draw_b, gw_b, gb_b, galog_b, gdtb_b,
        dbc, tail_bc, head_bc, ci_bc, taps_bc, gw_bc, gb_bc, ci_a, next_age, gskip, ggain, share,
    ), refs = refs[:23], refs[23:]
    (
        dx_a, draw_a, keep_a, send_a, small_a, small_send_a, last_b, last_bc, g_bc, small_bc,
        far, small_far, grad_out,
    ), refs = refs[:13], refs[13:]
    back_scr, refs = refs[:6], refs[6:]
    (
        tail_a, head_a, gw_a, gb_a, galog_a, gdtb_a, scr_b, scr_bc, keep_b, send_b, got_b, far_out,
        small_b, small_send_b, small_got, small_out, small_in, far_in, edge_b, edge_bc, edge_a, edge_sems, sems,
    ), refs = refs[:23], refs[23:]
    u = pl.program_id(0)
    par_a, red = back_in[20], back_in[23]
    s_me = lax.axis_index("seq")
    h_me = lax.axis_index("head")
    near = h_me + 1 - 2 * lax.rem(h_me, 2)
    across = lax.rem(h_me + 2, 4)
    half = lax.rem(h_me, parts)
    to_seq = s_me - 1 + half
    has_before = to_seq >= 0
    has_after = s_me + half < n
    gathered = Gather(n, refs)
    part = keep_a.shape[1]
    first_back, first_bc, first_a = tiles + 1, tiles + count, 2 * tiles + count

    def trade(src, dst, sem, head):
        return pltpu.make_async_remote_copy(
            src_ref=src,
            dst_ref=dst,
            send_sem=sems.at[0, sem],
            recv_sem=sems.at[1, sem],
            device_id={"head": head},
            device_id_type=MESH,
        )

    def edge(k):
        src, dst = ((head_b, edge_b), (head_bc, edge_bc), (head_a, edge_a))[k]
        return pltpu.make_async_remote_copy(
            src_ref=src,
            dst_ref=dst,
            send_sem=edge_sems.at[0, k],
            recv_sem=edge_sems.at[1, k],
            device_id={"seq": lax.max(to_seq, 0), "head": near},
            device_id_type=MESH,
        )

    def send_edge(k):
        pl.when(has_before)(edge(k).start)

    def take_edge(k):
        pl.when(has_before)(edge(k).wait_send)
        pl.when(has_after)(edge(k).wait_recv)

    swap_b = trade(send_b, got_b, 0, near)
    swap_small = trade(small_send_b, small_got, 1, near)
    cross_b = trade(far_out, far_in, 2, across)
    cross_small = trade(small_out, small_in, 3, across)

    @pl.when(u == 0)
    def _():
        for to in (edge_b, edge_bc, edge_a):
            to[...] = jnp.zeros_like(to)
        barrier = pltpu.get_barrier_semaphore()
        for head in (near, across):
            pl.semaphore_signal(barrier, inc=1, device_id={"head": head}, device_id_type=MESH)
        for d in range(1, n):
            pl.semaphore_signal(barrier, inc=1, device_id={"seq": lax.rem(s_me + d, n)}, device_id_type=MESH)
        other_seq = s_me - 1 + 2 * half
        has_other = (other_seq >= 0) & (other_seq < n)

        @pl.when(has_other)
        def _():
            pl.semaphore_signal(
                barrier, inc=1, device_id={"seq": other_seq, "head": near}, device_id_type=MESH
            )

        pl.semaphore_wait(barrier, n + 1 + has_other.astype(jnp.int32))
        send_edge(0)
        send_edge(1)
        gathered.start(share[...])

    block = jnp.clip(u - tiles, 0, count - 1)

    @pl.when((u == 0) | ((u >= first_back) & (u < first_bc)))
    def _():
        rows = pl.ds(pl.multiple_of((count - 1 - block) * GROUP, GROUP), GROUP)
        outs = (dx_a.at[rows], tail_a, head_a, draw_a.at[rows], gw_a, gb_a, galog_a, gdtb_a)
        back_step(0, block, *back_in, *outs, *back_scr)

    @pl.when(u == 1)
    def _():
        take_edge(0)
        fix = mend(edge_b, tail_b, ci_b, next_age, par_b, dx_b, scr_b, last_b, True)
        small_sums(1, fix, gw_b, gb_b, galog_b, gdtb_b, gskip, ggain, red, small_b, small_send_b)

    @pl.when((u >= 1) & (u <= tiles))
    def _():
        rows = pl.ds(pl.multiple_of((u - 1) * GROUP, GROUP), GROUP)
        half_tile(u - 1, normed, scr_b, draw_b, keep_b.at[rows], send_b.at[rows], small_b, small_send_b)

    @pl.when(u == first_back)
    def _():
        swap_b.start()
        swap_small.start()

    @pl.when(u == first_back + 1)
    def _():
        swap_b.wait()
        far_out[...] = (keep_b[...] + got_b[...].astype(f32)).astype(bf16)
        cross_b.start()
        swap_small.wait()
        small_out[...] = small_b[...] + small_got[...]
        cross_small.start()

    @pl.when(u == first_bc)
    def _():
        send_edge(2)
        take_edge(1)
        fix = mend(edge_bc, tail_bc, ci_bc, next_age, taps_bc, dbc, scr_bc, last_bc, False)
        small_bc[...] = jnp.zeros_like(small_bc)
        sums = [jnp.sum(gw_bc[8 * k : 8 * k + 8], axis=0, keepdims=True) for k in range(4)]
        small_bc[0:4] = jnp.concatenate(sums, axis=0) + fix
        small_bc[4:5] = jnp.sum(gb_bc[...], axis=0, keepdims=True)

    @pl.when((u >= first_bc) & (u < first_a))
    def _():
        g_bc[...] = dot(normed[...], scr_bc[...], 0, 0)

    @pl.when(u == first_a)
    def _():
        take_edge(2)
        fix = mend(edge_a, tail_a, ci_a, next_age, par_a, None, dx_a, None, True)
        small_sums(0, fix, gw_a, gb_a, galog_a, gdtb_a, gskip, ggain, red, small_a, small_send_a)

    @pl.when(u >= first_a)
    def _():
        half_tile(u - first_a, normed, dx_a, draw_a, keep_a, send_a, small_a, small_send_a)

    @pl.when(u == first_a + tiles - 1)
    def _():
        cross_b.wait()
        far[...] = far_in[...]
        cross_small.wait()
        small_far[...] = small_in[...]
        gathered.finish()
        rows = grad_out.shape[1] // n
        grad_out[...] = jnp.concatenate([gathered.rows(s, rows) for s in range(n)], axis=0).T


def unpack_kernel(
    quarter, heads, me, small, gi, dt, taps, bias, maps, maps_bias, step, log, skip, gain
):
    features = small.shape[1]
    piece = gi.shape[1]
    row = pltpu.roll(small[24:32], lax.rem(features - me[0] * piece, features), 1)
    gi[...] = row[0:1, :piece]
    dt[...] = small[8 : 8 + heads]
    taps[...] = small[0:4, :quarter]
    bias[...] = small[4:5, :quarter]
    gain[...] = small[5:6, :quarter]
    maps[...] = small[16:20, : 2 * LANES]
    maps_bias[...] = small[20:21, : 2 * LANES]
    row = jnp.broadcast_to(small[6:7, 0:LANES], (8, LANES))
    for k, to in enumerate((step, log, skip)):
        to[...] = pltpu.roll(row, LANES - k * heads, 1)[0:1, :heads] if k else row[0:1, :heads]


def shards(
    hidden_in,
    output_cotangent,
    input_norm_scale_gain,
    z_proj,
    x_proj,
    bc_proj,
    dt_proj,
    conv_x_weight,
    conv_x_bias,
    conv_bc_weight,
    conv_bc_bias,
    dt_bias,
    a_log,
    d_skip,
    out_norm_gain,
    out_proj,
    doc_starts,
):
    batch, tokens, features = hidden_in.shape
    quarter = z_proj.shape[1]
    width = 2 * quarter
    inner = 4 * quarter
    heads = dt_proj.shape[1]
    seqs = lax.axis_size("seq")
    head_devices = lax.axis_size("head")
    parts = head_devices // batch
    chunk = tokens // parts
    count = chunk // GROUP
    si, hi_ = lax.axis_index("seq"), lax.axis_index("head")
    seq_of, half = hi_ // parts, hi_ % parts
    core = [(h, h ^ 1) for h in range(head_devices)]
    across = [(h, h ^ 2) for h in range(head_devices)]
    corner = [(h, h ^ 3) for h in range(head_devices)]
    meta = jnp.reshape(hi_, (1,)).astype(jnp.int32)

    def swap(x):
        return lax.ppermute(x, "head", core)

    def cross(x):
        return lax.ppermute(x, "head", across)

    def after(x, *others):
        return lax.optimization_barrier((x,) + others)[0]

    hid_map = lambda i, m: (m[0] // parts, lax.rem(m[0], parts) * count + i, 0)
    rev_hid = lambda i, m: (m[0] // parts, lax.rem(m[0], parts) * count + count - 1 - i, 0)
    here = lambda i, *_: (i, 0)
    here3 = lambda i, *_: (i, 0, 0)
    rev = lambda i, *_: (count - 1 - i, 0)
    rev3 = lambda i, *_: (count - 1 - i, 0, 0)
    gain_in = input_norm_scale_gain[None]
    taps_bc = conv_bc_weight.T
    lane_block = (GROUP, LANES)
    map_block = (GROUP, 2 * LANES)
    wide = (GROUP, inner)
    half_in = (GROUP, width)
    state_block = (1, LANES, width)
    keep_block = (1, 8, width)
    piece = features // head_devices

    normed, ci_bc = run(
        norm_kernel,
        (count,),
        [
            (hidden_in, (1, GROUP, features), hid_map),
            (gain_in, None, None),
            (bc_proj, None, None),
        ],
        [
            ((chunk, features), bf16, (GROUP, features), here),
            ((chunk, 2 * LANES), bf16, map_block, here),
        ],
        flops=2 * chunk * features * 256,
        moved=6_000_000,
        prefetch=(meta,),
    )

    small = jnp.concatenate(
        [
            jnp.pad(conv_x_weight.T, ((0, 0), (0, features - quarter))),
            jnp.pad(conv_x_bias, (0, features - quarter))[None],
            jnp.pad(out_norm_gain, (0, features - quarter))[None],
            jnp.pad(jnp.concatenate([dt_bias, a_log, d_skip]), (0, features - 3 * heads))[None],
            jnp.zeros((1, features), f32),
            jnp.pad(dt_proj.T.astype(f32), ((0, 8 - heads), (0, 0))),
        ],
        axis=0,
    )
    small = after(small, ci_bc)
    x_far = cross(x_proj)
    small_far = cross(small)
    z_far = cross(after(z_proj, x_far))
    o_far = cross(after(out_proj, z_far))
    xs = [x_proj, swap(x_proj), x_far, swap(x_far)]
    smalls = [small, swap(small), small_far, swap(small_far)]
    zs = [z_proj, swap(z_proj), z_far, swap(z_far)]
    os_ = [out_proj, swap(out_proj), o_far, swap(o_far)]
    edge_far = lax.ppermute(
        lax.dynamic_slice(hidden_in, (seq_of, tokens - 16, 0), (1, 16, features))[0],
        "seq",
        [(s, s + 1) for s in range(seqs - 1)],
    )
    cotangent = after(jnp.swapaxes(output_cotangent, 1, 2), x_far)
    cots = []
    for k in range(4):
        to = hi_ ^ k
        mine = lax.dynamic_slice(
            cotangent, (to // parts, 0, (to % parts) * chunk), (1, piece, chunk)
        )[0]
        if k == 1:
            mine = swap(mine)
        elif k:
            mine = lax.ppermute(after(mine, o_far), "head", across if k == 2 else corner)
        cots.append(mine)

    first_pos = si * tokens + half * chunk
    starts = lax.dynamic_slice(doc_starts, (seq_of, 0), (1, doc_starts.shape[1]))[0]

    def age_of(places):
        found = jnp.where(starts[None, :] <= places[:, None], starts[None, :], 0)
        return places - jnp.max(found, axis=1)

    age1 = age_of(first_pos + jnp.arange(chunk, dtype=jnp.int32))
    next_age = age_of(first_pos + chunk + jnp.arange(8, dtype=jnp.int32))
    next_age = jnp.broadcast_to(next_age[:, None], (8, LANES))
    age = jnp.broadcast_to(age1[:, None], (chunk, LANES))
    ager = jnp.broadcast_to(age1[None, :], (8, chunk))

    ex, red = expansion(width)
    tril = jnp.asarray(np.tril(np.ones((GROUP, GROUP), np.float32)))

    halves = []
    for n, k in enumerate((0, 2)):
        maps_in = [
            (ci_bc, map_block, here),
            (bc_proj, None, None),
            (taps_bc, None, None),
            (conv_bc_bias[None], None, None),
        ]
        maps_out = [
            ((chunk, 2 * LANES), f32, map_block, here),
            ((chunk, LANES), bf16, lane_block, here),
            ((chunk, LANES), bf16, lane_block, here),
        ]
        outs = run(
            functools.partial(front_kernel, n == 0, parts),
            (count,),
            [
                (normed, (GROUP, features), here),
                (edge_far, None, None),
                (hidden_in, (1, 16, features), lambda i, m: (m[0] // parts, chunk // 16 - 1, 0)),
                (gain_in, None, None),
                (xs[k], None, None),
                (xs[k + 1], None, None),
                (smalls[k], None, None),
                (smalls[k + 1], None, None),
                (age, lane_block, here),
                (tril, None, None),
                (ex, None, None),
            ]
            + (maps_in if n == 0 else [(bmat, lane_block, here)]),
            [
                ((chunk, width), bf16, half_in, here),
                ((chunk, width), f32, half_in, here),
                ((chunk, width), bf16, half_in, here),
                ((chunk, LANES), f32, lane_block, here),
                ((chunk, LANES), f32, lane_block, here),
                ((count, LANES, width), f32, state_block, here3),
                ((count, 8, width), f32, keep_block, here3),
                ((count, 8, width), f32, keep_block, here3),
                ((LANES, width), f32, None, None),
                ((8, LANES), f32, None, None),
                ((8, width), f32, None, None),
                ((LANES, features), bf16, None, None),
            ]
            + (maps_out if n == 0 else []),
            [
                pltpu.VMEM((GROUP + 8, width), f32),
                pltpu.VMEM((LANES, width), f32),
                pltpu.VMEM((8, LANES), f32),
                pltpu.VMEM(half_in, f32),
                pltpu.VMEM(half_in, bf16),
                pltpu.VMEM(half_in, bf16),
                pltpu.VMEM((LANES, features), f32),
            ]
            + ([pltpu.VMEM((GROUP + 8, 2 * LANES), f32)] if n == 0 else []),
            flops=2 * chunk * features * 1024 * 4,
            moved=16_000_000,
            prefetch=(meta,),
        )
        names = ("ci", "co", "val", "pre", "cum", "lin", "kb", "ck", "tot", "kout", "par", "dtp")
        d = dict(zip(names, outs))
        if n == 0:
            co_bc, bmat, cmat = outs[12:]
        halves.append(d)
    ha, hb = halves

    lo_block = lambda u: (jnp.minimum(u, count - 1), 0)
    hi_block = lambda u: (jnp.maximum(u - count, 0), 0)
    any_block = lambda u: (lax.rem(u, count), 0)

    def both(name, block):
        return [(ha[name], block, lo_block), (hb[name], block, hi_block)]

    def whole(*arrays):
        return [(a, None, None) for a in arrays]

    ha["part"], hb["part"], *arr = run(
        functools.partial(intra_kernel, seqs, parts, count),
        (2 * count,),
        both("val", half_in)
        + [(bmat, lane_block, any_block), (cmat, lane_block, any_block), (age, lane_block, any_block)]
        + both("pre", lane_block)
        + both("cum", lane_block)
        + whole(ha["par"], hb["par"], ha["tot"], hb["tot"], ha["kout"], hb["kout"], ex),
        [
            ((chunk, width), f32, half_in, lo_block),
            ((chunk, width), f32, half_in, hi_block),
            ((LANES, width), f32, None, None),
            ((LANES, width), f32, None, None),
        ],
        Exchange.scratch(seqs, width),
        flops=25_000_000_000,
        moved=16_000_000,
        collective=1,
    )

    outs = run(
        mid_kernel,
        (count,),
        [
            (hidden_in, (1, GROUP, features), rev_hid),
            (normed, (GROUP, features), rev),
            *whole(*zs, *os_),
            *[(c, (piece, GROUP), lambda i, *_: (0, count - 1 - i)) for c in cots],
            (cmat, lane_block, rev),
            (age, lane_block, rev),
            *whole(ex, red, ha["par"], hb["par"]),
            *[(d["part"], half_in, rev) for d in halves],
            *[(d["val"], half_in, rev) for d in halves],
            *[(d["cum"], lane_block, rev) for d in halves],
            *[(d["lin"], state_block, rev3) for d in halves],
            *[(d["kb"], keep_block, rev3) for d in halves],
            *[(d["ck"], keep_block, rev3) for d in halves],
            *whole(*arr),
        ],
        [
            ((4, piece, chunk), bf16, (4, piece, GROUP), lambda i, *_: (0, 0, count - 1 - i)),
            ((chunk, features), bf16, (GROUP, features), rev),
            ((chunk, inner), bf16, wide, rev),
            ((chunk, features), bf16, (GROUP, features), rev),
            ((chunk, inner), bf16, wide, rev),
            ((chunk, inner), bf16, wide, rev),
            ((chunk, LANES), f32, lane_block, rev),
            ((chunk, LANES), f32, lane_block, rev),
            ((chunk, LANES), f32, lane_block, rev),
            ((count, LANES, width), f32, state_block, rev3),
            ((count, LANES, width), f32, state_block, rev3),
            ((count, 8, width), f32, keep_block, rev3),
            ((count, 8, width), f32, keep_block, rev3),
            ((LANES, width), f32, None, None),
            ((LANES, width), f32, None, None),
            ((8, LANES), f32, None, None),
            ((8, LANES), f32, None, None),
            ((8, inner), f32, None, None),
            ((8, inner), f32, None, None),
        ],
        [pltpu.VMEM(wide, f32)] * 6
        + [pltpu.VMEM(wide, bf16)] * 4
        + [pltpu.VMEM((LANES, width), f32)] * 2
        + [pltpu.VMEM((8, LANES), f32)] * 2
        + [pltpu.VMEM((4, piece, GROUP), bf16)],
        flops=30_000_000_000,
        moved=50_000_000,
        prefetch=(meta,),
    )
    pieces, hidc, outs = outs[0], outs[1], outs[2:]
    nout, cotx, dssd, dgate, dcin, ha["dkk"], hb["dkk"], ha["lout"], hb["lout"], ha["ka"], hb["ka"] = outs[:11]
    dtot_a, dtot_b, dk_a, dk_b, ggain_out, gskip = outs[11:]

    tiles = features // GROUP
    lead = 4 * tiles
    tile_block = lambda u: (0, lax.rem(jnp.minimum(u, lead - 1), tiles))
    first_half = lambda u: (0, 1 - jnp.minimum(u // (2 * tiles), 1))
    after_lead = lambda u: jnp.maximum(u - lead, 0)
    lo_unit = lambda u: (jnp.clip(u - lead, 0, count - 1), 0)
    hi_unit = lambda u: (jnp.clip(u - lead - count, 0, count - 1), 0)
    any_unit = lambda u: (lax.rem(after_lead(u), count), 0)
    quarter_grad = (2, features, quarter)
    share_rows = features // seqs
    outs = run(
        functools.partial(outer_kernel, seqs, parts, count, tiles),
        (lead + 2 * count,),
        [
            (normed, (chunk, GROUP), tile_block),
            (cotx, (chunk, GROUP), tile_block),
            (dgate, (chunk, width), first_half),
            (nout, (chunk, width), first_half),
            (ha["val"], half_in, lo_unit),
            (hb["val"], half_in, hi_unit),
            (dssd, half_in, lambda u: (lax.rem(after_lead(u), count), after_lead(u) // count)),
            (bmat, lane_block, any_unit),
            (cmat, lane_block, any_unit),
            (ager, (8, GROUP), lambda u: (0, lax.rem(after_lead(u), count))),
            (ha["pre"], lane_block, lo_unit),
            (hb["pre"], lane_block, hi_unit),
            (ha["cum"], lane_block, lo_unit),
            (hb["cum"], lane_block, hi_unit),
            *whole(dtot_a, dtot_b, dk_a, dk_b, ex),
        ],
        [
            (shape, f32, (GROUP, shape[1]), imap)
            for imap in (lo_unit, hi_unit)
            for shape in [(chunk, width)] + [(chunk, LANES)] * 4
        ]
        + [((LANES, width), f32, None, None)] * 2
        + [((up16(share_rows), quarter), bf16, None, None), ((features, quarter), bf16, None, None)],
        [
            pltpu.VMEM((LANES, GROUP), f32),
            pltpu.VMEM((2,) + quarter_grad, f32),
            pltpu.VMEM((2,) + quarter_grad, bf16),
            pltpu.VMEM((2,) + quarter_grad, bf16),
            pltpu.VMEM(quarter_grad, bf16),
            pltpu.VMEM(quarter_grad, bf16),
            pltpu.SemaphoreType.DMA((2, 6)),
        ]
        + Scatter.scratch(seqs, share_rows, quarter)
        + Exchange.scratch(seqs, width),
        flops=30_000_000_000,
        moved=40_000_000,
        collective=2,
    )
    names = ("dvi", "dbi", "dci_c", "rflow", "cflow")
    ha.update(zip(names, outs[:5]))
    hb.update(zip(names, outs[5:10]))
    leav = outs[10:12]
    share_z, grad_o = outs[12:]

    def back_ins(n, block, block3):
        d = halves[n]
        return [
            (d["val"], half_in, block),
            (dssd, half_in, lambda u: (block(u)[0], n)),
            (d["dvi"], half_in, block),
            (bmat, lane_block, block),
            (d["co"], half_in, block),
            (d["ci"], half_in, block),
            (age, lane_block, block),
            (d["pre"], lane_block, block),
            (d["cum"], lane_block, block),
            (d["lout"], state_block, block3),
            (d["ka"], keep_block, block3),
            *whole(*leav),
            (d["lin"], state_block, block3),
            (d["kb"], keep_block, block3),
            *whole(*arr),
            (d["rflow"], lane_block, block),
            (d["cflow"], lane_block, block),
            (d["dkk"], lane_block, block),
            *whole(d["par"], tril, ex, red),
        ]

    back_scratch = [
        pltpu.VMEM((GROUP + 8, width), f32),
        pltpu.VMEM((GROUP + 8, LANES), jnp.int32),
        pltpu.VMEM(half_in, f32),
        pltpu.VMEM(half_in, f32),
        pltpu.VMEM(half_in, bf16),
        pltpu.VMEM(half_in, bf16),
    ]

    def both_outs(cols, block):
        return [
            ((chunk, cols), bf16, (GROUP, cols), block),
            ((8, cols), f32, None, None),
            ((8, cols), f32, None, None),
        ]

    early_rev = lambda u: (count - 1 - jnp.minimum(u, count - 1), 0)
    late_rev = lambda u: (count - 1 - jnp.maximum(u - count, 0), 0)
    early_rev3 = lambda u: (count - 1 - jnp.minimum(u, count - 1), 0, 0)
    late_rev3 = lambda u: (count - 1 - jnp.maximum(u - count, 0), 0, 0)
    outs = run(
        functools.partial(turn_kernel, seqs, parts, count),
        (2 * count,),
        [
            *[(d["dbi"], lane_block, early_rev) for d in halves],
            *[(d["dci_c"], lane_block, early_rev) for d in halves],
            (dcin, lane_block, early_rev),
            (co_bc, map_block, early_rev),
            (ci_bc, map_block, early_rev),
            (age, lane_block, early_rev),
            (taps_bc, None, None),
            *[(d["val"], half_in, early_rev) for d in halves],
            *[(d["pre"], lane_block, early_rev) for d in halves],
            *[(d["cum"], lane_block, early_rev) for d in halves],
            *[(d["lout"], state_block, early_rev3) for d in halves],
            *[(d["ka"], keep_block, early_rev3) for d in halves],
            *whole(*leav, ex),
            *back_ins(1, late_rev, late_rev3),
            *whole(grad_o, share_z),
            (pieces, pl.ANY, None),
        ],
        both_outs(2 * LANES, early_rev)
        + [((32, 2 * LANES), f32, None, None), ((8, 2 * LANES), f32, None, None)]
        + both_outs(width, late_rev)
        + [
            ((chunk, LANES), bf16, lane_block, late_rev),
            ((32, width), f32, None, None),
            ((8, width), f32, None, None),
            ((8, LANES), f32, None, None),
            ((8, LANES), f32, None, None),
            ((up16(share_rows), quarter), bf16, None, None),
            ((features, quarter), f32, None, None),
            ((batch, piece, tokens), bf16, pl.ANY, None),
        ],
        [
            pltpu.VMEM((GROUP + 8, 2 * LANES), f32),
            pltpu.VMEM((GROUP + 8, LANES), jnp.int32),
            pltpu.VMEM(lane_block, f32),
        ]
        + back_scratch
        + [pltpu.SemaphoreType.DMA((2, 4))]
        + Scatter.scratch(seqs, share_rows, quarter)
        + Gather.scratch(seqs, share_rows, quarter),
        flops=30_000_000_000,
        moved=40_000_000,
        collective=4,
    )
    dbc, tail_bc, head_bc, gw_bc, gb_bc = outs[:5]
    hb.update(zip(("dx", "tail", "head", "draw", "gw", "gb", "galog", "gdtb"), outs[5:13]))
    share, grad_z, layer_out = outs[13:]

    steps = 3 * tiles + count
    back_unit = lambda u: (count - 1 - jnp.clip(u - tiles, 0, count - 1), 0)
    back_unit3 = lambda u: (count - 1 - jnp.clip(u - tiles, 0, count - 1), 0, 0)

    def grad_tile(u):
        later = u // (tiles + count)
        first = jnp.clip(u - 1, 0, tiles - 1)
        return 0, (1 - later) * first + later * lax.rem(jnp.maximum(u - tiles - count, 0), tiles)

    bc_tile = lambda u: (jnp.clip(u - tiles - count, 0, tiles - 1), 0)
    a_tile = lambda u: (jnp.clip(u - 2 * tiles - count, 0, tiles - 1), 0)
    ending = lambda *_: (chunk // 16 - 1, 0)
    outs = run(
        functools.partial(late_kernel, seqs, parts, count, tiles),
        (steps,),
        [
            *back_ins(0, back_unit, back_unit3),
            (normed, (chunk, GROUP), grad_tile),
            *whole(hb["dx"], hb["tail"], hb["head"]),
            (hb["ci"], (16, width), ending),
            *whole(hb["par"], hb["draw"], hb["gw"], hb["gb"], hb["galog"], hb["gdtb"]),
            *whole(dbc, tail_bc, head_bc),
            (ci_bc, (16, 2 * LANES), ending),
            *whole(taps_bc, gw_bc, gb_bc),
            (ha["ci"], (16, width), ending),
            *whole(next_age, gskip, ggain_out, share),
        ],
        [
            ((chunk, width), bf16, None, None),
            ((chunk, LANES), bf16, None, None),
            ((features, quarter), f32, (GROUP, quarter), a_tile),
            ((features, quarter), bf16, (GROUP, quarter), a_tile),
            ((16, features), f32, None, None),
            ((16, features), f32, None, None),
            ((16, width), bf16, None, None),
            ((16, 2 * LANES), bf16, None, None),
            ((features, 2 * LANES), f32, map_block, bc_tile),
            ((8, 2 * LANES), f32, None, None),
            ((features, quarter), bf16, None, None),
            ((16, features), f32, None, None),
            ((quarter, features), f32, None, None),
        ],
        back_scratch
        + [
            pltpu.VMEM((8, width), f32),
            pltpu.VMEM((8, width), f32),
            pltpu.VMEM((32, width), f32),
            pltpu.VMEM((8, width), f32),
            pltpu.VMEM((8, LANES), f32),
            pltpu.VMEM((8, LANES), f32),
            pltpu.VMEM((chunk, width), bf16),
            pltpu.VMEM((chunk, 2 * LANES), bf16),
            pltpu.VMEM((features, quarter), f32),
            pltpu.VMEM((features, quarter), bf16),
            pltpu.VMEM((features, quarter), bf16),
            pltpu.VMEM((features, quarter), bf16),
        ]
        + [pltpu.VMEM((16, features), f32)] * 5
        + [
            pltpu.VMEM((features, quarter), bf16),
            pltpu.VMEM((8, width), f32),
            pltpu.VMEM((8, 2 * LANES), f32),
            pltpu.VMEM((8, width), f32),
            pltpu.SemaphoreType.DMA((2, 3)),
            pltpu.SemaphoreType.DMA((2, 4)),
        ]
        + Gather.scratch(seqs, share_rows, quarter),
        flops=30_000_000_000,
        moved=40_000_000,
        collective=5,
    )
    dx_a, draw_a, keep_a, send_a, small_a, small_send_a, last_b, last_bc, g_bc, small_bc = outs[:10]
    far, small_far, grad_out = outs[10:]

    input_grad, sum2, g_bc, small_sum = run(
        functools.partial(tail_kernel, seqs, parts, count),
        (count,),
        [
            (hidc, (GROUP, features), here),
            (cotx, (GROUP, features), here),
            (gain_in, None, None),
            (dgate, wide, here),
            *whole(*zs),
            (dbc, map_block, here),
            *whole(last_bc, bc_proj),
            (hb["dx"], half_in, here),
            *whole(last_b, xs[2], xs[3]),
            (hb["draw"], lane_block, here),
            (hb["dtp"], None, None),
            (dx_a, half_in, here),
            *whole(xs[0], xs[1]),
            (draw_a, lane_block, here),
            *whole(ha["dtp"], keep_a, send_a, far, small_a, small_send_a, small_far, small_bc, g_bc),
        ],
        [
            ((batch, piece, tokens), bf16, pl.ANY, None),
            ((features, quarter), f32, None, None),
            ((features, 2 * LANES), f32, None, None),
            ((32, features), f32, None, None),
        ],
        [
            pltpu.VMEM((GROUP, features), f32),
            pltpu.VMEM((GROUP, features), bf16),
            pltpu.VMEM((count, 4, piece, GROUP), bf16),
            pltpu.VMEM(half_in, bf16),
            pltpu.VMEM(map_block, bf16),
            pltpu.VMEM((8, features), f32),
            pltpu.VMEM((features, quarter), bf16),
            pltpu.VMEM((16, features), f32),
            pltpu.VMEM((seqs, 24, LANES), f32),
            pltpu.VMEM((4, 8, 2 * LANES), f32),
            pltpu.VMEM((8, features), f32),
            pltpu.VMEM((4, 8, features), f32),
            pltpu.VMEM((8, features), f32),
            pltpu.VMEM((seqs, 8, features), f32),
            pltpu.VMEM((seqs, 24, LANES), f32),
            pltpu.VMEM((24, LANES), f32),
            pltpu.VMEM((seqs, 24, LANES), f32),
            pltpu.VMEM((4, features // 4, 2 * LANES), bf16),
            pltpu.VMEM((4, features // 4, 2 * LANES), bf16),
            pltpu.VMEM((features // 4, 2 * LANES), f32),
            pltpu.VMEM((4, seqs, up16(features // 4 // seqs), 2 * LANES), bf16),
            pltpu.SemaphoreType.DMA((count, 4)),
            pltpu.SemaphoreType.DMA((count, 4)),
            pltpu.SemaphoreType.DMA((32,)),
            pltpu.SemaphoreType.DMA((6, seqs)),
        ]
        + Scatter.scratch(seqs, features // seqs, quarter)
        + Gather.scratch(seqs, features // seqs, quarter)
        + Scatter.scratch(seqs, features // 4 // seqs, 2 * LANES)
        + Gather.scratch(seqs, features // 4 // seqs, 2 * LANES),
        collective=3,
    )
    vector = lambda size: ((1, size), f32, None, None)
    gi, g_dt, g_taps, g_bias, g_maps, g_maps_bias, g_step, g_log, g_skip, g_gain = run(
        functools.partial(unpack_kernel, quarter, heads),
        (1,),
        whole(small_sum),
        [
            vector(piece),
            ((heads, features), f32, None, None),
            ((4, quarter), f32, None, None),
            vector(quarter),
            ((4, 2 * LANES), f32, None, None),
            vector(2 * LANES),
            vector(heads),
            vector(heads),
            vector(heads),
            vector(quarter),
        ],
        prefetch=(meta,),
    )
    return (
        jnp.swapaxes(layer_out, 1, 2),
        jnp.swapaxes(input_grad, 1, 2),
        gi[0],
        grad_z,
        sum2,
        g_bc,
        g_dt.T,
        g_taps.T,
        g_bias[0],
        g_maps.T,
        g_maps_bias[0],
        g_step[0],
        g_log[0],
        g_skip[0],
        g_gain[0],
        grad_out,
    )


def solution(mesh):
    return jax.shard_map(
        shards,
        mesh=mesh,
        in_specs=(
            P(None, "seq", None),
            P(None, "seq", "head"),
            P(),
            P(None, "head"),
            P(None, "head"),
            P(),
            P(None, "head"),
            P("head", None),
            P("head"),
            P(),
            P(),
            P("head"),
            P("head"),
            P("head"),
            P("head"),
            P("head", None),
            P(),
        ),
        out_specs=(
            P(None, "seq", "head"),
            P(None, "seq", "head"),
            P("head"),
            P(None, "head"),
            P(None, "head"),
            P(),
            P(None, "head"),
            P("head", None),
            P("head"),
            P(),
            P(),
            P("head"),
            P("head"),
            P("head"),
            P("head"),
            P("head", None),
        ),
        check_vma=False,
    )
```

```python
import functools

import jax
import jax.numpy as jnp
import numpy as np
from jax import lax
from jax.experimental import pallas as pl
from jax.experimental.pallas import tpu as pltpu
from jax.sharding import PartitionSpec as P

GROUP = 256
HALF = 128
LANES = 128
HEAD_DIM = 64
EPS = 1e-05
LOG2E = 1.4426950408889634
f32 = jnp.float32
bf16 = jnp.bfloat16
HIGHEST = lax.Precision.HIGHEST
ROWS = 32
MESH = pl.DeviceIdType.MESH


def dot(a, b, ca=1, cb=0, precision=None):
    return lax.dot_general(
        a, b, (((ca,), (cb,)), ((), ())), precision=precision, preferred_element_type=f32
    )


def split2(x):
    hi = x.astype(bf16)
    return hi, (x - hi.astype(f32)).astype(bf16)


def pack(x):
    hi = x.astype(bf16).astype(f32)
    rest = x - hi
    mid = rest.astype(bf16).astype(f32)
    return (hi + pltpu.roll(mid, 32, 1) + pltpu.roll(rest - mid, 64, 1)).astype(bf16)


def unpack(x):
    x = x.astype(f32)
    return lanes_below(x + pltpu.roll(x, LANES - 32, 1) + pltpu.roll(x, LANES - 64, 1), 12)


def expand(x, ex):
    return dot(pack(x), ex)


def lanes_below(x, count):
    return jnp.where(lax.broadcasted_iota(jnp.int32, x.shape, 1) < count, x, 0.0)


def sigmoid(x):
    return 1.0 / (1.0 + jnp.exp(-x))


def softplus(x):
    return jnp.maximum(x, 0.0) + jnp.log1p(jnp.exp(-jnp.abs(x)))


def fold8(x):
    total = x[0:8]
    for r in range(8, x.shape[0], 8):
        total = total + x[r : r + 8]
    return total


def expansion(width):
    heads = width // HEAD_DIM
    ex = np.zeros((LANES, width), np.float32)
    for part in range(3):
        for h in range(heads):
            ex[32 * part + h, h * HEAD_DIM : (h + 1) * HEAD_DIM] = 1.0
    red = np.zeros((width, LANES), np.float32)
    for h in range(heads):
        red[h * HEAD_DIM : (h + 1) * HEAD_DIM, h] = 1.0
    return jnp.asarray(ex, bf16), jnp.asarray(red, bf16)


def run(kernel, grid, ins, outs, scratch=(), flops=0, moved=0, prefetch=(), collective=None):
    def spec(shape, block, imap):
        if block is pl.ANY:
            return pl.BlockSpec(memory_space=pl.ANY)
        if block is None:
            rank = len(shape)
            return pl.BlockSpec(shape, lambda *_: (0,) * rank)
        return pl.BlockSpec(block, imap)

    extra = {} if collective is None else {"collective_id": collective, "has_side_effects": True}
    return pl.pallas_call(
        kernel,
        grid_spec=pltpu.PrefetchScalarGridSpec(
            num_scalar_prefetch=len(prefetch),
            grid=grid,
            in_specs=[spec(a.shape, b, m) for a, b, m in ins],
            out_specs=[spec(s, b, m) for s, _, b, m in outs],
            scratch_shapes=list(scratch),
        ),
        out_shape=[jax.ShapeDtypeStruct(s, d) for s, d, _, _ in outs],
        compiler_params=pltpu.CompilerParams(vmem_limit_bytes=56 << 20, **extra),
        cost_estimate=pl.CostEstimate(flops=flops, bytes_accessed=moved, transcendentals=0),
    )(*prefetch, *[a for a, _, _ in ins])


def conv_rows(ext, age, taps, bias, r, cols):
    acc = jnp.broadcast_to(bias[:, cols], (ROWS, LANES))
    for k in range(4):
        back = 3 - k
        term = ext[8 + r - back : 8 + r - back + ROWS, cols] * taps[k : k + 1, cols]
        if back:
            term = jnp.where(age >= back, term, 0.0)
        acc = acc + term
    return acc


def rms(x, gain):
    x = x.astype(f32)
    r = lax.rsqrt(jnp.sum(x * x, axis=1, keepdims=True) / x.shape[1] + EPS)
    return (x * r * gain).astype(bf16)


def spread_ages(starts, first, rows):
    token = first + lax.broadcasted_iota(jnp.int32, (rows, starts.shape[1]), 0)
    begun = jnp.where(starts <= token, starts, 0).astype(f32)
    begun = jnp.max(begun, axis=1, keepdims=True).astype(jnp.int32)
    place = first + lax.broadcasted_iota(jnp.int32, (rows, LANES), 0)
    return place - begun


def front_step(
    with_maps, i, normed, before, wa, wb, sa, sb, age, tril, ex, maps_in,
    ci, co, val, pre, cum, lin, kb, ck, tot, kout, par, dtp, maps_out,
    ext, running, kept, omx, ohi, olo, dts, ext_bc,
):
    width = val.shape[1]
    part = width // 2
    heads = part // HEAD_DIM
    if with_maps:
        ci_bc, bc, taps_bc, bias_bc = maps_in
        bias_bc = bias_bc[0:1]
        co_bc, bmat, cmat = maps_out
    else:
        (bmat,) = maps_in

    @pl.when(i == 0)
    def _():
        running[...] = jnp.zeros_like(running)
        kept[...] = jnp.ones_like(kept)
        for w, at in ((wa, 0), (wb, part)):
            ext[0:8, at : at + part] = dot(before[...], w[...]).astype(bf16).astype(f32)[8:16]
        if with_maps:
            ext_bc[0:8] = dot(before[...], bc[...]).astype(bf16).astype(f32)[8:16]
        par[...] = jnp.zeros_like(par)
        for s, at in ((sa, 0), (sb, part)):
            par[0:6, at : at + part] = s[0:6, :part]
        rows_a, rows_b = (jnp.broadcast_to(s[6:7, 0:LANES], (8, LANES)) for s in (sa, sb))

        def lanes(k):
            a = lanes_below(pltpu.roll(rows_a, (LANES - k * heads) % LANES, 1), heads)
            b = lanes_below(pltpu.roll(rows_b, (LANES - k * heads) % LANES, 1), heads)
            return a + pltpu.roll(b, heads, 1)

        par[7:8, LANES : 2 * LANES] = lanes(0)[0:1]
        par[7:8, 0:LANES] = -jnp.exp(lanes(1)[0:1])
        par[6:7] = expand(lanes(2), ex[...])[0:1]
        dts[...] = jnp.zeros_like(dts)
        dts[0:heads] = sa[8 : 8 + heads]
        dts[heads : 2 * heads] = sb[8 : 8 + heads]
        dtp[...] = dts[...].astype(bf16)

    @pl.when(i > 0)
    def _():
        ext[0:8] = ext[GROUP : GROUP + 8]
        if with_maps:
            ext_bc[0:8] = ext_bc[GROUP : GROUP + 8]

    taps, bias = par, par[4:5]
    rate, dtb = par[7:8, 0:LANES], par[7:8, LANES : 2 * LANES]
    for w, at in ((wa, 0), (wb, part)):
        low = dot(normed[...], w[...]).astype(bf16)
        ci[:, at : at + part] = low
        ext[8 : 8 + GROUP, at : at + part] = low.astype(f32)
    raw = dot(normed[...], dtp[...], 1, 1) + dtb
    pre[...] = raw
    delta = softplus(raw)
    c = dot(tril[...], delta * rate, precision=HIGHEST)
    cum[...] = c
    end = c[GROUP - 1 : GROUP]
    age_end = age[GROUP - 1 : GROUP]
    left = GROUP - 1 - lax.broadcasted_iota(jnp.int32, c.shape, 0)
    omega = jnp.where(left <= age_end, jnp.exp(end - c), 0.0) * delta
    omx[...] = expand(lanes_below(omega, 2 * heads), ex[...])
    keep = jnp.where(age_end >= GROUP, jnp.exp(end), 0.0)
    keep = lanes_below(jnp.broadcast_to(keep, (8, LANES)), 2 * heads)
    keepx = expand(keep, ex[...])
    if with_maps:
        ext_bc[8 : 8 + GROUP] = ci_bc[...].astype(f32)
        for r in range(0, GROUP, ROWS):
            a = age[r : r + ROWS]
            for j, out in enumerate((bmat, cmat)):
                cols = slice(j * LANES, (j + 1) * LANES)
                v = conv_rows(ext_bc, a, taps_bc, bias_bc, r, cols)
                co_bc[r : r + ROWS, cols] = v
                out[r : r + ROWS] = (v * sigmoid(v)).astype(bf16)
    for r in range(0, GROUP, ROWS):
        a = age[r : r + ROWS]
        rows = slice(r, r + ROWS)
        for j in range(width // LANES):
            cols = slice(j * LANES, (j + 1) * LANES)
            v = conv_rows(ext, a, taps, bias, r, cols)
            co[rows, cols] = v
            act = (v * sigmoid(v)).astype(bf16)
            val[rows, cols] = act
            ohi[rows, cols], olo[rows, cols] = split2(omx[rows, cols] * act.astype(f32))
    own = dot(bmat[...], ohi[...], 0, 0) + dot(bmat[...], olo[...], 0, 0)
    lin[0] = running[...]
    kb[0] = expand(lanes_below(kept[...], 2 * heads), ex[...])
    ck[0] = keepx
    running[...] = keepx[0:1] * running[...] + own
    kept[...] = keep * kept[...]
    tot[...] = running[...]
    kout[...] = kept[...]


def head_peers():
    head = lax.axis_index("head")
    near = head + 1 - 2 * lax.rem(head, 2)
    return [head, near, lax.rem(head + 2, 4), lax.rem(near + 2, 4)]


def meet(heads, n, extra=0):
    me = lax.axis_index("seq")
    barrier = pltpu.get_barrier_semaphore()
    for head in heads:
        pl.semaphore_signal(barrier, inc=1, device_id={"head": head}, device_id_type=MESH)
    for d in range(1, n):
        pl.semaphore_signal(barrier, inc=1, device_id={"seq": lax.rem(me + d, n)}, device_id_type=MESH)
    pl.semaphore_wait(barrier, n - 1 + len(heads))


def send(src, dst, sems, k, device):
    return pltpu.make_async_remote_copy(
        src_ref=src, dst_ref=dst, send_sem=sems.at[0, k], recv_sem=sems.at[1, k],
        device_id=device, device_id_type=MESH,
    )


class Weights:
    def __init__(self, n, own, outs, scratch):
        self.own, self.outs = own, outs
        self.near, self.far, self.far_near, self.sems = scratch
        me = lax.axis_index("seq")
        odd = lax.rem(me, 2)
        heads = head_peers()
        half = own.shape[0] // 2
        rows = pl.ds(pl.multiple_of(odd * half, half), half)
        near, mate = {"head": heads[1]}, {"seq": me + 1 - 2 * odd}
        self.copies = [
            send(own, self.near, self.sems, 0, near),
            send(own.at[rows], self.far.at[rows], self.sems, 1, {"head": heads[2]}),
            send(self.far.at[rows], self.far.at[rows], self.sems, 2, mate),
            send(self.far, self.far_near, self.sems, 3, near),
        ]

    @staticmethod
    def scratch(rows, cols):
        return [pltpu.VMEM((rows, cols), bf16)] * 3 + [pltpu.SemaphoreType.DMA((2, 4))]

    def begin(self):
        self.copies[1].start()
        self.copies[0].start()

    def share(self):
        self.copies[1].wait()
        self.copies[2].start()

    def back(self):
        self.copies[2].wait()
        self.copies[3].start()

    def finish(self):
        self.copies[0].wait()
        self.copies[3].wait()
        for to, x in zip(self.outs, (self.near, self.far, self.far_near)):
            to[...] = x[...]


def cot_copies(cotangent, outs, which, parts, sems):
    heads = head_peers()
    copies = []
    for k, out in zip(which, outs):
        chunk = out.shape[1]
        cols = pl.ds(pl.multiple_of(lax.rem(heads[k], parts) * chunk, chunk), chunk)
        copies.append(send(cotangent.at[heads[k] // parts, :, cols], out, sems, k, {"head": heads[k]}))
    return copies


class Exchange:
    def __init__(self, reverse, n, parts, tots, kouts, ex, own, other, scratch):
        self.reverse, self.n, self.tots, self.kouts, self.ex = reverse, n, tots, kouts, ex
        self.own, self.other = own, other
        (
            self.out, self.got, self.payload, self.spread, self.scanned, self.home, self.lead, self.lead_k, self.arr,
            self.theirs, self.last, self.swap_sems, self.to_sems, self.from_sems, self.back_to, self.back_from,
        ) = scratch
        self.me = lax.axis_index("seq")
        head = lax.axis_index("head")
        self.partner = head + 1 - 2 * lax.rem(head, 2)
        half = lax.rem(head, parts)
        self.leads = (half if reverse else 1 - half).astype(f32)
        self.per = LANES // n

    @staticmethod
    def scratch(n, width):
        rows = max(LANES // n, 8)
        return [
            pltpu.VMEM((LANES + 8, width), f32),
            pltpu.VMEM((LANES + 8, width), f32),
            pltpu.VMEM((n, rows, width + LANES), f32),
            pltpu.VMEM((n, rows, width + LANES), f32),
            pltpu.VMEM((n, rows, width), f32),
            pltpu.VMEM((n, rows, width), f32),
            pltpu.VMEM((LANES, width), f32),
            pltpu.VMEM((8, LANES), f32),
            pltpu.VMEM((LANES, width), f32),
            pltpu.VMEM((LANES, width), f32),
            pltpu.VMEM((LANES, width), f32),
            pltpu.SemaphoreType.DMA((4,)),
            pltpu.SemaphoreType.DMA((n,)),
            pltpu.SemaphoreType.DMA((n,)),
            pltpu.SemaphoreType.DMA((n,)),
            pltpu.SemaphoreType.DMA((n,)),
        ]

    def peers(self):
        for d in range(1, self.n):
            yield d, lax.rem(self.me + d, self.n), lax.rem(self.me + self.n - d, self.n)

    def swap(self, src, dst, sem):
        return pltpu.make_async_remote_copy(
            src_ref=src,
            dst_ref=dst,
            send_sem=self.swap_sems.at[sem],
            recv_sem=self.swap_sems.at[sem + 1],
            device_id={"head": self.partner},
            device_id_type=MESH,
        )

    def move(self, src, dst, d, to, send_sems, recv_sems):
        return pltpu.make_async_remote_copy(
            src_ref=src.at[to],
            dst_ref=dst.at[self.me],
            send_sem=send_sems.at[d],
            recv_sem=recv_sems.at[d],
            device_id={"seq": to},
            device_id_type=MESH,
        )

    def begin(self):
        part = self.tots[0].shape[1] // 2
        heads = part // HEAD_DIM
        for k in range(len(self.tots)):
            self.out[0:LANES, k * part : (k + 1) * part] = self.tots[k][:, part:]
            rolled = pltpu.roll(self.kouts[k][...], LANES - heads, 1)
            self.out[LANES : LANES + 8, k * LANES : (k + 1) * LANES] = lanes_below(rolled, heads)
        used = len(self.tots) * LANES
        self.out[LANES : LANES + 8, used:] = jnp.zeros((8, self.out.shape[1] - used), f32)
        self.swap(self.out, self.got, 0).start()

    def combine(self):
        self.swap(self.out, self.got, 0).wait()
        part = self.tots[0].shape[1] // 2
        heads = part // HEAD_DIM
        width = len(self.tots) * part
        leads, follows = self.leads, 1.0 - self.leads
        mine_k, got_k = jnp.zeros((8, LANES), f32), jnp.zeros((8, LANES), f32)
        for k, kout in enumerate(self.kouts):
            both = (lanes_below(kout[...], heads), self.got[LANES : LANES + 8, k * LANES : (k + 1) * LANES])
            both = [pltpu.roll(x, k * heads, 1) if k else x for x in both]
            mine_k, got_k = mine_k + both[0], got_k + both[1]
        lk = leads * mine_k + follows * got_k
        fk = leads * got_k + follows * mine_k
        fkx = expand(fk, self.ex[:, :width])[0:1]
        self.lead_k[...] = lk
        for k in range(len(self.tots)):
            cols = slice(k * part, (k + 1) * part)
            mine, got = self.tots[k][:, :part], self.got[0:LANES, cols]
            ls = leads * mine + follows * got
            self.lead[:, cols] = ls
            self.arr[:, cols] = fkx[:, cols] * ls + (leads * got + follows * mine)
        keep = (lk * fk)[0:1]
        rows = self.payload.shape[1]
        for s in range(self.n):
            self.payload[s, 0 : self.per, 0:width] = self.arr[s * self.per : (s + 1) * self.per]
            self.payload[s, :, width:] = jnp.broadcast_to(keep, (rows, LANES))
        for d, to, _ in self.peers():
            self.move(self.payload, self.spread, d, to, self.to_sems, self.from_sems).start()
        self.spread[self.me] = self.payload[self.me]

    def scan(self):
        for d, to, _ in self.peers():
            self.move(self.payload, self.spread, d, to, self.to_sems, self.from_sems).wait()
        width = self.scanned.shape[2]
        rows = self.scanned.shape[1]
        state = jnp.zeros((rows, width), f32)
        for step in range(self.n):
            at = self.n - 1 - step if self.reverse else step
            self.scanned[at] = state
            if step < self.n - 1:
                keep = expand(self.spread[at, :, width:], self.ex[:, :width])
                state = keep * state + self.spread[at, :, 0:width]
        for d, to, _ in self.peers():
            self.move(self.scanned, self.home, d, to, self.back_to, self.back_from).start()
        self.home[self.me] = self.scanned[self.me]

    def settle(self):
        for d, to, _ in self.peers():
            self.move(self.scanned, self.home, d, to, self.back_to, self.back_from).wait()
        for s in range(self.n):
            self.arr[s * self.per : (s + 1) * self.per] = self.home[s, 0 : self.per]
        leads, follows = self.leads, 1.0 - self.leads
        first = self.arr[...]
        second = expand(self.lead_k[...], self.ex[:, : first.shape[1]])[0:1] * first + self.lead[...]
        self.theirs[...] = leads * second + follows * first
        self.swap(self.theirs, self.last, 2).start()
        self.own[...] = leads * first + follows * second

    def close(self):
        self.swap(self.theirs, self.last, 2).wait()
        self.other[...] = self.last[...]


def pair_masks(x, lane_axis_shape):
    lane = lax.broadcasted_iota(jnp.int32, lane_axis_shape, 1)
    zero = jnp.zeros_like(x)
    return jnp.where(lane < HEAD_DIM, x, zero), jnp.where(lane >= HEAD_DIM, x, zero)


def intra_unit(val, bmat, cmat, age, pre, cum, dskip, part):
    t = lax.broadcasted_iota(jnp.int32, (HALF, HALF), 0)
    s = lax.broadcasted_iota(jnp.int32, (HALF, HALF), 1)
    scores = dot(cmat[...], bmat[...], 1, 1)
    a0, a1 = age[0:HALF], age[HALF:]
    gap = t - s
    s00 = jnp.where((gap >= 0) & (gap <= a0), scores[:HALF, :HALF], 0.0)
    s11 = jnp.where((gap >= 0) & (gap <= a1), scores[HALF:, HALF:], 0.0)
    s10 = jnp.where(gap + HALF <= a1, scores[HALF:, :HALF], 0.0)
    c2 = cum[...] * LOG2E
    rows = (c2 - jnp.log2(softplus(pre[...]))).T
    for j in range(val.shape[1] // LANES):
        cols = slice(j * LANES, (j + 1) * LANES)
        v = val[:, cols]
        vm = pair_masks(v, v.shape)
        tops, bottoms = [], []
        for which in range(2):
            h = 2 * j + which
            col0 = jnp.broadcast_to(c2[:HALF, h : h + 1], (HALF, HALF))
            col1 = jnp.broadcast_to(c2[HALF:, h : h + 1], (HALF, HALF))
            r0 = rows[h : h + 1, :HALF]
            r1 = rows[h : h + 1, HALF:]
            tops.append((s00 * jnp.exp2(jnp.minimum(col0 - r0, 60.0))).astype(bf16))
            bottoms.append((s10 * jnp.exp2(col1 - r0)).astype(bf16))
            bottoms.append((s11 * jnp.exp2(jnp.minimum(col1 - r1, 60.0))).astype(bf16))
        top = dot(jnp.concatenate(tops, axis=1), jnp.concatenate([vm[0][:HALF], vm[1][:HALF]], axis=0))
        bottom = dot(jnp.concatenate(bottoms, axis=1), jnp.concatenate([vm[0], vm[1]], axis=0))
        skip = dskip[6:7, cols]
        part[:HALF, cols] = top + skip * v[:HALF].astype(f32)
        part[HALF:, cols] = bottom + skip * v[HALF:].astype(f32)


def forward_kernel(
    n, parts, count, hid, tail_rows, edge_near, starts, vecs, taps_x, dt_own, x_own, z_own, o_own, bc, taps_bc,
    tril, ex, cotangent,
    normed, ci_bc, age, ager, next_age, gain_out, x_near, x_far, x_far_near, z_near, z_far, z_far_near,
    o_near, o_far, o_far_near, cot_near, cot_across, cot_corner, co_bc, bmat, cmat, *refs,
):
    (ci_a, co_a, val_a, pre_a, cum_a, lin_a, kb_a, ck_a, par_a, dtp_a, own_a, other_a, part_a), refs = refs[:13], refs[13:]
    (ci_b, co_b, val_b, pre_b, cum_b, lin_b, kb_b, ck_b, par_b, dtp_b, own_b, other_b, part_b), refs = refs[:13], refs[13:]
    (
        gain, bias_bc, before, edge_far, small_s, small_n, small_f, small_fn, xn, xf, xfn,
        tot_a, tot_b, kout_a, kout_b, sems, cot_sems,
    ), refs = refs[:17], refs[17:]
    front, refs = refs[:8], refs[8:]
    z_weights = Weights(n, z_own, (z_near, z_far, z_far_near), refs[:4])
    o_weights = Weights(n, o_own, (o_near, o_far, o_far_near), refs[4:8])
    refs = refs[8:]
    size = len(refs) // 2
    states_a = Exchange(False, n, parts, (tot_a,), (kout_a,), ex, own_a, other_a, refs[:size])
    states_b = Exchange(False, n, parts, (tot_b,), (kout_b,), ex, own_b, other_b, refs[size:])
    cots = cot_copies(cotangent, (cot_near, cot_across, cot_corner), (1, 2, 3), parts, cot_sems)
    u = pl.program_id(0)
    s_me = lax.axis_index("seq")
    heads = head_peers()
    near, across = {"head": heads[1]}, {"head": heads[2]}
    half = lax.rem(heads[0], parts)
    batch = heads[0] // parts
    chunk = count * GROUP
    features = bc.shape[0]
    part = x_own.shape[1]
    nh = dt_own.shape[0]
    first = (s_me * parts + half) * chunk
    row = starts[0:1]
    for b in range(1, starts.shape[0]):
        row = jnp.where(batch == b, starts[b : b + 1], row)

    swap_x = send(x_own, xn, sems, 0, near)
    swap_small = send(small_s, small_n, sems, 1, near)
    cross_x = send(x_own, xf, sems, 2, across)
    cross_small = send(small_s, small_f, sems, 3, across)
    swap_far = send(xf, xfn, sems, 4, near)
    swap_small_far = send(small_f, small_fn, sems, 5, near)
    edge = send(tail_rows.at[0], edge_far, sems, 6, {"seq": lax.min(s_me + 1, n - 1)})

    @pl.when(u == 0)
    def _():
        small_s[...] = jnp.zeros_like(small_s)
        small_s[0:4, 0:part] = taps_x[...]
        tiles = part // LANES
        for k in range(tiles):
            cols = slice(k * LANES, (k + 1) * LANES)
            small_s[4:5, cols] = vecs[k : k + 1]
            small_s[5:6, cols] = vecs[tiles + k : tiles + k + 1]
        small_s[6:7, 0:LANES] = vecs[2 * tiles : 2 * tiles + 1]
        small_s[8 : 8 + nh] = dt_own[...].astype(f32)
        at = 2 * tiles + 2
        for k in range(features // LANES):
            gain[0:1, k * LANES : (k + 1) * LANES] = vecs[at + k : at + k + 1]
        at = at + features // LANES
        for k in range(2):
            bias_bc[0:1, k * LANES : (k + 1) * LANES] = vecs[at + k : at + k + 1]
        gain_out[...] = jnp.broadcast_to(gain[0:1], gain_out.shape)
        edge_far[...] = jnp.zeros_like(edge_far)
        meet(heads[1:], n)
        swap_small.start()
        swap_x.start()
        pl.when(s_me < n - 1)(edge.start)
        cross_small.start()
        cross_x.start()
        next_age[...] = spread_ages(row, first + chunk, 8)

    rows = pl.ds(pl.multiple_of(lax.rem(u, count) * GROUP, GROUP), GROUP)

    @pl.when(u < count)
    def _():
        for r in range(0, GROUP, ROWS):
            at = pl.ds(pl.multiple_of(u * GROUP + r, ROWS), ROWS)
            normed[at] = rms(hid[0, r : r + ROWS], gain[0:1])
        ci_bc[rows] = dot(normed[rows], bc[...]).astype(bf16)
        a = spread_ages(row, first + u * GROUP, GROUP)
        age[rows] = a
        ager[...] = a.astype(f32).T[0:8].astype(jnp.int32)

    @pl.when(u == count)
    def _():
        swap_small.wait()
        swap_x.wait()
        pl.when(s_me < n - 1)(edge.wait_send)
        pl.when(s_me > 0)(edge.wait_recv)
        local = half.astype(f32)
        near_rows = local * edge_near[0].astype(f32) + (1.0 - local) * edge_far[...].astype(f32)
        before[...] = rms(near_rows, gain[0:1])

    @pl.when(u == 2 * count - 1)
    def _():
        cross_small.wait()
        swap_small_far.start()
        cross_x.wait()
        swap_far.start()
        z_weights.begin()

    @pl.when(u == 2 * count)
    def _():
        states_a.begin()
        swap_small_far.wait()
        swap_far.wait()
        x_near[...] = xn[...]
        x_far[...] = xf[...]
        x_far_near[...] = xfn[...]

    pl.when(u == 2 * count + 1)(states_a.combine)

    @pl.when(u == 2 * count + 2)
    def _():
        z_weights.share()
        o_weights.begin()

    pl.when(u == 2 * count + 3)(states_a.scan)

    @pl.when(u == 3 * count)
    def _():
        states_b.begin()
        z_weights.back()
        for copy in cots:
            copy.start()

    @pl.when(u == 3 * count + 1)
    def _():
        states_b.combine()
        o_weights.share()

    pl.when(u == 3 * count + 2)(states_a.settle)
    pl.when(u == 3 * count + 4)(states_a.close)

    @pl.when(u == 5 * count - 3)
    def _():
        states_b.scan()
        o_weights.back()

    for which in range(2):
        lo = (which + 1) * count
        outs = (ci_a, co_a, val_a, pre_a, cum_a, lin_a, kb_a, ck_a, tot_a, kout_a, par_a, dtp_a)
        weights = (x_own, xn, small_s, small_n)
        maps_in, maps_out = (ci_bc.at[rows], bc, taps_bc, bias_bc), (co_bc, bmat.at[rows], cmat.at[rows])
        if which:
            outs = (ci_b, co_b, val_b, pre_b, cum_b, lin_b, kb_b, ck_b, tot_b, kout_b, par_b, dtp_b)
            weights = (xf, xfn, small_f, small_fn)
            maps_in, maps_out = (bmat.at[rows],), ()
        outs = outs[:2] + tuple(x.at[rows] for x in outs[2:5]) + outs[5:]

        @pl.when((u >= lo) & (u < lo + count))
        def _():
            front_step(
                which == 0, u - lo, normed.at[rows], before, *weights, age.at[rows], tril, ex,
                maps_in, *outs, maps_out, *front,
            )

    for which in range(2):
        lo = (which + 3) * count
        val, pre, cum, par, to = ((val_a, pre_a, cum_a, par_a, part_a), (val_b, pre_b, cum_b, par_b, part_b))[which]

        @pl.when((u >= lo) & (u < lo + count))
        def _():
            intra_unit(
                val.at[rows], bmat.at[rows], cmat.at[rows], age.at[rows], pre.at[rows], cum.at[rows], par, to
            )

    @pl.when(u == 5 * count - 1)
    def _():
        z_weights.finish()
        o_weights.finish()
        states_b.settle()
        for copy in cots:
            copy.wait()
        states_b.close()


def arriving_half(own, other, half=None):
    if half is None:
        return jnp.concatenate([own[...], other[...]], axis=1)
    part = own.shape[1] // 2
    cols = slice(half * part, (half + 1) * part)
    return jnp.concatenate([own[:, cols].astype(f32), other[:, cols].astype(f32)], axis=1)


def mid_kernel(
    meta, hid, normed, z0, z1, z2, z3, o0, o1, o2, o3, cot0, cot1, cot2, cot3, cmat, age, ex, red, par_a, par_b,
    part_a, part_b, val_a, val_b, cum_a, cum_b, lin_a, lin_b, kb_a, kb_b, ck_a, ck_b, arr_a, arr_other_a, arr_b, arr_other_b,
    pieces, hidc, nout, cotx, dssd, dgate, dcin, dkk_a, dkk_b,
    lout_a, lout_b, ka_a, ka_b, tot_a, tot_b, kout_a, kout_b, ggain, gskip,
    gate, dno, read, kx, ssd_s, sig_s, khi, klo, rhi, rlo, run_a, run_b, kept_a, kept_b, shuffle,
):
    i = pl.program_id(0)
    inner = nout.shape[1]
    width = inner // 2
    tiles = inner // LANES
    heads = width // HEAD_DIM
    quarter = inner // 4

    @pl.when(i == 0)
    def _():
        for ref in (run_a, run_b, ggain, gskip):
            ref[...] = jnp.zeros_like(ref)
        for ref in (kept_a, kept_b):
            ref[...] = jnp.ones_like(ref)

    me = meta[0]
    hidc[...] = hid[0]
    for k, cot in enumerate((cot0.at[0], cot1, cot2, cot3)):
        shuffle[me ^ k] = cot[...]
    cotan = jnp.concatenate([shuffle[0], shuffle[1], shuffle[2], shuffle[3]], axis=0).T
    cotx[...] = cotan
    states = []
    for half, (lin, kb, cum, arr, arr_other) in enumerate(
        ((lin_a, kb_a, cum_a, arr_a, arr_other_a), (lin_b, kb_b, cum_b, arr_b, arr_other_b))
    ):
        cols = slice(half * width, (half + 1) * width)
        hi, lo = split2(lin[0] + kb[0, 0:1] * arriving_half(arr, arr_other))
        states.append((hi, lo))
        read[:, cols] = dot(cmat[...], hi) + dot(cmat[...], lo)
        since = lax.broadcasted_iota(jnp.int32, age.shape, 0)
        kappa = jnp.where(age[...] > since, jnp.exp(cum[...]), 0.0)
        kx[:, cols] = expand(lanes_below(kappa, heads), ex[...])
    for k, (z, o) in enumerate(((z0, o0), (z1, o1), (z2, o2), (z3, o3))):
        cols = slice(k * quarter, (k + 1) * quarter)
        gate[:, cols] = dot(normed[...], z[...])
        dno[:, cols] = dot(cotan, o[...], 1, 1)

    gains = [
        (par_a if j < tiles // 2 else par_b)[5:6, (j * LANES) % width : (j * LANES) % width + LANES]
        for j in range(tiles)
    ]

    def rows_body(step, _):
        rows = pl.ds(pl.multiple_of(step * ROWS, ROWS), ROWS)
        squares = jnp.zeros((ROWS, LANES), f32)
        inners = jnp.zeros((ROWS, LANES), f32)
        for j in range(tiles):
            cols = slice(j * LANES, (j + 1) * LANES)
            part = part_a if j < tiles // 2 else part_b
            pcols = slice(cols.start % width, cols.start % width + LANES)
            ssd = part[rows, pcols] + kx[rows, cols] * read[rows, cols]
            g = gate[rows, cols]
            sig = sigmoid(g)
            gated = ssd * (g * sig)
            squares += gated * gated
            inners += gated * (dno[rows, cols] * gains[j])
            ssd_s[rows, cols] = ssd
            sig_s[rows, cols] = sig
        rg = lax.rsqrt(jnp.sum(squares, axis=1, keepdims=True) / inner + EPS)
        stat = rg * rg * (jnp.sum(inners, axis=1, keepdims=True) / inner)
        rg = jnp.broadcast_to(rg, (ROWS, LANES))
        stat = jnp.broadcast_to(stat, (ROWS, LANES))
        for j in range(tiles):
            cols = slice(j * LANES, (j + 1) * LANES)
            val = val_a if j < tiles // 2 else val_b
            pcols = slice(cols.start % width, cols.start % width + LANES)
            ssd, sig, g, d = ssd_s[rows, cols], sig_s[rows, cols], gate[rows, cols], dno[rows, cols]
            act = g * sig
            gated = ssd * act
            yhat = gated * rg
            nout[rows, cols] = (yhat * gains[j]).astype(bf16)
            ggain[:, cols] += fold8(d * yhat)
            dgated = rg * (d * gains[j] - gated * stat)
            low = (dgated * act).astype(bf16)
            dssd[rows, cols] = low
            dgate[rows, cols] = (dgated * ssd * (sig * (1.0 + g * (1.0 - sig)))).astype(bf16)
            dy = low.astype(f32)
            gskip[:, cols] += fold8(dy * val[rows, pcols].astype(f32))
            kd = kx[rows, cols] * dy
            khi[rows, cols], klo[rows, cols] = split2(kd)
            rhi[rows, cols], rlo[rows, cols] = split2(kd * read[rows, cols])
        return 0

    lax.fori_loop(0, GROUP // ROWS, rows_body, 0)
    out = hid[0].astype(f32)
    for k, o in enumerate((o0, o1, o2, o3)):
        out = out + dot(nout[:, k * quarter : (k + 1) * quarter], o[...])
    out = out.astype(bf16).T
    piece = out.shape[0] // 4
    for k in range(4):
        pieces[k] = out[k * piece : (k + 1) * piece]
    dc = None
    age_end = age[GROUP - 1 : GROUP]
    for half, (dkk, ck, cum, lout, ka, tot, kout, running, kept) in enumerate(
        (
            (dkk_a, ck_a, cum_a, lout_a, ka_a, tot_a, kout_a, run_a, kept_a),
            (dkk_b, ck_b, cum_b, lout_b, ka_b, tot_b, kout_b, run_b, kept_b),
        )
    ):
        cols = slice(half * width, (half + 1) * width)
        hi, lo = states[half]
        dkk[...] = dot(rhi[:, cols], red[...]) + dot(rlo[:, cols], red[...])
        term = dot(khi[:, cols], hi, 1, 1) + dot(khi[:, cols], lo, 1, 1) + dot(klo[:, cols], hi, 1, 1)
        dc = term if dc is None else dc + term
        own = dot(cmat[...], khi[:, cols], 0, 0) + dot(cmat[...], klo[:, cols], 0, 0)
        lout[0] = running[...]
        ka[0] = expand(lanes_below(kept[...], heads), ex[...])
        running[...] = ck[0, 0:1] * running[...] + own
        keep = jnp.where(age_end >= GROUP, jnp.exp(cum[GROUP - 1 : GROUP]), 0.0)
        kept[...] = lanes_below(jnp.broadcast_to(keep, (8, LANES)), heads) * kept[...]
        tot[...] = running[...]
        kout[...] = kept[...]
    dcin[...] = dc


def pairs_unit(val, dssd, bmat, cmat, ager, pre, cum, dvi, dbi, dci, rflow, cflow, rft):
    s = lax.broadcasted_iota(jnp.int32, (HALF, HALF), 0)
    t = lax.broadcasted_iota(jnp.int32, (HALF, HALF), 1)
    scores = dot(bmat[...], cmat[...], 1, 1)
    a0, a1 = ager[0:1, :HALF], ager[0:1, HALF:]
    gap = t - s
    m00 = (gap >= 0) & (gap <= a0)
    m11 = (gap >= 0) & (gap <= a1)
    m01 = gap + HALF <= a1
    s00 = jnp.where(m00, scores[:HALF, :HALF], 0.0)
    s11 = jnp.where(m11, scores[HALF:, HALF:], 0.0)
    s01 = jnp.where(m01, scores[:HALF, HALF:], 0.0)
    c2 = cum[...] * LOG2E
    cr = c2 - jnp.log2(softplus(pre[...]))
    c2t = c2.T
    lane = lax.broadcasted_iota(jnp.int32, (HALF, LANES), 1)
    zero = jnp.zeros((HALF, HALF), f32)
    d00, d01, d11 = zero, zero, zero
    cf0, cf1 = zero, zero
    rft[...] = jnp.zeros_like(rft)
    for j in range(val.shape[1] // LANES):
        cols = slice(j * LANES, (j + 1) * LANES)
        v = val[:, cols]
        dy = dssd[:, cols]
        vm = pair_masks(v, v.shape)
        dm = pair_masks(dy, dy.shape)
        tops, bottoms = [], []
        for which in range(2):
            h = 2 * j + which
            col0 = jnp.broadcast_to(cr[:HALF, h : h + 1], (HALF, HALF))
            col1 = jnp.broadcast_to(cr[HALF:, h : h + 1], (HALF, HALF))
            r0 = c2t[h : h + 1, :HALF]
            r1 = c2t[h : h + 1, HALF:]
            e00 = jnp.exp2(jnp.minimum(r0 - col0, 60.0))
            e01 = jnp.exp2(r1 - col0)
            e11 = jnp.exp2(jnp.minimum(r1 - col1, 60.0))
            tops.append((s00 * e00).astype(bf16))
            tops.append((s01 * e01).astype(bf16))
            bottoms.append((s11 * e11).astype(bf16))
            w0 = dot(vm[which][:HALF], dy, 1, 1)
            w1 = dot(vm[which][HALF:], dy[HALF:], 1, 1)
            de00 = w0[:, :HALF] * e00
            de01 = w0[:, HALF:] * e01
            de11 = w1 * e11
            d00 += de00
            d01 += de01
            d11 += de11
            f00 = de00 * s00
            f01 = de01 * s01
            f11 = de11 * s11
            rft[h : h + 1, :HALF] = jnp.sum(f00, axis=0, keepdims=True)
            rft[h : h + 1, HALF:] = jnp.sum(f01 + f11, axis=0, keepdims=True)
            cf0 = jnp.where(lane == h, jnp.sum(f00 + f01, axis=1, keepdims=True), cf0)
            cf1 = jnp.where(lane == h, jnp.sum(f11, axis=1, keepdims=True), cf1)
        dvi[:HALF, cols] = dot(jnp.concatenate(tops, axis=1), jnp.concatenate([dm[0], dm[1]], axis=0))
        dvi[HALF:, cols] = dot(
            jnp.concatenate(bottoms, axis=1), jnp.concatenate([dm[0][HALF:], dm[1][HALF:]], axis=0)
        )
    cflow[:HALF] = cf0
    cflow[HALF:] = cf1
    rflow[...] = rft[...].T
    d00 = split2(jnp.where(m00, d00, 0.0))
    d01 = split2(jnp.where(m01, d01, 0.0))
    d11 = split2(jnp.where(m11, d11, 0.0))
    b0, b1, c0, c1 = bmat[:HALF], bmat[HALF:], cmat[:HALF], cmat[HALF:]
    dbi[:HALF] = dot(d00[0], c0) + dot(d00[1], c0) + dot(d01[0], c1) + dot(d01[1], c1)
    dbi[HALF:] = dot(d11[0], c1) + dot(d11[1], c1)
    dci[:HALF] = dot(d00[0], b0, 0, 0) + dot(d00[1], b0, 0, 0)
    dci[HALF:] = (
        dot(d01[0], b0, 0, 0) + dot(d01[1], b0, 0, 0) + dot(d11[0], b1, 0, 0) + dot(d11[1], b1, 0, 0)
    )


def outer_kernel(
    n, parts, count, tiles, normed, cotx, dgate, nout,
    val_a, val_b, dssd, bmat, cmat, ager, pre_a, pre_b, cum_a, cum_b, tot_a, tot_b, k_a, k_b, ex,
    dvi_a, dbi_a, dci_a, rflow_a, cflow_a, dvi_b, dbi_b, dci_b, rflow_b, cflow_b, own, other, share, zo,
    rft, keep, send, got, far_out, far_in, sems, *scratch
):
    u = pl.program_id(0)
    v = u - 4 * tiles
    states = Exchange(True, n, parts, (tot_a, tot_b), (k_a, k_b), ex, own, other, scratch[5:])
    sums = PairScatter(n, scratch[:5])
    share_rows = zo.shape[0] // n
    across = lax.rem(lax.axis_index("head") + 2, 4)

    def trade(src, dst, sem, head):
        return pltpu.make_async_remote_copy(
            src_ref=src,
            dst_ref=dst,
            send_sem=sems.at[0, sem],
            recv_sem=sems.at[1, sem],
            device_id={"head": head},
            device_id_type=MESH,
        )

    def swap(half, m):
        return trade(send.at[half, m], got.at[half, m], 2 * half + m, states.partner)

    def cross(m):
        return trade(far_out.at[m], far_in.at[m], 4 + m, across)

    def cross_after(m):
        swap(0, m).wait()
        far_out[m] = (keep[0, m] + got[0, m].astype(f32)).astype(bf16)
        cross(m).start()

    @pl.when(u == 0)
    def _():
        meet([states.partner, across], n)
        states.begin()


    @pl.when(u == tiles)
    def _():
        swap(0, 0).start()

    @pl.when(u == 2 * tiles)
    def _():
        swap(0, 1).start()
        cross_after(0)

    @pl.when(u == 3 * tiles)
    def _():
        swap(1, 0).start()
        cross_after(1)

    @pl.when(v == 0)
    def _():
        swap(1, 1).start()
        states.scan()

    part = keep.shape[3]
    rows = pl.ds(pl.multiple_of(lax.rem(u, tiles) * GROUP, GROUP), GROUP)
    for m, (a, b) in enumerate(((normed, dgate), (cotx, nout))):

        @pl.when((v < 0) & (lax.rem(u // tiles, 2) == m))
        def _():
            res = dot(a[...], b[...], 0, 0)
            half = u // (2 * tiles)
            keep[half, m, rows] = res[:, :part]
            send[half, m, rows] = res[:, part:].astype(bf16)

    @pl.when((v >= 0) & (v < count))
    def _():
        pairs_unit(val_a, dssd, bmat, cmat, ager, pre_a, cum_a, dvi_a, dbi_a, dci_a, rflow_a, cflow_a, rft)

    @pl.when(v >= count)
    def _():
        pairs_unit(val_b, dssd, bmat, cmat, ager, pre_b, cum_b, dvi_b, dbi_b, dci_b, rflow_b, cflow_b, rft)

    pl.when(u == 1)(states.combine)

    pl.when(v == 2 * count - 3)(sums.middle)

    @pl.when(v == count - 2)
    def _():
        swap(1, 0).wait()
        cross(0).wait()

        def total(s):
            at = slice(s * share_rows, (s + 1) * share_rows)
            return keep[1, 0, at] + got[1, 0, at].astype(f32) + far_in[0, at].astype(f32)

        sums.start(total)

    @pl.when(v == 2 * count - 1)
    def _():
        states.settle()
        states.close()
        swap(1, 1).wait()
        cross(1).wait()
        zo[...] = (keep[1, 1] + got[1, 1].astype(f32) + far_in[1].astype(f32)).astype(bf16)
        share[...] = sums.finish()


def slope(x):
    sig = sigmoid(x)
    return sig * (1.0 + x * (1.0 - sig))


def conv_back(i, dco, agex, age, ci, taps, dci, tail, head, gw):
    width = ci.shape[1]
    for r in range(0, GROUP, ROWS):
        ages = [agex[r + m : r + m + ROWS] for m in range(4)]
        for j in range(width // LANES):
            cols = slice(j * LANES, (j + 1) * LANES)
            c = ci[r : r + ROWS, cols].astype(f32)
            acc = None
            for m in range(4):
                x = dco[r + m : r + m + ROWS, cols]
                if m:
                    x = jnp.where(ages[m] >= m, x, 0.0)
                term = x * taps[3 - m : 4 - m, cols]
                acc = term if acc is None else acc + term
                gw[8 * (3 - m) : 8 * (3 - m) + 8, cols] += fold8(x * c)
            dci[r : r + ROWS, cols] = acc.astype(bf16)
            if r == GROUP - ROWS:

                @pl.when(i == 0)
                def _():
                    tail[:, cols] = acc[ROWS - 8 :]

    head[...] = dco[0:8]


def start_next(i, dco, agex, gw, gb):
    @pl.when(i == 0)
    def _():
        dco[GROUP : GROUP + 8] = jnp.zeros((8, dco.shape[1]), f32)
        agex[GROUP : GROUP + 8] = jnp.zeros((8, LANES), jnp.int32)
        gw[...] = jnp.zeros_like(gw)
        gb[...] = jnp.zeros_like(gb)

    @pl.when(i > 0)
    def _():
        dco[GROUP : GROUP + 8] = dco[0:8]
        agex[GROUP : GROUP + 8] = agex[0:8]


def back_step(
    half, i, val, dssd, dvi, bmat, co, ci, age, pre, cum, lout, ka, leav, leav_other, lin, kb, arr, arr_other,
    rflow, cflow, dkk, par, tril, ex, red,
    dci, tail, head, draw, gw, gb, galog, gdtb,
    dco, agex, back, omx, vhi, vlo,
):
    width = val.shape[1]
    heads = width // HEAD_DIM
    start_next(i, dco, agex, gw, gb)

    @pl.when(i == 0)
    def _():
        galog[...] = jnp.zeros_like(galog)
        gdtb[...] = jnp.zeros_like(gdtb)

    agex[0:GROUP] = age[...]
    ds = lout[0] + ka[0, 0:1] * arriving_half(leav, leav_other, half)
    dhi, dlo = split2(ds)
    back[...] = dot(bmat[...], dhi) + dot(bmat[...], dlo)
    p = pre[...]
    delta = softplus(p)
    c = cum[...]
    end = c[GROUP - 1 : GROUP]
    age_end = age[GROUP - 1 : GROUP]
    row = lax.broadcasted_iota(jnp.int32, c.shape, 0)
    tail_keep = jnp.where(GROUP - 1 - row <= age_end, jnp.exp(end - c), 0.0)
    omega = tail_keep * delta
    omx[...] = expand(lanes_below(omega, heads), ex[...])
    for r in range(0, GROUP, ROWS):
        rows = slice(r, r + ROWS)
        for j in range(width // LANES):
            cols = slice(j * LANES, (j + 1) * LANES)
            v = val[rows, cols].astype(f32)
            b = back[rows, cols]
            o = omx[rows, cols]
            dval = par[6:7, cols] * dssd[rows, cols].astype(f32) + dvi[rows, cols] + o * b
            vhi[rows, cols], vlo[rows, cols] = split2(v * b)
            d = dval * slope(co[rows, cols])
            dco[rows, cols] = d
            gb[:, cols] += fold8(d)
    domega = dot(vhi[...], red[...]) + dot(vlo[...], red[...])
    flow = domega * omega
    sin = lin[0] + kb[0, 0:1] * arriving_half(arr, arr_other)
    carry = jnp.broadcast_to(jnp.sum(ds * sin, axis=0, keepdims=True), (8, width))
    carry = dot(carry, red[...].astype(f32), precision=HIGHEST)[0:1]
    keep = jnp.where(age_end >= GROUP, jnp.exp(end), 0.0)
    dcum = rflow[...] - cflow[...] + dkk[...] - flow
    ending = jnp.sum(flow, axis=0, keepdims=True) + carry * keep
    dcum = dcum + jnp.where(row == GROUP - 1, ending, 0.0)
    dlog = dot(tril[...], dcum, 0, 0, precision=HIGHEST)
    sig = sigmoid(p)
    ratio = jnp.where(delta > 1e-30, sig / delta, 1.0)
    rate = par[7:8, 0:LANES]
    drf = cflow[...] * ratio + (domega * tail_keep + dlog * rate) * sig
    drf = lanes_below(drf, heads)
    draw[...] = drf.astype(bf16)
    gdtb[...] += fold8(drf)
    galog[...] += fold8(dlog * delta * rate)
    conv_back(i, dco, agex, age, ci, par, dci, tail, head, gw)


def maps_step(
    i, dbi_a, dbi_b, dci_a, dci_b, dcin, co, ci, age, taps,
    val_a, val_b, pre_a, pre_b, cum_a, cum_b, lout_a, lout_b, ka_a, ka_b, leav, leav_other, ex,
    dci, tail, head, gw, gb, dco, agex, dbin,
):
    start_next(i, dco, agex, gw, gb)
    agex[0:GROUP] = age[...]
    age_end = age[GROUP - 1 : GROUP]
    width = val_a.shape[1]
    row = lax.broadcasted_iota(jnp.int32, (GROUP, LANES), 0)
    total = dbi_a[...] + dbi_b[...]
    for half, (val, pre, cum, lout, ka) in enumerate(
        ((val_a, pre_a, cum_a, lout_a, ka_a), (val_b, pre_b, cum_b, lout_b, ka_b))
    ):
        dhi, dlo = split2(lout[0] + ka[0, 0:1] * arriving_half(leav, leav_other, half))
        c = cum[...]
        tail_keep = jnp.where(GROUP - 1 - row <= age_end, jnp.exp(c[GROUP - 1 : GROUP] - c), 0.0)
        omx = expand(lanes_below(tail_keep * softplus(pre[...]), width // HEAD_DIM), ex[...])
        ohi, olo = split2(omx * val[...].astype(f32))
        total = total + dot(ohi, dhi, 1, 1) + dot(ohi, dlo, 1, 1) + dot(olo, dhi, 1, 1)
    dbin[...] = total
    for r in range(0, GROUP, ROWS):
        rows = slice(r, r + ROWS)
        dc = dci_a[rows] + dci_b[rows] + dcin[rows]
        for j, d in enumerate((dbin[rows], dc)):
            cols = slice(j * LANES, (j + 1) * LANES)
            d = d * slope(co[rows, cols])
            dco[rows, cols] = d
            gb[:, cols] += fold8(d)
    conv_back(i, dco, agex, age, ci, taps, dci, tail, head, gw)


def mended(x, last, scr):
    scr[...] = x[...]

    @pl.when(pl.program_id(0) == pl.num_programs(0) - 1)
    def _():
        scr[GROUP - 16 :] = last[...]

    return scr


def padded_rows(x, rows):
    if x.shape[0] == rows:
        return x
    return jnp.concatenate([x, jnp.zeros((rows - x.shape[0], x.shape[1]), x.dtype)], axis=0)


def up16(rows):
    return (rows + 15) // 16 * 16


class Scatter:
    def __init__(self, n, scratch):
        self.n, self.me = n, lax.axis_index("seq")
        self.out, self.got, self.sems = scratch

    @staticmethod
    def scratch(n, rows, cols):
        pad = up16(rows)
        return [
            pltpu.VMEM((n, pad, cols), bf16),
            pltpu.VMEM((n, pad, cols), bf16),
            pltpu.SemaphoreType.DMA((2, n)),
        ]

    def move(self, d):
        to = lax.rem(self.me + d, self.n)
        return pltpu.make_async_remote_copy(
            src_ref=self.out.at[to],
            dst_ref=self.got.at[self.me],
            send_sem=self.sems.at[0, d],
            recv_sem=self.sems.at[1, d],
            device_id={"seq": to},
            device_id_type=MESH,
        )

    def start(self, share):
        for s in range(self.n):
            self.out[s] = padded_rows(share(s), self.out.shape[1]).astype(bf16)
        for d in range(1, self.n):
            self.move(d).start()
        self.got[self.me] = self.out[self.me]

    def finish(self):
        return self.finish_f32().astype(bf16)

    def finish_f32(self):
        for d in range(1, self.n):
            self.move(d).wait()
        total = self.got[0].astype(f32)
        for s in range(1, self.n):
            total = total + self.got[s].astype(f32)
        return total


class Gather:
    def __init__(self, n, scratch):
        self.n, self.me = n, lax.axis_index("seq")
        self.mine, self.all, self.sems = scratch

    @staticmethod
    def scratch(n, rows, cols):
        pad = up16(rows)
        return [
            pltpu.VMEM((pad, cols), bf16),
            pltpu.VMEM((n, pad, cols), bf16),
            pltpu.SemaphoreType.DMA((2, n)),
        ]

    def move(self, d):
        return pltpu.make_async_remote_copy(
            src_ref=self.mine,
            dst_ref=self.all.at[self.me],
            send_sem=self.sems.at[0, d],
            recv_sem=self.sems.at[1, d],
            device_id={"seq": lax.rem(self.me + d, self.n)},
            device_id_type=MESH,
        )

    def start(self, share):
        self.mine[...] = share
        for d in range(1, self.n):
            self.move(d).start()
        self.all[self.me] = share

    def finish(self):
        for d in range(1, self.n):
            self.move(d).wait()

    def rows(self, s, count):
        return self.all[s].astype(f32)[:count]


class PairScatter:
    def __init__(self, n, scratch):
        me = lax.axis_index("seq")
        self.n, self.m, self.odd, self.at = n, n // 2, lax.rem(me, 2), me // 2
        self.partner = me + 1 - 2 * self.odd
        self.out, self.near, self.part, self.got, self.sems = scratch

    @staticmethod
    def scratch(n, rows, cols):
        pad, m = up16(rows), n // 2
        return [
            pltpu.VMEM((2, m, pad, cols), bf16),
            pltpu.VMEM((m, pad, cols), bf16),
            pltpu.VMEM((m, pad, cols), bf16),
            pltpu.VMEM((m, pad, cols), bf16),
            pltpu.SemaphoreType.DMA((2, m)),
        ]

    def move(self, d):
        if d == 0:
            src, dst, to = self.out.at[1 - self.odd], self.near, self.partner
        else:
            to = lax.rem(self.at + d, self.m)
            src, dst, to = self.part.at[to], self.got.at[self.at], 2 * to + self.odd
        return pltpu.make_async_remote_copy(
            src_ref=src,
            dst_ref=dst,
            send_sem=self.sems.at[0, d],
            recv_sem=self.sems.at[1, d],
            device_id={"seq": to},
            device_id_type=MESH,
        )

    def start(self, share):
        for s in range(self.n):
            self.out[s % 2, s // 2] = padded_rows(share(s), self.near.shape[1]).astype(bf16)
        self.move(0).start()

    def middle(self):
        self.move(0).wait()
        for k in range(self.m):
            self.part[k] = (self.out[self.odd, k].astype(f32) + self.near[k].astype(f32)).astype(bf16)
        for d in range(1, self.m):
            self.move(d).start()
        self.got[self.at] = self.part[self.at]

    def finish(self):
        for d in range(1, self.m):
            self.move(d).wait()
        total = self.got[0].astype(f32)
        for k in range(1, self.m):
            total = total + self.got[k].astype(f32)
        return total.astype(bf16)


class PairGather:
    def __init__(self, n, scratch):
        me = lax.axis_index("seq")
        self.n, self.m, self.odd, self.at = n, n // 2, lax.rem(me, 2), me // 2
        self.partner = me + 1 - 2 * self.odd
        self.mine, self.all, self.sems = scratch

    @staticmethod
    def scratch(n, rows, cols):
        pad, m = up16(rows), n // 2
        return [
            pltpu.VMEM((pad, cols), bf16),
            pltpu.VMEM((2, m, pad, cols), bf16),
            pltpu.SemaphoreType.DMA((2, m)),
        ]

    def move(self, d):
        if d == 0:
            src, dst, to = self.all.at[self.odd], self.all.at[self.odd], self.partner
        else:
            src, dst = self.mine, self.all.at[self.odd, self.at]
            to = 2 * lax.rem(self.at + d, self.m) + self.odd
        return pltpu.make_async_remote_copy(
            src_ref=src,
            dst_ref=dst,
            send_sem=self.sems.at[0, d],
            recv_sem=self.sems.at[1, d],
            device_id={"seq": to},
            device_id_type=MESH,
        )

    def start(self, share):
        self.mine[...] = share
        for d in range(1, self.m):
            self.move(d).start()
        self.all[self.odd, self.at] = share

    def middle(self):
        for d in range(1, self.m):
            self.move(d).wait()
        self.move(0).start()

    def finish(self):
        self.move(0).wait()

    def rows(self, s, count):
        return self.all[s % 2, s // 2].astype(f32)[:count]


def mend(got, tail, ci, next_age, taps, dx, scr, last, flip):
    g = got[...]
    if flip:
        part = g.shape[1] // 2
        g = jnp.concatenate([g[:, part:], g[:, :part]], axis=1)
    rows = scr.shape[0]
    if dx is not None:
        scr[...] = dx[...]
    ending = ci[...].astype(f32)[8:16]
    row = lax.broadcasted_iota(jnp.int32, (8, LANES), 0)
    fixed, sums = [], []
    for j in range(g.shape[1] // LANES):
        cols = slice(j * LANES, (j + 1) * LANES)
        acc = tail[:, cols]
        parts = [jnp.zeros((1, LANES), f32)] * 4
        for m in range(1, 4):
            use = (row >= 8 - m) & (pltpu.roll(next_age[...], 8 - m, 0) >= m)
            x = jnp.where(use, pltpu.roll(g[:, cols], 8 - m, 0), 0.0)
            acc = acc + x * taps[3 - m : 4 - m, cols]
            parts[3 - m] = jnp.sum(x * ending[:, cols], axis=0, keepdims=True)
        fixed.append(acc)
        sums.append(jnp.concatenate(parts, axis=0))
    fixed = jnp.concatenate(fixed, axis=1)
    before = scr[rows - 16 :].astype(f32)[0:8]
    scr[rows - 16 :] = jnp.concatenate([before, fixed], axis=0).astype(bf16)
    if last is not None:
        last[...] = scr[rows - 16 :]
    return jnp.concatenate(sums, axis=1)


def small_sums(at, fix, gw, gb, galog, gdtb, gskip, ggain, red, small_keep, small_send):
    part = red.shape[0] // 2
    heads = part // HEAD_DIM
    width = 2 * part
    for to in (small_keep, small_send):
        to[...] = jnp.zeros_like(to)
    taps = [jnp.sum(gw[8 * k : 8 * k + 8], axis=0, keepdims=True) for k in range(4)]
    taps = jnp.concatenate(taps, axis=0) + fix
    bias = jnp.sum(gb[...], axis=0, keepdims=True)
    cols = slice(at * width, (at + 1) * width)
    gain = jnp.sum(ggain[:, cols], axis=0, keepdims=True)
    skip = jnp.broadcast_to(jnp.sum(gskip[:, cols], axis=0, keepdims=True), (8, width))
    skip = dot(skip, red[...].astype(f32), precision=HIGHEST)
    step = jnp.broadcast_to(jnp.sum(gdtb[...], axis=0, keepdims=True), (8, LANES))
    log = jnp.broadcast_to(jnp.sum(galog[...], axis=0, keepdims=True), (8, LANES))
    for k, to in enumerate((small_keep, small_send)):
        mine = slice(k * part, (k + 1) * part)
        to[0:4, 0:part] = taps[:, mine]
        to[4:5, 0:part] = bias[:, mine]
        to[5:6, 0:part] = gain[:, mine]
        row = jnp.zeros((8, LANES), f32)
        for place, x in enumerate((step, log, skip)):
            x = lanes_below(pltpu.roll(x, (LANES - k * heads) % LANES, 1), heads)
            row = row + pltpu.roll(x, place * heads, 1)
        to[6:7, 0:LANES] = row[0:1]


def half_tile(tile, normed, dx, draw, keep, send, small_keep, small_send):
    part = keep.shape[1]
    heads = part // HEAD_DIM
    res = dot(normed[...], dx[...], 0, 0)
    keep[...] = res[:, :part]
    send[...] = res[:, part:].astype(bf16)
    dt = dot(draw[...], normed[...], 0, 0)
    cols = pl.ds(pl.multiple_of(tile * GROUP, GROUP), GROUP)
    small_keep[8:16, cols] = dt[0:8]
    small_send[8:16, cols] = pltpu.roll(dt, LANES - heads, 0)[0:8]


def turn_kernel(n, parts, count, *refs):
    maps_in, refs = refs[:22], refs[22:]
    back_in, refs = refs[:24], refs[24:]
    (own, share, pieces), refs = refs[:3], refs[3:]
    maps_out, refs = refs[:5], refs[5:]
    back_out, refs = refs[:8], refs[8:]
    (share_out, gathered, placed), refs = refs[:3], refs[3:]
    maps_scr, refs = refs[:3], refs[3:]
    back_scr, refs = refs[:6], refs[6:]
    (piece_sems,), refs = refs[:1], refs[1:]
    u = pl.program_id(0)
    sums, shares = PairScatter(n, refs[:5]), PairGather(n, refs[5:])
    rows = own.shape[0] // n
    me = lax.axis_index("seq")
    head = lax.axis_index("head")
    near = head + 1 - 2 * lax.rem(head, 2)
    heads = [head, near, lax.rem(head + 2, 4), lax.rem(near + 2, 4)]
    chunk = pieces.shape[2]

    def piece_copy(k):
        cols = pl.ds(pl.multiple_of(lax.rem(head, parts) * chunk, chunk), chunk)
        src, dst = pieces.at[heads[k]], placed.at[head // parts, :, cols]
        if k == 0:
            return pltpu.make_async_copy(src, dst, piece_sems.at[0, 0])
        return pltpu.make_async_remote_copy(
            src_ref=src,
            dst_ref=dst,
            send_sem=piece_sems.at[0, k],
            recv_sem=piece_sems.at[1, k],
            device_id={"head": heads[k]},
            device_id_type=MESH,
        )

    @pl.when(u == 0)
    def _():
        barrier = pltpu.get_barrier_semaphore()
        for k in range(1, 4):
            pl.semaphore_signal(barrier, inc=1, device_id={"head": heads[k]}, device_id_type=MESH)
        for d in range(1, n):
            pl.semaphore_signal(barrier, inc=1, device_id={"seq": lax.rem(me + d, n)}, device_id_type=MESH)
        pl.semaphore_wait(barrier, n + 2)
        shares.start(share[...])
        sums.start(lambda s: own[s * rows : (s + 1) * rows].astype(f32))
        for k in (2, 3, 1, 0):
            piece_copy(k).start()

    @pl.when(u < count)
    def _():
        maps_step(u, *maps_in, *maps_out, *maps_scr)

    @pl.when(u >= count)
    def _():
        back_step(1, u - count, *back_in, *back_out, *back_scr)

    @pl.when(u == count - 1)
    def _():
        sums.middle()
        shares.middle()

    @pl.when(u == 2 * count - 1)
    def _():
        share_out[...] = sums.finish()
        shares.finish()
        for s in range(n):
            gathered[s * rows : (s + 1) * rows] = shares.rows(s, rows)
        for k in range(4):
            piece_copy(k).wait()


def late_kernel(n, parts, count, tiles, *refs):
    back_in, refs = refs[:24], refs[24:]
    (
        normed, dx_b, tail_b, head_b, ci_b, par_b, draw_b, gw_b, gb_b, galog_b, gdtb_b,
        dbc, tail_bc, head_bc, ci_bc, taps_bc, gw_bc, gb_bc, ci_a, next_age, gskip, ggain_out, share,
    ), refs = refs[:23], refs[23:]
    (hid, cotx, gain, dgate, z0, z1, z2, z3, bcw, x0, x1, x2, x3, dt_a, dt_b), refs = refs[:15], refs[15:]
    (grad_in, gx, gbc, small, grad_out), refs = refs[:5], refs[5:]
    back_scr, refs = refs[:6], refs[6:]
    (
        dx_a, draw_a, keep_a, send_a, small_a, small_send_a, got_a, small_got_a, last,
        tail_a, head_a, gw_a, gb_a, galog_a, gdtb_a, scr_b, scr_bc, keep_b, send_b, got_b, far_out,
        small_b, small_send_b, small_got, small_out, small_in, far_in, edge_b, edge_bc, edge_a,
        g_bc, bc_out, bc_got, bc_far_out, bc_far, bc_own, small_bc, com_got, bc_heads,
        acc_s, low, shuffle, landed, ggain, gi_got, gi_sum, edge_sems, sems, piece_sems,
    ), refs = refs[:49], refs[49:]
    u = pl.program_id(0)
    par_a, red = back_in[20], back_in[23]
    s_me = lax.axis_index("seq")
    heads = head_peers()
    h_me, near, across = heads[:3]
    half = lax.rem(h_me, parts)
    to_seq = s_me - 1 + half
    has_before = to_seq >= 0
    has_after = s_me + half < n
    chunk = count * GROUP
    part = keep_a.shape[1]
    features = gain.shape[1]
    lane_tiles = features // LANES
    first_bc, first_b, first_back, first_a = 1, tiles + 1, 2 * tiles + 1, 2 * tiles + count
    first_out = first_a + tiles
    pack_rows = -(-24 // n)
    pack = up16(4 * pack_rows + 4)
    bc_rows = features // 4
    share_rows = bc_rows // n
    gathered, gx_sum, gx_all = PairGather(n, refs[:3]), Scatter(n, refs[3:6]), Gather(n, refs[6:9])
    bc_sum, bc_all = Scatter(n, refs[9:12]), Gather(n, refs[12:15])

    def trade(src, dst, sem, head):
        return send(src, dst, sems, sem, {"head": head})

    def edge(k):
        src, dst = ((head_b, edge_b), (head_bc, edge_bc), (head_a, edge_a))[k]
        return send(src, dst, edge_sems, k, {"seq": lax.max(to_seq, 0), "head": near})

    def send_edge(k):
        pl.when(has_before)(edge(k).start)

    def take_edge(k):
        pl.when(has_before)(edge(k).wait_send)
        pl.when(has_after)(edge(k).wait_recv)

    swap_b = trade(send_b, got_b, 0, near)
    swap_small = trade(small_send_b, small_got, 1, near)
    cross_b = trade(far_out, far_in, 2, across)
    cross_small = trade(small_out, small_in, 3, across)
    swap_a = trade(send_a, got_a, 4, near)
    swap_small_a = trade(small_send_a, small_got_a, 5, near)

    swap_bc = trade(bc_out, bc_got, 6, near)
    cross_bc = trade(bc_far_out, bc_far, 7, across)

    def bc_quarter(k):
        return g_bc[pl.ds(pl.multiple_of(heads[k] * bc_rows, 8), bc_rows)]

    def common_trade(k):
        return trade(small_bc, com_got.at[k], 8 + k, heads[k])

    def heads_trade(k):
        return trade(bc_all.all, bc_heads.at[h_me], 11 + k, heads[k])

    def gi_trade(k):
        return trade(gi_sum, gi_got.at[k], 14 + k, heads[k])

    def piece_copy(step, k):
        return pltpu.make_async_remote_copy(
            src_ref=shuffle.at[step, heads[k]],
            dst_ref=landed.at[step, k],
            send_sem=piece_sems.at[0, step, k],
            recv_sem=piece_sems.at[1, step, k],
            device_id={"head": heads[k]},
            device_id_type=MESH,
        )

    def place(step, k):
        cols = pl.ds(pl.multiple_of(lax.rem(heads[k], parts) * chunk + step * GROUP, GROUP), GROUP)
        grad_in[heads[k] // parts, :, cols] = landed[step, k] if k else shuffle[step, h_me]

    @pl.when(u == 0)
    def _():
        for to in (edge_b, edge_bc, edge_a, ggain, gi_sum):
            to[...] = jnp.zeros_like(to)
        barrier = pltpu.get_barrier_semaphore()
        for head in heads[1:]:
            pl.semaphore_signal(barrier, inc=1, device_id={"head": head}, device_id_type=MESH)
        for d in range(1, n):
            pl.semaphore_signal(barrier, inc=1, device_id={"seq": lax.rem(s_me + d, n)}, device_id_type=MESH)
        other_seq = s_me - 1 + 2 * half
        has_other = (other_seq >= 0) & (other_seq < n)

        @pl.when(has_other)
        def _():
            pl.semaphore_signal(
                barrier, inc=1, device_id={"seq": other_seq, "head": near}, device_id_type=MESH
            )

        pl.semaphore_wait(barrier, n + 2 + has_other.astype(jnp.int32))
        send_edge(0)
        send_edge(1)
        gathered.start(share[...])

    block = jnp.clip(u - 2 * tiles, 0, count - 1)

    @pl.when((u == 0) | ((u >= first_back) & (u < first_a)))
    def _():
        rows = pl.ds(pl.multiple_of((count - 1 - block) * GROUP, GROUP), GROUP)
        outs = (dx_a.at[rows], tail_a, head_a, draw_a.at[rows], gw_a, gb_a, galog_a, gdtb_a)
        back_step(0, block, *back_in, *outs, *back_scr)

    @pl.when(u == first_bc)
    def _():
        take_edge(1)
        fix = mend(edge_bc, tail_bc, ci_bc, next_age, taps_bc, dbc, scr_bc, None, False)
        small_bc[...] = jnp.zeros_like(small_bc)
        sums = [jnp.sum(gw_bc[8 * k : 8 * k + 8], axis=0, keepdims=True) for k in range(4)]
        small_bc[0:4] = jnp.concatenate(sums, axis=0) + fix
        small_bc[4:5] = jnp.sum(gb_bc[...], axis=0, keepdims=True)
        for k in range(1, 4):
            common_trade(k).start()

    @pl.when((u >= first_bc) & (u < first_b))
    def _():
        rows = pl.ds(pl.multiple_of((u - first_bc) * GROUP, GROUP), GROUP)
        g_bc[rows] = dot(normed[...], scr_bc[...], 0, 0)

    @pl.when(u == first_b)
    def _():
        bc_out[0] = bc_quarter(1).astype(bf16)
        bc_out[1] = bc_quarter(3).astype(bf16)
        swap_bc.start()
        take_edge(0)
        fix = mend(edge_b, tail_b, ci_b, next_age, par_b, dx_b, scr_b, None, True)
        small_sums(1, fix, gw_b, gb_b, galog_b, gdtb_b, gskip, ggain_out, red, small_b, small_send_b)

    @pl.when(u == first_b + 1)
    def _():
        swap_bc.wait()
        bc_far_out[...] = (bc_quarter(2) + bc_got[1].astype(f32)).astype(bf16)
        cross_bc.start()
        gathered.middle()

    @pl.when((u >= first_b) & (u < first_back))
    def _():
        rows = pl.ds(pl.multiple_of((u - first_b) * GROUP, GROUP), GROUP)
        half_tile(u - first_b, normed, scr_b, draw_b, keep_b.at[rows], send_b.at[rows], small_b, small_send_b)

    @pl.when(u == first_back)
    def _():
        swap_b.start()
        swap_small.start()
        cross_bc.wait()
        bc_own[...] = bc_quarter(0) + bc_got[0].astype(f32) + bc_far[...].astype(f32)
        bc_sum.start(lambda s: bc_own[s * share_rows : (s + 1) * share_rows])

    @pl.when(u == first_back + 1)
    def _():
        swap_b.wait()
        far_out[...] = (keep_b[...] + got_b[...].astype(f32)).astype(bf16)
        cross_b.start()
        swap_small.wait()
        small_out[...] = small_b[...] + small_got[...]
        cross_small.start()
        bc_all.start(bc_sum.finish())

    @pl.when(u == first_back + 2)
    def _():
        bc_all.finish()
        for k in range(1, 4):
            heads_trade(k).start()
        bc_heads[h_me] = bc_all.all[...]

    @pl.when(u == first_a)
    def _():
        send_edge(2)
        gathered.finish()
        rows = grad_out.shape[1] // n
        grad_out[...] = jnp.concatenate([gathered.rows(s, rows) for s in range(n)], axis=0).T
        take_edge(2)
        fix = mend(edge_a, tail_a, ci_a, next_age, par_a, None, dx_a, None, True)
        small_sums(0, fix, gw_a, gb_a, galog_a, gdtb_a, gskip, ggain_out, red, small_a, small_send_a)

    @pl.when((u >= first_a) & (u < first_out))
    def _():
        rows = pl.ds(pl.multiple_of((u - first_a) * GROUP, GROUP), GROUP)
        half_tile(u - first_a, normed, dx_a, draw_a, keep_a.at[rows], send_a.at[rows], small_a, small_send_a)

    def halves_of(x):
        x = jnp.concatenate([x[:, :part], x[:, part:]], axis=0)
        hi = x.astype(bf16).astype(f32)
        return jnp.concatenate([hi, x - hi], axis=0)

    def joined(x, rows):
        x = x[0 : 2 * rows] + x[2 * rows : 4 * rows]
        return jnp.concatenate([x[:rows], x[rows:]], axis=1)

    @pl.when(u == first_out - 1)
    def _():
        swap_a.start()
        swap_small_a.start()

    @pl.when(u == first_out)
    def _():
        cross_small.wait()
        both = small_bc[...]
        for k in range(1, 4):
            common_trade(k).wait()
            both = both + com_got[k]
        both = jnp.concatenate([both, jnp.zeros((8, features - 2 * LANES), f32)], axis=1)
        cross_b.wait()
        swap_small_a.wait()
        both = jnp.concatenate([small_a[...] + small_got_a[...] + small_in[...], both], axis=0)
        swap_a.wait()
        rows = features // n

        def gx_share(s):
            at = slice(s * rows, (s + 1) * rows)
            x = keep_a[at] + got_a[at].astype(f32) + far_in[at].astype(f32)
            if s * pack_rows < 24:
                x = jnp.concatenate([x, halves_of(both[s * pack_rows : (s + 1) * pack_rows])], axis=0)
            return x

        gx_sum.start(gx_share)

    @pl.when(u >= first_out)
    def _():
        step = u - first_out
        at = pl.ds(pl.multiple_of(step * GROUP, GROUP), GROUP)
        acc = dot(scr_bc[at], bcw[...], 1, 1) + dot(draw_a[at], dt_a[...]) + dot(draw_b[at], dt_b[...])
        for k, (z, x) in enumerate(((z0, x0), (z1, x1), (z2, x2), (z3, x3))):
            d, col = (dx_a if k < 2 else scr_b), (k % 2) * part
            acc = acc + dot(dgate[:, k * part : (k + 1) * part], z[...], 1, 1)
            acc = acc + dot(d[at, col : col + part], x[...], 1, 1)
        acc_s[...] = acc
        piece = features // 4
        for r in range(0, GROUP, ROWS):
            rows = slice(r, r + ROWS)
            x = hid[rows].astype(f32)
            rinv = lax.rsqrt(jnp.sum(x * x, axis=1, keepdims=True) / x.shape[1] + EPS)
            xhat = x * rinv
            d = acc_s[rows]
            ggain[...] += fold8(d * xhat)
            dxh = d * gain[0:1]
            mean = jnp.sum(dxh * xhat, axis=1, keepdims=True) / x.shape[1]
            low[rows] = (cotx[rows].astype(f32) + rinv * (dxh - xhat * mean)).astype(bf16)
        turned = low[...].T
        for k in range(4):
            shuffle[step, k] = turned[k * piece : (k + 1) * piece]
        for k in (2, 3, 1):
            piece_copy(step, k).start()

    @pl.when(u == first_out + count - 1)
    def _():
        rows = features // n
        small_at = rows + 4 * pack_rows
        total = gx_sum.finish_f32()
        sums = halves_of(joined(total[rows:], pack_rows))
        row = halves_of(jnp.sum(ggain[...], axis=0, keepdims=True))
        gx_all.start(padded_rows(jnp.concatenate([total[:rows], sums, row], axis=0), total.shape[0]).astype(bf16))
        for k in range(1, 4):
            heads_trade(k).wait()
        for q in range(4):
            for s in range(n):
                at = (q * n + s) * share_rows
                gbc[at : at + share_rows] = bc_heads[q, s].astype(f32)[:share_rows]
        for step in range(count):
            for k in range(4):
                if k:
                    piece_copy(step, k).wait()
                place(step, k)
        gx_all.finish()
        row = joined(gx_all.rows(0, small_at + 4)[small_at:], 1)
        for s in range(1, n):
            row = row + joined(gx_all.rows(s, small_at + 4)[small_at:], 1)
        for t in range(lane_tiles):
            gi_sum[t : t + 1] = row[:, t * LANES : (t + 1) * LANES]
        for k in range(1, 4):
            gi_trade(k).start()
        for s in range(n):
            share_s = gx_all.rows(s, small_at)
            gx[s * rows : (s + 1) * rows] = share_s[:rows]
            if s * pack_rows < 24:
                small[s * pack_rows : (s + 1) * pack_rows] = joined(share_s[rows:], pack_rows)
        total = gi_sum[...]
        for k in range(1, 4):
            gi_trade(k).wait()
            total = total + gi_got[k]
        for t in range(lane_tiles):
            small[24:32, t * LANES : (t + 1) * LANES] = jnp.broadcast_to(total[t : t + 1], (8, LANES))


def unpack_kernel(
    quarter, heads, me, small, gi, dt, taps, bias, maps, maps_bias, step, log, skip, gain
):
    features = small.shape[1]
    piece = gi.shape[1]
    row = pltpu.roll(small[24:32], lax.rem(features - me[0] * piece, features), 1)
    gi[...] = row[0:1, :piece]
    dt[...] = small[8 : 8 + heads]
    taps[...] = small[0:4, :quarter]
    bias[...] = small[4:5, :quarter]
    gain[...] = small[5:6, :quarter]
    maps[...] = small[16:20, : 2 * LANES]
    maps_bias[...] = small[20:21, : 2 * LANES]
    row = jnp.broadcast_to(small[6:7, 0:LANES], (8, LANES))
    for k, to in enumerate((step, log, skip)):
        to[...] = pltpu.roll(row, LANES - k * heads, 1)[0:1, :heads] if k else row[0:1, :heads]


def shards(
    hidden_in,
    output_cotangent,
    input_norm_scale_gain,
    z_proj,
    x_proj,
    bc_proj,
    dt_proj,
    conv_x_weight,
    conv_x_bias,
    conv_bc_weight,
    conv_bc_bias,
    dt_bias,
    a_log,
    d_skip,
    out_norm_gain,
    out_proj,
    doc_starts,
):
    batch, tokens, features = hidden_in.shape
    quarter = z_proj.shape[1]
    width = 2 * quarter
    inner = 4 * quarter
    heads = dt_proj.shape[1]
    seqs = lax.axis_size("seq")
    head_devices = lax.axis_size("head")
    parts = head_devices // batch
    chunk = tokens // parts
    count = chunk // GROUP
    si, hi_ = lax.axis_index("seq"), lax.axis_index("head")
    seq_of, half = hi_ // parts, hi_ % parts
    meta = jnp.reshape(hi_, (1,)).astype(jnp.int32)

    here = lambda i, *_: (i, 0)
    here3 = lambda i, *_: (i, 0, 0)
    rev = lambda i, *_: (count - 1 - i, 0)
    rev3 = lambda i, *_: (count - 1 - i, 0, 0)
    rev_hid = lambda i, m: (m[0] // parts, lax.rem(m[0], parts) * count + count - 1 - i, 0)
    taps_bc = conv_bc_weight.T
    lane_block = (GROUP, LANES)
    map_block = (GROUP, 2 * LANES)
    wide = (GROUP, inner)
    half_in = (GROUP, width)
    state_block = (1, LANES, width)
    keep_block = (1, 8, width)
    piece = features // head_devices
    ex, red = expansion(width)
    tril = jnp.asarray(np.tril(np.ones((GROUP, GROUP), np.float32)))
    cotangent = jnp.swapaxes(output_cotangent, 1, 2)

    def whole(*arrays):
        return [(a, None, None) for a in arrays]

    vecs = jnp.concatenate(
        [
            conv_x_bias,
            out_norm_gain,
            jnp.pad(jnp.concatenate([dt_bias, a_log, d_skip]), (0, 2 * LANES - 3 * heads)),
            input_norm_scale_gain,
            conv_bc_bias,
        ]
    ).reshape(-1, LANES)
    front_scratch = [
        pltpu.VMEM((GROUP + 8, width), f32),
        pltpu.VMEM((LANES, width), f32),
        pltpu.VMEM((8, LANES), f32),
        pltpu.VMEM(half_in, f32),
        pltpu.VMEM(half_in, bf16),
        pltpu.VMEM(half_in, bf16),
        pltpu.VMEM((LANES, features), f32),
        pltpu.VMEM((GROUP + 8, 2 * LANES), f32),
    ]

    def front_outs(block, block3):
        return [
            ((chunk, width), bf16, half_in, block),
            ((chunk, width), f32, half_in, block),
            ((chunk, width), bf16, half_in, block),
            ((chunk, LANES), f32, lane_block, block),
            ((chunk, LANES), f32, lane_block, block),
            ((count, LANES, width), f32, state_block, block3),
            ((count, 8, width), f32, keep_block, block3),
            ((count, 8, width), f32, keep_block, block3),
            ((LANES, width), f32, None, None),
            ((8, LANES), f32, None, None),
            ((8, width), f32, None, None),
            ((LANES, features), bf16, None, None),
        ]

    own_head = lambda: lax.axis_index("head")
    x_shape = (features, quarter)

    def phase(k, rank):
        at = lambda u: jnp.clip(u - k * count, 0, count - 1)
        return (lambda u: (at(u), 0)) if rank == 2 else (lambda u: (at(u), 0, 0))

    def front_outs(k):
        return [
            ((chunk, width), bf16, half_in, phase(k, 2)),
            ((chunk, width), f32, half_in, phase(k, 2)),
            ((chunk, width), bf16, None, None),
            ((chunk, LANES), f32, None, None),
            ((chunk, LANES), f32, None, None),
            ((count, LANES, width), f32, state_block, phase(k, 3)),
            ((count, 8, width), f32, keep_block, phase(k, 3)),
            ((count, 8, width), f32, keep_block, phase(k, 3)),
            ((8, width), f32, None, None),
            ((LANES, features), bf16, None, None),
            ((LANES, quarter), f32, None, None),
            ((LANES, quarter), f32, None, None),
            ((chunk, width), f32, half_in, phase(k + 2, 2)),
        ]

    front_names = ("ci", "co", "val", "pre", "cum", "lin", "kb", "ck", "par", "dtp", "own", "other", "part")
    outs = run(
        functools.partial(forward_kernel, seqs, parts, count),
        (5 * count,),
        [
            (
                hidden_in,
                (1, GROUP, features),
                lambda u: (own_head() // parts, lax.rem(own_head(), parts) * count + jnp.minimum(u, count - 1), 0),
            ),
            (hidden_in, (1, 16, features), lambda u: (own_head() // parts, tokens // 16 - 1, 0)),
            (hidden_in, (1, 16, features), lambda u: (own_head() // parts, chunk // 16 - 1, 0)),
            *whole(doc_starts, vecs, conv_x_weight.T, dt_proj.T, x_proj, z_proj, out_proj, bc_proj, taps_bc, tril, ex),
            (cotangent, pl.ANY, None),
        ],
        [
            ((chunk, features), bf16, None, None),
            ((chunk, 2 * LANES), bf16, None, None),
            ((chunk, LANES), jnp.int32, None, None),
            ((8, chunk), jnp.int32, (8, GROUP), lambda u: (0, jnp.minimum(u, count - 1))),
            ((8, LANES), jnp.int32, None, None),
            ((8, features), f32, None, None),
        ]
        + [(x_shape, bf16, None, None)] * 6
        + [((quarter, features), bf16, None, None)] * 3
        + [((piece, chunk), bf16, pl.ANY, None)] * 3
        + [
            ((chunk, 2 * LANES), f32, map_block, phase(1, 2)),
            ((chunk, LANES), bf16, None, None),
            ((chunk, LANES), bf16, None, None),
        ]
        + front_outs(1)
        + front_outs(2),
        [
            pltpu.VMEM((8, features), f32),
            pltpu.VMEM((8, 2 * LANES), f32),
            pltpu.VMEM((16, features), bf16),
            pltpu.VMEM((16, features), bf16),
        ]
        + [pltpu.VMEM((16, features), f32)] * 4
        + [pltpu.VMEM(x_shape, bf16)] * 3
        + [pltpu.VMEM((LANES, width), f32)] * 2
        + [pltpu.VMEM((8, LANES), f32)] * 2
        + [pltpu.SemaphoreType.DMA((2, 7)), pltpu.SemaphoreType.DMA((2, 4))]
        + front_scratch
        + Weights.scratch(features, quarter)
        + Weights.scratch(quarter, features)
        + Exchange.scratch(seqs, quarter) * 2,
        flops=40_000_000_000,
        moved=50_000_000,
        collective=1,
    )
    normed, ci_bc, age, ager, next_age, gain_in = outs[:6]
    xs, zs, os_ = [x_proj, *outs[6:9]], [z_proj, *outs[9:12]], [out_proj, *outs[12:15]]
    cots = outs[15:18]
    co_bc, bmat, cmat = outs[18:21]
    ha, hb = dict(zip(front_names, outs[21:34])), dict(zip(front_names, outs[34:47]))
    halves = [ha, hb]
    for d in halves:
        d["arr"] = [d["own"], d["other"]]

    outs = run(
        mid_kernel,
        (count,),
        [
            (hidden_in, (1, GROUP, features), rev_hid),
            (normed, (GROUP, features), rev),
            *whole(*zs, *os_),
            (
                cotangent,
                (1, piece, GROUP),
                lambda i, m: (m[0] // parts, 0, lax.rem(m[0], parts) * count + count - 1 - i),
            ),
            *[(c, (piece, GROUP), lambda i, *_: (0, count - 1 - i)) for c in cots],
            (cmat, lane_block, rev),
            (age, lane_block, rev),
            *whole(ex, red, ha["par"], hb["par"]),
            *[(d["part"], half_in, rev) for d in halves],
            *[(d["val"], half_in, rev) for d in halves],
            *[(d["cum"], lane_block, rev) for d in halves],
            *[(d["lin"], state_block, rev3) for d in halves],
            *[(d["kb"], keep_block, rev3) for d in halves],
            *[(d["ck"], keep_block, rev3) for d in halves],
            *whole(*ha["arr"], *hb["arr"]),
        ],
        [
            ((4, piece, chunk), bf16, (4, piece, GROUP), lambda i, *_: (0, 0, count - 1 - i)),
            ((chunk, features), bf16, (GROUP, features), rev),
            ((chunk, inner), bf16, wide, rev),
            ((chunk, features), bf16, (GROUP, features), rev),
            ((chunk, inner), bf16, wide, rev),
            ((chunk, inner), bf16, wide, rev),
            ((chunk, LANES), f32, lane_block, rev),
            ((chunk, LANES), f32, lane_block, rev),
            ((chunk, LANES), f32, lane_block, rev),
            ((count, LANES, width), f32, state_block, rev3),
            ((count, LANES, width), f32, state_block, rev3),
            ((count, 8, width), f32, keep_block, rev3),
            ((count, 8, width), f32, keep_block, rev3),
            ((LANES, width), f32, None, None),
            ((LANES, width), f32, None, None),
            ((8, LANES), f32, None, None),
            ((8, LANES), f32, None, None),
            ((8, inner), f32, None, None),
            ((8, inner), f32, None, None),
        ],
        [pltpu.VMEM(wide, f32)] * 6
        + [pltpu.VMEM(wide, bf16)] * 4
        + [pltpu.VMEM((LANES, width), f32)] * 2
        + [pltpu.VMEM((8, LANES), f32)] * 2
        + [pltpu.VMEM((4, piece, GROUP), bf16)],
        flops=30_000_000_000,
        moved=50_000_000,
        prefetch=(meta,),
    )
    pieces, hidc, outs = outs[0], outs[1], outs[2:]
    nout, cotx, dssd, dgate, dcin, ha["dkk"], hb["dkk"], ha["lout"], hb["lout"], ha["ka"], hb["ka"] = outs[:11]
    dtot_a, dtot_b, dk_a, dk_b, ggain_out, gskip = outs[11:]

    tiles = features // GROUP
    lead = 4 * tiles
    tile_block = lambda u: (0, lax.rem(jnp.minimum(u, lead - 1), tiles))
    first_half = lambda u: (0, 1 - jnp.minimum(u // (2 * tiles), 1))
    after_lead = lambda u: jnp.maximum(u - lead, 0)
    lo_unit = lambda u: (jnp.clip(u - lead, 0, count - 1), 0)
    hi_unit = lambda u: (jnp.clip(u - lead - count, 0, count - 1), 0)
    any_unit = lambda u: (lax.rem(after_lead(u), count), 0)
    quarter_grad = (2, features, quarter)
    share_rows = features // seqs
    outs = run(
        functools.partial(outer_kernel, seqs, parts, count, tiles),
        (lead + 2 * count,),
        [
            (normed, (chunk, GROUP), tile_block),
            (cotx, (chunk, GROUP), tile_block),
            (dgate, (chunk, width), first_half),
            (nout, (chunk, width), first_half),
            (ha["val"], half_in, lo_unit),
            (hb["val"], half_in, hi_unit),
            (dssd, half_in, lambda u: (lax.rem(after_lead(u), count), after_lead(u) // count)),
            (bmat, lane_block, any_unit),
            (cmat, lane_block, any_unit),
            (ager, (8, GROUP), lambda u: (0, lax.rem(after_lead(u), count))),
            (ha["pre"], lane_block, lo_unit),
            (hb["pre"], lane_block, hi_unit),
            (ha["cum"], lane_block, lo_unit),
            (hb["cum"], lane_block, hi_unit),
            *whole(dtot_a, dtot_b, dk_a, dk_b, ex),
        ],
        [
            (shape, f32, (GROUP, shape[1]), imap)
            for imap in (lo_unit, hi_unit)
            for shape in [(chunk, width)] + [(chunk, LANES)] * 4
        ]
        + [((LANES, width), f32, None, None)] * 2
        + [((up16(share_rows), quarter), bf16, None, None), ((features, quarter), bf16, None, None)],
        [
            pltpu.VMEM((LANES, GROUP), f32),
            pltpu.VMEM((2,) + quarter_grad, f32),
            pltpu.VMEM((2,) + quarter_grad, bf16),
            pltpu.VMEM((2,) + quarter_grad, bf16),
            pltpu.VMEM(quarter_grad, bf16),
            pltpu.VMEM(quarter_grad, bf16),
            pltpu.SemaphoreType.DMA((2, 6)),
        ]
        + PairScatter.scratch(seqs, share_rows, quarter)
        + Exchange.scratch(seqs, width),
        flops=30_000_000_000,
        moved=40_000_000,
        collective=2,
    )
    names = ("dvi", "dbi", "dci_c", "rflow", "cflow")
    ha.update(zip(names, outs[:5]))
    hb.update(zip(names, outs[5:10]))
    leav = outs[10:12]
    share_z, grad_o = outs[12:]

    def back_ins(n, block, block3):
        d = halves[n]
        return [
            (d["val"], half_in, block),
            (dssd, half_in, lambda u: (block(u)[0], n)),
            (d["dvi"], half_in, block),
            (bmat, lane_block, block),
            (d["co"], half_in, block),
            (d["ci"], half_in, block),
            (age, lane_block, block),
            (d["pre"], lane_block, block),
            (d["cum"], lane_block, block),
            (d["lout"], state_block, block3),
            (d["ka"], keep_block, block3),
            *whole(*leav),
            (d["lin"], state_block, block3),
            (d["kb"], keep_block, block3),
            *whole(*d["arr"]),
            (d["rflow"], lane_block, block),
            (d["cflow"], lane_block, block),
            (d["dkk"], lane_block, block),
            *whole(d["par"], tril, ex, red),
        ]

    back_scratch = [
        pltpu.VMEM((GROUP + 8, width), f32),
        pltpu.VMEM((GROUP + 8, LANES), jnp.int32),
        pltpu.VMEM(half_in, f32),
        pltpu.VMEM(half_in, f32),
        pltpu.VMEM(half_in, bf16),
        pltpu.VMEM(half_in, bf16),
    ]

    def both_outs(cols, block):
        return [
            ((chunk, cols), bf16, (GROUP, cols), block),
            ((8, cols), f32, None, None),
            ((8, cols), f32, None, None),
        ]

    early_rev = lambda u: (count - 1 - jnp.minimum(u, count - 1), 0)
    late_rev = lambda u: (count - 1 - jnp.maximum(u - count, 0), 0)
    early_rev3 = lambda u: (count - 1 - jnp.minimum(u, count - 1), 0, 0)
    late_rev3 = lambda u: (count - 1 - jnp.maximum(u - count, 0), 0, 0)
    outs = run(
        functools.partial(turn_kernel, seqs, parts, count),
        (2 * count,),
        [
            *[(d["dbi"], lane_block, early_rev) for d in halves],
            *[(d["dci_c"], lane_block, early_rev) for d in halves],
            (dcin, lane_block, early_rev),
            (co_bc, map_block, early_rev),
            (ci_bc, map_block, early_rev),
            (age, lane_block, early_rev),
            (taps_bc, None, None),
            *[(d["val"], half_in, early_rev) for d in halves],
            *[(d["pre"], lane_block, early_rev) for d in halves],
            *[(d["cum"], lane_block, early_rev) for d in halves],
            *[(d["lout"], state_block, early_rev3) for d in halves],
            *[(d["ka"], keep_block, early_rev3) for d in halves],
            *whole(*leav, ex),
            *back_ins(1, late_rev, late_rev3),
            *whole(grad_o, share_z),
            (pieces, pl.ANY, None),
        ],
        both_outs(2 * LANES, early_rev)
        + [((32, 2 * LANES), f32, None, None), ((8, 2 * LANES), f32, None, None)]
        + both_outs(width, late_rev)
        + [
            ((chunk, LANES), bf16, lane_block, late_rev),
            ((32, width), f32, None, None),
            ((8, width), f32, None, None),
            ((8, LANES), f32, None, None),
            ((8, LANES), f32, None, None),
            ((up16(share_rows), quarter), bf16, None, None),
            ((features, quarter), f32, None, None),
            ((batch, piece, tokens), bf16, pl.ANY, None),
        ],
        [
            pltpu.VMEM((GROUP + 8, 2 * LANES), f32),
            pltpu.VMEM((GROUP + 8, LANES), jnp.int32),
            pltpu.VMEM(lane_block, f32),
        ]
        + back_scratch
        + [pltpu.SemaphoreType.DMA((2, 4))]
        + PairScatter.scratch(seqs, share_rows, quarter)
        + PairGather.scratch(seqs, share_rows, quarter),
        flops=30_000_000_000,
        moved=40_000_000,
        collective=4,
    )
    dbc, tail_bc, head_bc, gw_bc, gb_bc = outs[:5]
    hb.update(zip(("dx", "tail", "head", "draw", "gw", "gb", "galog", "gdtb"), outs[5:13]))
    share, grad_z, layer_out = outs[13:]

    steps = 3 * tiles + 2 * count
    back_unit = lambda u: (count - 1 - jnp.clip(u - 2 * tiles, 0, count - 1), 0)
    back_unit3 = lambda u: (count - 1 - jnp.clip(u - 2 * tiles, 0, count - 1), 0, 0)
    out_unit = lambda u: (jnp.clip(u - 3 * tiles - count, 0, count - 1), 0)

    def grad_tile(u):
        first = lax.rem(jnp.clip(u - 1, 0, 2 * tiles - 1), tiles)
        third = jnp.clip(u - 2 * tiles - count, 0, tiles - 1)
        later = jnp.minimum(u // (2 * tiles + count), 1)
        return 0, (1 - later) * first + later * third

    ending = lambda *_: (chunk // 16 - 1, 0)
    small_pack = (16, features)
    packed_rows = share_rows + 4 * -(-24 // seqs) + 4
    input_grad, sum2, g_bc, small_sum, grad_out = run(
        functools.partial(late_kernel, seqs, parts, count, tiles),
        (steps,),
        [
            *back_ins(0, back_unit, back_unit3),
            (normed, (chunk, GROUP), grad_tile),
            *whole(hb["dx"], hb["tail"], hb["head"]),
            (hb["ci"], (16, width), ending),
            *whole(hb["par"], hb["draw"], hb["gw"], hb["gb"], hb["galog"], hb["gdtb"]),
            *whole(dbc, tail_bc, head_bc),
            (ci_bc, (16, 2 * LANES), ending),
            *whole(taps_bc, gw_bc, gb_bc),
            (ha["ci"], (16, width), ending),
            *whole(next_age, gskip, ggain_out, share),
            (hidc, (GROUP, features), out_unit),
            (cotx, (GROUP, features), out_unit),
            (gain_in, None, None),
            (dgate, wide, out_unit),
            *whole(*zs, bc_proj, *xs, ha["dtp"], hb["dtp"]),
        ],
        [
            ((batch, piece, tokens), bf16, None, None),
            ((features, quarter), f32, None, None),
            ((features, 2 * LANES), f32, None, None),
            ((32, features), f32, None, None),
            ((quarter, features), f32, None, None),
        ],
        back_scratch
        + [
            pltpu.VMEM((chunk, width), bf16),
            pltpu.VMEM((chunk, LANES), bf16),
            pltpu.VMEM(x_shape, f32),
            pltpu.VMEM(x_shape, bf16),
            pltpu.VMEM(small_pack, f32),
            pltpu.VMEM(small_pack, f32),
            pltpu.VMEM(x_shape, bf16),
            pltpu.VMEM(small_pack, f32),
            pltpu.VMEM((16, width), bf16),
            pltpu.VMEM((8, width), f32),
            pltpu.VMEM((8, width), f32),
            pltpu.VMEM((32, width), f32),
            pltpu.VMEM((8, width), f32),
            pltpu.VMEM((8, LANES), f32),
            pltpu.VMEM((8, LANES), f32),
            pltpu.VMEM((chunk, width), bf16),
            pltpu.VMEM((chunk, 2 * LANES), bf16),
            pltpu.VMEM(x_shape, f32),
            pltpu.VMEM(x_shape, bf16),
            pltpu.VMEM(x_shape, bf16),
            pltpu.VMEM(x_shape, bf16),
        ]
        + [pltpu.VMEM(small_pack, f32)] * 5
        + [
            pltpu.VMEM(x_shape, bf16),
            pltpu.VMEM((8, width), f32),
            pltpu.VMEM((8, 2 * LANES), f32),
            pltpu.VMEM((8, width), f32),
            pltpu.VMEM((features, 2 * LANES), f32),
            pltpu.VMEM((2, features // 4, 2 * LANES), bf16),
            pltpu.VMEM((2, features // 4, 2 * LANES), bf16),
            pltpu.VMEM((features // 4, 2 * LANES), bf16),
            pltpu.VMEM((features // 4, 2 * LANES), bf16),
            pltpu.VMEM((features // 4, 2 * LANES), f32),
            pltpu.VMEM((8, 2 * LANES), f32),
            pltpu.VMEM((4, 8, 2 * LANES), f32),
            pltpu.VMEM((4, seqs, up16(features // 4 // seqs), 2 * LANES), bf16),
            pltpu.VMEM((GROUP, features), f32),
            pltpu.VMEM((GROUP, features), bf16),
            pltpu.VMEM((count, 4, piece, GROUP), bf16),
            pltpu.VMEM((count, 4, piece, GROUP), bf16),
            pltpu.VMEM((8, features), f32),
            pltpu.VMEM((4, 8, LANES), f32),
            pltpu.VMEM((8, LANES), f32),
            pltpu.SemaphoreType.DMA((2, 3)),
            pltpu.SemaphoreType.DMA((2, 18)),
            pltpu.SemaphoreType.DMA((2, count, 4)),
        ]
        + PairGather.scratch(seqs, share_rows, quarter)
        + Scatter.scratch(seqs, packed_rows, quarter)
        + Gather.scratch(seqs, packed_rows, quarter)
        + Scatter.scratch(seqs, features // 4 // seqs, 2 * LANES)
        + Gather.scratch(seqs, features // 4 // seqs, 2 * LANES),
        flops=40_000_000_000,
        moved=60_000_000,
        collective=5,
    )
    vector = lambda size: ((1, size), f32, None, None)
    gi, g_dt, g_taps, g_bias, g_maps, g_maps_bias, g_step, g_log, g_skip, g_gain = run(
        functools.partial(unpack_kernel, quarter, heads),
        (1,),
        whole(small_sum),
        [
            vector(piece),
            ((heads, features), f32, None, None),
            ((4, quarter), f32, None, None),
            vector(quarter),
            ((4, 2 * LANES), f32, None, None),
            vector(2 * LANES),
            vector(heads),
            vector(heads),
            vector(heads),
            vector(quarter),
        ],
        prefetch=(meta,),
    )
    return (
        jnp.swapaxes(layer_out, 1, 2),
        jnp.swapaxes(input_grad, 1, 2),
        gi[0],
        grad_z,
        sum2,
        g_bc,
        g_dt.T,
        g_taps.T,
        g_bias[0],
        g_maps.T,
        g_maps_bias[0],
        g_step[0],
        g_log[0],
        g_skip[0],
        g_gain[0],
        grad_out,
    )


def solution(mesh):
    return jax.shard_map(
        shards,
        mesh=mesh,
        in_specs=(
            P(None, "seq", None),
            P(None, "seq", "head"),
            P(),
            P(None, "head"),
            P(None, "head"),
            P(),
            P(None, "head"),
            P("head", None),
            P("head"),
            P(),
            P(),
            P("head"),
            P("head"),
            P("head"),
            P("head"),
            P("head", None),
            P(),
        ),
        out_specs=(
            P(None, "seq", "head"),
            P(None, "seq", "head"),
            P("head"),
            P(None, "head"),
            P(None, "head"),
            P(),
            P(None, "head"),
            P("head", None),
            P("head"),
            P(),
            P(),
            P("head"),
            P("head"),
            P("head"),
            P("head"),
            P("head", None),
        ),
        check_vma=False,
    )
```

```python
import functools

import jax
import jax.numpy as jnp
import numpy as np
from jax import lax
from jax.experimental import pallas as pl
from jax.experimental.pallas import tpu as pltpu
from jax.sharding import PartitionSpec as P

GROUP = 256
HALF = 128
LANES = 128
HEAD_DIM = 64
EPS = 1e-05
LOG2E = 1.4426950408889634
f32 = jnp.float32
bf16 = jnp.bfloat16
HIGHEST = lax.Precision.HIGHEST
ROWS = 32
MESH = pl.DeviceIdType.MESH


def dot(a, b, ca=1, cb=0, precision=None):
    return lax.dot_general(
        a, b, (((ca,), (cb,)), ((), ())), precision=precision, preferred_element_type=f32
    )


def split2(x):
    hi = x.astype(bf16)
    return hi, (x - hi.astype(f32)).astype(bf16)


def pack(x):
    hi = x.astype(bf16).astype(f32)
    rest = x - hi
    mid = rest.astype(bf16).astype(f32)
    return (hi + pltpu.roll(mid, 32, 1) + pltpu.roll(rest - mid, 64, 1)).astype(bf16)


def unpack(x):
    x = x.astype(f32)
    return lanes_below(x + pltpu.roll(x, LANES - 32, 1) + pltpu.roll(x, LANES - 64, 1), 12)


def expand(x, ex):
    return dot(pack(x), ex)


def lanes_below(x, count):
    return jnp.where(lax.broadcasted_iota(jnp.int32, x.shape, 1) < count, x, 0.0)


def sigmoid(x):
    return 1.0 / (1.0 + jnp.exp(-x))


def softplus(x):
    return jnp.maximum(x, 0.0) + jnp.log1p(jnp.exp(-jnp.abs(x)))


def fold8(x):
    total = x[0:8]
    for r in range(8, x.shape[0], 8):
        total = total + x[r : r + 8]
    return total


def expansion(width):
    heads = width // HEAD_DIM
    ex = np.zeros((LANES, width), np.float32)
    for part in range(3):
        for h in range(heads):
            ex[32 * part + h, h * HEAD_DIM : (h + 1) * HEAD_DIM] = 1.0
    red = np.zeros((width, LANES), np.float32)
    for h in range(heads):
        red[h * HEAD_DIM : (h + 1) * HEAD_DIM, h] = 1.0
    return jnp.asarray(ex, bf16), jnp.asarray(red, bf16)


def run(kernel, grid, ins, outs, scratch=(), flops=0, moved=0, prefetch=(), collective=None):
    def spec(shape, block, imap):
        if block is pl.ANY:
            return pl.BlockSpec(memory_space=pl.ANY)
        if block is None:
            rank = len(shape)
            return pl.BlockSpec(shape, lambda *_: (0,) * rank)
        return pl.BlockSpec(block, imap)

    extra = {} if collective is None else {"collective_id": collective, "has_side_effects": True}
    return pl.pallas_call(
        kernel,
        grid_spec=pltpu.PrefetchScalarGridSpec(
            num_scalar_prefetch=len(prefetch),
            grid=grid,
            in_specs=[spec(a.shape, b, m) for a, b, m in ins],
            out_specs=[spec(s, b, m) for s, _, b, m in outs],
            scratch_shapes=list(scratch),
        ),
        out_shape=[jax.ShapeDtypeStruct(s, d) for s, d, _, _ in outs],
        compiler_params=pltpu.CompilerParams(vmem_limit_bytes=56 << 20, **extra),
        cost_estimate=pl.CostEstimate(flops=flops, bytes_accessed=moved, transcendentals=0),
    )(*prefetch, *[a for a, _, _ in ins])


def conv_rows(ext, age, taps, bias, r, cols):
    acc = jnp.broadcast_to(bias[:, cols], (ROWS, LANES))
    for k in range(4):
        back = 3 - k
        term = ext[8 + r - back : 8 + r - back + ROWS, cols] * taps[k : k + 1, cols]
        if back:
            term = jnp.where(age >= back, term, 0.0)
        acc = acc + term
    return acc


def rms(x, gain):
    x = x.astype(f32)
    r = lax.rsqrt(jnp.sum(x * x, axis=1, keepdims=True) / x.shape[1] + EPS)
    return (x * r * gain).astype(bf16)


def spread_ages(starts, first, rows):
    token = first + lax.broadcasted_iota(jnp.int32, (rows, starts.shape[1]), 0)
    begun = jnp.where(starts <= token, starts, 0).astype(f32)
    begun = jnp.max(begun, axis=1, keepdims=True).astype(jnp.int32)
    place = first + lax.broadcasted_iota(jnp.int32, (rows, LANES), 0)
    return place - begun


def front_step(
    with_maps, i, normed, before, wa, wb, sa, sb, age, tril, ex, maps_in,
    ci, co, val, pre, cum, lin, kb, ck, tot, kout, par, dtp, maps_out,
    ext, running, kept, omx, ohi, olo, dts, ext_bc,
):
    width = val.shape[1]
    part = width // 2
    heads = part // HEAD_DIM
    if with_maps:
        ci_bc, bc, taps_bc, bias_bc = maps_in
        bias_bc = bias_bc[0:1]
        co_bc, bmat, cmat = maps_out
    else:
        (bmat,) = maps_in

    @pl.when(i == 0)
    def _():
        running[...] = jnp.zeros_like(running)
        kept[...] = jnp.ones_like(kept)
        for w, at in ((wa, 0), (wb, part)):
            ext[0:8, at : at + part] = dot(before[...], w[...]).astype(bf16).astype(f32)[8:16]
        if with_maps:
            ext_bc[0:8] = dot(before[...], bc[...]).astype(bf16).astype(f32)[8:16]
        par[...] = jnp.zeros_like(par)
        for s, at in ((sa, 0), (sb, part)):
            par[0:6, at : at + part] = s[0:6, :part]
        rows_a, rows_b = (jnp.broadcast_to(s[6:7, 0:LANES], (8, LANES)) for s in (sa, sb))

        def lanes(k):
            a = lanes_below(pltpu.roll(rows_a, (LANES - k * heads) % LANES, 1), heads)
            b = lanes_below(pltpu.roll(rows_b, (LANES - k * heads) % LANES, 1), heads)
            return a + pltpu.roll(b, heads, 1)

        par[7:8, LANES : 2 * LANES] = lanes(0)[0:1]
        par[7:8, 0:LANES] = -jnp.exp(lanes(1)[0:1])
        par[6:7] = expand(lanes(2), ex[...])[0:1]
        dts[...] = jnp.zeros_like(dts)
        dts[0:heads] = sa[8 : 8 + heads]
        dts[heads : 2 * heads] = sb[8 : 8 + heads]
        dtp[...] = dts[...].astype(bf16)

    @pl.when(i > 0)
    def _():
        ext[0:8] = ext[GROUP : GROUP + 8]
        if with_maps:
            ext_bc[0:8] = ext_bc[GROUP : GROUP + 8]

    taps, bias = par, par[4:5]
    rate, dtb = par[7:8, 0:LANES], par[7:8, LANES : 2 * LANES]
    for w, at in ((wa, 0), (wb, part)):
        low = dot(normed[...], w[...]).astype(bf16)
        ci[:, at : at + part] = low
        ext[8 : 8 + GROUP, at : at + part] = low.astype(f32)
    raw = dot(normed[...], dtp[...], 1, 1) + dtb
    pre[...] = raw
    delta = softplus(raw)
    c = dot(tril[...], delta * rate, precision=HIGHEST)
    cum[...] = c
    end = c[GROUP - 1 : GROUP]
    age_end = age[GROUP - 1 : GROUP]
    left = GROUP - 1 - lax.broadcasted_iota(jnp.int32, c.shape, 0)
    omega = jnp.where(left <= age_end, jnp.exp(end - c), 0.0) * delta
    omx[...] = expand(lanes_below(omega, 2 * heads), ex[...])
    keep = jnp.where(age_end >= GROUP, jnp.exp(end), 0.0)
    keep = lanes_below(jnp.broadcast_to(keep, (8, LANES)), 2 * heads)
    keepx = expand(keep, ex[...])
    if with_maps:
        ext_bc[8 : 8 + GROUP] = ci_bc[...].astype(f32)
        for r in range(0, GROUP, ROWS):
            a = age[r : r + ROWS]
            for j, out in enumerate((bmat, cmat)):
                cols = slice(j * LANES, (j + 1) * LANES)
                v = conv_rows(ext_bc, a, taps_bc, bias_bc, r, cols)
                co_bc[r : r + ROWS, cols] = v
                out[r : r + ROWS] = (v * sigmoid(v)).astype(bf16)
    for r in range(0, GROUP, ROWS):
        a = age[r : r + ROWS]
        rows = slice(r, r + ROWS)
        for j in range(width // LANES):
            cols = slice(j * LANES, (j + 1) * LANES)
            v = conv_rows(ext, a, taps, bias, r, cols)
            co[rows, cols] = v
            act = (v * sigmoid(v)).astype(bf16)
            val[rows, cols] = act
            ohi[rows, cols], olo[rows, cols] = split2(omx[rows, cols] * act.astype(f32))
    own = dot(bmat[...], ohi[...], 0, 0) + dot(bmat[...], olo[...], 0, 0)
    lin[0] = running[...]
    kb[0] = expand(lanes_below(kept[...], 2 * heads), ex[...])
    ck[0] = keepx
    running[...] = keepx[0:1] * running[...] + own
    kept[...] = keep * kept[...]
    tot[...] = running[...]
    kout[...] = kept[...]


def head_peers():
    head = lax.axis_index("head")
    near = head + 1 - 2 * lax.rem(head, 2)
    return [head, near, lax.rem(head + 2, 4), lax.rem(near + 2, 4)]


def meet(heads, n, extra=0):
    me = lax.axis_index("seq")
    barrier = pltpu.get_barrier_semaphore()
    for head in heads:
        pl.semaphore_signal(barrier, inc=1, device_id={"head": head}, device_id_type=MESH)
    for d in range(1, n):
        pl.semaphore_signal(barrier, inc=1, device_id={"seq": lax.rem(me + d, n)}, device_id_type=MESH)
    pl.semaphore_wait(barrier, n - 1 + len(heads))


def send(src, dst, sems, k, device):
    return pltpu.make_async_remote_copy(
        src_ref=src, dst_ref=dst, send_sem=sems.at[0, k], recv_sem=sems.at[1, k],
        device_id=device, device_id_type=MESH,
    )


class Weights:
    def __init__(self, n, own, outs, scratch):
        self.own, self.outs = own, outs
        self.near, self.far, self.far_near, self.sems = scratch
        me = lax.axis_index("seq")
        odd = lax.rem(me, 2)
        heads = head_peers()
        half = own.shape[0] // 2
        rows = pl.ds(pl.multiple_of(odd * half, half), half)
        near, mate = {"head": heads[1]}, {"seq": me + 1 - 2 * odd}
        self.copies = [
            send(own, self.near, self.sems, 0, near),
            send(own.at[rows], self.far.at[rows], self.sems, 1, {"head": heads[2]}),
            send(self.far.at[rows], self.far.at[rows], self.sems, 2, mate),
            send(self.far, self.far_near, self.sems, 3, near),
        ]

    @staticmethod
    def scratch(rows, cols):
        return [pltpu.VMEM((rows, cols), bf16)] * 3 + [pltpu.SemaphoreType.DMA((2, 4))]

    def begin(self):
        self.copies[1].start()
        self.copies[0].start()

    def share(self):
        self.copies[1].wait()
        self.copies[2].start()

    def back(self):
        self.copies[2].wait()
        self.copies[3].start()

    def finish(self):
        self.copies[0].wait()
        self.copies[3].wait()
        for to, x in zip(self.outs, (self.near, self.far, self.far_near)):
            to[...] = x[...]


def cot_copies(cotangent, outs, which, parts, sems):
    heads = head_peers()
    copies = []
    for k, out in zip(which, outs):
        chunk = out.shape[1]
        cols = pl.ds(pl.multiple_of(lax.rem(heads[k], parts) * chunk, chunk), chunk)
        copies.append(send(cotangent.at[heads[k] // parts, :, cols], out, sems, k, {"head": heads[k]}))
    return copies


class Exchange:
    def __init__(self, reverse, n, parts, tots, kouts, ex, own, other, scratch):
        self.reverse, self.n, self.tots, self.kouts, self.ex = reverse, n, tots, kouts, ex
        self.own, self.other = own, other
        (
            self.out, self.got, self.payload, self.spread, self.scanned, self.home, self.lead, self.lead_k, self.arr,
            self.theirs, self.last, self.swap_sems, self.to_sems, self.from_sems, self.back_to, self.back_from,
        ) = scratch
        self.me = lax.axis_index("seq")
        head = lax.axis_index("head")
        self.partner = head + 1 - 2 * lax.rem(head, 2)
        half = lax.rem(head, parts)
        self.leads = (half if reverse else 1 - half).astype(f32)
        self.per = LANES // n

    @staticmethod
    def scratch(n, width):
        rows = max(LANES // n, 8)
        return [
            pltpu.VMEM((LANES + 8, width), f32),
            pltpu.VMEM((LANES + 8, width), f32),
            pltpu.VMEM((n, rows, width + LANES), f32),
            pltpu.VMEM((n, rows, width + LANES), f32),
            pltpu.VMEM((n, rows, width), f32),
            pltpu.VMEM((n, rows, width), f32),
            pltpu.VMEM((LANES, width), f32),
            pltpu.VMEM((8, LANES), f32),
            pltpu.VMEM((LANES, width), f32),
            pltpu.VMEM((LANES, width), f32),
            pltpu.VMEM((LANES, width), f32),
            pltpu.SemaphoreType.DMA((4,)),
            pltpu.SemaphoreType.DMA((n,)),
            pltpu.SemaphoreType.DMA((n,)),
            pltpu.SemaphoreType.DMA((n,)),
            pltpu.SemaphoreType.DMA((n,)),
        ]

    def peers(self):
        for d in range(1, self.n):
            yield d, lax.rem(self.me + d, self.n), lax.rem(self.me + self.n - d, self.n)

    def swap(self, src, dst, sem):
        return pltpu.make_async_remote_copy(
            src_ref=src,
            dst_ref=dst,
            send_sem=self.swap_sems.at[sem],
            recv_sem=self.swap_sems.at[sem + 1],
            device_id={"head": self.partner},
            device_id_type=MESH,
        )

    def move(self, src, dst, d, to, send_sems, recv_sems):
        return pltpu.make_async_remote_copy(
            src_ref=src.at[to],
            dst_ref=dst.at[self.me],
            send_sem=send_sems.at[d],
            recv_sem=recv_sems.at[d],
            device_id={"seq": to},
            device_id_type=MESH,
        )

    def begin(self):
        part = self.tots[0].shape[1] // 2
        heads = part // HEAD_DIM
        for k in range(len(self.tots)):
            self.out[0:LANES, k * part : (k + 1) * part] = self.tots[k][:, part:]
            rolled = pltpu.roll(self.kouts[k][...], LANES - heads, 1)
            self.out[LANES : LANES + 8, k * LANES : (k + 1) * LANES] = lanes_below(rolled, heads)
        used = len(self.tots) * LANES
        self.out[LANES : LANES + 8, used:] = jnp.zeros((8, self.out.shape[1] - used), f32)
        self.swap(self.out, self.got, 0).start()

    def combine(self):
        self.swap(self.out, self.got, 0).wait()
        part = self.tots[0].shape[1] // 2
        heads = part // HEAD_DIM
        width = len(self.tots) * part
        leads, follows = self.leads, 1.0 - self.leads
        mine_k, got_k = jnp.zeros((8, LANES), f32), jnp.zeros((8, LANES), f32)
        for k, kout in enumerate(self.kouts):
            both = (lanes_below(kout[...], heads), self.got[LANES : LANES + 8, k * LANES : (k + 1) * LANES])
            both = [pltpu.roll(x, k * heads, 1) if k else x for x in both]
            mine_k, got_k = mine_k + both[0], got_k + both[1]
        lk = leads * mine_k + follows * got_k
        fk = leads * got_k + follows * mine_k
        fkx = expand(fk, self.ex[:, :width])[0:1]
        self.lead_k[...] = lk
        for k in range(len(self.tots)):
            cols = slice(k * part, (k + 1) * part)
            mine, got = self.tots[k][:, :part], self.got[0:LANES, cols]
            ls = leads * mine + follows * got
            self.lead[:, cols] = ls
            self.arr[:, cols] = fkx[:, cols] * ls + (leads * got + follows * mine)
        keep = (lk * fk)[0:1]
        rows = self.payload.shape[1]
        for s in range(self.n):
            self.payload[s, 0 : self.per, 0:width] = self.arr[s * self.per : (s + 1) * self.per]
            self.payload[s, :, width:] = jnp.broadcast_to(keep, (rows, LANES))
        for d, to, _ in self.peers():
            self.move(self.payload, self.spread, d, to, self.to_sems, self.from_sems).start()
        self.spread[self.me] = self.payload[self.me]

    def scan(self):
        for d, to, _ in self.peers():
            self.move(self.payload, self.spread, d, to, self.to_sems, self.from_sems).wait()
        width = self.scanned.shape[2]
        rows = self.scanned.shape[1]
        state = jnp.zeros((rows, width), f32)
        for step in range(self.n):
            at = self.n - 1 - step if self.reverse else step
            self.scanned[at] = state
            if step < self.n - 1:
                keep = expand(self.spread[at, :, width:], self.ex[:, :width])
                state = keep * state + self.spread[at, :, 0:width]
        for d, to, _ in self.peers():
            self.move(self.scanned, self.home, d, to, self.back_to, self.back_from).start()
        self.home[self.me] = self.scanned[self.me]

    def settle(self):
        for d, to, _ in self.peers():
            self.move(self.scanned, self.home, d, to, self.back_to, self.back_from).wait()
        for s in range(self.n):
            self.arr[s * self.per : (s + 1) * self.per] = self.home[s, 0 : self.per]
        leads, follows = self.leads, 1.0 - self.leads
        first = self.arr[...]
        second = expand(self.lead_k[...], self.ex[:, : first.shape[1]])[0:1] * first + self.lead[...]
        self.theirs[...] = leads * second + follows * first
        self.swap(self.theirs, self.last, 2).start()
        self.own[...] = leads * first + follows * second

    def close(self):
        self.swap(self.theirs, self.last, 2).wait()
        self.other[...] = self.last[...]


def pair_masks(x, lane_axis_shape):
    lane = lax.broadcasted_iota(jnp.int32, lane_axis_shape, 1)
    zero = jnp.zeros_like(x)
    return jnp.where(lane < HEAD_DIM, x, zero), jnp.where(lane >= HEAD_DIM, x, zero)


def intra_unit(val, bmat, cmat, age, pre, cum, dskip, part):
    t = lax.broadcasted_iota(jnp.int32, (HALF, HALF), 0)
    s = lax.broadcasted_iota(jnp.int32, (HALF, HALF), 1)
    scores = dot(cmat[...], bmat[...], 1, 1)
    a0, a1 = age[0:HALF], age[HALF:]
    gap = t - s
    s00 = jnp.where((gap >= 0) & (gap <= a0), scores[:HALF, :HALF], 0.0)
    s11 = jnp.where((gap >= 0) & (gap <= a1), scores[HALF:, HALF:], 0.0)
    s10 = jnp.where(gap + HALF <= a1, scores[HALF:, :HALF], 0.0)
    c2 = cum[...] * LOG2E
    rows = (c2 - jnp.log2(softplus(pre[...]))).T
    for j in range(val.shape[1] // LANES):
        cols = slice(j * LANES, (j + 1) * LANES)
        v = val[:, cols]
        vm = pair_masks(v, v.shape)
        tops, bottoms = [], []
        for which in range(2):
            h = 2 * j + which
            col0 = jnp.broadcast_to(c2[:HALF, h : h + 1], (HALF, HALF))
            col1 = jnp.broadcast_to(c2[HALF:, h : h + 1], (HALF, HALF))
            r0 = rows[h : h + 1, :HALF]
            r1 = rows[h : h + 1, HALF:]
            tops.append((s00 * jnp.exp2(jnp.minimum(col0 - r0, 60.0))).astype(bf16))
            bottoms.append((s10 * jnp.exp2(col1 - r0)).astype(bf16))
            bottoms.append((s11 * jnp.exp2(jnp.minimum(col1 - r1, 60.0))).astype(bf16))
        top = dot(jnp.concatenate(tops, axis=1), jnp.concatenate([vm[0][:HALF], vm[1][:HALF]], axis=0))
        bottom = dot(jnp.concatenate(bottoms, axis=1), jnp.concatenate([vm[0], vm[1]], axis=0))
        skip = dskip[6:7, cols]
        part[:HALF, cols] = top + skip * v[:HALF].astype(f32)
        part[HALF:, cols] = bottom + skip * v[HALF:].astype(f32)


def forward_kernel(
    n, parts, count, hid, tail_rows, edge_near, starts, bias_x, gain_x, head_vecs, gain_in, bias_maps, taps_x, dt_own, x_own, z_own, o_own, bc, taps_bc,
    tril, ex, cotangent,
    normed, ci_bc, age, ager, next_age, gain_out, x_near, x_far, x_far_near, z_near, z_far, z_far_near,
    o_near, o_far, o_far_near, cot_near, cot_across, cot_corner, co_bc, bmat, cmat, *refs,
):
    (ci_a, co_a, val_a, pre_a, cum_a, lin_a, kb_a, ck_a, par_a, dtp_a, own_a, other_a, part_a), refs = refs[:13], refs[13:]
    (ci_b, co_b, val_b, pre_b, cum_b, lin_b, kb_b, ck_b, par_b, dtp_b, own_b, other_b, part_b), refs = refs[:13], refs[13:]
    (
        gain, bias_bc, before, edge_far, small_s, small_n, small_f, small_fn, xn, xf, xfn,
        tot_a, tot_b, kout_a, kout_b, sems, cot_sems,
    ), refs = refs[:17], refs[17:]
    front, refs = refs[:8], refs[8:]
    z_weights = Weights(n, z_own, (z_near, z_far, z_far_near), refs[:4])
    o_weights = Weights(n, o_own, (o_near, o_far, o_far_near), refs[4:8])
    refs = refs[8:]
    size = len(refs) // 2
    states_a = Exchange(False, n, parts, (tot_a,), (kout_a,), ex, own_a, other_a, refs[:size])
    states_b = Exchange(False, n, parts, (tot_b,), (kout_b,), ex, own_b, other_b, refs[size:])
    cots = cot_copies(cotangent, (cot_near, cot_across, cot_corner), (1, 2, 3), parts, cot_sems)
    u = pl.program_id(0)
    s_me = lax.axis_index("seq")
    heads = head_peers()
    near, across = {"head": heads[1]}, {"head": heads[2]}
    half = lax.rem(heads[0], parts)
    batch = heads[0] // parts
    chunk = count * GROUP
    features = bc.shape[0]
    part = x_own.shape[1]
    nh = dt_own.shape[0]
    first = (s_me * parts + half) * chunk
    row = starts[0:1]
    for b in range(1, starts.shape[0]):
        row = jnp.where(batch == b, starts[b : b + 1], row)

    swap_x = send(x_own, xn, sems, 0, near)
    swap_small = send(small_s, small_n, sems, 1, near)
    cross_x = send(x_own, xf, sems, 2, across)
    cross_small = send(small_s, small_f, sems, 3, across)
    swap_far = send(xf, xfn, sems, 4, near)
    swap_small_far = send(small_f, small_fn, sems, 5, near)
    edge = send(tail_rows.at[0], edge_far, sems, 6, {"seq": lax.min(s_me + 1, n - 1)})

    @pl.when(u == 0)
    def _():
        small_s[...] = jnp.zeros_like(small_s)
        small_s[0:4, 0:part] = taps_x[...]
        for k in range(part // LANES):
            cols = slice(k * LANES, (k + 1) * LANES)
            small_s[4:5, cols] = bias_x[k : k + 1]
            small_s[5:6, cols] = gain_x[k : k + 1]
        small_s[6:7, 0:LANES] = head_vecs[...]
        small_s[8 : 8 + nh] = dt_own[...].astype(f32)
        for k in range(features // LANES):
            gain[0:1, k * LANES : (k + 1) * LANES] = gain_in[k : k + 1]
        for k in range(2):
            bias_bc[0:1, k * LANES : (k + 1) * LANES] = bias_maps[k : k + 1]
        gain_out[...] = jnp.broadcast_to(gain[0:1], gain_out.shape)
        edge_far[...] = jnp.zeros_like(edge_far)
        meet(heads[1:], n)
        swap_small.start()
        swap_x.start()
        pl.when(s_me < n - 1)(edge.start)
        cross_small.start()
        cross_x.start()
        next_age[...] = spread_ages(row, first + chunk, 8)

    rows = pl.ds(pl.multiple_of(lax.rem(u, count) * GROUP, GROUP), GROUP)

    @pl.when(u < count)
    def _():
        for r in range(0, GROUP, ROWS):
            at = pl.ds(pl.multiple_of(u * GROUP + r, ROWS), ROWS)
            normed[at] = rms(hid[0, r : r + ROWS], gain[0:1])
        ci_bc[rows] = dot(normed[rows], bc[...]).astype(bf16)
        a = spread_ages(row, first + u * GROUP, GROUP)
        age[rows] = a
        ager[...] = a.astype(f32).T[0:8].astype(jnp.int32)

    @pl.when(u == count)
    def _():
        swap_small.wait()
        swap_x.wait()
        pl.when(s_me < n - 1)(edge.wait_send)
        pl.when(s_me > 0)(edge.wait_recv)
        local = half.astype(f32)
        near_rows = local * edge_near[0].astype(f32) + (1.0 - local) * edge_far[...].astype(f32)
        before[...] = rms(near_rows, gain[0:1])

    @pl.when(u == 2 * count - 1)
    def _():
        cross_small.wait()
        swap_small_far.start()
        cross_x.wait()
        swap_far.start()
        z_weights.begin()

    @pl.when(u == 2 * count)
    def _():
        states_a.begin()
        swap_small_far.wait()
        swap_far.wait()
        x_near[...] = xn[...]
        x_far[...] = xf[...]
        x_far_near[...] = xfn[...]

    pl.when(u == 2 * count + 1)(states_a.combine)

    @pl.when(u == 2 * count + 2)
    def _():
        z_weights.share()
        o_weights.begin()

    pl.when(u == 2 * count + 3)(states_a.scan)

    @pl.when(u == 3 * count)
    def _():
        states_b.begin()
        z_weights.back()
        for copy in cots:
            copy.start()

    @pl.when(u == 3 * count + 1)
    def _():
        states_b.combine()
        o_weights.share()

    pl.when(u == 3 * count + 2)(states_a.settle)
    pl.when(u == 3 * count + 4)(states_a.close)

    @pl.when(u == 5 * count - 3)
    def _():
        states_b.scan()
        o_weights.back()

    for which in range(2):
        lo = (which + 1) * count
        outs = (ci_a, co_a, val_a, pre_a, cum_a, lin_a, kb_a, ck_a, tot_a, kout_a, par_a, dtp_a)
        weights = (x_own, xn, small_s, small_n)
        maps_in, maps_out = (ci_bc.at[rows], bc, taps_bc, bias_bc), (co_bc, bmat.at[rows], cmat.at[rows])
        if which:
            outs = (ci_b, co_b, val_b, pre_b, cum_b, lin_b, kb_b, ck_b, tot_b, kout_b, par_b, dtp_b)
            weights = (xf, xfn, small_f, small_fn)
            maps_in, maps_out = (bmat.at[rows],), ()
        outs = outs[:2] + tuple(x.at[rows] for x in outs[2:5]) + outs[5:]

        @pl.when((u >= lo) & (u < lo + count))
        def _():
            front_step(
                which == 0, u - lo, normed.at[rows], before, *weights, age.at[rows], tril, ex,
                maps_in, *outs, maps_out, *front,
            )

    for which in range(2):
        lo = (which + 3) * count
        val, pre, cum, par, to = ((val_a, pre_a, cum_a, par_a, part_a), (val_b, pre_b, cum_b, par_b, part_b))[which]

        @pl.when((u >= lo) & (u < lo + count))
        def _():
            intra_unit(
                val.at[rows], bmat.at[rows], cmat.at[rows], age.at[rows], pre.at[rows], cum.at[rows], par, to
            )

    @pl.when(u == 5 * count - 1)
    def _():
        z_weights.finish()
        o_weights.finish()
        states_b.settle()
        for copy in cots:
            copy.wait()
        states_b.close()


def arriving_half(own, other, half=None):
    if half is None:
        return jnp.concatenate([own[...], other[...]], axis=1)
    part = own.shape[1] // 2
    cols = slice(half * part, (half + 1) * part)
    return jnp.concatenate([own[:, cols].astype(f32), other[:, cols].astype(f32)], axis=1)


def mid_kernel(
    meta, hid, normed, z0, z1, z2, z3, o0, o1, o2, o3, cot0, cot1, cot2, cot3, cmat, age, ex, red, par_a, par_b,
    part_a, part_b, val_a, val_b, cum_a, cum_b, lin_a, lin_b, kb_a, kb_b, ck_a, ck_b, arr_a, arr_other_a, arr_b, arr_other_b,
    pieces, hidc, nout, cotx, dssd, dgate, dcin, dkk_a, dkk_b,
    lout_a, lout_b, ka_a, ka_b, tot_a, tot_b, kout_a, kout_b, ggain, gskip,
    gate, dno, read, kx, ssd_s, sig_s, khi, klo, rhi, rlo, run_a, run_b, kept_a, kept_b, shuffle,
):
    i = pl.program_id(0)
    inner = nout.shape[1]
    width = inner // 2
    tiles = inner // LANES
    heads = width // HEAD_DIM
    quarter = inner // 4

    @pl.when(i == 0)
    def _():
        for ref in (run_a, run_b, ggain, gskip):
            ref[...] = jnp.zeros_like(ref)
        for ref in (kept_a, kept_b):
            ref[...] = jnp.ones_like(ref)

    me = meta[0]
    hidc[...] = hid[0]
    for k, cot in enumerate((cot0.at[0], cot1, cot2, cot3)):
        shuffle[me ^ k] = cot[...]
    cotan = jnp.concatenate([shuffle[0], shuffle[1], shuffle[2], shuffle[3]], axis=0).T
    cotx[...] = cotan
    states = []
    for half, (lin, kb, cum, arr, arr_other) in enumerate(
        ((lin_a, kb_a, cum_a, arr_a, arr_other_a), (lin_b, kb_b, cum_b, arr_b, arr_other_b))
    ):
        cols = slice(half * width, (half + 1) * width)
        hi, lo = split2(lin[0] + kb[0, 0:1] * arriving_half(arr, arr_other))
        states.append((hi, lo))
        read[:, cols] = dot(cmat[...], hi) + dot(cmat[...], lo)
        since = lax.broadcasted_iota(jnp.int32, age.shape, 0)
        kappa = jnp.where(age[...] > since, jnp.exp(cum[...]), 0.0)
        kx[:, cols] = expand(lanes_below(kappa, heads), ex[...])
    for k, (z, o) in enumerate(((z0, o0), (z1, o1), (z2, o2), (z3, o3))):
        cols = slice(k * quarter, (k + 1) * quarter)
        gate[:, cols] = dot(normed[...], z[...])
        dno[:, cols] = dot(cotan, o[...], 1, 1)

    gains = [
        (par_a if j < tiles // 2 else par_b)[5:6, (j * LANES) % width : (j * LANES) % width + LANES]
        for j in range(tiles)
    ]

    def rows_body(step, _):
        rows = pl.ds(pl.multiple_of(step * ROWS, ROWS), ROWS)
        squares = jnp.zeros((ROWS, LANES), f32)
        inners = jnp.zeros((ROWS, LANES), f32)
        for j in range(tiles):
            cols = slice(j * LANES, (j + 1) * LANES)
            part = part_a if j < tiles // 2 else part_b
            pcols = slice(cols.start % width, cols.start % width + LANES)
            ssd = part[rows, pcols] + kx[rows, cols] * read[rows, cols]
            g = gate[rows, cols]
            sig = sigmoid(g)
            gated = ssd * (g * sig)
            squares += gated * gated
            inners += gated * (dno[rows, cols] * gains[j])
            ssd_s[rows, cols] = ssd
            sig_s[rows, cols] = sig
        rg = lax.rsqrt(jnp.sum(squares, axis=1, keepdims=True) / inner + EPS)
        stat = rg * rg * (jnp.sum(inners, axis=1, keepdims=True) / inner)
        rg = jnp.broadcast_to(rg, (ROWS, LANES))
        stat = jnp.broadcast_to(stat, (ROWS, LANES))
        for j in range(tiles):
            cols = slice(j * LANES, (j + 1) * LANES)
            val = val_a if j < tiles // 2 else val_b
            pcols = slice(cols.start % width, cols.start % width + LANES)
            ssd, sig, g, d = ssd_s[rows, cols], sig_s[rows, cols], gate[rows, cols], dno[rows, cols]
            act = g * sig
            gated = ssd * act
            yhat = gated * rg
            nout[rows, cols] = (yhat * gains[j]).astype(bf16)
            ggain[:, cols] += fold8(d * yhat)
            dgated = rg * (d * gains[j] - gated * stat)
            low = (dgated * act).astype(bf16)
            dssd[rows, cols] = low
            dgate[rows, cols] = (dgated * ssd * (sig * (1.0 + g * (1.0 - sig)))).astype(bf16)
            dy = low.astype(f32)
            gskip[:, cols] += fold8(dy * val[rows, pcols].astype(f32))
            kd = kx[rows, cols] * dy
            khi[rows, cols], klo[rows, cols] = split2(kd)
            rhi[rows, cols], rlo[rows, cols] = split2(kd * read[rows, cols])
        return 0

    lax.fori_loop(0, GROUP // ROWS, rows_body, 0)
    out = hid[0].astype(f32)
    for k, o in enumerate((o0, o1, o2, o3)):
        out = out + dot(nout[:, k * quarter : (k + 1) * quarter], o[...])
    out = out.astype(bf16).T
    piece = out.shape[0] // 4
    for k in range(4):
        pieces[k] = out[k * piece : (k + 1) * piece]
    dc = None
    age_end = age[GROUP - 1 : GROUP]
    for half, (dkk, ck, cum, lout, ka, tot, kout, running, kept) in enumerate(
        (
            (dkk_a, ck_a, cum_a, lout_a, ka_a, tot_a, kout_a, run_a, kept_a),
            (dkk_b, ck_b, cum_b, lout_b, ka_b, tot_b, kout_b, run_b, kept_b),
        )
    ):
        cols = slice(half * width, (half + 1) * width)
        hi, lo = states[half]
        dkk[...] = dot(rhi[:, cols], red[...]) + dot(rlo[:, cols], red[...])
        term = dot(khi[:, cols], hi, 1, 1) + dot(khi[:, cols], lo, 1, 1) + dot(klo[:, cols], hi, 1, 1)
        dc = term if dc is None else dc + term
        own = dot(cmat[...], khi[:, cols], 0, 0) + dot(cmat[...], klo[:, cols], 0, 0)
        lout[0] = running[...]
        ka[0] = expand(lanes_below(kept[...], heads), ex[...])
        running[...] = ck[0, 0:1] * running[...] + own
        keep = jnp.where(age_end >= GROUP, jnp.exp(cum[GROUP - 1 : GROUP]), 0.0)
        kept[...] = lanes_below(jnp.broadcast_to(keep, (8, LANES)), heads) * kept[...]
        tot[...] = running[...]
        kout[...] = kept[...]
    dcin[...] = dc


def pairs_unit(val, dssd, bmat, cmat, ager, pre, cum, dvi, dbi, dci, rflow, cflow, rft):
    s = lax.broadcasted_iota(jnp.int32, (HALF, HALF), 0)
    t = lax.broadcasted_iota(jnp.int32, (HALF, HALF), 1)
    scores = dot(bmat[...], cmat[...], 1, 1)
    a0, a1 = ager[0:1, :HALF], ager[0:1, HALF:]
    gap = t - s
    m00 = (gap >= 0) & (gap <= a0)
    m11 = (gap >= 0) & (gap <= a1)
    m01 = gap + HALF <= a1
    s00 = jnp.where(m00, scores[:HALF, :HALF], 0.0)
    s11 = jnp.where(m11, scores[HALF:, HALF:], 0.0)
    s01 = jnp.where(m01, scores[:HALF, HALF:], 0.0)
    c2 = cum[...] * LOG2E
    cr = c2 - jnp.log2(softplus(pre[...]))
    c2t = c2.T
    lane = lax.broadcasted_iota(jnp.int32, (HALF, LANES), 1)
    zero = jnp.zeros((HALF, HALF), f32)
    d00, d01, d11 = zero, zero, zero
    cf0, cf1 = zero, zero
    rft[...] = jnp.zeros_like(rft)
    for j in range(val.shape[1] // LANES):
        cols = slice(j * LANES, (j + 1) * LANES)
        v = val[:, cols]
        dy = dssd[:, cols]
        vm = pair_masks(v, v.shape)
        dm = pair_masks(dy, dy.shape)
        tops, bottoms = [], []
        for which in range(2):
            h = 2 * j + which
            col0 = jnp.broadcast_to(cr[:HALF, h : h + 1], (HALF, HALF))
            col1 = jnp.broadcast_to(cr[HALF:, h : h + 1], (HALF, HALF))
            r0 = c2t[h : h + 1, :HALF]
            r1 = c2t[h : h + 1, HALF:]
            e00 = jnp.exp2(jnp.minimum(r0 - col0, 60.0))
            e01 = jnp.exp2(r1 - col0)
            e11 = jnp.exp2(jnp.minimum(r1 - col1, 60.0))
            tops.append((s00 * e00).astype(bf16))
            tops.append((s01 * e01).astype(bf16))
            bottoms.append((s11 * e11).astype(bf16))
            w0 = dot(vm[which][:HALF], dy, 1, 1)
            w1 = dot(vm[which][HALF:], dy[HALF:], 1, 1)
            de00 = w0[:, :HALF] * e00
            de01 = w0[:, HALF:] * e01
            de11 = w1 * e11
            d00 += de00
            d01 += de01
            d11 += de11
            f00 = de00 * s00
            f01 = de01 * s01
            f11 = de11 * s11
            rft[h : h + 1, :HALF] = jnp.sum(f00, axis=0, keepdims=True)
            rft[h : h + 1, HALF:] = jnp.sum(f01 + f11, axis=0, keepdims=True)
            cf0 = jnp.where(lane == h, jnp.sum(f00 + f01, axis=1, keepdims=True), cf0)
            cf1 = jnp.where(lane == h, jnp.sum(f11, axis=1, keepdims=True), cf1)
        dvi[:HALF, cols] = dot(jnp.concatenate(tops, axis=1), jnp.concatenate([dm[0], dm[1]], axis=0))
        dvi[HALF:, cols] = dot(
            jnp.concatenate(bottoms, axis=1), jnp.concatenate([dm[0][HALF:], dm[1][HALF:]], axis=0)
        )
    cflow[:HALF] = cf0
    cflow[HALF:] = cf1
    rflow[...] = rft[...].T
    d00 = split2(jnp.where(m00, d00, 0.0))
    d01 = split2(jnp.where(m01, d01, 0.0))
    d11 = split2(jnp.where(m11, d11, 0.0))
    b0, b1, c0, c1 = bmat[:HALF], bmat[HALF:], cmat[:HALF], cmat[HALF:]
    dbi[:HALF] = dot(d00[0], c0) + dot(d00[1], c0) + dot(d01[0], c1) + dot(d01[1], c1)
    dbi[HALF:] = dot(d11[0], c1) + dot(d11[1], c1)
    dci[:HALF] = dot(d00[0], b0, 0, 0) + dot(d00[1], b0, 0, 0)
    dci[HALF:] = (
        dot(d01[0], b0, 0, 0) + dot(d01[1], b0, 0, 0) + dot(d11[0], b1, 0, 0) + dot(d11[1], b1, 0, 0)
    )


def outer_kernel(
    n, parts, count, tiles, normed, cotx, dgate, nout,
    val_a, val_b, dssd, bmat, cmat, ager, pre_a, pre_b, cum_a, cum_b, tot_a, tot_b, k_a, k_b, ex,
    dvi_a, dbi_a, dci_a, rflow_a, cflow_a, dvi_b, dbi_b, dci_b, rflow_b, cflow_b, own, other, share, zo,
    rft, keep, send, got, far_out, far_in, sems, *scratch
):
    u = pl.program_id(0)
    v = u - 4 * tiles
    states = Exchange(True, n, parts, (tot_a, tot_b), (k_a, k_b), ex, own, other, scratch[5:])
    sums = PairScatter(n, scratch[:5])
    share_rows = zo.shape[0] // n
    across = lax.rem(lax.axis_index("head") + 2, 4)

    def trade(src, dst, sem, head):
        return pltpu.make_async_remote_copy(
            src_ref=src,
            dst_ref=dst,
            send_sem=sems.at[0, sem],
            recv_sem=sems.at[1, sem],
            device_id={"head": head},
            device_id_type=MESH,
        )

    def swap(half, m):
        return trade(send.at[half, m], got.at[half, m], 2 * half + m, states.partner)

    def cross(m):
        return trade(far_out.at[m], far_in.at[m], 4 + m, across)

    def cross_after(m):
        swap(0, m).wait()
        far_out[m] = (keep[0, m] + got[0, m].astype(f32)).astype(bf16)
        cross(m).start()

    @pl.when(u == 0)
    def _():
        meet([states.partner, across], n)
        states.begin()


    @pl.when(u == tiles)
    def _():
        swap(0, 0).start()

    @pl.when(u == 2 * tiles)
    def _():
        swap(0, 1).start()
        cross_after(0)

    @pl.when(u == 3 * tiles)
    def _():
        swap(1, 0).start()
        cross_after(1)

    @pl.when(v == 0)
    def _():
        swap(1, 1).start()
        states.scan()

    part = keep.shape[3]
    rows = pl.ds(pl.multiple_of(lax.rem(u, tiles) * GROUP, GROUP), GROUP)
    for m, (a, b) in enumerate(((normed, dgate), (cotx, nout))):

        @pl.when((v < 0) & (lax.rem(u // tiles, 2) == m))
        def _():
            res = dot(a[...], b[...], 0, 0)
            half = u // (2 * tiles)
            keep[half, m, rows] = res[:, :part]
            send[half, m, rows] = res[:, part:].astype(bf16)

    @pl.when((v >= 0) & (v < count))
    def _():
        pairs_unit(val_a, dssd, bmat, cmat, ager, pre_a, cum_a, dvi_a, dbi_a, dci_a, rflow_a, cflow_a, rft)

    @pl.when(v >= count)
    def _():
        pairs_unit(val_b, dssd, bmat, cmat, ager, pre_b, cum_b, dvi_b, dbi_b, dci_b, rflow_b, cflow_b, rft)

    pl.when(u == 1)(states.combine)

    pl.when(v == 2 * count - 3)(sums.middle)

    @pl.when(v == count - 2)
    def _():
        swap(1, 0).wait()
        cross(0).wait()

        def total(s):
            at = slice(s * share_rows, (s + 1) * share_rows)
            return keep[1, 0, at] + got[1, 0, at].astype(f32) + far_in[0, at].astype(f32)

        sums.start(total)

    @pl.when(v == 2 * count - 1)
    def _():
        states.settle()
        states.close()
        swap(1, 1).wait()
        cross(1).wait()
        zo[...] = (keep[1, 1] + got[1, 1].astype(f32) + far_in[1].astype(f32)).astype(bf16)
        share[...] = sums.finish()


def slope(x):
    sig = sigmoid(x)
    return sig * (1.0 + x * (1.0 - sig))


def conv_back(i, dco, agex, age, ci, taps, dci, tail, head, gw):
    width = ci.shape[1]
    for r in range(0, GROUP, ROWS):
        ages = [agex[r + m : r + m + ROWS] for m in range(4)]
        for j in range(width // LANES):
            cols = slice(j * LANES, (j + 1) * LANES)
            c = ci[r : r + ROWS, cols].astype(f32)
            acc = None
            for m in range(4):
                x = dco[r + m : r + m + ROWS, cols]
                if m:
                    x = jnp.where(ages[m] >= m, x, 0.0)
                term = x * taps[3 - m : 4 - m, cols]
                acc = term if acc is None else acc + term
                gw[8 * (3 - m) : 8 * (3 - m) + 8, cols] += fold8(x * c)
            dci[r : r + ROWS, cols] = acc.astype(bf16)
            if r == GROUP - ROWS:

                @pl.when(i == 0)
                def _():
                    tail[:, cols] = acc[ROWS - 8 :]

    head[...] = dco[0:8]


def start_next(i, dco, agex, gw, gb):
    @pl.when(i == 0)
    def _():
        dco[GROUP : GROUP + 8] = jnp.zeros((8, dco.shape[1]), f32)
        agex[GROUP : GROUP + 8] = jnp.zeros((8, LANES), jnp.int32)
        gw[...] = jnp.zeros_like(gw)
        gb[...] = jnp.zeros_like(gb)

    @pl.when(i > 0)
    def _():
        dco[GROUP : GROUP + 8] = dco[0:8]
        agex[GROUP : GROUP + 8] = agex[0:8]


def back_step(
    half, i, val, dssd, dvi, bmat, co, ci, age, pre, cum, lout, ka, leav, leav_other, lin, kb, arr, arr_other,
    rflow, cflow, dkk, par, tril, ex, red,
    dci, tail, head, draw, gw, gb, galog, gdtb,
    dco, agex, back, omx, vhi, vlo,
):
    width = val.shape[1]
    heads = width // HEAD_DIM
    start_next(i, dco, agex, gw, gb)

    @pl.when(i == 0)
    def _():
        galog[...] = jnp.zeros_like(galog)
        gdtb[...] = jnp.zeros_like(gdtb)

    agex[0:GROUP] = age[...]
    ds = lout[0] + ka[0, 0:1] * arriving_half(leav, leav_other, half)
    dhi, dlo = split2(ds)
    back[...] = dot(bmat[...], dhi) + dot(bmat[...], dlo)
    p = pre[...]
    delta = softplus(p)
    c = cum[...]
    end = c[GROUP - 1 : GROUP]
    age_end = age[GROUP - 1 : GROUP]
    row = lax.broadcasted_iota(jnp.int32, c.shape, 0)
    tail_keep = jnp.where(GROUP - 1 - row <= age_end, jnp.exp(end - c), 0.0)
    omega = tail_keep * delta
    omx[...] = expand(lanes_below(omega, heads), ex[...])
    for r in range(0, GROUP, ROWS):
        rows = slice(r, r + ROWS)
        for j in range(width // LANES):
            cols = slice(j * LANES, (j + 1) * LANES)
            v = val[rows, cols].astype(f32)
            b = back[rows, cols]
            o = omx[rows, cols]
            dval = par[6:7, cols] * dssd[rows, cols].astype(f32) + dvi[rows, cols] + o * b
            vhi[rows, cols], vlo[rows, cols] = split2(v * b)
            d = dval * slope(co[rows, cols])
            dco[rows, cols] = d
            gb[:, cols] += fold8(d)
    domega = dot(vhi[...], red[...]) + dot(vlo[...], red[...])
    flow = domega * omega
    sin = lin[0] + kb[0, 0:1] * arriving_half(arr, arr_other)
    carry = jnp.broadcast_to(jnp.sum(ds * sin, axis=0, keepdims=True), (8, width))
    carry = dot(carry, red[...].astype(f32), precision=HIGHEST)[0:1]
    keep = jnp.where(age_end >= GROUP, jnp.exp(end), 0.0)
    dcum = rflow[...] - cflow[...] + dkk[...] - flow
    ending = jnp.sum(flow, axis=0, keepdims=True) + carry * keep
    dcum = dcum + jnp.where(row == GROUP - 1, ending, 0.0)
    dlog = dot(tril[...], dcum, 0, 0, precision=HIGHEST)
    sig = sigmoid(p)
    ratio = jnp.where(delta > 1e-30, sig / delta, 1.0)
    rate = par[7:8, 0:LANES]
    drf = cflow[...] * ratio + (domega * tail_keep + dlog * rate) * sig
    drf = lanes_below(drf, heads)
    draw[...] = drf.astype(bf16)
    gdtb[...] += fold8(drf)
    galog[...] += fold8(dlog * delta * rate)
    conv_back(i, dco, agex, age, ci, par, dci, tail, head, gw)


def maps_step(
    i, dbi_a, dbi_b, dci_a, dci_b, dcin, co, ci, age, taps,
    val_a, val_b, pre_a, pre_b, cum_a, cum_b, lout_a, lout_b, ka_a, ka_b, leav, leav_other, ex,
    dci, tail, head, gw, gb, dco, agex, dbin,
):
    start_next(i, dco, agex, gw, gb)
    agex[0:GROUP] = age[...]
    age_end = age[GROUP - 1 : GROUP]
    width = val_a.shape[1]
    row = lax.broadcasted_iota(jnp.int32, (GROUP, LANES), 0)
    total = dbi_a[...] + dbi_b[...]
    for half, (val, pre, cum, lout, ka) in enumerate(
        ((val_a, pre_a, cum_a, lout_a, ka_a), (val_b, pre_b, cum_b, lout_b, ka_b))
    ):
        dhi, dlo = split2(lout[0] + ka[0, 0:1] * arriving_half(leav, leav_other, half))
        c = cum[...]
        tail_keep = jnp.where(GROUP - 1 - row <= age_end, jnp.exp(c[GROUP - 1 : GROUP] - c), 0.0)
        omx = expand(lanes_below(tail_keep * softplus(pre[...]), width // HEAD_DIM), ex[...])
        ohi, olo = split2(omx * val[...].astype(f32))
        total = total + dot(ohi, dhi, 1, 1) + dot(ohi, dlo, 1, 1) + dot(olo, dhi, 1, 1)
    dbin[...] = total
    for r in range(0, GROUP, ROWS):
        rows = slice(r, r + ROWS)
        dc = dci_a[rows] + dci_b[rows] + dcin[rows]
        for j, d in enumerate((dbin[rows], dc)):
            cols = slice(j * LANES, (j + 1) * LANES)
            d = d * slope(co[rows, cols])
            dco[rows, cols] = d
            gb[:, cols] += fold8(d)
    conv_back(i, dco, agex, age, ci, taps, dci, tail, head, gw)


def mended(x, last, scr):
    scr[...] = x[...]

    @pl.when(pl.program_id(0) == pl.num_programs(0) - 1)
    def _():
        scr[GROUP - 16 :] = last[...]

    return scr


def padded_rows(x, rows):
    if x.shape[0] == rows:
        return x
    return jnp.concatenate([x, jnp.zeros((rows - x.shape[0], x.shape[1]), x.dtype)], axis=0)


def up16(rows):
    return (rows + 15) // 16 * 16


class Scatter:
    def __init__(self, n, scratch):
        self.n, self.me = n, lax.axis_index("seq")
        self.out, self.got, self.sems = scratch

    @staticmethod
    def scratch(n, rows, cols):
        pad = up16(rows)
        return [
            pltpu.VMEM((n, pad, cols), bf16),
            pltpu.VMEM((n, pad, cols), bf16),
            pltpu.SemaphoreType.DMA((2, n)),
        ]

    def move(self, d):
        to = lax.rem(self.me + d, self.n)
        return pltpu.make_async_remote_copy(
            src_ref=self.out.at[to],
            dst_ref=self.got.at[self.me],
            send_sem=self.sems.at[0, d],
            recv_sem=self.sems.at[1, d],
            device_id={"seq": to},
            device_id_type=MESH,
        )

    def start(self, share):
        for s in range(self.n):
            self.out[s] = padded_rows(share(s), self.out.shape[1]).astype(bf16)
        for d in range(1, self.n):
            self.move(d).start()
        self.got[self.me] = self.out[self.me]

    def finish(self):
        return self.finish_f32().astype(bf16)

    def finish_f32(self):
        for d in range(1, self.n):
            self.move(d).wait()
        total = self.got[0].astype(f32)
        for s in range(1, self.n):
            total = total + self.got[s].astype(f32)
        return total


class Gather:
    def __init__(self, n, scratch):
        self.n, self.me = n, lax.axis_index("seq")
        self.mine, self.all, self.sems = scratch

    @staticmethod
    def scratch(n, rows, cols):
        pad = up16(rows)
        return [
            pltpu.VMEM((pad, cols), bf16),
            pltpu.VMEM((n, pad, cols), bf16),
            pltpu.SemaphoreType.DMA((2, n)),
        ]

    def move(self, d):
        return pltpu.make_async_remote_copy(
            src_ref=self.mine,
            dst_ref=self.all.at[self.me],
            send_sem=self.sems.at[0, d],
            recv_sem=self.sems.at[1, d],
            device_id={"seq": lax.rem(self.me + d, self.n)},
            device_id_type=MESH,
        )

    def start(self, share):
        self.mine[...] = share
        for d in range(1, self.n):
            self.move(d).start()
        self.all[self.me] = share

    def finish(self):
        for d in range(1, self.n):
            self.move(d).wait()

    def rows(self, s, count):
        return self.all[s].astype(f32)[:count]


class PairScatter:
    def __init__(self, n, scratch):
        me = lax.axis_index("seq")
        self.n, self.m, self.odd, self.at = n, n // 2, lax.rem(me, 2), me // 2
        self.partner = me + 1 - 2 * self.odd
        self.out, self.near, self.part, self.got, self.sems = scratch

    @staticmethod
    def scratch(n, rows, cols):
        pad, m = up16(rows), n // 2
        return [
            pltpu.VMEM((2, m, pad, cols), bf16),
            pltpu.VMEM((m, pad, cols), bf16),
            pltpu.VMEM((m, pad, cols), bf16),
            pltpu.VMEM((m, pad, cols), bf16),
            pltpu.SemaphoreType.DMA((2, m)),
        ]

    def move(self, d):
        if d == 0:
            src, dst, to = self.out.at[1 - self.odd], self.near, self.partner
        else:
            to = lax.rem(self.at + d, self.m)
            src, dst, to = self.part.at[to], self.got.at[self.at], 2 * to + self.odd
        return pltpu.make_async_remote_copy(
            src_ref=src,
            dst_ref=dst,
            send_sem=self.sems.at[0, d],
            recv_sem=self.sems.at[1, d],
            device_id={"seq": to},
            device_id_type=MESH,
        )

    def start(self, share):
        for s in range(self.n):
            self.out[s % 2, s // 2] = padded_rows(share(s), self.near.shape[1]).astype(bf16)
        self.move(0).start()

    def middle(self):
        self.move(0).wait()
        for k in range(self.m):
            self.part[k] = (self.out[self.odd, k].astype(f32) + self.near[k].astype(f32)).astype(bf16)
        for d in range(1, self.m):
            self.move(d).start()
        self.got[self.at] = self.part[self.at]

    def finish(self):
        for d in range(1, self.m):
            self.move(d).wait()
        total = self.got[0].astype(f32)
        for k in range(1, self.m):
            total = total + self.got[k].astype(f32)
        return total.astype(bf16)


class PairGather:
    def __init__(self, n, scratch):
        me = lax.axis_index("seq")
        self.n, self.m, self.odd, self.at = n, n // 2, lax.rem(me, 2), me // 2
        self.partner = me + 1 - 2 * self.odd
        self.mine, self.all, self.sems = scratch

    @staticmethod
    def scratch(n, rows, cols):
        pad, m = up16(rows), n // 2
        return [
            pltpu.VMEM((pad, cols), bf16),
            pltpu.VMEM((2, m, pad, cols), bf16),
            pltpu.SemaphoreType.DMA((2, m)),
        ]

    def move(self, d):
        if d == 0:
            src, dst, to = self.all.at[self.odd], self.all.at[self.odd], self.partner
        else:
            src, dst = self.mine, self.all.at[self.odd, self.at]
            to = 2 * lax.rem(self.at + d, self.m) + self.odd
        return pltpu.make_async_remote_copy(
            src_ref=src,
            dst_ref=dst,
            send_sem=self.sems.at[0, d],
            recv_sem=self.sems.at[1, d],
            device_id={"seq": to},
            device_id_type=MESH,
        )

    def start(self, share):
        self.mine[...] = share
        for d in range(1, self.m):
            self.move(d).start()
        self.all[self.odd, self.at] = share

    def middle(self):
        for d in range(1, self.m):
            self.move(d).wait()
        self.move(0).start()

    def finish(self):
        self.move(0).wait()

    def rows(self, s, count):
        return self.all[s % 2, s // 2].astype(f32)[:count]


def mend(got, tail, ci, next_age, taps, dx, scr, last, flip):
    g = got[...]
    if flip:
        part = g.shape[1] // 2
        g = jnp.concatenate([g[:, part:], g[:, :part]], axis=1)
    rows = scr.shape[0]
    if dx is not None:
        scr[...] = dx[...]
    ending = ci[...].astype(f32)[8:16]
    row = lax.broadcasted_iota(jnp.int32, (8, LANES), 0)
    fixed, sums = [], []
    for j in range(g.shape[1] // LANES):
        cols = slice(j * LANES, (j + 1) * LANES)
        acc = tail[:, cols]
        parts = [jnp.zeros((1, LANES), f32)] * 4
        for m in range(1, 4):
            use = (row >= 8 - m) & (pltpu.roll(next_age[...], 8 - m, 0) >= m)
            x = jnp.where(use, pltpu.roll(g[:, cols], 8 - m, 0), 0.0)
            acc = acc + x * taps[3 - m : 4 - m, cols]
            parts[3 - m] = jnp.sum(x * ending[:, cols], axis=0, keepdims=True)
        fixed.append(acc)
        sums.append(jnp.concatenate(parts, axis=0))
    fixed = jnp.concatenate(fixed, axis=1)
    before = scr[rows - 16 :].astype(f32)[0:8]
    scr[rows - 16 :] = jnp.concatenate([before, fixed], axis=0).astype(bf16)
    if last is not None:
        last[...] = scr[rows - 16 :]
    return jnp.concatenate(sums, axis=1)


def small_sums(at, fix, gw, gb, galog, gdtb, gskip, ggain, red, small_keep, small_send):
    part = red.shape[0] // 2
    heads = part // HEAD_DIM
    width = 2 * part
    for to in (small_keep, small_send):
        to[...] = jnp.zeros_like(to)
    taps = [jnp.sum(gw[8 * k : 8 * k + 8], axis=0, keepdims=True) for k in range(4)]
    taps = jnp.concatenate(taps, axis=0) + fix
    bias = jnp.sum(gb[...], axis=0, keepdims=True)
    cols = slice(at * width, (at + 1) * width)
    gain = jnp.sum(ggain[:, cols], axis=0, keepdims=True)
    skip = jnp.broadcast_to(jnp.sum(gskip[:, cols], axis=0, keepdims=True), (8, width))
    skip = dot(skip, red[...].astype(f32), precision=HIGHEST)
    step = jnp.broadcast_to(jnp.sum(gdtb[...], axis=0, keepdims=True), (8, LANES))
    log = jnp.broadcast_to(jnp.sum(galog[...], axis=0, keepdims=True), (8, LANES))
    for k, to in enumerate((small_keep, small_send)):
        mine = slice(k * part, (k + 1) * part)
        to[0:4, 0:part] = taps[:, mine]
        to[4:5, 0:part] = bias[:, mine]
        to[5:6, 0:part] = gain[:, mine]
        row = jnp.zeros((8, LANES), f32)
        for place, x in enumerate((step, log, skip)):
            x = lanes_below(pltpu.roll(x, (LANES - k * heads) % LANES, 1), heads)
            row = row + pltpu.roll(x, place * heads, 1)
        to[6:7, 0:LANES] = row[0:1]


def half_tile(tile, normed, dx, draw, keep, send, small_keep, small_send):
    part = keep.shape[1]
    heads = part // HEAD_DIM
    res = dot(normed[...], dx[...], 0, 0)
    keep[...] = res[:, :part]
    send[...] = res[:, part:].astype(bf16)
    dt = dot(draw[...], normed[...], 0, 0)
    cols = pl.ds(pl.multiple_of(tile * GROUP, GROUP), GROUP)
    small_keep[8:16, cols] = dt[0:8]
    small_send[8:16, cols] = pltpu.roll(dt, LANES - heads, 0)[0:8]


def turn_kernel(n, parts, count, *refs):
    maps_in, refs = refs[:22], refs[22:]
    back_in, refs = refs[:24], refs[24:]
    (own, share, pieces), refs = refs[:3], refs[3:]
    maps_out, refs = refs[:5], refs[5:]
    back_out, refs = refs[:8], refs[8:]
    (share_out, gathered, placed), refs = refs[:3], refs[3:]
    maps_scr, refs = refs[:3], refs[3:]
    back_scr, refs = refs[:6], refs[6:]
    (piece_sems,), refs = refs[:1], refs[1:]
    u = pl.program_id(0)
    sums, shares = PairScatter(n, refs[:5]), PairGather(n, refs[5:])
    rows = own.shape[0] // n
    me = lax.axis_index("seq")
    head = lax.axis_index("head")
    near = head + 1 - 2 * lax.rem(head, 2)
    heads = [head, near, lax.rem(head + 2, 4), lax.rem(near + 2, 4)]
    chunk = pieces.shape[2]

    def piece_copy(k):
        cols = pl.ds(pl.multiple_of(lax.rem(head, parts) * chunk, chunk), chunk)
        src, dst = pieces.at[heads[k]], placed.at[head // parts, :, cols]
        if k == 0:
            return pltpu.make_async_copy(src, dst, piece_sems.at[0, 0])
        return pltpu.make_async_remote_copy(
            src_ref=src,
            dst_ref=dst,
            send_sem=piece_sems.at[0, k],
            recv_sem=piece_sems.at[1, k],
            device_id={"head": heads[k]},
            device_id_type=MESH,
        )

    @pl.when(u == 0)
    def _():
        barrier = pltpu.get_barrier_semaphore()
        for k in range(1, 4):
            pl.semaphore_signal(barrier, inc=1, device_id={"head": heads[k]}, device_id_type=MESH)
        for d in range(1, n):
            pl.semaphore_signal(barrier, inc=1, device_id={"seq": lax.rem(me + d, n)}, device_id_type=MESH)
        pl.semaphore_wait(barrier, n + 2)
        shares.start(share[...])
        sums.start(lambda s: own[s * rows : (s + 1) * rows].astype(f32))
        for k in (2, 3, 1, 0):
            piece_copy(k).start()

    @pl.when(u < count)
    def _():
        maps_step(u, *maps_in, *maps_out, *maps_scr)

    @pl.when(u >= count)
    def _():
        back_step(1, u - count, *back_in, *back_out, *back_scr)

    @pl.when(u == count - 1)
    def _():
        sums.middle()
        shares.middle()

    @pl.when(u == 2 * count - 1)
    def _():
        share_out[...] = sums.finish()
        shares.finish()
        for s in range(n):
            gathered[s * rows : (s + 1) * rows] = shares.rows(s, rows)
        for k in range(4):
            piece_copy(k).wait()


def late_kernel(n, parts, count, tiles, *refs):
    back_in, refs = refs[:24], refs[24:]
    (
        normed, dx_b, tail_b, head_b, ci_b, par_b, draw_b, gw_b, gb_b, galog_b, gdtb_b,
        dbc, tail_bc, head_bc, ci_bc, taps_bc, gw_bc, gb_bc, ci_a, next_age, gskip, ggain_out, share,
    ), refs = refs[:23], refs[23:]
    (hid, cotx, gain, dgate, z0, z1, z2, z3, bcw, x0, x1, x2, x3, dt_a, dt_b), refs = refs[:15], refs[15:]
    (grad_in, gx, gbc, small, grad_out), refs = refs[:5], refs[5:]
    back_scr, refs = refs[:6], refs[6:]
    (
        dx_a, draw_a, keep_a, send_a, small_a, small_send_a, got_a, small_got_a, last,
        tail_a, head_a, gw_a, gb_a, galog_a, gdtb_a, scr_b, scr_bc, keep_b, send_b, got_b, far_out,
        small_b, small_send_b, small_got, small_out, small_in, far_in, edge_b, edge_bc, edge_a,
        g_bc, bc_out, bc_got, bc_far_out, bc_far, bc_own, small_bc, com_got, bc_heads,
        acc_s, low, shuffle, landed, ggain, gi_got, gi_sum, edge_sems, sems, piece_sems,
    ), refs = refs[:49], refs[49:]
    u = pl.program_id(0)
    par_a, red = back_in[20], back_in[23]
    s_me = lax.axis_index("seq")
    heads = head_peers()
    h_me, near, across = heads[:3]
    half = lax.rem(h_me, parts)
    to_seq = s_me - 1 + half
    has_before = to_seq >= 0
    has_after = s_me + half < n
    chunk = count * GROUP
    part = keep_a.shape[1]
    features = gain.shape[1]
    lane_tiles = features // LANES
    first_bc, first_b, first_back, first_a = 1, tiles + 1, 2 * tiles + 1, 2 * tiles + count
    first_out = first_a + tiles
    pack_rows = -(-24 // n)
    pack = up16(4 * pack_rows + 4)
    bc_rows = features // 4
    share_rows = bc_rows // n
    gathered, gx_sum, gx_all = PairGather(n, refs[:3]), Scatter(n, refs[3:6]), Gather(n, refs[6:9])
    bc_sum, bc_all = Scatter(n, refs[9:12]), Gather(n, refs[12:15])

    def trade(src, dst, sem, head):
        return send(src, dst, sems, sem, {"head": head})

    def edge(k):
        src, dst = ((head_b, edge_b), (head_bc, edge_bc), (head_a, edge_a))[k]
        return send(src, dst, edge_sems, k, {"seq": lax.max(to_seq, 0), "head": near})

    def send_edge(k):
        pl.when(has_before)(edge(k).start)

    def take_edge(k):
        pl.when(has_before)(edge(k).wait_send)
        pl.when(has_after)(edge(k).wait_recv)

    swap_b = trade(send_b, got_b, 0, near)
    swap_small = trade(small_send_b, small_got, 1, near)
    cross_b = trade(far_out, far_in, 2, across)
    cross_small = trade(small_out, small_in, 3, across)
    swap_a = trade(send_a, got_a, 4, near)
    swap_small_a = trade(small_send_a, small_got_a, 5, near)

    swap_bc = trade(bc_out, bc_got, 6, near)
    cross_bc = trade(bc_far_out, bc_far, 7, across)

    def bc_quarter(k):
        return g_bc[pl.ds(pl.multiple_of(heads[k] * bc_rows, 8), bc_rows)]

    def common_trade(k):
        return trade(small_bc, com_got.at[k], 8 + k, heads[k])

    def heads_trade(k):
        return trade(bc_all.all, bc_heads.at[h_me], 11 + k, heads[k])

    def gi_trade(k):
        return trade(gi_sum, gi_got.at[k], 14 + k, heads[k])

    def piece_copy(step, k):
        return pltpu.make_async_remote_copy(
            src_ref=shuffle.at[step, heads[k]],
            dst_ref=landed.at[step, k],
            send_sem=piece_sems.at[0, step, k],
            recv_sem=piece_sems.at[1, step, k],
            device_id={"head": heads[k]},
            device_id_type=MESH,
        )

    def place(step, k):
        cols = pl.ds(pl.multiple_of(lax.rem(heads[k], parts) * chunk + step * GROUP, GROUP), GROUP)
        grad_in[heads[k] // parts, :, cols] = landed[step, k] if k else shuffle[step, h_me]

    @pl.when(u == 0)
    def _():
        for to in (edge_b, edge_bc, edge_a, ggain, gi_sum):
            to[...] = jnp.zeros_like(to)
        barrier = pltpu.get_barrier_semaphore()
        for head in heads[1:]:
            pl.semaphore_signal(barrier, inc=1, device_id={"head": head}, device_id_type=MESH)
        for d in range(1, n):
            pl.semaphore_signal(barrier, inc=1, device_id={"seq": lax.rem(s_me + d, n)}, device_id_type=MESH)
        other_seq = s_me - 1 + 2 * half
        has_other = (other_seq >= 0) & (other_seq < n)

        @pl.when(has_other)
        def _():
            pl.semaphore_signal(
                barrier, inc=1, device_id={"seq": other_seq, "head": near}, device_id_type=MESH
            )

        pl.semaphore_wait(barrier, n + 2 + has_other.astype(jnp.int32))
        send_edge(0)
        send_edge(1)
        gathered.start(share[...])

    block = jnp.clip(u - 2 * tiles, 0, count - 1)

    @pl.when((u == 0) | ((u >= first_back) & (u < first_a)))
    def _():
        rows = pl.ds(pl.multiple_of((count - 1 - block) * GROUP, GROUP), GROUP)
        outs = (dx_a.at[rows], tail_a, head_a, draw_a.at[rows], gw_a, gb_a, galog_a, gdtb_a)
        back_step(0, block, *back_in, *outs, *back_scr)

    @pl.when(u == first_bc)
    def _():
        take_edge(1)
        fix = mend(edge_bc, tail_bc, ci_bc, next_age, taps_bc, dbc, scr_bc, None, False)
        small_bc[...] = jnp.zeros_like(small_bc)
        sums = [jnp.sum(gw_bc[8 * k : 8 * k + 8], axis=0, keepdims=True) for k in range(4)]
        small_bc[0:4] = jnp.concatenate(sums, axis=0) + fix
        small_bc[4:5] = jnp.sum(gb_bc[...], axis=0, keepdims=True)
        for k in range(1, 4):
            common_trade(k).start()

    @pl.when((u >= first_bc) & (u < first_b))
    def _():
        rows = pl.ds(pl.multiple_of((u - first_bc) * GROUP, GROUP), GROUP)
        g_bc[rows] = dot(normed[...], scr_bc[...], 0, 0)

    @pl.when(u == first_b)
    def _():
        bc_out[0] = bc_quarter(1).astype(bf16)
        bc_out[1] = bc_quarter(3).astype(bf16)
        swap_bc.start()
        take_edge(0)
        fix = mend(edge_b, tail_b, ci_b, next_age, par_b, dx_b, scr_b, None, True)
        small_sums(1, fix, gw_b, gb_b, galog_b, gdtb_b, gskip, ggain_out, red, small_b, small_send_b)

    @pl.when(u == first_b + 1)
    def _():
        swap_bc.wait()
        bc_far_out[...] = (bc_quarter(2) + bc_got[1].astype(f32)).astype(bf16)
        cross_bc.start()
        gathered.middle()

    @pl.when((u >= first_b) & (u < first_back))
    def _():
        rows = pl.ds(pl.multiple_of((u - first_b) * GROUP, GROUP), GROUP)
        half_tile(u - first_b, normed, scr_b, draw_b, keep_b.at[rows], send_b.at[rows], small_b, small_send_b)

    @pl.when(u == first_back)
    def _():
        swap_b.start()
        swap_small.start()
        cross_bc.wait()
        bc_own[...] = bc_quarter(0) + bc_got[0].astype(f32) + bc_far[...].astype(f32)
        bc_sum.start(lambda s: bc_own[s * share_rows : (s + 1) * share_rows])

    @pl.when(u == first_back + 1)
    def _():
        swap_b.wait()
        far_out[...] = (keep_b[...] + got_b[...].astype(f32)).astype(bf16)
        cross_b.start()
        swap_small.wait()
        small_out[...] = small_b[...] + small_got[...]
        cross_small.start()
        bc_all.start(bc_sum.finish())

    @pl.when(u == first_back + 2)
    def _():
        bc_all.finish()
        for k in range(1, 4):
            heads_trade(k).start()
        bc_heads[h_me] = bc_all.all[...]

    @pl.when(u == first_a)
    def _():
        send_edge(2)
        gathered.finish()
        rows = grad_out.shape[1] // n
        grad_out[...] = jnp.concatenate([gathered.rows(s, rows) for s in range(n)], axis=0).T
        take_edge(2)
        fix = mend(edge_a, tail_a, ci_a, next_age, par_a, None, dx_a, None, True)
        small_sums(0, fix, gw_a, gb_a, galog_a, gdtb_a, gskip, ggain_out, red, small_a, small_send_a)

    @pl.when((u >= first_a) & (u < first_out))
    def _():
        rows = pl.ds(pl.multiple_of((u - first_a) * GROUP, GROUP), GROUP)
        half_tile(u - first_a, normed, dx_a, draw_a, keep_a.at[rows], send_a.at[rows], small_a, small_send_a)

    def halves_of(x):
        x = jnp.concatenate([x[:, :part], x[:, part:]], axis=0)
        hi = x.astype(bf16).astype(f32)
        return jnp.concatenate([hi, x - hi], axis=0)

    def joined(x, rows):
        x = x[0 : 2 * rows] + x[2 * rows : 4 * rows]
        return jnp.concatenate([x[:rows], x[rows:]], axis=1)

    @pl.when(u == first_out - 1)
    def _():
        swap_a.start()
        swap_small_a.start()

    @pl.when(u == first_out)
    def _():
        cross_small.wait()
        both = small_bc[...]
        for k in range(1, 4):
            common_trade(k).wait()
            both = both + com_got[k]
        both = jnp.concatenate([both, jnp.zeros((8, features - 2 * LANES), f32)], axis=1)
        cross_b.wait()
        swap_small_a.wait()
        both = jnp.concatenate([small_a[...] + small_got_a[...] + small_in[...], both], axis=0)
        swap_a.wait()
        rows = features // n

        def gx_share(s):
            at = slice(s * rows, (s + 1) * rows)
            x = keep_a[at] + got_a[at].astype(f32) + far_in[at].astype(f32)
            if s * pack_rows < 24:
                x = jnp.concatenate([x, halves_of(both[s * pack_rows : (s + 1) * pack_rows])], axis=0)
            return x

        gx_sum.start(gx_share)

    @pl.when(u >= first_out)
    def _():
        step = u - first_out
        at = pl.ds(pl.multiple_of(step * GROUP, GROUP), GROUP)
        acc = dot(scr_bc[at], bcw[...], 1, 1) + dot(draw_a[at], dt_a[...]) + dot(draw_b[at], dt_b[...])
        for k, (z, x) in enumerate(((z0, x0), (z1, x1), (z2, x2), (z3, x3))):
            d, col = (dx_a if k < 2 else scr_b), (k % 2) * part
            acc = acc + dot(dgate[:, k * part : (k + 1) * part], z[...], 1, 1)
            acc = acc + dot(d[at, col : col + part], x[...], 1, 1)
        acc_s[...] = acc
        piece = features // 4
        for r in range(0, GROUP, ROWS):
            rows = slice(r, r + ROWS)
            x = hid[rows].astype(f32)
            rinv = lax.rsqrt(jnp.sum(x * x, axis=1, keepdims=True) / x.shape[1] + EPS)
            xhat = x * rinv
            d = acc_s[rows]
            ggain[...] += fold8(d * xhat)
            dxh = d * gain[0:1]
            mean = jnp.sum(dxh * xhat, axis=1, keepdims=True) / x.shape[1]
            low[rows] = (cotx[rows].astype(f32) + rinv * (dxh - xhat * mean)).astype(bf16)
        turned = low[...].T
        for k in range(4):
            shuffle[step, k] = turned[k * piece : (k + 1) * piece]
        for k in (2, 3, 1):
            piece_copy(step, k).start()

    @pl.when(u == first_out + count - 1)
    def _():
        rows = features // n
        small_at = rows + 4 * pack_rows
        total = gx_sum.finish_f32()
        sums = halves_of(joined(total[rows:], pack_rows))
        row = halves_of(jnp.sum(ggain[...], axis=0, keepdims=True))
        gx_all.start(padded_rows(jnp.concatenate([total[:rows], sums, row], axis=0), total.shape[0]).astype(bf16))
        for k in range(1, 4):
            heads_trade(k).wait()
        for q in range(4):
            for s in range(n):
                at = (q * n + s) * share_rows
                gbc[at : at + share_rows] = bc_heads[q, s].astype(f32)[:share_rows]
        for step in range(count):
            for k in range(4):
                if k:
                    piece_copy(step, k).wait()
                place(step, k)
        gx_all.finish()
        row = joined(gx_all.rows(0, small_at + 4)[small_at:], 1)
        for s in range(1, n):
            row = row + joined(gx_all.rows(s, small_at + 4)[small_at:], 1)
        for t in range(lane_tiles):
            gi_sum[t : t + 1] = row[:, t * LANES : (t + 1) * LANES]
        for k in range(1, 4):
            gi_trade(k).start()
        for s in range(n):
            share_s = gx_all.rows(s, small_at)
            gx[s * rows : (s + 1) * rows] = share_s[:rows]
            if s * pack_rows < 24:
                small[s * pack_rows : (s + 1) * pack_rows] = joined(share_s[rows:], pack_rows)
        total = gi_sum[...]
        for k in range(1, 4):
            gi_trade(k).wait()
            total = total + gi_got[k]
        for t in range(lane_tiles):
            small[24:32, t * LANES : (t + 1) * LANES] = jnp.broadcast_to(total[t : t + 1], (8, LANES))


def unpack_kernel(
    quarter, heads, me, small, *refs
):
    large, refs = refs[:6], refs[6:]
    (gi, dt, taps, bias, maps, maps_bias, step, log, skip, gain), refs = refs[:10], refs[10:]
    for a, b in zip(large, refs):
        b[...] = a[...]
    features = small.shape[1]
    piece = gi.shape[1]
    row = pltpu.roll(small[24:32], lax.rem(features - me[0] * piece, features), 1)
    gi[...] = row[0:1, :piece]
    dt[...] = small[8 : 8 + heads]
    taps[...] = small[0:4, :quarter]
    for k in range(quarter // LANES):
        cols = slice(k * LANES, (k + 1) * LANES)
        bias[k : k + 1] = small[4:5, cols]
        gain[k : k + 1] = small[5:6, cols]
    maps[...] = small[16:20, : 2 * LANES]
    maps_bias[...] = small[20:21, : 2 * LANES]
    row = jnp.broadcast_to(small[6:7, 0:LANES], (8, LANES))
    for k, to in enumerate((step, log, skip)):
        to[...] = pltpu.roll(row, LANES - k * heads, 1)[0:1, :heads] if k else row[0:1, :heads]


def shards(
    hidden_in,
    output_cotangent,
    input_norm_scale_gain,
    z_proj,
    x_proj,
    bc_proj,
    dt_proj,
    conv_x_weight,
    conv_x_bias,
    conv_bc_weight,
    conv_bc_bias,
    dt_bias,
    a_log,
    d_skip,
    out_norm_gain,
    out_proj,
    doc_starts,
):
    batch, tokens, features = hidden_in.shape
    quarter = z_proj.shape[1]
    width = 2 * quarter
    inner = 4 * quarter
    heads = dt_proj.shape[1]
    seqs = lax.axis_size("seq")
    head_devices = lax.axis_size("head")
    parts = head_devices // batch
    chunk = tokens // parts
    count = chunk // GROUP
    si, hi_ = lax.axis_index("seq"), lax.axis_index("head")
    seq_of, half = hi_ // parts, hi_ % parts
    meta = jnp.reshape(hi_, (1,)).astype(jnp.int32)

    here = lambda i, *_: (i, 0)
    here3 = lambda i, *_: (i, 0, 0)
    rev = lambda i, *_: (count - 1 - i, 0)
    rev3 = lambda i, *_: (count - 1 - i, 0, 0)
    rev_hid = lambda i, m: (m[0] // parts, lax.rem(m[0], parts) * count + count - 1 - i, 0)
    taps_bc = conv_bc_weight.T
    lane_block = (GROUP, LANES)
    map_block = (GROUP, 2 * LANES)
    wide = (GROUP, inner)
    half_in = (GROUP, width)
    state_block = (1, LANES, width)
    keep_block = (1, 8, width)
    piece = features // head_devices
    ex, red = expansion(width)
    tril = jnp.asarray(np.tril(np.ones((GROUP, GROUP), np.float32)))
    cotangent = jnp.swapaxes(output_cotangent, 1, 2)

    def whole(*arrays):
        return [(a, None, None) for a in arrays]

    by_lanes = lambda x: x.reshape(-1, LANES)
    head_vecs = jnp.pad(jnp.concatenate([dt_bias, a_log, d_skip]), (0, LANES - 3 * heads))[None]
    front_scratch = [
        pltpu.VMEM((GROUP + 8, width), f32),
        pltpu.VMEM((LANES, width), f32),
        pltpu.VMEM((8, LANES), f32),
        pltpu.VMEM(half_in, f32),
        pltpu.VMEM(half_in, bf16),
        pltpu.VMEM(half_in, bf16),
        pltpu.VMEM((LANES, features), f32),
        pltpu.VMEM((GROUP + 8, 2 * LANES), f32),
    ]

    def front_outs(block, block3):
        return [
            ((chunk, width), bf16, half_in, block),
            ((chunk, width), f32, half_in, block),
            ((chunk, width), bf16, half_in, block),
            ((chunk, LANES), f32, lane_block, block),
            ((chunk, LANES), f32, lane_block, block),
            ((count, LANES, width), f32, state_block, block3),
            ((count, 8, width), f32, keep_block, block3),
            ((count, 8, width), f32, keep_block, block3),
            ((LANES, width), f32, None, None),
            ((8, LANES), f32, None, None),
            ((8, width), f32, None, None),
            ((LANES, features), bf16, None, None),
        ]

    own_head = lambda: lax.axis_index("head")
    x_shape = (features, quarter)

    def phase(k, rank):
        at = lambda u: jnp.clip(u - k * count, 0, count - 1)
        return (lambda u: (at(u), 0)) if rank == 2 else (lambda u: (at(u), 0, 0))

    def front_outs(k):
        return [
            ((chunk, width), bf16, half_in, phase(k, 2)),
            ((chunk, width), f32, half_in, phase(k, 2)),
            ((chunk, width), bf16, None, None),
            ((chunk, LANES), f32, None, None),
            ((chunk, LANES), f32, None, None),
            ((count, LANES, width), f32, state_block, phase(k, 3)),
            ((count, 8, width), f32, keep_block, phase(k, 3)),
            ((count, 8, width), f32, keep_block, phase(k, 3)),
            ((8, width), f32, None, None),
            ((LANES, features), bf16, None, None),
            ((LANES, quarter), f32, None, None),
            ((LANES, quarter), f32, None, None),
            ((chunk, width), f32, half_in, phase(k + 2, 2)),
        ]

    front_names = ("ci", "co", "val", "pre", "cum", "lin", "kb", "ck", "par", "dtp", "own", "other", "part")
    outs = run(
        functools.partial(forward_kernel, seqs, parts, count),
        (5 * count,),
        [
            (
                hidden_in,
                (1, GROUP, features),
                lambda u: (own_head() // parts, lax.rem(own_head(), parts) * count + jnp.minimum(u, count - 1), 0),
            ),
            (hidden_in, (1, 16, features), lambda u: (own_head() // parts, tokens // 16 - 1, 0)),
            (hidden_in, (1, 16, features), lambda u: (own_head() // parts, chunk // 16 - 1, 0)),
            *whole(doc_starts, by_lanes(conv_x_bias), by_lanes(out_norm_gain), head_vecs),
            *whole(by_lanes(input_norm_scale_gain), by_lanes(conv_bc_bias), conv_x_weight.T, dt_proj.T, x_proj, z_proj, out_proj, bc_proj, taps_bc, tril, ex),
            (cotangent, pl.ANY, None),
        ],
        [
            ((chunk, features), bf16, None, None),
            ((chunk, 2 * LANES), bf16, None, None),
            ((chunk, LANES), jnp.int32, None, None),
            ((8, chunk), jnp.int32, (8, GROUP), lambda u: (0, jnp.minimum(u, count - 1))),
            ((8, LANES), jnp.int32, None, None),
            ((8, features), f32, None, None),
        ]
        + [(x_shape, bf16, None, None)] * 6
        + [((quarter, features), bf16, None, None)] * 3
        + [((piece, chunk), bf16, pl.ANY, None)] * 3
        + [
            ((chunk, 2 * LANES), f32, map_block, phase(1, 2)),
            ((chunk, LANES), bf16, None, None),
            ((chunk, LANES), bf16, None, None),
        ]
        + front_outs(1)
        + front_outs(2),
        [
            pltpu.VMEM((8, features), f32),
            pltpu.VMEM((8, 2 * LANES), f32),
            pltpu.VMEM((16, features), bf16),
            pltpu.VMEM((16, features), bf16),
        ]
        + [pltpu.VMEM((16, features), f32)] * 4
        + [pltpu.VMEM(x_shape, bf16)] * 3
        + [pltpu.VMEM((LANES, width), f32)] * 2
        + [pltpu.VMEM((8, LANES), f32)] * 2
        + [pltpu.SemaphoreType.DMA((2, 7)), pltpu.SemaphoreType.DMA((2, 4))]
        + front_scratch
        + Weights.scratch(features, quarter)
        + Weights.scratch(quarter, features)
        + Exchange.scratch(seqs, quarter) * 2,
        flops=40_000_000_000,
        moved=50_000_000,
        collective=1,
    )
    normed, ci_bc, age, ager, next_age, gain_in = outs[:6]
    xs, zs, os_ = [x_proj, *outs[6:9]], [z_proj, *outs[9:12]], [out_proj, *outs[12:15]]
    cots = outs[15:18]
    co_bc, bmat, cmat = outs[18:21]
    ha, hb = dict(zip(front_names, outs[21:34])), dict(zip(front_names, outs[34:47]))
    halves = [ha, hb]
    for d in halves:
        d["arr"] = [d["own"], d["other"]]

    outs = run(
        mid_kernel,
        (count,),
        [
            (hidden_in, (1, GROUP, features), rev_hid),
            (normed, (GROUP, features), rev),
            *whole(*zs, *os_),
            (
                cotangent,
                (1, piece, GROUP),
                lambda i, m: (m[0] // parts, 0, lax.rem(m[0], parts) * count + count - 1 - i),
            ),
            *[(c, (piece, GROUP), lambda i, *_: (0, count - 1 - i)) for c in cots],
            (cmat, lane_block, rev),
            (age, lane_block, rev),
            *whole(ex, red, ha["par"], hb["par"]),
            *[(d["part"], half_in, rev) for d in halves],
            *[(d["val"], half_in, rev) for d in halves],
            *[(d["cum"], lane_block, rev) for d in halves],
            *[(d["lin"], state_block, rev3) for d in halves],
            *[(d["kb"], keep_block, rev3) for d in halves],
            *[(d["ck"], keep_block, rev3) for d in halves],
            *whole(*ha["arr"], *hb["arr"]),
        ],
        [
            ((4, piece, chunk), bf16, (4, piece, GROUP), lambda i, *_: (0, 0, count - 1 - i)),
            ((chunk, features), bf16, (GROUP, features), rev),
            ((chunk, inner), bf16, wide, rev),
            ((chunk, features), bf16, (GROUP, features), rev),
            ((chunk, inner), bf16, wide, rev),
            ((chunk, inner), bf16, wide, rev),
            ((chunk, LANES), f32, lane_block, rev),
            ((chunk, LANES), f32, lane_block, rev),
            ((chunk, LANES), f32, lane_block, rev),
            ((count, LANES, width), f32, state_block, rev3),
            ((count, LANES, width), f32, state_block, rev3),
            ((count, 8, width), f32, keep_block, rev3),
            ((count, 8, width), f32, keep_block, rev3),
            ((LANES, width), f32, None, None),
            ((LANES, width), f32, None, None),
            ((8, LANES), f32, None, None),
            ((8, LANES), f32, None, None),
            ((8, inner), f32, None, None),
            ((8, inner), f32, None, None),
        ],
        [pltpu.VMEM(wide, f32)] * 6
        + [pltpu.VMEM(wide, bf16)] * 4
        + [pltpu.VMEM((LANES, width), f32)] * 2
        + [pltpu.VMEM((8, LANES), f32)] * 2
        + [pltpu.VMEM((4, piece, GROUP), bf16)],
        flops=30_000_000_000,
        moved=50_000_000,
        prefetch=(meta,),
    )
    pieces, hidc, outs = outs[0], outs[1], outs[2:]
    nout, cotx, dssd, dgate, dcin, ha["dkk"], hb["dkk"], ha["lout"], hb["lout"], ha["ka"], hb["ka"] = outs[:11]
    dtot_a, dtot_b, dk_a, dk_b, ggain_out, gskip = outs[11:]

    tiles = features // GROUP
    lead = 4 * tiles
    tile_block = lambda u: (0, lax.rem(jnp.minimum(u, lead - 1), tiles))
    first_half = lambda u: (0, 1 - jnp.minimum(u // (2 * tiles), 1))
    after_lead = lambda u: jnp.maximum(u - lead, 0)
    lo_unit = lambda u: (jnp.clip(u - lead, 0, count - 1), 0)
    hi_unit = lambda u: (jnp.clip(u - lead - count, 0, count - 1), 0)
    any_unit = lambda u: (lax.rem(after_lead(u), count), 0)
    quarter_grad = (2, features, quarter)
    share_rows = features // seqs
    outs = run(
        functools.partial(outer_kernel, seqs, parts, count, tiles),
        (lead + 2 * count,),
        [
            (normed, (chunk, GROUP), tile_block),
            (cotx, (chunk, GROUP), tile_block),
            (dgate, (chunk, width), first_half),
            (nout, (chunk, width), first_half),
            (ha["val"], half_in, lo_unit),
            (hb["val"], half_in, hi_unit),
            (dssd, half_in, lambda u: (lax.rem(after_lead(u), count), after_lead(u) // count)),
            (bmat, lane_block, any_unit),
            (cmat, lane_block, any_unit),
            (ager, (8, GROUP), lambda u: (0, lax.rem(after_lead(u), count))),
            (ha["pre"], lane_block, lo_unit),
            (hb["pre"], lane_block, hi_unit),
            (ha["cum"], lane_block, lo_unit),
            (hb["cum"], lane_block, hi_unit),
            *whole(dtot_a, dtot_b, dk_a, dk_b, ex),
        ],
        [
            (shape, f32, (GROUP, shape[1]), imap)
            for imap in (lo_unit, hi_unit)
            for shape in [(chunk, width)] + [(chunk, LANES)] * 4
        ]
        + [((LANES, width), f32, None, None)] * 2
        + [((up16(share_rows), quarter), bf16, None, None), ((features, quarter), bf16, None, None)],
        [
            pltpu.VMEM((LANES, GROUP), f32),
            pltpu.VMEM((2,) + quarter_grad, f32),
            pltpu.VMEM((2,) + quarter_grad, bf16),
            pltpu.VMEM((2,) + quarter_grad, bf16),
            pltpu.VMEM(quarter_grad, bf16),
            pltpu.VMEM(quarter_grad, bf16),
            pltpu.SemaphoreType.DMA((2, 6)),
        ]
        + PairScatter.scratch(seqs, share_rows, quarter)
        + Exchange.scratch(seqs, width),
        flops=30_000_000_000,
        moved=40_000_000,
        collective=2,
    )
    names = ("dvi", "dbi", "dci_c", "rflow", "cflow")
    ha.update(zip(names, outs[:5]))
    hb.update(zip(names, outs[5:10]))
    leav = outs[10:12]
    share_z, grad_o = outs[12:]

    def back_ins(n, block, block3):
        d = halves[n]
        return [
            (d["val"], half_in, block),
            (dssd, half_in, lambda u: (block(u)[0], n)),
            (d["dvi"], half_in, block),
            (bmat, lane_block, block),
            (d["co"], half_in, block),
            (d["ci"], half_in, block),
            (age, lane_block, block),
            (d["pre"], lane_block, block),
            (d["cum"], lane_block, block),
            (d["lout"], state_block, block3),
            (d["ka"], keep_block, block3),
            *whole(*leav),
            (d["lin"], state_block, block3),
            (d["kb"], keep_block, block3),
            *whole(*d["arr"]),
            (d["rflow"], lane_block, block),
            (d["cflow"], lane_block, block),
            (d["dkk"], lane_block, block),
            *whole(d["par"], tril, ex, red),
        ]

    back_scratch = [
        pltpu.VMEM((GROUP + 8, width), f32),
        pltpu.VMEM((GROUP + 8, LANES), jnp.int32),
        pltpu.VMEM(half_in, f32),
        pltpu.VMEM(half_in, f32),
        pltpu.VMEM(half_in, bf16),
        pltpu.VMEM(half_in, bf16),
    ]

    def both_outs(cols, block):
        return [
            ((chunk, cols), bf16, (GROUP, cols), block),
            ((8, cols), f32, None, None),
            ((8, cols), f32, None, None),
        ]

    early_rev = lambda u: (count - 1 - jnp.minimum(u, count - 1), 0)
    late_rev = lambda u: (count - 1 - jnp.maximum(u - count, 0), 0)
    early_rev3 = lambda u: (count - 1 - jnp.minimum(u, count - 1), 0, 0)
    late_rev3 = lambda u: (count - 1 - jnp.maximum(u - count, 0), 0, 0)
    outs = run(
        functools.partial(turn_kernel, seqs, parts, count),
        (2 * count,),
        [
            *[(d["dbi"], lane_block, early_rev) for d in halves],
            *[(d["dci_c"], lane_block, early_rev) for d in halves],
            (dcin, lane_block, early_rev),
            (co_bc, map_block, early_rev),
            (ci_bc, map_block, early_rev),
            (age, lane_block, early_rev),
            (taps_bc, None, None),
            *[(d["val"], half_in, early_rev) for d in halves],
            *[(d["pre"], lane_block, early_rev) for d in halves],
            *[(d["cum"], lane_block, early_rev) for d in halves],
            *[(d["lout"], state_block, early_rev3) for d in halves],
            *[(d["ka"], keep_block, early_rev3) for d in halves],
            *whole(*leav, ex),
            *back_ins(1, late_rev, late_rev3),
            *whole(grad_o, share_z),
            (pieces, pl.ANY, None),
        ],
        both_outs(2 * LANES, early_rev)
        + [((32, 2 * LANES), f32, None, None), ((8, 2 * LANES), f32, None, None)]
        + both_outs(width, late_rev)
        + [
            ((chunk, LANES), bf16, lane_block, late_rev),
            ((32, width), f32, None, None),
            ((8, width), f32, None, None),
            ((8, LANES), f32, None, None),
            ((8, LANES), f32, None, None),
            ((up16(share_rows), quarter), bf16, None, None),
            ((features, quarter), f32, None, None),
            ((batch, piece, tokens), bf16, pl.ANY, None),
        ],
        [
            pltpu.VMEM((GROUP + 8, 2 * LANES), f32),
            pltpu.VMEM((GROUP + 8, LANES), jnp.int32),
            pltpu.VMEM(lane_block, f32),
        ]
        + back_scratch
        + [pltpu.SemaphoreType.DMA((2, 4))]
        + PairScatter.scratch(seqs, share_rows, quarter)
        + PairGather.scratch(seqs, share_rows, quarter),
        flops=30_000_000_000,
        moved=40_000_000,
        collective=4,
    )
    dbc, tail_bc, head_bc, gw_bc, gb_bc = outs[:5]
    hb.update(zip(("dx", "tail", "head", "draw", "gw", "gb", "galog", "gdtb"), outs[5:13]))
    share, grad_z, layer_out = outs[13:]

    steps = 3 * tiles + 2 * count
    back_unit = lambda u: (count - 1 - jnp.clip(u - 2 * tiles, 0, count - 1), 0)
    back_unit3 = lambda u: (count - 1 - jnp.clip(u - 2 * tiles, 0, count - 1), 0, 0)
    out_unit = lambda u: (jnp.clip(u - 3 * tiles - count, 0, count - 1), 0)

    def grad_tile(u):
        first = lax.rem(jnp.clip(u - 1, 0, 2 * tiles - 1), tiles)
        third = jnp.clip(u - 2 * tiles - count, 0, tiles - 1)
        later = jnp.minimum(u // (2 * tiles + count), 1)
        return 0, (1 - later) * first + later * third

    ending = lambda *_: (chunk // 16 - 1, 0)
    small_pack = (16, features)
    packed_rows = share_rows + 4 * -(-24 // seqs) + 4
    input_grad, sum2, g_bc, small_sum, grad_out = run(
        functools.partial(late_kernel, seqs, parts, count, tiles),
        (steps,),
        [
            *back_ins(0, back_unit, back_unit3),
            (normed, (chunk, GROUP), grad_tile),
            *whole(hb["dx"], hb["tail"], hb["head"]),
            (hb["ci"], (16, width), ending),
            *whole(hb["par"], hb["draw"], hb["gw"], hb["gb"], hb["galog"], hb["gdtb"]),
            *whole(dbc, tail_bc, head_bc),
            (ci_bc, (16, 2 * LANES), ending),
            *whole(taps_bc, gw_bc, gb_bc),
            (ha["ci"], (16, width), ending),
            *whole(next_age, gskip, ggain_out, share),
            (hidc, (GROUP, features), out_unit),
            (cotx, (GROUP, features), out_unit),
            (gain_in, None, None),
            (dgate, wide, out_unit),
            *whole(*zs, bc_proj, *xs, ha["dtp"], hb["dtp"]),
        ],
        [
            ((batch, piece, tokens), bf16, None, None),
            ((features, quarter), f32, None, None),
            ((features, 2 * LANES), f32, None, None),
            ((32, features), f32, None, None),
            ((quarter, features), f32, None, None),
        ],
        back_scratch
        + [
            pltpu.VMEM((chunk, width), bf16),
            pltpu.VMEM((chunk, LANES), bf16),
            pltpu.VMEM(x_shape, f32),
            pltpu.VMEM(x_shape, bf16),
            pltpu.VMEM(small_pack, f32),
            pltpu.VMEM(small_pack, f32),
            pltpu.VMEM(x_shape, bf16),
            pltpu.VMEM(small_pack, f32),
            pltpu.VMEM((16, width), bf16),
            pltpu.VMEM((8, width), f32),
            pltpu.VMEM((8, width), f32),
            pltpu.VMEM((32, width), f32),
            pltpu.VMEM((8, width), f32),
            pltpu.VMEM((8, LANES), f32),
            pltpu.VMEM((8, LANES), f32),
            pltpu.VMEM((chunk, width), bf16),
            pltpu.VMEM((chunk, 2 * LANES), bf16),
            pltpu.VMEM(x_shape, f32),
            pltpu.VMEM(x_shape, bf16),
            pltpu.VMEM(x_shape, bf16),
            pltpu.VMEM(x_shape, bf16),
        ]
        + [pltpu.VMEM(small_pack, f32)] * 5
        + [
            pltpu.VMEM(x_shape, bf16),
            pltpu.VMEM((8, width), f32),
            pltpu.VMEM((8, 2 * LANES), f32),
            pltpu.VMEM((8, width), f32),
            pltpu.VMEM((features, 2 * LANES), f32),
            pltpu.VMEM((2, features // 4, 2 * LANES), bf16),
            pltpu.VMEM((2, features // 4, 2 * LANES), bf16),
            pltpu.VMEM((features // 4, 2 * LANES), bf16),
            pltpu.VMEM((features // 4, 2 * LANES), bf16),
            pltpu.VMEM((features // 4, 2 * LANES), f32),
            pltpu.VMEM((8, 2 * LANES), f32),
            pltpu.VMEM((4, 8, 2 * LANES), f32),
            pltpu.VMEM((4, seqs, up16(features // 4 // seqs), 2 * LANES), bf16),
            pltpu.VMEM((GROUP, features), f32),
            pltpu.VMEM((GROUP, features), bf16),
            pltpu.VMEM((count, 4, piece, GROUP), bf16),
            pltpu.VMEM((count, 4, piece, GROUP), bf16),
            pltpu.VMEM((8, features), f32),
            pltpu.VMEM((4, 8, LANES), f32),
            pltpu.VMEM((8, LANES), f32),
            pltpu.SemaphoreType.DMA((2, 3)),
            pltpu.SemaphoreType.DMA((2, 18)),
            pltpu.SemaphoreType.DMA((2, count, 4)),
        ]
        + PairGather.scratch(seqs, share_rows, quarter)
        + Scatter.scratch(seqs, packed_rows, quarter)
        + Gather.scratch(seqs, packed_rows, quarter)
        + Scatter.scratch(seqs, features // 4 // seqs, 2 * LANES)
        + Gather.scratch(seqs, features // 4 // seqs, 2 * LANES),
        flops=40_000_000_000,
        moved=60_000_000,
        collective=5,
    )
    vector = lambda size: ((1, size), f32, None, None)
    large = (layer_out, input_grad, grad_z, sum2, g_bc, grad_out)

    def in_blocks(x):
        if x.ndim == 3:
            return x.shape[:2] + (x.shape[2] // 4,), lambda i, *_: (0, 0, i)
        return (x.shape[0] // 4, x.shape[1]), lambda i, *_: (i, 0)

    by_rows = ((quarter // LANES, LANES), f32, None, None)
    outs = run(
        functools.partial(unpack_kernel, quarter, heads),
        (4,),
        whole(small_sum) + [(a, *in_blocks(a)) for a in large],
        [
            vector(piece),
            ((heads, features), f32, None, None),
            ((4, quarter), f32, None, None),
            by_rows,
            ((4, 2 * LANES), f32, None, None),
            vector(2 * LANES),
            vector(heads),
            vector(heads),
            vector(heads),
            by_rows,
        ]
        + [(a.shape, a.dtype, *in_blocks(a)) for a in large],
        prefetch=(meta,),
    )
    gi, g_dt, g_taps, g_bias, g_maps, g_maps_bias, g_step, g_log, g_skip, g_gain = outs[:10]
    layer_out, input_grad, grad_z, sum2, g_bc, grad_out = outs[10:]
    return (
        jnp.swapaxes(layer_out, 1, 2),
        jnp.swapaxes(input_grad, 1, 2),
        gi[0],
        grad_z,
        sum2,
        g_bc,
        g_dt.T,
        g_taps.T,
        g_bias.reshape(quarter),
        g_maps.T,
        g_maps_bias[0],
        g_step[0],
        g_log[0],
        g_skip[0],
        g_gain.reshape(quarter),
        grad_out,
    )


def solution(mesh):
    return jax.shard_map(
        shards,
        mesh=mesh,
        in_specs=(
            P(None, "seq", None),
            P(None, "seq", "head"),
            P(),
            P(None, "head"),
            P(None, "head"),
            P(),
            P(None, "head"),
            P("head", None),
            P("head"),
            P(),
            P(),
            P("head"),
            P("head"),
            P("head"),
            P("head"),
            P("head", None),
            P(),
        ),
        out_specs=(
            P(None, "seq", "head"),
            P(None, "seq", "head"),
            P("head"),
            P(None, "head"),
            P(None, "head"),
            P(),
            P(None, "head"),
            P("head", None),
            P("head"),
            P(),
            P(),
            P("head"),
            P("head"),
            P("head"),
            P("head"),
            P("head", None),
        ),
        check_vma=False,
    )
```

```python
import functools

import jax
import jax.numpy as jnp
import numpy as np
from jax import lax
from jax.experimental import pallas as pl
from jax.experimental.pallas import tpu as pltpu
from jax.sharding import PartitionSpec as P

GROUP = 256
HALF = 128
LANES = 128
HEAD_DIM = 64
EPS = 1e-05
LOG2E = 1.4426950408889634
f32 = jnp.float32
bf16 = jnp.bfloat16
HIGHEST = lax.Precision.HIGHEST
ROWS = 32
MESH = pl.DeviceIdType.MESH


def dot(a, b, ca=1, cb=0, precision=None):
    return lax.dot_general(
        a, b, (((ca,), (cb,)), ((), ())), precision=precision, preferred_element_type=f32
    )


def split2(x):
    hi = x.astype(bf16)
    return hi, (x - hi.astype(f32)).astype(bf16)


def pack(x):
    hi = x.astype(bf16).astype(f32)
    rest = x - hi
    mid = rest.astype(bf16).astype(f32)
    return (hi + pltpu.roll(mid, 32, 1) + pltpu.roll(rest - mid, 64, 1)).astype(bf16)


def unpack(x):
    x = x.astype(f32)
    return lanes_below(x + pltpu.roll(x, LANES - 32, 1) + pltpu.roll(x, LANES - 64, 1), 12)


def expand(x, ex):
    return dot(pack(x), ex)


def lanes_below(x, count):
    return jnp.where(lax.broadcasted_iota(jnp.int32, x.shape, 1) < count, x, 0.0)


def sigmoid(x):
    return 1.0 / (1.0 + jnp.exp(-x))


def softplus(x):
    return jnp.maximum(x, 0.0) + jnp.log1p(jnp.exp(-jnp.abs(x)))


def fold8(x):
    total = x[0:8]
    for r in range(8, x.shape[0], 8):
        total = total + x[r : r + 8]
    return total


def expansion(width):
    heads = width // HEAD_DIM
    ex = np.zeros((LANES, width), np.float32)
    for part in range(3):
        for h in range(heads):
            ex[32 * part + h, h * HEAD_DIM : (h + 1) * HEAD_DIM] = 1.0
    red = np.zeros((width, LANES), np.float32)
    for h in range(heads):
        red[h * HEAD_DIM : (h + 1) * HEAD_DIM, h] = 1.0
    return jnp.asarray(ex, bf16), jnp.asarray(red, bf16)


def run(kernel, grid, ins, outs, scratch=(), flops=0, moved=0, prefetch=(), collective=None):
    def spec(shape, block, imap):
        if block is pl.ANY:
            return pl.BlockSpec(memory_space=pl.ANY)
        if block is None:
            rank = len(shape)
            return pl.BlockSpec(shape, lambda *_: (0,) * rank)
        return pl.BlockSpec(block, imap)

    extra = {} if collective is None else {"collective_id": collective, "has_side_effects": True}
    return pl.pallas_call(
        kernel,
        grid_spec=pltpu.PrefetchScalarGridSpec(
            num_scalar_prefetch=len(prefetch),
            grid=grid,
            in_specs=[spec(a.shape, b, m) for a, b, m in ins],
            out_specs=[spec(s, b, m) for s, _, b, m in outs],
            scratch_shapes=list(scratch),
        ),
        out_shape=[jax.ShapeDtypeStruct(s, d) for s, d, _, _ in outs],
        compiler_params=pltpu.CompilerParams(vmem_limit_bytes=56 << 20, **extra),
        cost_estimate=pl.CostEstimate(flops=flops, bytes_accessed=moved, transcendentals=0),
    )(*prefetch, *[a for a, _, _ in ins])


def conv_rows(ext, age, taps, bias, r, cols):
    acc = jnp.broadcast_to(bias[:, cols], (ROWS, LANES))
    for k in range(4):
        back = 3 - k
        term = ext[8 + r - back : 8 + r - back + ROWS, cols] * taps[k : k + 1, cols]
        if back:
            term = jnp.where(age >= back, term, 0.0)
        acc = acc + term
    return acc


def rms(x, gain):
    x = x.astype(f32)
    r = lax.rsqrt(jnp.sum(x * x, axis=1, keepdims=True) / x.shape[1] + EPS)
    return (x * r * gain).astype(bf16)


def spread_ages(starts, first, rows):
    token = first + lax.broadcasted_iota(jnp.int32, (rows, starts.shape[1]), 0)
    begun = jnp.where(starts <= token, starts, 0).astype(f32)
    begun = jnp.max(begun, axis=1, keepdims=True).astype(jnp.int32)
    place = first + lax.broadcasted_iota(jnp.int32, (rows, LANES), 0)
    return place - begun


def front_step(
    with_maps, i, normed, before, wa, wb, sa, sb, age, tril, ex, maps_in,
    ci, co, val, pre, cum, lin, kb, ck, tot, kout, par, dtp, maps_out,
    ext, running, kept, omx, ohi, olo, dts, ext_bc,
):
    width = val.shape[1]
    part = width // 2
    heads = part // HEAD_DIM
    if with_maps:
        ci_bc, bc, taps_bc, bias_bc = maps_in
        bias_bc = bias_bc[0:1]
        co_bc, bmat, cmat = maps_out
    else:
        (bmat,) = maps_in

    @pl.when(i == 0)
    def _():
        running[...] = jnp.zeros_like(running)
        kept[...] = jnp.ones_like(kept)
        for w, at in ((wa, 0), (wb, part)):
            ext[0:8, at : at + part] = dot(before[...], w[...]).astype(bf16).astype(f32)[8:16]
        if with_maps:
            ext_bc[0:8] = dot(before[...], bc[...]).astype(bf16).astype(f32)[8:16]
        par[...] = jnp.zeros_like(par)
        for s, at in ((sa, 0), (sb, part)):
            par[0:6, at : at + part] = s[0:6, :part]
        rows_a, rows_b = (jnp.broadcast_to(s[6:7, 0:LANES], (8, LANES)) for s in (sa, sb))

        def lanes(k):
            a = lanes_below(pltpu.roll(rows_a, (LANES - k * heads) % LANES, 1), heads)
            b = lanes_below(pltpu.roll(rows_b, (LANES - k * heads) % LANES, 1), heads)
            return a + pltpu.roll(b, heads, 1)

        par[7:8, LANES : 2 * LANES] = lanes(0)[0:1]
        par[7:8, 0:LANES] = -jnp.exp(lanes(1)[0:1])
        par[6:7] = expand(lanes(2), ex[...])[0:1]
        dts[...] = jnp.zeros_like(dts)
        dts[0:heads] = sa[8 : 8 + heads]
        dts[heads : 2 * heads] = sb[8 : 8 + heads]
        dtp[...] = dts[...].astype(bf16)

    @pl.when(i > 0)
    def _():
        ext[0:8] = ext[GROUP : GROUP + 8]
        if with_maps:
            ext_bc[0:8] = ext_bc[GROUP : GROUP + 8]

    taps, bias = par, par[4:5]
    rate, dtb = par[7:8, 0:LANES], par[7:8, LANES : 2 * LANES]
    for w, at in ((wa, 0), (wb, part)):
        low = dot(normed[...], w[...]).astype(bf16)
        ci[:, at : at + part] = low
        ext[8 : 8 + GROUP, at : at + part] = low.astype(f32)
    raw = dot(normed[...], dtp[...], 1, 1) + dtb
    pre[...] = raw
    delta = softplus(raw)
    c = dot(tril[...], delta * rate, precision=HIGHEST)
    cum[...] = c
    end = c[GROUP - 1 : GROUP]
    age_end = age[GROUP - 1 : GROUP]
    left = GROUP - 1 - lax.broadcasted_iota(jnp.int32, c.shape, 0)
    omega = jnp.where(left <= age_end, jnp.exp(end - c), 0.0) * delta
    omx[...] = expand(lanes_below(omega, 2 * heads), ex[...])
    keep = jnp.where(age_end >= GROUP, jnp.exp(end), 0.0)
    keep = lanes_below(jnp.broadcast_to(keep, (8, LANES)), 2 * heads)
    keepx = expand(keep, ex[...])
    if with_maps:
        ext_bc[8 : 8 + GROUP] = ci_bc[...].astype(f32)
        for r in range(0, GROUP, ROWS):
            a = age[r : r + ROWS]
            for j, out in enumerate((bmat, cmat)):
                cols = slice(j * LANES, (j + 1) * LANES)
                v = conv_rows(ext_bc, a, taps_bc, bias_bc, r, cols)
                co_bc[r : r + ROWS, cols] = v
                out[r : r + ROWS] = (v * sigmoid(v)).astype(bf16)
    for r in range(0, GROUP, ROWS):
        a = age[r : r + ROWS]
        rows = slice(r, r + ROWS)
        for j in range(width // LANES):
            cols = slice(j * LANES, (j + 1) * LANES)
            v = conv_rows(ext, a, taps, bias, r, cols)
            co[rows, cols] = v
            act = (v * sigmoid(v)).astype(bf16)
            val[rows, cols] = act
            ohi[rows, cols], olo[rows, cols] = split2(omx[rows, cols] * act.astype(f32))
    own = dot(bmat[...], ohi[...], 0, 0) + dot(bmat[...], olo[...], 0, 0)
    lin[0] = running[...]
    kb[0] = expand(lanes_below(kept[...], 2 * heads), ex[...])
    ck[0] = keepx
    running[...] = keepx[0:1] * running[...] + own
    kept[...] = keep * kept[...]
    tot[...] = running[...]
    kout[...] = kept[...]


def head_peers():
    head = lax.axis_index("head")
    near = head + 1 - 2 * lax.rem(head, 2)
    return [head, near, lax.rem(head + 2, 4), lax.rem(near + 2, 4)]


def meet(heads, n, extra=0):
    me = lax.axis_index("seq")
    barrier = pltpu.get_barrier_semaphore()
    for head in heads:
        pl.semaphore_signal(barrier, inc=1, device_id={"head": head}, device_id_type=MESH)
    for d in range(1, n):
        pl.semaphore_signal(barrier, inc=1, device_id={"seq": lax.rem(me + d, n)}, device_id_type=MESH)
    pl.semaphore_wait(barrier, n - 1 + len(heads))


def send(src, dst, sems, k, device):
    return pltpu.make_async_remote_copy(
        src_ref=src, dst_ref=dst, send_sem=sems.at[0, k], recv_sem=sems.at[1, k],
        device_id=device, device_id_type=MESH,
    )


class Weights:
    def __init__(self, n, own, outs, scratch):
        self.own, self.outs = own, outs
        self.near, self.far, self.far_near, self.sems = scratch
        me = lax.axis_index("seq")
        odd = lax.rem(me, 2)
        heads = head_peers()
        half = own.shape[0] // 2
        rows = pl.ds(pl.multiple_of(odd * half, half), half)
        near, mate = {"head": heads[1]}, {"seq": me + 1 - 2 * odd}
        self.copies = [
            send(own, self.near, self.sems, 0, near),
            send(own.at[rows], self.far.at[rows], self.sems, 1, {"head": heads[2]}),
            send(self.far.at[rows], self.far.at[rows], self.sems, 2, mate),
            send(self.far, self.far_near, self.sems, 3, near),
        ]

    @staticmethod
    def scratch(rows, cols):
        return [pltpu.VMEM((rows, cols), bf16)] * 3 + [pltpu.SemaphoreType.DMA((2, 4))]

    def begin(self):
        self.copies[1].start()
        self.copies[0].start()

    def share(self):
        self.copies[1].wait()
        self.copies[2].start()

    def back(self):
        self.copies[2].wait()
        self.copies[3].start()

    def finish(self):
        self.copies[0].wait()
        self.copies[3].wait()
        for to, x in zip(self.outs, (self.near, self.far, self.far_near)):
            to[...] = x[...]


def cot_copies(cotangent, outs, which, parts, sems):
    heads = head_peers()
    copies = []
    for k, out in zip(which, outs):
        chunk = out.shape[1]
        cols = pl.ds(pl.multiple_of(lax.rem(heads[k], parts) * chunk, chunk), chunk)
        copies.append(send(cotangent.at[heads[k] // parts, :, cols], out, sems, k, {"head": heads[k]}))
    return copies


class Exchange:
    def __init__(self, reverse, n, parts, tots, kouts, ex, own, other, scratch):
        self.reverse, self.n, self.tots, self.kouts, self.ex = reverse, n, tots, kouts, ex
        self.own, self.other = own, other
        (
            self.out, self.got, self.payload, self.spread, self.scanned, self.home, self.lead, self.lead_k, self.arr,
            self.theirs, self.last, self.swap_sems, self.to_sems, self.from_sems, self.back_to, self.back_from,
        ) = scratch
        self.me = lax.axis_index("seq")
        head = lax.axis_index("head")
        self.partner = head + 1 - 2 * lax.rem(head, 2)
        half = lax.rem(head, parts)
        self.leads = (half if reverse else 1 - half).astype(f32)
        self.per = LANES // n

    @staticmethod
    def scratch(n, width):
        rows = max(LANES // n, 8)
        return [
            pltpu.VMEM((LANES + 8, width), f32),
            pltpu.VMEM((LANES + 8, width), f32),
            pltpu.VMEM((n, rows, width + LANES), f32),
            pltpu.VMEM((n, rows, width + LANES), f32),
            pltpu.VMEM((n, rows, width), f32),
            pltpu.VMEM((n, rows, width), f32),
            pltpu.VMEM((LANES, width), f32),
            pltpu.VMEM((8, LANES), f32),
            pltpu.VMEM((LANES, width), f32),
            pltpu.VMEM((LANES, width), f32),
            pltpu.VMEM((LANES, width), f32),
            pltpu.SemaphoreType.DMA((4,)),
            pltpu.SemaphoreType.DMA((n,)),
            pltpu.SemaphoreType.DMA((n,)),
            pltpu.SemaphoreType.DMA((n,)),
            pltpu.SemaphoreType.DMA((n,)),
        ]

    def peers(self):
        for d in range(1, self.n):
            yield d, lax.rem(self.me + d, self.n), lax.rem(self.me + self.n - d, self.n)

    def swap(self, src, dst, sem):
        return pltpu.make_async_remote_copy(
            src_ref=src,
            dst_ref=dst,
            send_sem=self.swap_sems.at[sem],
            recv_sem=self.swap_sems.at[sem + 1],
            device_id={"head": self.partner},
            device_id_type=MESH,
        )

    def move(self, src, dst, d, to, send_sems, recv_sems):
        return pltpu.make_async_remote_copy(
            src_ref=src.at[to],
            dst_ref=dst.at[self.me],
            send_sem=send_sems.at[d],
            recv_sem=recv_sems.at[d],
            device_id={"seq": to},
            device_id_type=MESH,
        )

    def begin(self):
        part = self.tots[0].shape[1] // 2
        heads = part // HEAD_DIM
        for k in range(len(self.tots)):
            self.out[0:LANES, k * part : (k + 1) * part] = self.tots[k][:, part:]
            rolled = pltpu.roll(self.kouts[k][...], LANES - heads, 1)
            self.out[LANES : LANES + 8, k * LANES : (k + 1) * LANES] = lanes_below(rolled, heads)
        used = len(self.tots) * LANES
        self.out[LANES : LANES + 8, used:] = jnp.zeros((8, self.out.shape[1] - used), f32)
        self.swap(self.out, self.got, 0).start()

    def combine(self):
        self.swap(self.out, self.got, 0).wait()
        part = self.tots[0].shape[1] // 2
        heads = part // HEAD_DIM
        width = len(self.tots) * part
        leads, follows = self.leads, 1.0 - self.leads
        mine_k, got_k = jnp.zeros((8, LANES), f32), jnp.zeros((8, LANES), f32)
        for k, kout in enumerate(self.kouts):
            both = (lanes_below(kout[...], heads), self.got[LANES : LANES + 8, k * LANES : (k + 1) * LANES])
            both = [pltpu.roll(x, k * heads, 1) if k else x for x in both]
            mine_k, got_k = mine_k + both[0], got_k + both[1]
        lk = leads * mine_k + follows * got_k
        fk = leads * got_k + follows * mine_k
        fkx = expand(fk, self.ex[:, :width])[0:1]
        self.lead_k[...] = lk
        for k in range(len(self.tots)):
            cols = slice(k * part, (k + 1) * part)
            mine, got = self.tots[k][:, :part], self.got[0:LANES, cols]
            ls = leads * mine + follows * got
            self.lead[:, cols] = ls
            self.arr[:, cols] = fkx[:, cols] * ls + (leads * got + follows * mine)
        keep = (lk * fk)[0:1]
        rows = self.payload.shape[1]
        for s in range(self.n):
            self.payload[s, 0 : self.per, 0:width] = self.arr[s * self.per : (s + 1) * self.per]
            self.payload[s, :, width:] = jnp.broadcast_to(keep, (rows, LANES))
        for d, to, _ in self.peers():
            self.move(self.payload, self.spread, d, to, self.to_sems, self.from_sems).start()
        self.spread[self.me] = self.payload[self.me]

    def scan(self):
        for d, to, _ in self.peers():
            self.move(self.payload, self.spread, d, to, self.to_sems, self.from_sems).wait()
        width = self.scanned.shape[2]
        rows = self.scanned.shape[1]
        state = jnp.zeros((rows, width), f32)
        for step in range(self.n):
            at = self.n - 1 - step if self.reverse else step
            self.scanned[at] = state
            if step < self.n - 1:
                keep = expand(self.spread[at, :, width:], self.ex[:, :width])
                state = keep * state + self.spread[at, :, 0:width]
        for d, to, _ in self.peers():
            self.move(self.scanned, self.home, d, to, self.back_to, self.back_from).start()
        self.home[self.me] = self.scanned[self.me]

    def settle(self):
        for d, to, _ in self.peers():
            self.move(self.scanned, self.home, d, to, self.back_to, self.back_from).wait()
        for s in range(self.n):
            self.arr[s * self.per : (s + 1) * self.per] = self.home[s, 0 : self.per]
        leads, follows = self.leads, 1.0 - self.leads
        first = self.arr[...]
        second = expand(self.lead_k[...], self.ex[:, : first.shape[1]])[0:1] * first + self.lead[...]
        self.theirs[...] = leads * second + follows * first
        self.swap(self.theirs, self.last, 2).start()
        self.own[...] = leads * first + follows * second

    def close(self):
        self.swap(self.theirs, self.last, 2).wait()
        self.other[...] = self.last[...]


def pair_masks(x, lane_axis_shape):
    lane = lax.broadcasted_iota(jnp.int32, lane_axis_shape, 1)
    zero = jnp.zeros_like(x)
    return jnp.where(lane < HEAD_DIM, x, zero), jnp.where(lane >= HEAD_DIM, x, zero)


def intra_unit(val, bmat, cmat, age, pre, cum, dskip, part):
    t = lax.broadcasted_iota(jnp.int32, (HALF, HALF), 0)
    s = lax.broadcasted_iota(jnp.int32, (HALF, HALF), 1)
    scores = dot(cmat[...], bmat[...], 1, 1)
    a0, a1 = age[0:HALF], age[HALF:]
    gap = t - s
    s00 = jnp.where((gap >= 0) & (gap <= a0), scores[:HALF, :HALF], 0.0)
    s11 = jnp.where((gap >= 0) & (gap <= a1), scores[HALF:, HALF:], 0.0)
    s10 = jnp.where(gap + HALF <= a1, scores[HALF:, :HALF], 0.0)
    c2 = cum[...] * LOG2E
    rows = (c2 - jnp.log2(softplus(pre[...]))).T
    for j in range(val.shape[1] // LANES):
        cols = slice(j * LANES, (j + 1) * LANES)
        v = val[:, cols]
        vm = pair_masks(v, v.shape)
        tops, bottoms = [], []
        for which in range(2):
            h = 2 * j + which
            col0 = jnp.broadcast_to(c2[:HALF, h : h + 1], (HALF, HALF))
            col1 = jnp.broadcast_to(c2[HALF:, h : h + 1], (HALF, HALF))
            r0 = rows[h : h + 1, :HALF]
            r1 = rows[h : h + 1, HALF:]
            tops.append((s00 * jnp.exp2(jnp.minimum(col0 - r0, 60.0))).astype(bf16))
            bottoms.append((s10 * jnp.exp2(col1 - r0)).astype(bf16))
            bottoms.append((s11 * jnp.exp2(jnp.minimum(col1 - r1, 60.0))).astype(bf16))
        top = dot(jnp.concatenate(tops, axis=1), jnp.concatenate([vm[0][:HALF], vm[1][:HALF]], axis=0))
        bottom = dot(jnp.concatenate(bottoms, axis=1), jnp.concatenate([vm[0], vm[1]], axis=0))
        skip = dskip[6:7, cols]
        part[:HALF, cols] = top + skip * v[:HALF].astype(f32)
        part[HALF:, cols] = bottom + skip * v[HALF:].astype(f32)


def forward_kernel(
    n, parts, count, hid, tail_rows, edge_near, starts, bias_x, gain_x, head_vecs, gain_in, bias_maps, taps_x, dt_own, x_own, z_own, o_own, bc, taps_bc,
    tril, ex, cotangent,
    normed, ci_bc, age, ager, next_age, gain_out, x_near, x_far, x_far_near, z_near, z_far, z_far_near,
    o_near, o_far, o_far_near, cot_near, cot_across, cot_corner, co_bc, bmat, cmat, *refs,
):
    (ci_a, co_a, val_a, pre_a, cum_a, lin_a, kb_a, ck_a, par_a, dtp_a, own_a, other_a, part_a), refs = refs[:13], refs[13:]
    (ci_b, co_b, val_b, pre_b, cum_b, lin_b, kb_b, ck_b, par_b, dtp_b, own_b, other_b, part_b), refs = refs[:13], refs[13:]
    (
        gain, bias_bc, before, edge_far, small_s, small_n, small_f, small_fn, xn, xf, xfn,
        tot_a, tot_b, kout_a, kout_b, sems, cot_sems,
    ), refs = refs[:17], refs[17:]
    front, refs = refs[:8], refs[8:]
    z_weights = Weights(n, z_own, (z_near, z_far, z_far_near), refs[:4])
    o_weights = Weights(n, o_own, (o_near, o_far, o_far_near), refs[4:8])
    refs = refs[8:]
    size = len(refs) // 2
    states_a = Exchange(False, n, parts, (tot_a,), (kout_a,), ex, own_a, other_a, refs[:size])
    states_b = Exchange(False, n, parts, (tot_b,), (kout_b,), ex, own_b, other_b, refs[size:])
    cots = cot_copies(cotangent, (cot_near, cot_across, cot_corner), (1, 2, 3), parts, cot_sems)
    u = pl.program_id(0)
    s_me = lax.axis_index("seq")
    heads = head_peers()
    near, across = {"head": heads[1]}, {"head": heads[2]}
    half = lax.rem(heads[0], parts)
    batch = heads[0] // parts
    chunk = count * GROUP
    features = bc.shape[0]
    part = x_own.shape[1]
    nh = dt_own.shape[0]
    first = (s_me * parts + half) * chunk
    row = starts[0:1]
    for b in range(1, starts.shape[0]):
        row = jnp.where(batch == b, starts[b : b + 1], row)

    swap_x = send(x_own, xn, sems, 0, near)
    swap_small = send(small_s, small_n, sems, 1, near)
    cross_x = send(x_own, xf, sems, 2, across)
    cross_small = send(small_s, small_f, sems, 3, across)
    swap_far = send(xf, xfn, sems, 4, near)
    swap_small_far = send(small_f, small_fn, sems, 5, near)
    edge = send(tail_rows.at[0], edge_far, sems, 6, {"seq": lax.min(s_me + 1, n - 1)})

    @pl.when(u == 0)
    def _():
        small_s[...] = jnp.zeros_like(small_s)
        small_s[0:4, 0:part] = taps_x[...]
        for k in range(part // LANES):
            cols = slice(k * LANES, (k + 1) * LANES)
            small_s[4:5, cols] = bias_x[k : k + 1]
            small_s[5:6, cols] = gain_x[k : k + 1]
        small_s[6:7, 0:LANES] = head_vecs[...]
        small_s[8 : 8 + nh] = dt_own[...].astype(f32)
        for k in range(features // LANES):
            gain[0:1, k * LANES : (k + 1) * LANES] = gain_in[k : k + 1]
        for k in range(2):
            bias_bc[0:1, k * LANES : (k + 1) * LANES] = bias_maps[k : k + 1]
        gain_out[...] = jnp.broadcast_to(gain[0:1], gain_out.shape)
        edge_far[...] = jnp.zeros_like(edge_far)
        meet(heads[1:], n)
        swap_small.start()
        swap_x.start()
        pl.when(s_me < n - 1)(edge.start)
        cross_small.start()
        cross_x.start()
        next_age[...] = spread_ages(row, first + chunk, 8)

    rows = pl.ds(pl.multiple_of(lax.rem(u, count) * GROUP, GROUP), GROUP)

    @pl.when(u < count)
    def _():
        for r in range(0, GROUP, ROWS):
            at = pl.ds(pl.multiple_of(u * GROUP + r, ROWS), ROWS)
            normed[at] = rms(hid[0, r : r + ROWS], gain[0:1])
        ci_bc[rows] = dot(normed[rows], bc[...]).astype(bf16)
        a = spread_ages(row, first + u * GROUP, GROUP)
        age[rows] = a
        ager[...] = a.astype(f32).T[0:8].astype(jnp.int32)

    @pl.when(u == count)
    def _():
        swap_small.wait()
        swap_x.wait()
        pl.when(s_me < n - 1)(edge.wait_send)
        pl.when(s_me > 0)(edge.wait_recv)
        local = half.astype(f32)
        near_rows = local * edge_near[0].astype(f32) + (1.0 - local) * edge_far[...].astype(f32)
        before[...] = rms(near_rows, gain[0:1])

    @pl.when(u == 2 * count - 1)
    def _():
        cross_small.wait()
        swap_small_far.start()
        cross_x.wait()
        swap_far.start()
        z_weights.begin()

    @pl.when(u == 2 * count)
    def _():
        states_a.begin()
        swap_small_far.wait()
        swap_far.wait()
        x_near[...] = xn[...]
        x_far[...] = xf[...]
        x_far_near[...] = xfn[...]

    pl.when(u == 2 * count + 1)(states_a.combine)

    @pl.when(u == 2 * count + 2)
    def _():
        z_weights.share()
        o_weights.begin()

    pl.when(u == 2 * count + 3)(states_a.scan)

    @pl.when(u == 3 * count)
    def _():
        states_b.begin()
        z_weights.back()
        for copy in cots:
            copy.start()

    @pl.when(u == 3 * count + 1)
    def _():
        states_b.combine()
        o_weights.share()

    pl.when(u == 3 * count + 2)(states_a.settle)
    pl.when(u == 3 * count + 4)(states_a.close)

    @pl.when(u == 5 * count - 3)
    def _():
        states_b.scan()
        o_weights.back()

    for which in range(2):
        lo = (which + 1) * count
        outs = (ci_a, co_a, val_a, pre_a, cum_a, lin_a, kb_a, ck_a, tot_a, kout_a, par_a, dtp_a)
        weights = (x_own, xn, small_s, small_n)
        maps_in, maps_out = (ci_bc.at[rows], bc, taps_bc, bias_bc), (co_bc, bmat.at[rows], cmat.at[rows])
        if which:
            outs = (ci_b, co_b, val_b, pre_b, cum_b, lin_b, kb_b, ck_b, tot_b, kout_b, par_b, dtp_b)
            weights = (xf, xfn, small_f, small_fn)
            maps_in, maps_out = (bmat.at[rows],), ()
        outs = outs[:2] + tuple(x.at[rows] for x in outs[2:5]) + outs[5:]

        @pl.when((u >= lo) & (u < lo + count))
        def _():
            front_step(
                which == 0, u - lo, normed.at[rows], before, *weights, age.at[rows], tril, ex,
                maps_in, *outs, maps_out, *front,
            )

    for which in range(2):
        lo = (which + 3) * count
        val, pre, cum, par, to = ((val_a, pre_a, cum_a, par_a, part_a), (val_b, pre_b, cum_b, par_b, part_b))[which]

        @pl.when((u >= lo) & (u < lo + count))
        def _():
            intra_unit(
                val.at[rows], bmat.at[rows], cmat.at[rows], age.at[rows], pre.at[rows], cum.at[rows], par, to
            )

    @pl.when(u == 5 * count - 1)
    def _():
        z_weights.finish()
        o_weights.finish()
        states_b.settle()
        for copy in cots:
            copy.wait()
        states_b.close()


def arriving_half(own, other, half=None):
    if half is None:
        return jnp.concatenate([own[...], other[...]], axis=1)
    part = own.shape[1] // 2
    cols = slice(half * part, (half + 1) * part)
    return jnp.concatenate([own[:, cols].astype(f32), other[:, cols].astype(f32)], axis=1)


def mid_kernel(
    meta, hid, normed, z0, z1, z2, z3, o0, o1, o2, o3, cot0, cot1, cot2, cot3, cmat, age, ex, red, par_a, par_b,
    part_a, part_b, val_a, val_b, cum_a, cum_b, lin_a, lin_b, kb_a, kb_b, ck_a, ck_b, arr_a, arr_other_a, arr_b, arr_other_b,
    pieces, hidc, nout, cotx, dssd, dgate, dcin, dkk_a, dkk_b,
    lout_a, lout_b, ka_a, ka_b, tot_a, tot_b, kout_a, kout_b, ggain, gskip,
    gate, dno, read, kx, ssd_s, sig_s, khi, klo, rhi, rlo, run_a, run_b, kept_a, kept_b, shuffle,
):
    i = pl.program_id(0)
    inner = nout.shape[1]
    width = inner // 2
    tiles = inner // LANES
    heads = width // HEAD_DIM
    quarter = inner // 4

    @pl.when(i == 0)
    def _():
        for ref in (run_a, run_b, ggain, gskip):
            ref[...] = jnp.zeros_like(ref)
        for ref in (kept_a, kept_b):
            ref[...] = jnp.ones_like(ref)

    me = meta[0]
    hidc[...] = hid[0]
    for k, cot in enumerate((cot0.at[0], cot1, cot2, cot3)):
        shuffle[me ^ k] = cot[...]
    cotan = jnp.concatenate([shuffle[0], shuffle[1], shuffle[2], shuffle[3]], axis=0).T
    cotx[...] = cotan
    states = []
    for half, (lin, kb, cum, arr, arr_other) in enumerate(
        ((lin_a, kb_a, cum_a, arr_a, arr_other_a), (lin_b, kb_b, cum_b, arr_b, arr_other_b))
    ):
        cols = slice(half * width, (half + 1) * width)
        hi, lo = split2(lin[0] + kb[0, 0:1] * arriving_half(arr, arr_other))
        states.append((hi, lo))
        read[:, cols] = dot(cmat[...], hi) + dot(cmat[...], lo)
        since = lax.broadcasted_iota(jnp.int32, age.shape, 0)
        kappa = jnp.where(age[...] > since, jnp.exp(cum[...]), 0.0)
        kx[:, cols] = expand(lanes_below(kappa, heads), ex[...])
    for k, (z, o) in enumerate(((z0, o0), (z1, o1), (z2, o2), (z3, o3))):
        cols = slice(k * quarter, (k + 1) * quarter)
        gate[:, cols] = dot(normed[...], z[...])
        dno[:, cols] = dot(cotan, o[...], 1, 1)

    gains = [
        (par_a if j < tiles // 2 else par_b)[5:6, (j * LANES) % width : (j * LANES) % width + LANES]
        for j in range(tiles)
    ]

    def rows_body(step, _):
        rows = pl.ds(pl.multiple_of(step * ROWS, ROWS), ROWS)
        squares = jnp.zeros((ROWS, LANES), f32)
        inners = jnp.zeros((ROWS, LANES), f32)
        for j in range(tiles):
            cols = slice(j * LANES, (j + 1) * LANES)
            part = part_a if j < tiles // 2 else part_b
            pcols = slice(cols.start % width, cols.start % width + LANES)
            ssd = part[rows, pcols] + kx[rows, cols] * read[rows, cols]
            g = gate[rows, cols]
            sig = sigmoid(g)
            gated = ssd * (g * sig)
            squares += gated * gated
            inners += gated * (dno[rows, cols] * gains[j])
            ssd_s[rows, cols] = ssd
            sig_s[rows, cols] = sig
        rg = lax.rsqrt(jnp.sum(squares, axis=1, keepdims=True) / inner + EPS)
        stat = rg * rg * (jnp.sum(inners, axis=1, keepdims=True) / inner)
        rg = jnp.broadcast_to(rg, (ROWS, LANES))
        stat = jnp.broadcast_to(stat, (ROWS, LANES))
        for j in range(tiles):
            cols = slice(j * LANES, (j + 1) * LANES)
            val = val_a if j < tiles // 2 else val_b
            pcols = slice(cols.start % width, cols.start % width + LANES)
            ssd, sig, g, d = ssd_s[rows, cols], sig_s[rows, cols], gate[rows, cols], dno[rows, cols]
            act = g * sig
            gated = ssd * act
            yhat = gated * rg
            nout[rows, cols] = (yhat * gains[j]).astype(bf16)
            ggain[:, cols] += fold8(d * yhat)
            dgated = rg * (d * gains[j] - gated * stat)
            low = (dgated * act).astype(bf16)
            dssd[rows, cols] = low
            dgate[rows, cols] = (dgated * ssd * (sig * (1.0 + g * (1.0 - sig)))).astype(bf16)
            dy = low.astype(f32)
            gskip[:, cols] += fold8(dy * val[rows, pcols].astype(f32))
            kd = kx[rows, cols] * dy
            khi[rows, cols], klo[rows, cols] = split2(kd)
            rhi[rows, cols], rlo[rows, cols] = split2(kd * read[rows, cols])
        return 0

    lax.fori_loop(0, GROUP // ROWS, rows_body, 0)
    out = hid[0].astype(f32)
    for k, o in enumerate((o0, o1, o2, o3)):
        out = out + dot(nout[:, k * quarter : (k + 1) * quarter], o[...])
    out = out.astype(bf16).T
    piece = out.shape[0] // 4
    for k in range(4):
        pieces[k] = out[k * piece : (k + 1) * piece]
    dc = None
    age_end = age[GROUP - 1 : GROUP]
    for half, (dkk, ck, cum, lout, ka, tot, kout, running, kept) in enumerate(
        (
            (dkk_a, ck_a, cum_a, lout_a, ka_a, tot_a, kout_a, run_a, kept_a),
            (dkk_b, ck_b, cum_b, lout_b, ka_b, tot_b, kout_b, run_b, kept_b),
        )
    ):
        cols = slice(half * width, (half + 1) * width)
        hi, lo = states[half]
        dkk[...] = dot(rhi[:, cols], red[...]) + dot(rlo[:, cols], red[...])
        term = dot(khi[:, cols], hi, 1, 1) + dot(khi[:, cols], lo, 1, 1) + dot(klo[:, cols], hi, 1, 1)
        dc = term if dc is None else dc + term
        own = dot(cmat[...], khi[:, cols], 0, 0) + dot(cmat[...], klo[:, cols], 0, 0)
        lout[0] = running[...]
        ka[0] = expand(lanes_below(kept[...], heads), ex[...])
        running[...] = ck[0, 0:1] * running[...] + own
        keep = jnp.where(age_end >= GROUP, jnp.exp(cum[GROUP - 1 : GROUP]), 0.0)
        kept[...] = lanes_below(jnp.broadcast_to(keep, (8, LANES)), heads) * kept[...]
        tot[...] = running[...]
        kout[...] = kept[...]
    dcin[...] = dc


def pairs_unit(val, dssd, bmat, cmat, ager, pre, cum, dvi, dbi, dci, rflow, cflow, rft):
    s = lax.broadcasted_iota(jnp.int32, (HALF, HALF), 0)
    t = lax.broadcasted_iota(jnp.int32, (HALF, HALF), 1)
    scores = dot(bmat[...], cmat[...], 1, 1)
    a0, a1 = ager[0:1, :HALF], ager[0:1, HALF:]
    gap = t - s
    m00 = (gap >= 0) & (gap <= a0)
    m11 = (gap >= 0) & (gap <= a1)
    m01 = gap + HALF <= a1
    s00 = jnp.where(m00, scores[:HALF, :HALF], 0.0)
    s11 = jnp.where(m11, scores[HALF:, HALF:], 0.0)
    s01 = jnp.where(m01, scores[:HALF, HALF:], 0.0)
    c2 = cum[...] * LOG2E
    cr = c2 - jnp.log2(softplus(pre[...]))
    c2t = c2.T
    lane = lax.broadcasted_iota(jnp.int32, (HALF, LANES), 1)
    zero = jnp.zeros((HALF, HALF), f32)
    d00, d01, d11 = zero, zero, zero
    cf0, cf1 = zero, zero
    rft[...] = jnp.zeros_like(rft)
    for j in range(val.shape[1] // LANES):
        cols = slice(j * LANES, (j + 1) * LANES)
        v = val[:, cols]
        dy = dssd[:, cols]
        vm = pair_masks(v, v.shape)
        dm = pair_masks(dy, dy.shape)
        tops, bottoms = [], []
        for which in range(2):
            h = 2 * j + which
            col0 = jnp.broadcast_to(cr[:HALF, h : h + 1], (HALF, HALF))
            col1 = jnp.broadcast_to(cr[HALF:, h : h + 1], (HALF, HALF))
            r0 = c2t[h : h + 1, :HALF]
            r1 = c2t[h : h + 1, HALF:]
            e00 = jnp.exp2(jnp.minimum(r0 - col0, 60.0))
            e01 = jnp.exp2(r1 - col0)
            e11 = jnp.exp2(jnp.minimum(r1 - col1, 60.0))
            tops.append((s00 * e00).astype(bf16))
            tops.append((s01 * e01).astype(bf16))
            bottoms.append((s11 * e11).astype(bf16))
            w0 = dot(vm[which][:HALF], dy, 1, 1)
            w1 = dot(vm[which][HALF:], dy[HALF:], 1, 1)
            de00 = w0[:, :HALF] * e00
            de01 = w0[:, HALF:] * e01
            de11 = w1 * e11
            d00 += de00
            d01 += de01
            d11 += de11
            f00 = de00 * s00
            f01 = de01 * s01
            f11 = de11 * s11
            rft[h : h + 1, :HALF] = jnp.sum(f00, axis=0, keepdims=True)
            rft[h : h + 1, HALF:] = jnp.sum(f01 + f11, axis=0, keepdims=True)
            cf0 = jnp.where(lane == h, jnp.sum(f00 + f01, axis=1, keepdims=True), cf0)
            cf1 = jnp.where(lane == h, jnp.sum(f11, axis=1, keepdims=True), cf1)
        dvi[:HALF, cols] = dot(jnp.concatenate(tops, axis=1), jnp.concatenate([dm[0], dm[1]], axis=0))
        dvi[HALF:, cols] = dot(
            jnp.concatenate(bottoms, axis=1), jnp.concatenate([dm[0][HALF:], dm[1][HALF:]], axis=0)
        )
    cflow[:HALF] = cf0
    cflow[HALF:] = cf1
    rflow[...] = rft[...].T
    d00 = split2(jnp.where(m00, d00, 0.0))
    d01 = split2(jnp.where(m01, d01, 0.0))
    d11 = split2(jnp.where(m11, d11, 0.0))
    b0, b1, c0, c1 = bmat[:HALF], bmat[HALF:], cmat[:HALF], cmat[HALF:]
    dbi[:HALF] = dot(d00[0], c0) + dot(d00[1], c0) + dot(d01[0], c1) + dot(d01[1], c1)
    dbi[HALF:] = dot(d11[0], c1) + dot(d11[1], c1)
    dci[:HALF] = dot(d00[0], b0, 0, 0) + dot(d00[1], b0, 0, 0)
    dci[HALF:] = (
        dot(d01[0], b0, 0, 0) + dot(d01[1], b0, 0, 0) + dot(d11[0], b1, 0, 0) + dot(d11[1], b1, 0, 0)
    )


def outer_kernel(
    n, parts, count, tiles, normed, cotx, dgate, nout,
    val_a, val_b, dssd, bmat, cmat, ager, pre_a, pre_b, cum_a, cum_b, tot_a, tot_b, k_a, k_b, ex,
    dvi_a, dbi_a, dci_a, rflow_a, cflow_a, dvi_b, dbi_b, dci_b, rflow_b, cflow_b, own, other, share, zo,
    rft, keep, send, got, far_out, far_in, sems, *scratch
):
    u = pl.program_id(0)
    v = u - 4 * tiles
    states = Exchange(True, n, parts, (tot_a, tot_b), (k_a, k_b), ex, own, other, scratch[5:])
    sums = PairScatter(n, scratch[:5])
    share_rows = zo.shape[0] // n
    across = lax.rem(lax.axis_index("head") + 2, 4)

    def trade(src, dst, sem, head):
        return pltpu.make_async_remote_copy(
            src_ref=src,
            dst_ref=dst,
            send_sem=sems.at[0, sem],
            recv_sem=sems.at[1, sem],
            device_id={"head": head},
            device_id_type=MESH,
        )

    def swap(half, m):
        return trade(send.at[half, m], got.at[half, m], 2 * half + m, states.partner)

    def cross(m):
        return trade(far_out.at[m], far_in.at[m], 4 + m, across)

    def cross_after(m):
        swap(0, m).wait()
        far_out[m] = (keep[0, m] + got[0, m].astype(f32)).astype(bf16)
        cross(m).start()

    @pl.when(u == 0)
    def _():
        meet([states.partner, across], n)
        states.begin()


    @pl.when(u == tiles)
    def _():
        swap(0, 0).start()

    @pl.when(u == 2 * tiles)
    def _():
        swap(0, 1).start()
        cross_after(0)

    @pl.when(u == 3 * tiles)
    def _():
        swap(1, 0).start()
        states.scan()
        cross_after(1)

    @pl.when(v == 0)
    def _():
        swap(1, 1).start()

    part = keep.shape[3]
    rows = pl.ds(pl.multiple_of(lax.rem(u, tiles) * GROUP, GROUP), GROUP)
    for m, (a, b) in enumerate(((normed, dgate), (cotx, nout))):

        @pl.when((v < 0) & (lax.rem(u // tiles, 2) == m))
        def _():
            res = dot(a[...], b[...], 0, 0)
            half = u // (2 * tiles)
            keep[half, m, rows] = res[:, :part]
            send[half, m, rows] = res[:, part:].astype(bf16)

    @pl.when((v >= 0) & (v < count))
    def _():
        pairs_unit(val_a, dssd, bmat, cmat, ager, pre_a, cum_a, dvi_a, dbi_a, dci_a, rflow_a, cflow_a, rft)

    @pl.when(v >= count)
    def _():
        pairs_unit(val_b, dssd, bmat, cmat, ager, pre_b, cum_b, dvi_b, dbi_b, dci_b, rflow_b, cflow_b, rft)

    pl.when(u == 0)(states.combine)

    pl.when(v == 2 * count - 3)(sums.middle)

    @pl.when(v == count - 2)
    def _():
        swap(1, 0).wait()
        cross(0).wait()

        def total(s):
            at = slice(s * share_rows, (s + 1) * share_rows)
            return keep[1, 0, at] + got[1, 0, at].astype(f32) + far_in[0, at].astype(f32)

        sums.start(total)

    @pl.when(v == 2 * count - 1)
    def _():
        states.settle()
        states.close()
        swap(1, 1).wait()
        cross(1).wait()
        zo[...] = (keep[1, 1] + got[1, 1].astype(f32) + far_in[1].astype(f32)).astype(bf16)
        share[...] = sums.finish()


def slope(x):
    sig = sigmoid(x)
    return sig * (1.0 + x * (1.0 - sig))


def conv_back(i, dco, agex, age, ci, taps, dci, tail, head, gw):
    width = ci.shape[1]
    for r in range(0, GROUP, ROWS):
        ages = [agex[r + m : r + m + ROWS] for m in range(4)]
        for j in range(width // LANES):
            cols = slice(j * LANES, (j + 1) * LANES)
            c = ci[r : r + ROWS, cols].astype(f32)
            acc = None
            for m in range(4):
                x = dco[r + m : r + m + ROWS, cols]
                if m:
                    x = jnp.where(ages[m] >= m, x, 0.0)
                term = x * taps[3 - m : 4 - m, cols]
                acc = term if acc is None else acc + term
                gw[8 * (3 - m) : 8 * (3 - m) + 8, cols] += fold8(x * c)
            dci[r : r + ROWS, cols] = acc.astype(bf16)
            if r == GROUP - ROWS:

                @pl.when(i == 0)
                def _():
                    tail[:, cols] = acc[ROWS - 8 :]

    head[...] = dco[0:8]


def start_next(i, dco, agex, gw, gb):
    @pl.when(i == 0)
    def _():
        dco[GROUP : GROUP + 8] = jnp.zeros((8, dco.shape[1]), f32)
        agex[GROUP : GROUP + 8] = jnp.zeros((8, LANES), jnp.int32)
        gw[...] = jnp.zeros_like(gw)
        gb[...] = jnp.zeros_like(gb)

    @pl.when(i > 0)
    def _():
        dco[GROUP : GROUP + 8] = dco[0:8]
        agex[GROUP : GROUP + 8] = agex[0:8]


def back_step(
    half, i, val, dssd, dvi, bmat, co, ci, age, pre, cum, lout, ka, leav, leav_other, lin, kb, arr, arr_other,
    rflow, cflow, dkk, par, tril, ex, red,
    dci, tail, head, draw, gw, gb, galog, gdtb,
    dco, agex, back, omx, vhi, vlo,
):
    width = val.shape[1]
    heads = width // HEAD_DIM
    start_next(i, dco, agex, gw, gb)

    @pl.when(i == 0)
    def _():
        galog[...] = jnp.zeros_like(galog)
        gdtb[...] = jnp.zeros_like(gdtb)

    agex[0:GROUP] = age[...]
    ds = lout[0] + ka[0, 0:1] * arriving_half(leav, leav_other, half)
    dhi, dlo = split2(ds)
    back[...] = dot(bmat[...], dhi) + dot(bmat[...], dlo)
    p = pre[...]
    delta = softplus(p)
    c = cum[...]
    end = c[GROUP - 1 : GROUP]
    age_end = age[GROUP - 1 : GROUP]
    row = lax.broadcasted_iota(jnp.int32, c.shape, 0)
    tail_keep = jnp.where(GROUP - 1 - row <= age_end, jnp.exp(end - c), 0.0)
    omega = tail_keep * delta
    omx[...] = expand(lanes_below(omega, heads), ex[...])
    for r in range(0, GROUP, ROWS):
        rows = slice(r, r + ROWS)
        for j in range(width // LANES):
            cols = slice(j * LANES, (j + 1) * LANES)
            v = val[rows, cols].astype(f32)
            b = back[rows, cols]
            o = omx[rows, cols]
            dval = par[6:7, cols] * dssd[rows, cols].astype(f32) + dvi[rows, cols] + o * b
            vhi[rows, cols], vlo[rows, cols] = split2(v * b)
            d = dval * slope(co[rows, cols])
            dco[rows, cols] = d
            gb[:, cols] += fold8(d)
    domega = dot(vhi[...], red[...]) + dot(vlo[...], red[...])
    flow = domega * omega
    sin = lin[0] + kb[0, 0:1] * arriving_half(arr, arr_other)
    carry = jnp.broadcast_to(jnp.sum(ds * sin, axis=0, keepdims=True), (8, width))
    carry = dot(carry, red[...].astype(f32), precision=HIGHEST)[0:1]
    keep = jnp.where(age_end >= GROUP, jnp.exp(end), 0.0)
    dcum = rflow[...] - cflow[...] + dkk[...] - flow
    ending = jnp.sum(flow, axis=0, keepdims=True) + carry * keep
    dcum = dcum + jnp.where(row == GROUP - 1, ending, 0.0)
    dlog = dot(tril[...], dcum, 0, 0, precision=HIGHEST)
    sig = sigmoid(p)
    ratio = jnp.where(delta > 1e-30, sig / delta, 1.0)
    rate = par[7:8, 0:LANES]
    drf = cflow[...] * ratio + (domega * tail_keep + dlog * rate) * sig
    drf = lanes_below(drf, heads)
    draw[...] = drf.astype(bf16)
    gdtb[...] += fold8(drf)
    galog[...] += fold8(dlog * delta * rate)
    conv_back(i, dco, agex, age, ci, par, dci, tail, head, gw)


def maps_step(
    i, dbi_a, dbi_b, dci_a, dci_b, dcin, co, ci, age, taps,
    val_a, val_b, pre_a, pre_b, cum_a, cum_b, lout_a, lout_b, ka_a, ka_b, leav, leav_other, ex,
    dci, tail, head, gw, gb, dco, agex, dbin,
):
    start_next(i, dco, agex, gw, gb)
    agex[0:GROUP] = age[...]
    age_end = age[GROUP - 1 : GROUP]
    width = val_a.shape[1]
    row = lax.broadcasted_iota(jnp.int32, (GROUP, LANES), 0)
    total = dbi_a[...] + dbi_b[...]
    for half, (val, pre, cum, lout, ka) in enumerate(
        ((val_a, pre_a, cum_a, lout_a, ka_a), (val_b, pre_b, cum_b, lout_b, ka_b))
    ):
        dhi, dlo = split2(lout[0] + ka[0, 0:1] * arriving_half(leav, leav_other, half))
        c = cum[...]
        tail_keep = jnp.where(GROUP - 1 - row <= age_end, jnp.exp(c[GROUP - 1 : GROUP] - c), 0.0)
        omx = expand(lanes_below(tail_keep * softplus(pre[...]), width // HEAD_DIM), ex[...])
        ohi, olo = split2(omx * val[...].astype(f32))
        total = total + dot(ohi, dhi, 1, 1) + dot(ohi, dlo, 1, 1) + dot(olo, dhi, 1, 1)
    dbin[...] = total
    for r in range(0, GROUP, ROWS):
        rows = slice(r, r + ROWS)
        dc = dci_a[rows] + dci_b[rows] + dcin[rows]
        for j, d in enumerate((dbin[rows], dc)):
            cols = slice(j * LANES, (j + 1) * LANES)
            d = d * slope(co[rows, cols])
            dco[rows, cols] = d
            gb[:, cols] += fold8(d)
    conv_back(i, dco, agex, age, ci, taps, dci, tail, head, gw)


def mended(x, last, scr):
    scr[...] = x[...]

    @pl.when(pl.program_id(0) == pl.num_programs(0) - 1)
    def _():
        scr[GROUP - 16 :] = last[...]

    return scr


def padded_rows(x, rows):
    if x.shape[0] == rows:
        return x
    return jnp.concatenate([x, jnp.zeros((rows - x.shape[0], x.shape[1]), x.dtype)], axis=0)


def up16(rows):
    return (rows + 15) // 16 * 16


class Scatter:
    def __init__(self, n, scratch):
        self.n, self.me = n, lax.axis_index("seq")
        self.out, self.got, self.sems = scratch

    @staticmethod
    def scratch(n, rows, cols):
        pad = up16(rows)
        return [
            pltpu.VMEM((n, pad, cols), bf16),
            pltpu.VMEM((n, pad, cols), bf16),
            pltpu.SemaphoreType.DMA((2, n)),
        ]

    def move(self, d):
        to = lax.rem(self.me + d, self.n)
        return pltpu.make_async_remote_copy(
            src_ref=self.out.at[to],
            dst_ref=self.got.at[self.me],
            send_sem=self.sems.at[0, d],
            recv_sem=self.sems.at[1, d],
            device_id={"seq": to},
            device_id_type=MESH,
        )

    def start(self, share):
        for s in range(self.n):
            self.out[s] = padded_rows(share(s), self.out.shape[1]).astype(bf16)
        for d in range(1, self.n):
            self.move(d).start()
        self.got[self.me] = self.out[self.me]

    def finish(self):
        return self.finish_f32().astype(bf16)

    def finish_f32(self):
        for d in range(1, self.n):
            self.move(d).wait()
        total = self.got[0].astype(f32)
        for s in range(1, self.n):
            total = total + self.got[s].astype(f32)
        return total


class Gather:
    def __init__(self, n, scratch):
        self.n, self.me = n, lax.axis_index("seq")
        self.mine, self.all, self.sems = scratch

    @staticmethod
    def scratch(n, rows, cols):
        pad = up16(rows)
        return [
            pltpu.VMEM((pad, cols), bf16),
            pltpu.VMEM((n, pad, cols), bf16),
            pltpu.SemaphoreType.DMA((2, n)),
        ]

    def move(self, d):
        return pltpu.make_async_remote_copy(
            src_ref=self.mine,
            dst_ref=self.all.at[self.me],
            send_sem=self.sems.at[0, d],
            recv_sem=self.sems.at[1, d],
            device_id={"seq": lax.rem(self.me + d, self.n)},
            device_id_type=MESH,
        )

    def start(self, share):
        self.mine[...] = share
        for d in range(1, self.n):
            self.move(d).start()
        self.all[self.me] = share

    def finish(self):
        for d in range(1, self.n):
            self.move(d).wait()

    def rows(self, s, count):
        return self.all[s].astype(f32)[:count]


class PairScatter:
    def __init__(self, n, scratch):
        me = lax.axis_index("seq")
        self.n, self.m, self.odd, self.at = n, n // 2, lax.rem(me, 2), me // 2
        self.partner = me + 1 - 2 * self.odd
        self.out, self.near, self.part, self.got, self.sems = scratch

    @staticmethod
    def scratch(n, rows, cols):
        pad, m = up16(rows), n // 2
        return [
            pltpu.VMEM((2, m, pad, cols), bf16),
            pltpu.VMEM((m, pad, cols), bf16),
            pltpu.VMEM((m, pad, cols), bf16),
            pltpu.VMEM((m, pad, cols), bf16),
            pltpu.SemaphoreType.DMA((2, m)),
        ]

    def move(self, d):
        if d == 0:
            src, dst, to = self.out.at[1 - self.odd], self.near, self.partner
        else:
            to = lax.rem(self.at + d, self.m)
            src, dst, to = self.part.at[to], self.got.at[self.at], 2 * to + self.odd
        return pltpu.make_async_remote_copy(
            src_ref=src,
            dst_ref=dst,
            send_sem=self.sems.at[0, d],
            recv_sem=self.sems.at[1, d],
            device_id={"seq": to},
            device_id_type=MESH,
        )

    def start(self, share):
        for s in range(self.n):
            self.out[s % 2, s // 2] = padded_rows(share(s), self.near.shape[1]).astype(bf16)
        self.move(0).start()

    def middle(self):
        self.move(0).wait()
        for k in range(self.m):
            self.part[k] = (self.out[self.odd, k].astype(f32) + self.near[k].astype(f32)).astype(bf16)
        for d in range(1, self.m):
            self.move(d).start()
        self.got[self.at] = self.part[self.at]

    def finish(self):
        for d in range(1, self.m):
            self.move(d).wait()
        total = self.got[0].astype(f32)
        for k in range(1, self.m):
            total = total + self.got[k].astype(f32)
        return total.astype(bf16)


class PairGather:
    def __init__(self, n, scratch):
        me = lax.axis_index("seq")
        self.n, self.m, self.odd, self.at = n, n // 2, lax.rem(me, 2), me // 2
        self.partner = me + 1 - 2 * self.odd
        self.mine, self.all, self.sems = scratch

    @staticmethod
    def scratch(n, rows, cols):
        pad, m = up16(rows), n // 2
        return [
            pltpu.VMEM((pad, cols), bf16),
            pltpu.VMEM((2, m, pad, cols), bf16),
            pltpu.SemaphoreType.DMA((2, m)),
        ]

    def move(self, d):
        if d == 0:
            src, dst, to = self.all.at[self.odd], self.all.at[self.odd], self.partner
        else:
            src, dst = self.mine, self.all.at[self.odd, self.at]
            to = 2 * lax.rem(self.at + d, self.m) + self.odd
        return pltpu.make_async_remote_copy(
            src_ref=src,
            dst_ref=dst,
            send_sem=self.sems.at[0, d],
            recv_sem=self.sems.at[1, d],
            device_id={"seq": to},
            device_id_type=MESH,
        )

    def start(self, share):
        self.mine[...] = share
        for d in range(1, self.m):
            self.move(d).start()
        self.all[self.odd, self.at] = share

    def middle(self):
        for d in range(1, self.m):
            self.move(d).wait()
        self.move(0).start()

    def finish(self):
        self.move(0).wait()

    def rows(self, s, count):
        return self.all[s % 2, s // 2].astype(f32)[:count]


def mend(got, tail, ci, next_age, taps, dx, scr, last, flip):
    g = got[...]
    if flip:
        part = g.shape[1] // 2
        g = jnp.concatenate([g[:, part:], g[:, :part]], axis=1)
    rows = scr.shape[0]
    if dx is not None:
        scr[...] = dx[...]
    ending = ci[...].astype(f32)[8:16]
    row = lax.broadcasted_iota(jnp.int32, (8, LANES), 0)
    fixed, sums = [], []
    for j in range(g.shape[1] // LANES):
        cols = slice(j * LANES, (j + 1) * LANES)
        acc = tail[:, cols]
        parts = [jnp.zeros((1, LANES), f32)] * 4
        for m in range(1, 4):
            use = (row >= 8 - m) & (pltpu.roll(next_age[...], 8 - m, 0) >= m)
            x = jnp.where(use, pltpu.roll(g[:, cols], 8 - m, 0), 0.0)
            acc = acc + x * taps[3 - m : 4 - m, cols]
            parts[3 - m] = jnp.sum(x * ending[:, cols], axis=0, keepdims=True)
        fixed.append(acc)
        sums.append(jnp.concatenate(parts, axis=0))
    fixed = jnp.concatenate(fixed, axis=1)
    before = scr[rows - 16 :].astype(f32)[0:8]
    scr[rows - 16 :] = jnp.concatenate([before, fixed], axis=0).astype(bf16)
    if last is not None:
        last[...] = scr[rows - 16 :]
    return jnp.concatenate(sums, axis=1)


def small_sums(at, fix, gw, gb, galog, gdtb, gskip, ggain, red, small_keep, small_send):
    part = red.shape[0] // 2
    heads = part // HEAD_DIM
    width = 2 * part
    for to in (small_keep, small_send):
        to[...] = jnp.zeros_like(to)
    taps = [jnp.sum(gw[8 * k : 8 * k + 8], axis=0, keepdims=True) for k in range(4)]
    taps = jnp.concatenate(taps, axis=0) + fix
    bias = jnp.sum(gb[...], axis=0, keepdims=True)
    cols = slice(at * width, (at + 1) * width)
    gain = jnp.sum(ggain[:, cols], axis=0, keepdims=True)
    skip = jnp.broadcast_to(jnp.sum(gskip[:, cols], axis=0, keepdims=True), (8, width))
    skip = dot(skip, red[...].astype(f32), precision=HIGHEST)
    step = jnp.broadcast_to(jnp.sum(gdtb[...], axis=0, keepdims=True), (8, LANES))
    log = jnp.broadcast_to(jnp.sum(galog[...], axis=0, keepdims=True), (8, LANES))
    for k, to in enumerate((small_keep, small_send)):
        mine = slice(k * part, (k + 1) * part)
        to[0:4, 0:part] = taps[:, mine]
        to[4:5, 0:part] = bias[:, mine]
        to[5:6, 0:part] = gain[:, mine]
        row = jnp.zeros((8, LANES), f32)
        for place, x in enumerate((step, log, skip)):
            x = lanes_below(pltpu.roll(x, (LANES - k * heads) % LANES, 1), heads)
            row = row + pltpu.roll(x, place * heads, 1)
        to[6:7, 0:LANES] = row[0:1]


def half_tile(tile, normed, dx, draw, keep, send, small_keep, small_send):
    part = keep.shape[1]
    heads = part // HEAD_DIM
    res = dot(normed[...], dx[...], 0, 0)
    keep[...] = res[:, :part]
    send[...] = res[:, part:].astype(bf16)
    dt = dot(draw[...], normed[...], 0, 0)
    cols = pl.ds(pl.multiple_of(tile * GROUP, GROUP), GROUP)
    small_keep[8:16, cols] = dt[0:8]
    small_send[8:16, cols] = pltpu.roll(dt, LANES - heads, 0)[0:8]


def turn_kernel(n, parts, count, *refs):
    maps_in, refs = refs[:22], refs[22:]
    back_in, refs = refs[:24], refs[24:]
    (own, share, pieces), refs = refs[:3], refs[3:]
    maps_out, refs = refs[:5], refs[5:]
    back_out, refs = refs[:8], refs[8:]
    (share_out, gathered, placed), refs = refs[:3], refs[3:]
    maps_scr, refs = refs[:3], refs[3:]
    back_scr, refs = refs[:6], refs[6:]
    (piece_sems,), refs = refs[:1], refs[1:]
    u = pl.program_id(0)
    sums, shares = PairScatter(n, refs[:5]), PairGather(n, refs[5:])
    rows = own.shape[0] // n
    me = lax.axis_index("seq")
    head = lax.axis_index("head")
    near = head + 1 - 2 * lax.rem(head, 2)
    heads = [head, near, lax.rem(head + 2, 4), lax.rem(near + 2, 4)]
    chunk = pieces.shape[2]

    def piece_copy(k):
        cols = pl.ds(pl.multiple_of(lax.rem(head, parts) * chunk, chunk), chunk)
        src, dst = pieces.at[heads[k]], placed.at[head // parts, :, cols]
        if k == 0:
            return pltpu.make_async_copy(src, dst, piece_sems.at[0, 0])
        return pltpu.make_async_remote_copy(
            src_ref=src,
            dst_ref=dst,
            send_sem=piece_sems.at[0, k],
            recv_sem=piece_sems.at[1, k],
            device_id={"head": heads[k]},
            device_id_type=MESH,
        )

    @pl.when(u == 0)
    def _():
        barrier = pltpu.get_barrier_semaphore()
        for k in range(1, 4):
            pl.semaphore_signal(barrier, inc=1, device_id={"head": heads[k]}, device_id_type=MESH)
        for d in range(1, n):
            pl.semaphore_signal(barrier, inc=1, device_id={"seq": lax.rem(me + d, n)}, device_id_type=MESH)
        pl.semaphore_wait(barrier, n + 2)
        shares.start(share[...])
        sums.start(lambda s: own[s * rows : (s + 1) * rows].astype(f32))
        for k in (2, 3, 1, 0):
            piece_copy(k).start()

    @pl.when(u < count)
    def _():
        maps_step(u, *maps_in, *maps_out, *maps_scr)

    @pl.when(u >= count)
    def _():
        back_step(1, u - count, *back_in, *back_out, *back_scr)

    @pl.when(u == count - 1)
    def _():
        sums.middle()
        shares.middle()

    @pl.when(u == 2 * count - 1)
    def _():
        share_out[...] = sums.finish()
        shares.finish()
        for s in range(n):
            gathered[s * rows : (s + 1) * rows] = shares.rows(s, rows)
        for k in range(4):
            piece_copy(k).wait()


def late_kernel(n, parts, count, tiles, *refs):
    back_in, refs = refs[:24], refs[24:]
    (
        normed, dx_b, tail_b, head_b, ci_b, par_b, draw_b, gw_b, gb_b, galog_b, gdtb_b,
        dbc, tail_bc, head_bc, ci_bc, taps_bc, gw_bc, gb_bc, ci_a, next_age, gskip, ggain_out, share,
    ), refs = refs[:23], refs[23:]
    (hid, cotx, gain, dgate, z0, z1, z2, z3, bcw, x0, x1, x2, x3, dt_a, dt_b), refs = refs[:15], refs[15:]
    (grad_in, gx, gbc, small, grad_out), refs = refs[:5], refs[5:]
    back_scr, refs = refs[:6], refs[6:]
    (
        dx_a, draw_a, keep_a, send_a, small_a, small_send_a, got_a, small_got_a, last,
        tail_a, head_a, gw_a, gb_a, galog_a, gdtb_a, scr_b, scr_bc, keep_b, send_b, got_b, far_out,
        small_b, small_send_b, small_got, small_out, small_in, far_in, edge_b, edge_bc, edge_a,
        g_bc, bc_out, bc_got, bc_far_out, bc_far, bc_own, small_bc, com_got, bc_heads,
        acc_s, low, shuffle, landed, ggain, gi_got, gi_sum, edge_sems, sems, piece_sems,
    ), refs = refs[:49], refs[49:]
    u = pl.program_id(0)
    par_a, red = back_in[20], back_in[23]
    s_me = lax.axis_index("seq")
    heads = head_peers()
    h_me, near, across = heads[:3]
    half = lax.rem(h_me, parts)
    to_seq = s_me - 1 + half
    has_before = to_seq >= 0
    has_after = s_me + half < n
    chunk = count * GROUP
    part = keep_a.shape[1]
    features = gain.shape[1]
    lane_tiles = features // LANES
    first_bc, first_b, first_back, first_a = 1, tiles + 1, 2 * tiles + 1, 2 * tiles + count
    first_out = first_a + tiles
    pack_rows = -(-24 // n)
    pack = up16(4 * pack_rows + 4)
    bc_rows = features // 4
    share_rows = bc_rows // n
    gathered, gx_sum, gx_all = PairGather(n, refs[:3]), Scatter(n, refs[3:6]), Gather(n, refs[6:9])
    bc_sum, bc_all = Scatter(n, refs[9:12]), Gather(n, refs[12:15])

    def trade(src, dst, sem, head):
        return send(src, dst, sems, sem, {"head": head})

    def edge(k):
        src, dst = ((head_b, edge_b), (head_bc, edge_bc), (head_a, edge_a))[k]
        return send(src, dst, edge_sems, k, {"seq": lax.max(to_seq, 0), "head": near})

    def send_edge(k):
        pl.when(has_before)(edge(k).start)

    def take_edge(k):
        pl.when(has_before)(edge(k).wait_send)
        pl.when(has_after)(edge(k).wait_recv)

    swap_b = trade(send_b, got_b, 0, near)
    swap_small = trade(small_send_b, small_got, 1, near)
    cross_b = trade(far_out, far_in, 2, across)
    cross_small = trade(small_out, small_in, 3, across)
    swap_a = trade(send_a, got_a, 4, near)
    swap_small_a = trade(small_send_a, small_got_a, 5, near)

    swap_bc = trade(bc_out, bc_got, 6, near)
    cross_bc = trade(bc_far_out, bc_far, 7, across)

    def bc_quarter(k):
        return g_bc[pl.ds(pl.multiple_of(heads[k] * bc_rows, 8), bc_rows)]

    def common_trade(k):
        return trade(small_bc, com_got.at[k], 8 + k, heads[k])

    def heads_trade(k):
        return trade(bc_all.all, bc_heads.at[h_me], 11 + k, heads[k])

    def gi_trade(k):
        return trade(gi_sum, gi_got.at[k], 14 + k, heads[k])

    def piece_copy(step, k):
        return pltpu.make_async_remote_copy(
            src_ref=shuffle.at[step, heads[k]],
            dst_ref=landed.at[step, k],
            send_sem=piece_sems.at[0, step, k],
            recv_sem=piece_sems.at[1, step, k],
            device_id={"head": heads[k]},
            device_id_type=MESH,
        )

    def place(step, k):
        cols = pl.ds(pl.multiple_of(lax.rem(heads[k], parts) * chunk + step * GROUP, GROUP), GROUP)
        grad_in[heads[k] // parts, :, cols] = landed[step, k] if k else shuffle[step, h_me]

    @pl.when(u == 0)
    def _():
        for to in (edge_b, edge_bc, edge_a, ggain, gi_sum):
            to[...] = jnp.zeros_like(to)
        barrier = pltpu.get_barrier_semaphore()
        for head in heads[1:]:
            pl.semaphore_signal(barrier, inc=1, device_id={"head": head}, device_id_type=MESH)
        for d in range(1, n):
            pl.semaphore_signal(barrier, inc=1, device_id={"seq": lax.rem(s_me + d, n)}, device_id_type=MESH)
        other_seq = s_me - 1 + 2 * half
        has_other = (other_seq >= 0) & (other_seq < n)

        @pl.when(has_other)
        def _():
            pl.semaphore_signal(
                barrier, inc=1, device_id={"seq": other_seq, "head": near}, device_id_type=MESH
            )

        pl.semaphore_wait(barrier, n + 2 + has_other.astype(jnp.int32))
        send_edge(0)
        send_edge(1)
        gathered.start(share[...])

    block = jnp.clip(u - 2 * tiles, 0, count - 1)

    @pl.when((u == 0) | ((u >= first_back) & (u < first_a)))
    def _():
        rows = pl.ds(pl.multiple_of((count - 1 - block) * GROUP, GROUP), GROUP)
        outs = (dx_a.at[rows], tail_a, head_a, draw_a.at[rows], gw_a, gb_a, galog_a, gdtb_a)
        back_step(0, block, *back_in, *outs, *back_scr)

    @pl.when(u == first_bc)
    def _():
        take_edge(1)
        fix = mend(edge_bc, tail_bc, ci_bc, next_age, taps_bc, dbc, scr_bc, None, False)
        small_bc[...] = jnp.zeros_like(small_bc)
        sums = [jnp.sum(gw_bc[8 * k : 8 * k + 8], axis=0, keepdims=True) for k in range(4)]
        small_bc[0:4] = jnp.concatenate(sums, axis=0) + fix
        small_bc[4:5] = jnp.sum(gb_bc[...], axis=0, keepdims=True)
        for k in range(1, 4):
            common_trade(k).start()

    @pl.when((u >= first_bc) & (u < first_b))
    def _():
        rows = pl.ds(pl.multiple_of((u - first_bc) * GROUP, GROUP), GROUP)
        g_bc[rows] = dot(normed[...], scr_bc[...], 0, 0)

    @pl.when(u == first_b)
    def _():
        bc_out[0] = bc_quarter(1).astype(bf16)
        bc_out[1] = bc_quarter(3).astype(bf16)
        swap_bc.start()
        take_edge(0)
        fix = mend(edge_b, tail_b, ci_b, next_age, par_b, dx_b, scr_b, None, True)
        small_sums(1, fix, gw_b, gb_b, galog_b, gdtb_b, gskip, ggain_out, red, small_b, small_send_b)

    @pl.when(u == first_b + 1)
    def _():
        swap_bc.wait()
        bc_far_out[...] = (bc_quarter(2) + bc_got[1].astype(f32)).astype(bf16)
        cross_bc.start()
        gathered.middle()

    @pl.when((u >= first_b) & (u < first_back))
    def _():
        rows = pl.ds(pl.multiple_of((u - first_b) * GROUP, GROUP), GROUP)
        half_tile(u - first_b, normed, scr_b, draw_b, keep_b.at[rows], send_b.at[rows], small_b, small_send_b)

    @pl.when(u == first_back)
    def _():
        swap_b.start()
        swap_small.start()
        cross_bc.wait()
        bc_own[...] = bc_quarter(0) + bc_got[0].astype(f32) + bc_far[...].astype(f32)
        bc_sum.start(lambda s: bc_own[s * share_rows : (s + 1) * share_rows])

    @pl.when(u == first_back + 1)
    def _():
        swap_b.wait()
        far_out[...] = (keep_b[...] + got_b[...].astype(f32)).astype(bf16)
        cross_b.start()
        swap_small.wait()
        small_out[...] = small_b[...] + small_got[...]
        cross_small.start()
        bc_all.start(bc_sum.finish())

    @pl.when(u == first_back + 2)
    def _():
        bc_all.finish()
        for k in range(1, 4):
            heads_trade(k).start()
        bc_heads[h_me] = bc_all.all[...]

    @pl.when(u == first_a)
    def _():
        send_edge(2)
        gathered.finish()
        rows = grad_out.shape[1] // n
        grad_out[...] = jnp.concatenate([gathered.rows(s, rows) for s in range(n)], axis=0).T
        take_edge(2)
        fix = mend(edge_a, tail_a, ci_a, next_age, par_a, None, dx_a, None, True)
        small_sums(0, fix, gw_a, gb_a, galog_a, gdtb_a, gskip, ggain_out, red, small_a, small_send_a)

    @pl.when((u >= first_a) & (u < first_out))
    def _():
        rows = pl.ds(pl.multiple_of((u - first_a) * GROUP, GROUP), GROUP)
        half_tile(u - first_a, normed, dx_a, draw_a, keep_a.at[rows], send_a.at[rows], small_a, small_send_a)

    def halves_of(x):
        x = jnp.concatenate([x[:, :part], x[:, part:]], axis=0)
        hi = x.astype(bf16).astype(f32)
        return jnp.concatenate([hi, x - hi], axis=0)

    def joined(x, rows):
        x = x[0 : 2 * rows] + x[2 * rows : 4 * rows]
        return jnp.concatenate([x[:rows], x[rows:]], axis=1)

    @pl.when(u == first_out - 1)
    def _():
        swap_a.start()
        swap_small_a.start()

    @pl.when(u == first_out)
    def _():
        cross_small.wait()
        both = small_bc[...]
        for k in range(1, 4):
            common_trade(k).wait()
            both = both + com_got[k]
        both = jnp.concatenate([both, jnp.zeros((8, features - 2 * LANES), f32)], axis=1)
        cross_b.wait()
        swap_small_a.wait()
        both = jnp.concatenate([small_a[...] + small_got_a[...] + small_in[...], both], axis=0)
        swap_a.wait()
        rows = features // n

        def gx_share(s):
            at = slice(s * rows, (s + 1) * rows)
            x = keep_a[at] + got_a[at].astype(f32) + far_in[at].astype(f32)
            if s * pack_rows < 24:
                x = jnp.concatenate([x, halves_of(both[s * pack_rows : (s + 1) * pack_rows])], axis=0)
            return x

        gx_sum.start(gx_share)

    @pl.when(u >= first_out)
    def _():
        step = u - first_out
        at = pl.ds(pl.multiple_of(step * GROUP, GROUP), GROUP)
        acc = dot(scr_bc[at], bcw[...], 1, 1) + dot(draw_a[at], dt_a[...]) + dot(draw_b[at], dt_b[...])
        for k, (z, x) in enumerate(((z0, x0), (z1, x1), (z2, x2), (z3, x3))):
            d, col = (dx_a if k < 2 else scr_b), (k % 2) * part
            acc = acc + dot(dgate[:, k * part : (k + 1) * part], z[...], 1, 1)
            acc = acc + dot(d[at, col : col + part], x[...], 1, 1)
        acc_s[...] = acc
        piece = features // 4
        for r in range(0, GROUP, ROWS):
            rows = slice(r, r + ROWS)
            x = hid[rows].astype(f32)
            rinv = lax.rsqrt(jnp.sum(x * x, axis=1, keepdims=True) / x.shape[1] + EPS)
            xhat = x * rinv
            d = acc_s[rows]
            ggain[...] += fold8(d * xhat)
            dxh = d * gain[0:1]
            mean = jnp.sum(dxh * xhat, axis=1, keepdims=True) / x.shape[1]
            low[rows] = (cotx[rows].astype(f32) + rinv * (dxh - xhat * mean)).astype(bf16)
        turned = low[...].T
        for k in range(4):
            shuffle[step, k] = turned[k * piece : (k + 1) * piece]
        for k in (2, 3, 1):
            piece_copy(step, k).start()

    @pl.when(u == first_out + count - 1)
    def _():
        rows = features // n
        small_at = rows + 4 * pack_rows
        total = gx_sum.finish_f32()
        sums = halves_of(joined(total[rows:], pack_rows))
        row = halves_of(jnp.sum(ggain[...], axis=0, keepdims=True))
        gx_all.start(padded_rows(jnp.concatenate([total[:rows], sums, row], axis=0), total.shape[0]).astype(bf16))
        for k in range(1, 4):
            heads_trade(k).wait()
        for q in range(4):
            for s in range(n):
                at = (q * n + s) * share_rows
                gbc[at : at + share_rows] = bc_heads[q, s].astype(f32)[:share_rows]
        for step in range(count):
            for k in range(4):
                if k:
                    piece_copy(step, k).wait()
                place(step, k)
        gx_all.finish()
        row = joined(gx_all.rows(0, small_at + 4)[small_at:], 1)
        for s in range(1, n):
            row = row + joined(gx_all.rows(s, small_at + 4)[small_at:], 1)
        for t in range(lane_tiles):
            gi_sum[t : t + 1] = row[:, t * LANES : (t + 1) * LANES]
        for k in range(1, 4):
            gi_trade(k).start()
        for s in range(n):
            share_s = gx_all.rows(s, small_at)
            gx[s * rows : (s + 1) * rows] = share_s[:rows]
            if s * pack_rows < 24:
                small[s * pack_rows : (s + 1) * pack_rows] = joined(share_s[rows:], pack_rows)
        total = gi_sum[...]
        for k in range(1, 4):
            gi_trade(k).wait()
            total = total + gi_got[k]
        for t in range(lane_tiles):
            small[24:32, t * LANES : (t + 1) * LANES] = jnp.broadcast_to(total[t : t + 1], (8, LANES))


def unpack_kernel(
    quarter, heads, me, small, *refs
):
    large, refs = refs[:6], refs[6:]
    (gi, dt, taps, bias, maps, maps_bias, step, log, skip, gain), refs = refs[:10], refs[10:]
    for a, b in zip(large, refs):
        b[...] = a[...]
    features = small.shape[1]
    piece = gi.shape[1]
    row = pltpu.roll(small[24:32], lax.rem(features - me[0] * piece, features), 1)
    gi[...] = row[0:1, :piece]
    dt[...] = small[8 : 8 + heads]
    taps[...] = small[0:4, :quarter]
    for k in range(quarter // LANES):
        cols = slice(k * LANES, (k + 1) * LANES)
        bias[k : k + 1] = small[4:5, cols]
        gain[k : k + 1] = small[5:6, cols]
    maps[...] = small[16:20, : 2 * LANES]
    maps_bias[...] = small[20:21, : 2 * LANES]
    row = jnp.broadcast_to(small[6:7, 0:LANES], (8, LANES))
    for k, to in enumerate((step, log, skip)):
        to[...] = pltpu.roll(row, LANES - k * heads, 1)[0:1, :heads] if k else row[0:1, :heads]


def shards(
    hidden_in,
    output_cotangent,
    input_norm_scale_gain,
    z_proj,
    x_proj,
    bc_proj,
    dt_proj,
    conv_x_weight,
    conv_x_bias,
    conv_bc_weight,
    conv_bc_bias,
    dt_bias,
    a_log,
    d_skip,
    out_norm_gain,
    out_proj,
    doc_starts,
):
    batch, tokens, features = hidden_in.shape
    quarter = z_proj.shape[1]
    width = 2 * quarter
    inner = 4 * quarter
    heads = dt_proj.shape[1]
    seqs = lax.axis_size("seq")
    head_devices = lax.axis_size("head")
    parts = head_devices // batch
    chunk = tokens // parts
    count = chunk // GROUP
    si, hi_ = lax.axis_index("seq"), lax.axis_index("head")
    seq_of, half = hi_ // parts, hi_ % parts
    meta = jnp.reshape(hi_, (1,)).astype(jnp.int32)

    here = lambda i, *_: (i, 0)
    here3 = lambda i, *_: (i, 0, 0)
    rev = lambda i, *_: (count - 1 - i, 0)
    rev3 = lambda i, *_: (count - 1 - i, 0, 0)
    rev_hid = lambda i, m: (m[0] // parts, lax.rem(m[0], parts) * count + count - 1 - i, 0)
    taps_bc = conv_bc_weight.T
    lane_block = (GROUP, LANES)
    map_block = (GROUP, 2 * LANES)
    wide = (GROUP, inner)
    half_in = (GROUP, width)
    state_block = (1, LANES, width)
    keep_block = (1, 8, width)
    piece = features // head_devices
    ex, red = expansion(width)
    tril = jnp.asarray(np.tril(np.ones((GROUP, GROUP), np.float32)))
    cotangent = jnp.swapaxes(output_cotangent, 1, 2)

    def whole(*arrays):
        return [(a, None, None) for a in arrays]

    by_lanes = lambda x: x.reshape(-1, LANES)
    head_vecs = jnp.pad(jnp.concatenate([dt_bias, a_log, d_skip]), (0, LANES - 3 * heads))[None]
    front_scratch = [
        pltpu.VMEM((GROUP + 8, width), f32),
        pltpu.VMEM((LANES, width), f32),
        pltpu.VMEM((8, LANES), f32),
        pltpu.VMEM(half_in, f32),
        pltpu.VMEM(half_in, bf16),
        pltpu.VMEM(half_in, bf16),
        pltpu.VMEM((LANES, features), f32),
        pltpu.VMEM((GROUP + 8, 2 * LANES), f32),
    ]

    def front_outs(block, block3):
        return [
            ((chunk, width), bf16, half_in, block),
            ((chunk, width), f32, half_in, block),
            ((chunk, width), bf16, half_in, block),
            ((chunk, LANES), f32, lane_block, block),
            ((chunk, LANES), f32, lane_block, block),
            ((count, LANES, width), f32, state_block, block3),
            ((count, 8, width), f32, keep_block, block3),
            ((count, 8, width), f32, keep_block, block3),
            ((LANES, width), f32, None, None),
            ((8, LANES), f32, None, None),
            ((8, width), f32, None, None),
            ((LANES, features), bf16, None, None),
        ]

    own_head = lambda: lax.axis_index("head")
    x_shape = (features, quarter)

    def phase(k, rank):
        at = lambda u: jnp.clip(u - k * count, 0, count - 1)
        return (lambda u: (at(u), 0)) if rank == 2 else (lambda u: (at(u), 0, 0))

    def front_outs(k):
        return [
            ((chunk, width), bf16, half_in, phase(k, 2)),
            ((chunk, width), f32, half_in, phase(k, 2)),
            ((chunk, width), bf16, None, None),
            ((chunk, LANES), f32, None, None),
            ((chunk, LANES), f32, None, None),
            ((count, LANES, width), f32, state_block, phase(k, 3)),
            ((count, 8, width), f32, keep_block, phase(k, 3)),
            ((count, 8, width), f32, keep_block, phase(k, 3)),
            ((8, width), f32, None, None),
            ((LANES, features), bf16, None, None),
            ((LANES, quarter), f32, None, None),
            ((LANES, quarter), f32, None, None),
            ((chunk, width), f32, half_in, phase(k + 2, 2)),
        ]

    front_names = ("ci", "co", "val", "pre", "cum", "lin", "kb", "ck", "par", "dtp", "own", "other", "part")
    outs = run(
        functools.partial(forward_kernel, seqs, parts, count),
        (5 * count,),
        [
            (
                hidden_in,
                (1, GROUP, features),
                lambda u: (own_head() // parts, lax.rem(own_head(), parts) * count + jnp.minimum(u, count - 1), 0),
            ),
            (hidden_in, (1, 16, features), lambda u: (own_head() // parts, tokens // 16 - 1, 0)),
            (hidden_in, (1, 16, features), lambda u: (own_head() // parts, chunk // 16 - 1, 0)),
            *whole(doc_starts, by_lanes(conv_x_bias), by_lanes(out_norm_gain), head_vecs),
            *whole(by_lanes(input_norm_scale_gain), by_lanes(conv_bc_bias), conv_x_weight.T, dt_proj.T, x_proj, z_proj, out_proj, bc_proj, taps_bc, tril, ex),
            (cotangent, pl.ANY, None),
        ],
        [
            ((chunk, features), bf16, None, None),
            ((chunk, 2 * LANES), bf16, None, None),
            ((chunk, LANES), jnp.int32, None, None),
            ((8, chunk), jnp.int32, (8, GROUP), lambda u: (0, jnp.minimum(u, count - 1))),
            ((8, LANES), jnp.int32, None, None),
            ((8, features), f32, None, None),
        ]
        + [(x_shape, bf16, None, None)] * 6
        + [((quarter, features), bf16, None, None)] * 3
        + [((piece, chunk), bf16, pl.ANY, None)] * 3
        + [
            ((chunk, 2 * LANES), f32, map_block, phase(1, 2)),
            ((chunk, LANES), bf16, None, None),
            ((chunk, LANES), bf16, None, None),
        ]
        + front_outs(1)
        + front_outs(2),
        [
            pltpu.VMEM((8, features), f32),
            pltpu.VMEM((8, 2 * LANES), f32),
            pltpu.VMEM((16, features), bf16),
            pltpu.VMEM((16, features), bf16),
        ]
        + [pltpu.VMEM((16, features), f32)] * 4
        + [pltpu.VMEM(x_shape, bf16)] * 3
        + [pltpu.VMEM((LANES, width), f32)] * 2
        + [pltpu.VMEM((8, LANES), f32)] * 2
        + [pltpu.SemaphoreType.DMA((2, 7)), pltpu.SemaphoreType.DMA((2, 4))]
        + front_scratch
        + Weights.scratch(features, quarter)
        + Weights.scratch(quarter, features)
        + Exchange.scratch(seqs, quarter) * 2,
        flops=40_000_000_000,
        moved=50_000_000,
        collective=1,
    )
    normed, ci_bc, age, ager, next_age, gain_in = outs[:6]
    xs, zs, os_ = [x_proj, *outs[6:9]], [z_proj, *outs[9:12]], [out_proj, *outs[12:15]]
    cots = outs[15:18]
    co_bc, bmat, cmat = outs[18:21]
    ha, hb = dict(zip(front_names, outs[21:34])), dict(zip(front_names, outs[34:47]))
    halves = [ha, hb]
    for d in halves:
        d["arr"] = [d["own"], d["other"]]

    outs = run(
        mid_kernel,
        (count,),
        [
            (hidden_in, (1, GROUP, features), rev_hid),
            (normed, (GROUP, features), rev),
            *whole(*zs, *os_),
            (
                cotangent,
                (1, piece, GROUP),
                lambda i, m: (m[0] // parts, 0, lax.rem(m[0], parts) * count + count - 1 - i),
            ),
            *[(c, (piece, GROUP), lambda i, *_: (0, count - 1 - i)) for c in cots],
            (cmat, lane_block, rev),
            (age, lane_block, rev),
            *whole(ex, red, ha["par"], hb["par"]),
            *[(d["part"], half_in, rev) for d in halves],
            *[(d["val"], half_in, rev) for d in halves],
            *[(d["cum"], lane_block, rev) for d in halves],
            *[(d["lin"], state_block, rev3) for d in halves],
            *[(d["kb"], keep_block, rev3) for d in halves],
            *[(d["ck"], keep_block, rev3) for d in halves],
            *whole(*ha["arr"], *hb["arr"]),
        ],
        [
            ((4, piece, chunk), bf16, (4, piece, GROUP), lambda i, *_: (0, 0, count - 1 - i)),
            ((chunk, features), bf16, (GROUP, features), rev),
            ((chunk, inner), bf16, wide, rev),
            ((chunk, features), bf16, (GROUP, features), rev),
            ((chunk, inner), bf16, wide, rev),
            ((chunk, inner), bf16, wide, rev),
            ((chunk, LANES), f32, lane_block, rev),
            ((chunk, LANES), f32, lane_block, rev),
            ((chunk, LANES), f32, lane_block, rev),
            ((count, LANES, width), f32, state_block, rev3),
            ((count, LANES, width), f32, state_block, rev3),
            ((count, 8, width), f32, keep_block, rev3),
            ((count, 8, width), f32, keep_block, rev3),
            ((LANES, width), f32, None, None),
            ((LANES, width), f32, None, None),
            ((8, LANES), f32, None, None),
            ((8, LANES), f32, None, None),
            ((8, inner), f32, None, None),
            ((8, inner), f32, None, None),
        ],
        [pltpu.VMEM(wide, f32)] * 6
        + [pltpu.VMEM(wide, bf16)] * 4
        + [pltpu.VMEM((LANES, width), f32)] * 2
        + [pltpu.VMEM((8, LANES), f32)] * 2
        + [pltpu.VMEM((4, piece, GROUP), bf16)],
        flops=30_000_000_000,
        moved=50_000_000,
        prefetch=(meta,),
    )
    pieces, hidc, outs = outs[0], outs[1], outs[2:]
    nout, cotx, dssd, dgate, dcin, ha["dkk"], hb["dkk"], ha["lout"], hb["lout"], ha["ka"], hb["ka"] = outs[:11]
    dtot_a, dtot_b, dk_a, dk_b, ggain_out, gskip = outs[11:]

    tiles = features // GROUP
    lead = 4 * tiles
    tile_block = lambda u: (0, lax.rem(jnp.minimum(u, lead - 1), tiles))
    first_half = lambda u: (0, 1 - jnp.minimum(u // (2 * tiles), 1))
    after_lead = lambda u: jnp.maximum(u - lead, 0)
    lo_unit = lambda u: (jnp.clip(u - lead, 0, count - 1), 0)
    hi_unit = lambda u: (jnp.clip(u - lead - count, 0, count - 1), 0)
    any_unit = lambda u: (lax.rem(after_lead(u), count), 0)
    quarter_grad = (2, features, quarter)
    share_rows = features // seqs
    outs = run(
        functools.partial(outer_kernel, seqs, parts, count, tiles),
        (lead + 2 * count,),
        [
            (normed, (chunk, GROUP), tile_block),
            (cotx, (chunk, GROUP), tile_block),
            (dgate, (chunk, width), first_half),
            (nout, (chunk, width), first_half),
            (ha["val"], half_in, lo_unit),
            (hb["val"], half_in, hi_unit),
            (dssd, half_in, lambda u: (lax.rem(after_lead(u), count), after_lead(u) // count)),
            (bmat, lane_block, any_unit),
            (cmat, lane_block, any_unit),
            (ager, (8, GROUP), lambda u: (0, lax.rem(after_lead(u), count))),
            (ha["pre"], lane_block, lo_unit),
            (hb["pre"], lane_block, hi_unit),
            (ha["cum"], lane_block, lo_unit),
            (hb["cum"], lane_block, hi_unit),
            *whole(dtot_a, dtot_b, dk_a, dk_b, ex),
        ],
        [
            (shape, f32, (GROUP, shape[1]), imap)
            for imap in (lo_unit, hi_unit)
            for shape in [(chunk, width)] + [(chunk, LANES)] * 4
        ]
        + [((LANES, width), f32, None, None)] * 2
        + [((up16(share_rows), quarter), bf16, None, None), ((features, quarter), bf16, None, None)],
        [
            pltpu.VMEM((LANES, GROUP), f32),
            pltpu.VMEM((2,) + quarter_grad, f32),
            pltpu.VMEM((2,) + quarter_grad, bf16),
            pltpu.VMEM((2,) + quarter_grad, bf16),
            pltpu.VMEM(quarter_grad, bf16),
            pltpu.VMEM(quarter_grad, bf16),
            pltpu.SemaphoreType.DMA((2, 6)),
        ]
        + PairScatter.scratch(seqs, share_rows, quarter)
        + Exchange.scratch(seqs, width),
        flops=30_000_000_000,
        moved=40_000_000,
        collective=2,
    )
    names = ("dvi", "dbi", "dci_c", "rflow", "cflow")
    ha.update(zip(names, outs[:5]))
    hb.update(zip(names, outs[5:10]))
    leav = outs[10:12]
    share_z, grad_o = outs[12:]

    def back_ins(n, block, block3):
        d = halves[n]
        return [
            (d["val"], half_in, block),
            (dssd, half_in, lambda u: (block(u)[0], n)),
            (d["dvi"], half_in, block),
            (bmat, lane_block, block),
            (d["co"], half_in, block),
            (d["ci"], half_in, block),
            (age, lane_block, block),
            (d["pre"], lane_block, block),
            (d["cum"], lane_block, block),
            (d["lout"], state_block, block3),
            (d["ka"], keep_block, block3),
            *whole(*leav),
            (d["lin"], state_block, block3),
            (d["kb"], keep_block, block3),
            *whole(*d["arr"]),
            (d["rflow"], lane_block, block),
            (d["cflow"], lane_block, block),
            (d["dkk"], lane_block, block),
            *whole(d["par"], tril, ex, red),
        ]

    back_scratch = [
        pltpu.VMEM((GROUP + 8, width), f32),
        pltpu.VMEM((GROUP + 8, LANES), jnp.int32),
        pltpu.VMEM(half_in, f32),
        pltpu.VMEM(half_in, f32),
        pltpu.VMEM(half_in, bf16),
        pltpu.VMEM(half_in, bf16),
    ]

    def both_outs(cols, block):
        return [
            ((chunk, cols), bf16, (GROUP, cols), block),
            ((8, cols), f32, None, None),
            ((8, cols), f32, None, None),
        ]

    early_rev = lambda u: (count - 1 - jnp.minimum(u, count - 1), 0)
    late_rev = lambda u: (count - 1 - jnp.maximum(u - count, 0), 0)
    early_rev3 = lambda u: (count - 1 - jnp.minimum(u, count - 1), 0, 0)
    late_rev3 = lambda u: (count - 1 - jnp.maximum(u - count, 0), 0, 0)
    outs = run(
        functools.partial(turn_kernel, seqs, parts, count),
        (2 * count,),
        [
            *[(d["dbi"], lane_block, early_rev) for d in halves],
            *[(d["dci_c"], lane_block, early_rev) for d in halves],
            (dcin, lane_block, early_rev),
            (co_bc, map_block, early_rev),
            (ci_bc, map_block, early_rev),
            (age, lane_block, early_rev),
            (taps_bc, None, None),
            *[(d["val"], half_in, early_rev) for d in halves],
            *[(d["pre"], lane_block, early_rev) for d in halves],
            *[(d["cum"], lane_block, early_rev) for d in halves],
            *[(d["lout"], state_block, early_rev3) for d in halves],
            *[(d["ka"], keep_block, early_rev3) for d in halves],
            *whole(*leav, ex),
            *back_ins(1, late_rev, late_rev3),
            *whole(grad_o, share_z),
            (pieces, pl.ANY, None),
        ],
        both_outs(2 * LANES, early_rev)
        + [((32, 2 * LANES), f32, None, None), ((8, 2 * LANES), f32, None, None)]
        + both_outs(width, late_rev)
        + [
            ((chunk, LANES), bf16, lane_block, late_rev),
            ((32, width), f32, None, None),
            ((8, width), f32, None, None),
            ((8, LANES), f32, None, None),
            ((8, LANES), f32, None, None),
            ((up16(share_rows), quarter), bf16, None, None),
            ((features, quarter), f32, None, None),
            ((batch, piece, tokens), bf16, pl.ANY, None),
        ],
        [
            pltpu.VMEM((GROUP + 8, 2 * LANES), f32),
            pltpu.VMEM((GROUP + 8, LANES), jnp.int32),
            pltpu.VMEM(lane_block, f32),
        ]
        + back_scratch
        + [pltpu.SemaphoreType.DMA((2, 4))]
        + PairScatter.scratch(seqs, share_rows, quarter)
        + PairGather.scratch(seqs, share_rows, quarter),
        flops=30_000_000_000,
        moved=40_000_000,
        collective=4,
    )
    dbc, tail_bc, head_bc, gw_bc, gb_bc = outs[:5]
    hb.update(zip(("dx", "tail", "head", "draw", "gw", "gb", "galog", "gdtb"), outs[5:13]))
    share, grad_z, layer_out = outs[13:]

    steps = 3 * tiles + 2 * count
    back_unit = lambda u: (count - 1 - jnp.clip(u - 2 * tiles, 0, count - 1), 0)
    back_unit3 = lambda u: (count - 1 - jnp.clip(u - 2 * tiles, 0, count - 1), 0, 0)
    out_unit = lambda u: (jnp.clip(u - 3 * tiles - count, 0, count - 1), 0)

    def grad_tile(u):
        first = lax.rem(jnp.clip(u - 1, 0, 2 * tiles - 1), tiles)
        third = jnp.clip(u - 2 * tiles - count, 0, tiles - 1)
        later = jnp.minimum(u // (2 * tiles + count), 1)
        return 0, (1 - later) * first + later * third

    ending = lambda *_: (chunk // 16 - 1, 0)
    small_pack = (16, features)
    packed_rows = share_rows + 4 * -(-24 // seqs) + 4
    input_grad, sum2, g_bc, small_sum, grad_out = run(
        functools.partial(late_kernel, seqs, parts, count, tiles),
        (steps,),
        [
            *back_ins(0, back_unit, back_unit3),
            (normed, (chunk, GROUP), grad_tile),
            *whole(hb["dx"], hb["tail"], hb["head"]),
            (hb["ci"], (16, width), ending),
            *whole(hb["par"], hb["draw"], hb["gw"], hb["gb"], hb["galog"], hb["gdtb"]),
            *whole(dbc, tail_bc, head_bc),
            (ci_bc, (16, 2 * LANES), ending),
            *whole(taps_bc, gw_bc, gb_bc),
            (ha["ci"], (16, width), ending),
            *whole(next_age, gskip, ggain_out, share),
            (hidc, (GROUP, features), out_unit),
            (cotx, (GROUP, features), out_unit),
            (gain_in, None, None),
            (dgate, wide, out_unit),
            *whole(*zs, bc_proj, *xs, ha["dtp"], hb["dtp"]),
        ],
        [
            ((batch, piece, tokens), bf16, None, None),
            ((features, quarter), f32, None, None),
            ((features, 2 * LANES), f32, None, None),
            ((32, features), f32, None, None),
            ((quarter, features), f32, None, None),
        ],
        back_scratch
        + [
            pltpu.VMEM((chunk, width), bf16),
            pltpu.VMEM((chunk, LANES), bf16),
            pltpu.VMEM(x_shape, f32),
            pltpu.VMEM(x_shape, bf16),
            pltpu.VMEM(small_pack, f32),
            pltpu.VMEM(small_pack, f32),
            pltpu.VMEM(x_shape, bf16),
            pltpu.VMEM(small_pack, f32),
            pltpu.VMEM((16, width), bf16),
            pltpu.VMEM((8, width), f32),
            pltpu.VMEM((8, width), f32),
            pltpu.VMEM((32, width), f32),
            pltpu.VMEM((8, width), f32),
            pltpu.VMEM((8, LANES), f32),
            pltpu.VMEM((8, LANES), f32),
            pltpu.VMEM((chunk, width), bf16),
            pltpu.VMEM((chunk, 2 * LANES), bf16),
            pltpu.VMEM(x_shape, f32),
            pltpu.VMEM(x_shape, bf16),
            pltpu.VMEM(x_shape, bf16),
            pltpu.VMEM(x_shape, bf16),
        ]
        + [pltpu.VMEM(small_pack, f32)] * 5
        + [
            pltpu.VMEM(x_shape, bf16),
            pltpu.VMEM((8, width), f32),
            pltpu.VMEM((8, 2 * LANES), f32),
            pltpu.VMEM((8, width), f32),
            pltpu.VMEM((features, 2 * LANES), f32),
            pltpu.VMEM((2, features // 4, 2 * LANES), bf16),
            pltpu.VMEM((2, features // 4, 2 * LANES), bf16),
            pltpu.VMEM((features // 4, 2 * LANES), bf16),
            pltpu.VMEM((features // 4, 2 * LANES), bf16),
            pltpu.VMEM((features // 4, 2 * LANES), f32),
            pltpu.VMEM((8, 2 * LANES), f32),
            pltpu.VMEM((4, 8, 2 * LANES), f32),
            pltpu.VMEM((4, seqs, up16(features // 4 // seqs), 2 * LANES), bf16),
            pltpu.VMEM((GROUP, features), f32),
            pltpu.VMEM((GROUP, features), bf16),
            pltpu.VMEM((count, 4, piece, GROUP), bf16),
            pltpu.VMEM((count, 4, piece, GROUP), bf16),
            pltpu.VMEM((8, features), f32),
            pltpu.VMEM((4, 8, LANES), f32),
            pltpu.VMEM((8, LANES), f32),
            pltpu.SemaphoreType.DMA((2, 3)),
            pltpu.SemaphoreType.DMA((2, 18)),
            pltpu.SemaphoreType.DMA((2, count, 4)),
        ]
        + PairGather.scratch(seqs, share_rows, quarter)
        + Scatter.scratch(seqs, packed_rows, quarter)
        + Gather.scratch(seqs, packed_rows, quarter)
        + Scatter.scratch(seqs, features // 4 // seqs, 2 * LANES)
        + Gather.scratch(seqs, features // 4 // seqs, 2 * LANES),
        flops=40_000_000_000,
        moved=60_000_000,
        collective=5,
    )
    vector = lambda size: ((1, size), f32, None, None)
    large = (layer_out, input_grad, grad_z, sum2, g_bc, grad_out)

    def in_blocks(x):
        if x.ndim == 3:
            return x.shape[:2] + (x.shape[2] // 4,), lambda i, *_: (0, 0, i)
        return (x.shape[0] // 4, x.shape[1]), lambda i, *_: (i, 0)

    by_rows = ((quarter // LANES, LANES), f32, None, None)
    outs = run(
        functools.partial(unpack_kernel, quarter, heads),
        (4,),
        whole(small_sum) + [(a, *in_blocks(a)) for a in large],
        [
            vector(piece),
            ((heads, features), f32, None, None),
            ((4, quarter), f32, None, None),
            by_rows,
            ((4, 2 * LANES), f32, None, None),
            vector(2 * LANES),
            vector(heads),
            vector(heads),
            vector(heads),
            by_rows,
        ]
        + [(a.shape, a.dtype, *in_blocks(a)) for a in large],
        prefetch=(meta,),
    )
    gi, g_dt, g_taps, g_bias, g_maps, g_maps_bias, g_step, g_log, g_skip, g_gain = outs[:10]
    layer_out, input_grad, grad_z, sum2, g_bc, grad_out = outs[10:]
    return (
        jnp.swapaxes(layer_out, 1, 2),
        jnp.swapaxes(input_grad, 1, 2),
        gi[0],
        grad_z,
        sum2,
        g_bc,
        g_dt.T,
        g_taps.T,
        g_bias.reshape(quarter),
        g_maps.T,
        g_maps_bias[0],
        g_step[0],
        g_log[0],
        g_skip[0],
        g_gain.reshape(quarter),
        grad_out,
    )


def solution(mesh):
    return jax.shard_map(
        shards,
        mesh=mesh,
        in_specs=(
            P(None, "seq", None),
            P(None, "seq", "head"),
            P(),
            P(None, "head"),
            P(None, "head"),
            P(),
            P(None, "head"),
            P("head", None),
            P("head"),
            P(),
            P(),
            P("head"),
            P("head"),
            P("head"),
            P("head"),
            P("head", None),
            P(),
        ),
        out_specs=(
            P(None, "seq", "head"),
            P(None, "seq", "head"),
            P("head"),
            P(None, "head"),
            P(None, "head"),
            P(),
            P(None, "head"),
            P("head", None),
            P("head"),
            P(),
            P(),
            P("head"),
            P("head"),
            P("head"),
            P("head"),
            P("head", None),
        ),
        check_vma=False,
    )
```
